32 devices in a mesh: dp: 8 (over y, x, core), section: 4 (over z).
Axes of the slice: x: 2, y: 2, z: 4, core: 2. Of those that a mesh axis runs over, the one named last changes fastest.
Arguments:
- clean_lat: float32 [8, 16, 256, 8], P('dp', None, 'section'), may hold values from -6 to 6
- noise_lat: float32 [8, 16, 256, 8], P('dp', None, 'section'), may hold values from -6 to 6
- column_ids: int32 [8, 256], P('dp'), may hold values from 0 to 4, as said below
- timesteps: int32 [8, 4], P('dp'), may hold values from 0 to 999
- clap_emb: float32 [8, 4, 512], P('dp'), may hold values from -6 to 6
- conv_w: float32 [2, 2304, 256], P(None, 'dp'), may hold values from -0.125 to 0.125
- proj_w: float32 [256, 2048], P(None, 'dp')
- film_w: float32 [512, 512], P(None, 'dp'), may hold values from -0.25 to 0.25
- skip_w: float32 [512, 256], P(None, 'dp'), may hold values from -0.25 to 0.25
- down_w: float32 [1024, 256], P('dp'), may hold values from -0.1875 to 0.1875
- stem_w: float32 [72, 256], P(None, 'dp'), may hold values from -0.75 to 0.75
- head_w: float32 [2304, 8], P('dp'), may hold values from -0.125 to 0.125
- gains: float32 [8, 256], P(None, 'dp'), may hold values from 0.5 to 1.5
- conv_m: float32 [2, 2304, 256], P(None, 'dp'), may hold values from -7.6293945e-06 to 7.6293945e-06
- proj_m: float32 [256, 2048], P(None, 'dp'), may hold values from -7.6293945e-06 to 7.6293945e-06
- film_m: float32 [512, 512], P(None, 'dp'), may hold values from -7.6293945e-06 to 7.6293945e-06
- skip_m: float32 [512, 256], P(None, 'dp'), may hold values from -7.6293945e-06 to 7.6293945e-06
- down_m: float32 [1024, 256], P('dp'), may hold values from -7.6293945e-06 to 7.6293945e-06
- stem_m: float32 [72, 256], P(None, 'dp'), may hold values from -7.6293945e-06 to 7.6293945e-06
- head_m: float32 [2304, 8], P('dp'), may hold values from -7.6293945e-06 to 7.6293945e-06
- gains_m: float32 [8, 256], P(None, 'dp'), may hold values from -9.1552734e-05 to 9.1552734e-05
- conv_v: float32 [2, 2304, 256], P(None, 'dp'), may hold values from 1.6679121e-13 to 6.6716484e-13
- proj_v: float32 [256, 2048], P(None, 'dp'), may hold values from 1.6679121e-13 to 6.6716484e-13
- film_v: float32 [512, 512], P(None, 'dp'), may hold values from 1.6679121e-13 to 6.6716484e-13
- skip_v: float32 [512, 256], P(None, 'dp'), may hold values from 1.6679121e-13 to 6.6716484e-13
- down_v: float32 [1024, 256], P('dp'), may hold values from 1.6679121e-13 to 6.6716484e-13
- stem_v: float32 [72, 256], P(None, 'dp'), may hold values from 1.6679121e-13 to 6.6716484e-13
- head_v: float32 [2304, 8], P('dp'), may hold values from 1.6679121e-13 to 6.6716484e-13
- gains_v: float32 [8, 256], P(None, 'dp'), may hold values from 1.667912e-11 to 6.671648e-11
Outputs:
- conv_new: float32 [2, 2304, 256], P(None, 'dp')
- proj_new: float32 [256, 2048], P(None, 'dp')
- film_new: float32 [512, 512], P(None, 'dp')
- skip_new: float32 [512, 256], P(None, 'dp')
- down_new: float32 [1024, 256], P('dp')
- stem_new: float32 [72, 256], P(None, 'dp')
- head_new: float32 [2304, 8], P('dp')
- gains_new: float32 [8, 256], P(None, 'dp')
- conv_m_new: float32 [2, 2304, 256], P(None, 'dp')
- proj_m_new: float32 [256, 2048], P(None, 'dp')
- film_m_new: float32 [512, 512], P(None, 'dp')
- skip_m_new: float32 [512, 256], P(None, 'dp')
- down_m_new: float32 [1024, 256], P('dp')
- stem_m_new: float32 [72, 256], P(None, 'dp')
- head_m_new: float32 [2304, 8], P('dp')
- gains_m_new: float32 [8, 256], P(None, 'dp')
- conv_v_new: float32 [2, 2304, 256], P(None, 'dp')
- proj_v_new: float32 [256, 2048], P(None, 'dp')
- film_v_new: float32 [512, 512], P(None, 'dp')
- skip_v_new: float32 [512, 256], P(None, 'dp')
- down_v_new: float32 [1024, 256], P('dp')
- stem_v_new: float32 [72, 256], P(None, 'dp')
- head_v_new: float32 [2304, 8], P('dp')
- gains_v_new: float32 [8, 256], P(None, 'dp')
- grad_norm: float32 [], replicated
- loss_sum: float32 [], replicated
- pix_count: float32 [], replicated
The draws below stay inside these ranges and needn't reach their ends.
Inputs may be any that keep to these rules, and one draw needn't show every extreme that they name: `column_ids`: along a row the ids never fall: 4 clips of one or more columns in order, then one or more padding columns marked 4.
All inputs are finite; a program needn't handle non-finite values.
Results may differ from the reference program's by a relative error of at most 0.00095.
The reference program's roundings to bfloat16 on the way count: a program that leaves them out, or rounds other values in their place, can miss the bound.
Values may be sent and summed in bfloat16 or wider, within the bound.
A program may use at most 192 MiB of HBM per device.

```python
import math
import jax
import jax.numpy as jnp
from jax import lax

F = 16
CIN = 8
C = 256
HEADS = 8
HD = 32
MLP = 1024
COND = 512
GROUPS = 32
CLIPS = 4
STEP = 10
W = 256
PIX_ROW = 4096
BATCH = 8
PARAMS = 2398208


def draw_column_ids(key, part):
    key = jax.random.fold_in(key, 3)
    sub_keys = jax.random.split(key, 3)
    low_len = max(1, W // 64)
    high_len = max(2, W // 32)
    shorts = jax.random.randint(sub_keys[0], (BATCH, CLIPS - 1), low_len, high_len)
    pads = jax.random.randint(sub_keys[1], (BATCH, 1), 1, high_len)
    long_slot = jax.random.randint(sub_keys[2], (BATCH, 1), 0, CLIPS)
    longest = W - jnp.sum(shorts, axis=1, keepdims=True) - pads
    slot_idx = jnp.arange(CLIPS)[None, :]
    short_pick = jnp.clip(slot_idx - (slot_idx > long_slot).astype(jnp.int32), 0, CLIPS - 2)
    lengths = jnp.where(slot_idx == long_slot, longest, jnp.take_along_axis(shorts, short_pick, axis=1))
    clip_ends = jnp.cumsum(lengths, axis=1)
    column = jnp.arange(W)
    return jnp.sum((clip_ends[:, None, :] <= column[None, :, None]).astype(jnp.int32), axis=2)


def draw_proj_w(key, part):
    key = jax.random.fold_in(key, 7)
    normal_draw = jax.random.normal(key, (C, 4 * C + MLP), jnp.float32)
    column = jnp.arange(4 * C + MLP)
    boost = jnp.where((column >= 3 * C) & (column < 4 * C), PIX_ROW ** 0.5 / 8.0, 1.0)
    return normal_draw * (boost * C ** (-0.5))[None, :]


def place_ends(drawn, own_key, smallest, largest):
    dims = drawn.shape
    place = [jax.random.randint(jax.random.fold_in(own_key, axis), (), 0, dims[axis]) for axis in range(len(dims))]
    drawn = drawn.at[tuple(place)].set(smallest)
    longest = dims.index(max(dims))
    place[longest] = (place[longest] + 1) % dims[longest]
    return drawn.at[tuple(place)].set(largest)


def level_of(key, dims, pieces, low, largest):
    gain, own = 1.0, jax.random.fold_in(key, 6)
    for axis_at, blocks in pieces:
        draws = jnp.exp(jax.random.uniform(jax.random.fold_in(own, axis_at), (blocks,), jnp.float32, low / len(pieces), largest / len(pieces)))
        gain = gain * jnp.repeat(draws, dims[axis_at] // blocks).reshape([-1 if axis == axis_at else 1 for axis in range(len(dims))])
    return gain


def normal_values(stream_key, dims, deviation, reach, cuts=(), held_as=jnp.bfloat16):
    drawn = deviation * jax.random.normal(stream_key, dims, jnp.float32)
    if cuts:
        drawn = drawn * level_of(stream_key, dims, cuts, -0.22, 0.18)
    return jnp.clip(drawn, -reach, reach).astype(held_as)


def setup_inputs(seed: int = 0) -> dict:
    streams_of = jax.random.split(jax.random.key(seed), 30)
    clean_lat = normal_values(streams_of[0], (BATCH, F, W, CIN), 1.0, 6.0, ((0, 8), (2, 4)), jnp.float32)
    noise_lat = normal_values(streams_of[1], (BATCH, F, W, CIN), 1.0, 6.0, ((0, 8), (2, 4)), jnp.float32)
    column_ids = draw_column_ids(jax.random.fold_in(streams_of[29], 71), 0)
    timesteps = place_ends(jax.random.randint(streams_of[3], (BATCH, CLIPS), 0, 1000), jax.random.fold_in(streams_of[3], 1), 0, 999).astype(jnp.int32)
    clap_emb = normal_values(streams_of[4], (BATCH, CLIPS, COND), 1.0, 6.0, ((0, 8),), jnp.float32)
    conv_w = normal_values(streams_of[5], (2, 9 * C, C), (9 * C) ** -0.5, 0.125, ((1, 8),), jnp.float32)
    proj_w = draw_proj_w(jax.random.fold_in(streams_of[29], 71), 0)
    film_w = normal_values(streams_of[7], (COND, 2 * C), COND ** -0.5, 0.25, ((1, 8),), jnp.float32)
    skip_w = normal_values(streams_of[8], (2 * C, C), (2 * C) ** -0.5, 0.25, ((1, 8),), jnp.float32)
    down_w = normal_values(streams_of[9], (MLP, C), MLP ** -0.5, 0.1875, ((0, 8),), jnp.float32)
    stem_w = normal_values(streams_of[10], (9 * CIN, C), (9 * CIN) ** -0.5, 0.75, ((1, 8),), jnp.float32)
    head_w = normal_values(streams_of[11], (9 * C, CIN), (9 * C) ** -0.5, 0.125, ((0, 8),), jnp.float32)
    gains = jnp.clip(1.0 + 0.1 * jax.random.normal(streams_of[12], (8, C), jnp.float32), 0.5, 1.5)
    conv_m = normal_values(streams_of[13], (2, 9 * C, C), (0.0022 / PARAMS ** 0.5), 7.62939453125e-06, ((1, 8),), jnp.float32)
    proj_m = normal_values(streams_of[14], (C, 4 * C + MLP), (0.0022 / PARAMS ** 0.5), 7.62939453125e-06, ((1, 8),), jnp.float32)
    film_m = normal_values(streams_of[15], (COND, 2 * C), (0.0022 / PARAMS ** 0.5), 7.62939453125e-06, ((1, 8),), jnp.float32)
    skip_m = normal_values(streams_of[16], (2 * C, C), (0.0022 / PARAMS ** 0.5), 7.62939453125e-06, ((1, 8),), jnp.float32)
    down_m = normal_values(streams_of[17], (MLP, C), (0.0022 / PARAMS ** 0.5), 7.62939453125e-06, ((0, 8),), jnp.float32)
    stem_m = normal_values(streams_of[18], (9 * CIN, C), (0.0022 / PARAMS ** 0.5), 7.62939453125e-06, ((1, 8),), jnp.float32)
    head_m = normal_values(streams_of[19], (9 * C, CIN), (0.0022 / PARAMS ** 0.5), 7.62939453125e-06, ((0, 8),), jnp.float32)
    gains_m = normal_values(streams_of[20], (8, C), (0.022 / PARAMS ** 0.5), 9.1552734375e-05, ((1, 8),), jnp.float32)
    conv_v = jnp.clip(jnp.exp(math.log(6.67164836831019e-13) - 1.3862944 * jax.random.uniform(streams_of[21], (2, 9 * C, C), jnp.float32) ** level_of(streams_of[21], (2, 9 * C, C), ((1, 8),), -0.2, 0.2)), 1.6679120920775475e-13, 6.67164836831019e-13)
    proj_v = jnp.clip(jnp.exp(math.log(6.67164836831019e-13) - 1.3862944 * jax.random.uniform(streams_of[22], (C, 4 * C + MLP), jnp.float32) ** level_of(streams_of[22], (C, 4 * C + MLP), ((1, 8),), -0.2, 0.2)), 1.6679120920775475e-13, 6.67164836831019e-13)
    film_v = jnp.clip(jnp.exp(math.log(6.67164836831019e-13) - 1.3862944 * jax.random.uniform(streams_of[23], (COND, 2 * C), jnp.float32) ** level_of(streams_of[23], (COND, 2 * C), ((1, 8),), -0.2, 0.2)), 1.6679120920775475e-13, 6.67164836831019e-13)
    skip_v = jnp.clip(jnp.exp(math.log(6.67164836831019e-13) - 1.3862944 * jax.random.uniform(streams_of[24], (2 * C, C), jnp.float32) ** level_of(streams_of[24], (2 * C, C), ((1, 8),), -0.2, 0.2)), 1.6679120920775475e-13, 6.67164836831019e-13)
    down_v = jnp.clip(jnp.exp(math.log(6.67164836831019e-13) - 1.3862944 * jax.random.uniform(streams_of[25], (MLP, C), jnp.float32) ** level_of(streams_of[25], (MLP, C), ((0, 8),), -0.2, 0.2)), 1.6679120920775475e-13, 6.67164836831019e-13)
    stem_v = jnp.clip(jnp.exp(math.log(6.67164836831019e-13) - 1.3862944 * jax.random.uniform(streams_of[26], (9 * CIN, C), jnp.float32) ** level_of(streams_of[26], (9 * CIN, C), ((1, 8),), -0.2, 0.2)), 1.6679120920775475e-13, 6.67164836831019e-13)
    head_v = jnp.clip(jnp.exp(math.log(6.67164836831019e-13) - 1.3862944 * jax.random.uniform(streams_of[27], (9 * C, CIN), jnp.float32) ** level_of(streams_of[27], (9 * C, CIN), ((0, 8),), -0.2, 0.2)), 1.6679120920775475e-13, 6.67164836831019e-13)
    gains_v = jnp.clip(jnp.exp(math.log(6.671647956313365e-11) - 1.3862944 * jax.random.uniform(streams_of[28], (8, C), jnp.float32) ** level_of(streams_of[28], (8, C), ((1, 8),), -0.2, 0.2)), 1.667911989078341e-11, 6.671647956313365e-11)
    return {"clean_lat": clean_lat, "noise_lat": noise_lat, "column_ids": column_ids, "timesteps": timesteps, "clap_emb": clap_emb, "conv_w": conv_w, "proj_w": proj_w, "film_w": film_w, "skip_w": skip_w, "down_w": down_w, "stem_w": stem_w, "head_w": head_w, "gains": gains, "conv_m": conv_m, "proj_m": proj_m, "film_m": film_m, "skip_m": skip_m, "down_m": down_m, "stem_m": stem_m, "head_m": head_m, "gains_m": gains_m, "conv_v": conv_v, "proj_v": proj_v, "film_v": film_v, "skip_v": skip_v, "down_v": down_v, "stem_v": stem_v, "head_v": head_v, "gains_v": gains_v}


@jax.custom_vjp
def low(v):
    return lax.optimization_barrier(v.astype(jnp.bfloat16)).astype(jnp.float32)

@jax.custom_vjp
def low_back(v):
    return v

def low_keep(v):
    return (low(v), None)

def low_pass(kept, grad):
    return (grad,)

def back_keep(v):
    return (v, None)

def back_low(kept, grad):
    return (low(grad),)
low.defvjp(low_keep, low_pass)
low_back.defvjp(back_keep, back_low)
HIGH = lax.Precision.HIGHEST
EPS_NORM = 1e-05
CLIP_NORM = 0.02
RATE = 0.04
BETA_ONE = 0.9
BETA_TWO = 0.999
ADAM_EPS = 1e-08
DECAY = 0.1

def product(lhs_mat, rhs_mat):
    return jnp.dot(lhs_mat, rhs_mat, precision=HIGH, preferred_element_type=jnp.float32)

def edge_masks(column_ids):
    edge_pad = jnp.full((1,), -1, jnp.int32)
    padded = jnp.concatenate([edge_pad, column_ids, edge_pad])
    n_cols = column_ids.shape[0]
    return [(padded[offset:offset + n_cols] == column_ids).astype(jnp.float32) for offset in range(3)]

def conv_cols(inputs, masks_all):
    height, n_cols, n_in = inputs.shape
    padded = jnp.pad(inputs, ((1, 1), (1, 1), (0, 0)))
    taps = [padded[tap_row:tap_row + height, tap_col:tap_col + n_cols] * masks_all[tap_col][None, :, None] for tap_row in range(3) for tap_col in range(3)]
    return jnp.concatenate(taps, axis=2).reshape(height * n_cols, 9 * n_in)

def group_norm(inputs, onehot, gain_row, bias_row):
    height, n_cols, chans = inputs.shape
    per_group = chans // GROUPS
    sum_one = product(onehot.T, lax.optimization_barrier(jnp.sum(inputs, axis=0))).reshape(-1, GROUPS, per_group).sum(axis=2)
    sum_two = product(onehot.T, lax.optimization_barrier(jnp.sum(inputs * inputs, axis=0))).reshape(-1, GROUPS, per_group).sum(axis=2)
    counts = jnp.maximum(lax.optimization_barrier(jnp.sum(onehot, axis=0)) * (height * per_group), 1.0)[:, None]
    mean_row = sum_one / counts
    inv_std = lax.rsqrt(sum_two / counts - mean_row * mean_row + EPS_NORM)
    mean_col = jnp.repeat(product(onehot, mean_row), per_group, axis=1)
    std_col = jnp.repeat(product(onehot, inv_std), per_group, axis=1)
    return (inputs - mean_col[None]) * std_col[None] * gain_row + bias_row

def layer_norm(inputs, gain_row, bias_row):
    mean_row = lax.optimization_barrier(jnp.mean(inputs, axis=1, keepdims=True))
    centered = inputs - mean_row
    inv_std = lax.rsqrt(lax.optimization_barrier(jnp.mean(centered * centered, axis=1, keepdims=True)) + EPS_NORM)
    return centered * inv_std * gain_row + bias_row

def clip_terms(timesteps, clap_emb):
    half_cond = COND // 2
    frequency = jnp.exp(-math.log(10000.0) * jnp.arange(half_cond, dtype=jnp.float32) / half_cond)
    angles = timesteps.astype(jnp.float32)[:, None] * frequency[None]
    cond_vec = clap_emb + jnp.concatenate([jnp.sin(angles), jnp.cos(angles)], axis=1)
    theta_clip = 0.5 * math.pi * (timesteps.astype(jnp.float32) + 1.0) / 1001.0
    return (cond_vec, jnp.cos(theta_clip), jnp.sin(theta_clip))

def attention(qkv_rows, pixel_ids):
    n_pix = qkv_rows.shape[0]
    heads_x = qkv_rows.reshape(n_pix, HEADS, 3 * HD)
    queries = heads_x[..., :HD]
    key_rows = heads_x[..., HD:2 * HD]
    val_rows = heads_x[..., 2 * HD:]
    block_rows = min(512, n_pix)
    score_scale = HD ** (-0.5)

    def per_block(block_in):
        q_blk, i_blk = block_in
        scores = low_back(jnp.einsum('bhd,rhd->hbr', q_blk, key_rows, precision=HIGH) * score_scale)
        scores = jnp.where((i_blk[:, None] == pixel_ids[None, :])[None], scores, -1e+30)
        row_max = lax.optimization_barrier(jnp.max(scores, axis=2, keepdims=True))
        exp_rows = jnp.exp(scores - row_max)
        prob_rows = exp_rows / lax.optimization_barrier(jnp.sum(exp_rows, axis=2, keepdims=True))
        return jnp.einsum('hbr,rhd->bhd', low(prob_rows), val_rows, precision=HIGH)
    attended = lax.map(jax.checkpoint(per_block), (queries.reshape(-1, block_rows, HEADS, HD), pixel_ids.reshape(-1, block_rows)))
    return attended.reshape(n_pix, HEADS * HD)

def row_loss(params, clean_lat, noise_lat, column_ids, timesteps, clap_emb):
    conv_w, proj_w, film_w, skip_w, down_w, stem_w, head_w, gains = [low(item) for item in params]
    height, n_cols, _ = clean_lat.shape
    n_pix = height * n_cols
    onehot = (column_ids[:, None] == jnp.arange(CLIPS + 1)[None, :]).astype(jnp.float32)
    clip_hot = onehot[:, :CLIPS]
    valid_cols = lax.optimization_barrier(jnp.sum(clip_hot, axis=1))
    cond_vec, alpha_clip, sigma_clip = clip_terms(timesteps, clap_emb)
    alpha_col = product(clip_hot, alpha_clip[:, None])[:, 0][None, :, None]
    sigma_col = product(clip_hot, sigma_clip[:, None])[:, 0][None, :, None]
    noisy_in = alpha_col * clean_lat + sigma_col * noise_lat
    target = alpha_col * noise_lat - sigma_col * clean_lat
    masks_all = edge_masks(column_ids)
    stem = low_back(product(conv_cols(low(noisy_in), masks_all), stem_w)).reshape(height, n_cols, C)
    first_act = jax.nn.silu(group_norm(stem, onehot, gains[0], gains[1]))
    inner_out = low_back(product(conv_cols(low(first_act), masks_all), conv_w[0])).reshape(height, n_cols, C)
    film_out = product(low(jax.nn.silu(cond_vec)), film_w)
    film_col = product(clip_hot, film_out)
    second = jax.nn.silu(group_norm(inner_out, onehot, gains[2], gains[3]) * (1.0 + film_col[None, :, :C]) + film_col[None, :, C:])
    branch = low_back(product(conv_cols(low(second), masks_all), conv_w[1]))
    stem_rows = stem.reshape(n_pix, C)
    joined = low(jnp.concatenate([stem_rows + branch, stem_rows], axis=1))
    base_rows = low_back(product(joined, skip_w))
    qkv_rows = low_back(low(product(low(layer_norm(base_rows, gains[4], gains[5])), proj_w[:, :3 * C])))
    pixel_ids = jnp.broadcast_to(column_ids[None, :], (height, n_cols)).reshape(n_pix)
    attended = low_back(low(attention(qkv_rows, pixel_ids)))
    mid_rows = base_rows + low_back(product(attended, proj_w[:, 3 * C:4 * C]))
    hidden = low_back(product(low(layer_norm(mid_rows, gains[6], gains[7])), proj_w[:, 4 * C:]))
    top_rows = mid_rows + low_back(product(low(jax.nn.gelu(hidden)), down_w))
    pred = low_back(product(conv_cols(low(top_rows.reshape(height, n_cols, C)), masks_all), head_w))
    residue = pred.reshape(height, n_cols, CIN) - target
    return jnp.sum(valid_cols[None, :, None] * residue * residue)

def reference(clean_lat, noise_lat, column_ids, timesteps, clap_emb, conv_w, proj_w, film_w, skip_w, down_w, stem_w, head_w, gains, conv_m, proj_m, film_m, skip_m, down_m, stem_m, head_m, gains_m, conv_v, proj_v, film_v, skip_v, down_v, stem_v, head_v, gains_v):
    masters = (conv_w, proj_w, film_w, skip_w, down_w, stem_w, head_w, gains)
    firsts = (conv_m, proj_m, film_m, skip_m, down_m, stem_m, head_m, gains_m)
    seconds = (conv_v, proj_v, film_v, skip_v, down_v, stem_v, head_v, gains_v)

    def total_loss(params):

        def per_row(running, row_in):
            return (running + jax.checkpoint(row_loss)(params, *row_in), None)
        summed, _ = lax.scan(per_row, jnp.zeros((), jnp.float32), (clean_lat, noise_lat, column_ids, timesteps, clap_emb))
        return summed
    pix_count = jnp.sum((column_ids < CLIPS).astype(jnp.float32)) * (F * CIN)
    loss_sum, vjp_pull = jax.vjp(total_loss, masters)
    grads = vjp_pull(jnp.ones((), jnp.float32) / pix_count)[0]
    grad_norm = jnp.sqrt(sum((jnp.sum(grad_one * grad_one) for grad_one in grads)))
    factor = jnp.minimum(1.0, CLIP_NORM / grad_norm)
    new_w, new_m, new_v = ([], [], [])
    for weight, grad_one, m_old, v_old in zip(masters, grads, firsts, seconds):
        grad_one = grad_one * factor
        m_new = BETA_ONE * m_old + (1.0 - BETA_ONE) * grad_one
        v_new = BETA_TWO * v_old + (1.0 - BETA_TWO) * grad_one * grad_one
        step_dir = m_new / (1.0 - BETA_ONE ** STEP) / (jnp.sqrt(v_new / (1.0 - BETA_TWO ** STEP)) + ADAM_EPS)
        new_w.append(weight - RATE * (step_dir + DECAY * weight))
        new_m.append(m_new)
        new_v.append(v_new)
    return (new_w[0], new_w[1], new_w[2], new_w[3], new_w[4], new_w[5], new_w[6], new_w[7], new_m[0], new_m[1], new_m[2], new_m[3], new_m[4], new_m[5], new_m[6], new_m[7], new_v[0], new_v[1], new_v[2], new_v[3], new_v[4], new_v[5], new_v[6], new_v[7], grad_norm, loss_sum, pix_count)
```

```python
import functools
import math

import jax
import jax.numpy as jnp
from jax import lax
from jax.experimental import pallas as pl
from jax.experimental.pallas import tpu as pltpu
from jax.sharding import PartitionSpec as P

CIN = 8
C = 256
HEADS = 8
HD = 32
COND = 512
GROUPS = 32
CLIPS = 4
STEP = 10


EPS_NORM = 1e-05
CLIP_NORM = 0.02
RATE = 0.04
BETA_ONE = 0.9
BETA_TWO = 0.999
ADAM_EPS = 1e-08
DECAY = 0.1


def with_halo(cells, sides, width):
    for axis, dim in sides:
        count = lax.axis_size(axis)
        ends = count - 1
        head = lax.slice_in_dim(cells, 0, width, axis=dim)
        tail = lax.slice_in_dim(cells, cells.shape[dim] - width, cells.shape[dim], axis=dim)
        cells = jnp.concatenate(
            [
                lax.ppermute(tail, axis, [(i, (i + 1) % count) for i in range(ends)]),
                cells,
                lax.ppermute(head, axis, [((i + 1) % count, i) for i in range(ends)]),
            ],
            axis=dim,
        )
    return cells


def matmul(lhs_mat, rhs_mat):
    return jnp.dot(lhs_mat, rhs_mat, preferred_element_type=jnp.float32)


def left_product(lhs_mat, rhs_mat):
    return lax.dot_general(
        lhs_mat, rhs_mat, (((0,), (0,)), ((), ())), preferred_element_type=jnp.float32
    )


def exact(lhs_mat, rhs_mat):
    return jnp.dot(
        lhs_mat, rhs_mat, precision=lax.Precision.HIGHEST, preferred_element_type=jnp.float32
    )


def clip_terms(timesteps, clap_emb):
    half_cond = COND // 2
    frequency = jnp.exp(-math.log(10000.0) * jnp.arange(half_cond, dtype=jnp.float32) / half_cond)
    angles = timesteps.astype(jnp.float32)[:, None] * frequency[None]
    cond_vec = clap_emb + jnp.concatenate([jnp.sin(angles), jnp.cos(angles)], axis=1)
    theta_clip = 0.5 * math.pi * (timesteps.astype(jnp.float32) + 1.0) / 1001.0
    return (cond_vec, jnp.cos(theta_clip), jnp.sin(theta_clip))


def conv_forward(inputs, weight, masks_all):
    height, n_cols, n_in = inputs.shape
    widened = with_halo(inputs, (("section", 1),), 1)
    padded = jnp.pad(widened, ((1, 1), (0, 0), (0, 0)))
    taps = [
        padded[tap_row : tap_row + height, tap_col : tap_col + n_cols]
        * masks_all[tap_col][None, :, None]
        for tap_row in range(3)
        for tap_col in range(3)
    ]
    columns = jnp.concatenate(taps, axis=2).reshape(height * n_cols, 9 * n_in)
    return (columns, matmul(columns, weight))


def conv_backward(d_out, weight, masks_all):
    height, n_cols, n_out = d_out.shape
    widened = with_halo(d_out, (("section", 1),), 1)
    padded = jnp.pad(widened, ((1, 1), (0, 0), (0, 0)))
    taps = [
        padded[2 - tap_row : 2 - tap_row + height, 2 - tap_col : 2 - tap_col + n_cols]
        * masks_all[2 - tap_col][None, :, None]
        for tap_row in range(3)
        for tap_col in range(3)
    ]
    flipped = weight.reshape(9, -1, n_out).transpose(0, 2, 1).reshape(9 * n_out, -1)
    return matmul(jnp.concatenate(taps, axis=2).reshape(height * n_cols, 9 * n_out), flipped)


def group_forward(inputs, onehot, counts):
    per_group = inputs.shape[2] // GROUPS
    sum_one = exact(onehot.T, jnp.sum(inputs, axis=0)).reshape(-1, GROUPS, per_group).sum(axis=2)
    sum_two = (
        exact(onehot.T, jnp.sum(inputs * inputs, axis=0)).reshape(-1, GROUPS, per_group).sum(axis=2)
    )
    sum_one, sum_two = lax.psum((sum_one, sum_two), "section")
    mean_row = sum_one / counts
    inv_std = lax.rsqrt(sum_two / counts - mean_row * mean_row + EPS_NORM)
    mean_col = jnp.repeat(exact(onehot, mean_row), per_group, axis=1)
    std_col = jnp.repeat(exact(onehot, inv_std), per_group, axis=1)
    return ((inputs - mean_col[None]) * std_col[None], std_col)


def group_backward(d_out, normed, std_col, gain_row, onehot, counts):
    per_group = d_out.shape[2] // GROUPS
    scaled = d_out * gain_row
    sum_one = exact(onehot.T, jnp.sum(scaled, axis=0)).reshape(-1, GROUPS, per_group).sum(axis=2)
    sum_two = (
        exact(onehot.T, jnp.sum(scaled * normed, axis=0)).reshape(-1, GROUPS, per_group).sum(axis=2)
    )
    sum_one, sum_two = lax.psum((sum_one, sum_two), "section")
    mean_one = jnp.repeat(exact(onehot, sum_one / counts), per_group, axis=1)
    mean_two = jnp.repeat(exact(onehot, sum_two / counts), per_group, axis=1)
    d_in = std_col[None] * (scaled - mean_one[None] - normed * mean_two[None])
    return (d_in, jnp.sum(d_out * normed, axis=(0, 1)), jnp.sum(d_out, axis=(0, 1)))


def layer_forward(inputs, gain_row, bias_row):
    mean_row = jnp.mean(inputs, axis=1, keepdims=True)
    centered = inputs - mean_row
    inv_std = lax.rsqrt(jnp.mean(centered * centered, axis=1, keepdims=True) + EPS_NORM)
    normed = centered * inv_std
    return (normed * gain_row + bias_row, normed, inv_std)


def layer_backward(d_out, normed, inv_std, gain_row):
    scaled = d_out * gain_row
    d_in = inv_std * (
        scaled
        - jnp.mean(scaled, axis=1, keepdims=True)
        - normed * jnp.mean(scaled * normed, axis=1, keepdims=True)
    )
    return (d_in, jnp.sum(d_out * normed, axis=0), jnp.sum(d_out, axis=0))


BIG = 1e30
LOG2E = 1.4426950408889634
SCALE = HD**-0.5 * LOG2E
VMEM_LIMIT = 56 << 20
NN = (((1,), (0,)), ((), ()))
NT = (((1,), (1,)), ((), ()))


def mxu(lhs_mat, rhs_mat, dims=NN):
    return lax.dot_general(lhs_mat, rhs_mat, dims, preferred_element_type=jnp.float32)


def picker(rows, first, copies):
    row = lax.broadcasted_iota(jnp.int32, (rows, 128), 0) - first
    col = lax.broadcasted_iota(jnp.int32, (rows, 128), 1)
    hit = (row >= 0) & (row < HD) & (col < HD * copies) & ((col & (HD - 1)) == row)
    return hit.astype(jnp.bfloat16)


def picker_t(lanes, first):
    row = lax.broadcasted_iota(jnp.int32, (HD, lanes), 0)
    col = lax.broadcasted_iota(jnp.int32, (HD, lanes), 1) - first
    return (col == row).astype(jnp.bfloat16)


def split_three(value):
    high = value.astype(jnp.bfloat16).astype(jnp.float32)
    rest = value - high
    mid = rest.astype(jnp.bfloat16).astype(jnp.float32)
    return high, mid, rest - mid


def put(lane, first, parts):
    total = jnp.where(lane == first, parts[0], 0.0)
    for step, part in enumerate(parts[1:]):
        total = total + jnp.where(lane == first + 1 + step, part, 0.0)
    return total


def forward_kernel(heads, bq, bk, x_ref, ids_ref, out_ref, lse_ref, kaug, vt):
    n_pix, lanes = x_ref.shape
    step = pl.program_id(0)

    @pl.when(step == 0)
    def _():
        for head in range(heads):
            pick_k = picker(lanes, 3 * HD * head + HD, 1)
            pick_v = picker_t(lanes, 3 * HD * head + 2 * HD)
            for start in range(0, n_pix, 512):
                rows = x_ref[start : start + 512, :]
                lane = lax.broadcasted_iota(jnp.int32, (512, 128), 1)
                same = (lane - HD == ids_ref[start : start + 512, :]).astype(jnp.float32)
                kaug[head, start : start + 512, :] = (mxu(rows, pick_k) + same).astype(jnp.bfloat16)
                vt[head, :, start : start + 512] = mxu(pick_v, rows, NT).astype(jnp.bfloat16)

    block = pl.ds(pl.multiple_of(step * bq, bq), bq)
    own = x_ref[block, :]
    own_ids = ids_ref[block, :]
    lane = lax.broadcasted_iota(jnp.int32, (bq, 128), 1)
    other = (lane >= HD) & (lane < HD + CLIPS + 1) & (lane - HD != own_ids)
    tops, stats = [], []
    for head in range(heads):
        query = (mxu(own, picker(lanes, 3 * HD * head, 1)) + jnp.where(other, -BIG, 0.0)).astype(
            jnp.bfloat16
        )
        total = jnp.zeros((8, bq), jnp.float32)
        acc = jnp.zeros((HD, bq), jnp.float32)
        row_max = jnp.full((1, bq), -jnp.inf, jnp.float32)
        for start in range(0, n_pix, bk):
            scores = mxu(kaug[head, start : start + bk, :], query, NT)
            new_max = jnp.maximum(row_max, jnp.max(scores, axis=0, keepdims=True) * SCALE)
            probs = jnp.exp2(scores * SCALE - new_max)
            decay = jnp.exp2(row_max - new_max)
            total = total * decay + jnp.sum(probs.reshape(bk // 8, 8, bq), axis=0)
            acc = acc * decay + mxu(vt[head, :, start : start + bk], probs.astype(jnp.bfloat16))
            row_max = new_max
        total = jnp.sum(total, axis=0, keepdims=True)
        tops.append(acc / total)
        stats.append(jnp.broadcast_to(row_max + jnp.log2(total), (8, bq)))
    out_ref[...] = jnp.concatenate(tops, axis=0).T.astype(jnp.bfloat16)
    lse_ref[...] = jnp.concatenate(stats, axis=0).T


def attention_forward(heads_x, pixel_ids):
    n_pix, lanes = heads_x.shape
    heads = lanes // (3 * HD)
    bq, bk = min(2048, n_pix), min(512, n_pix)
    return pl.pallas_call(
        functools.partial(forward_kernel, heads, bq, bk),
        grid=(n_pix // bq,),
        in_specs=[
            pl.BlockSpec((n_pix, lanes), lambda i: (0, 0)),
            pl.BlockSpec((n_pix, 1), lambda i: (0, 0)),
        ],
        out_specs=[
            pl.BlockSpec((bq, heads * HD), lambda i: (i, 0)),
            pl.BlockSpec((bq, heads * 8), lambda i: (i, 0)),
        ],
        out_shape=[
            jax.ShapeDtypeStruct((n_pix, heads * HD), jnp.bfloat16),
            jax.ShapeDtypeStruct((n_pix, heads * 8), jnp.float32),
        ],
        scratch_shapes=[
            pltpu.VMEM((heads, n_pix, 128), jnp.bfloat16),
            pltpu.VMEM((heads, HD, n_pix), jnp.bfloat16),
        ],
        compiler_params=pltpu.CompilerParams(vmem_limit_bytes=VMEM_LIMIT),
    )(heads_x, pixel_ids)


def backward_kernel(
    heads, bq, bk, x_ref, ids_ref, do_ref, o_ref, lse_ref, out_ref, qaug, kaug, vaug, daug, kt, dqt
):
    n_pix, lanes = x_ref.shape
    step = pl.program_id(0)

    @pl.when(step == 0)
    def _():
        dqt[...] = jnp.zeros_like(dqt)
        for head in range(heads):
            base = 3 * HD * head
            pick_q, pick_k = picker(lanes, base, 3), picker(lanes, base + HD, 3)
            pick_v = picker(lanes, base + 2 * HD, 1)
            pick_d = picker(heads * HD, HD * head, 1)
            pick_kt = picker_t(lanes, base + HD)

            def prepare(part, carry):
                rows = pl.ds(pl.multiple_of(part * 512, 512), 512)
                cells, ids = x_ref[rows, :], ids_ref[rows, :]
                lane = lax.broadcasted_iota(jnp.int32, (512, 128), 1)
                ones = ((lane - 96 == ids) | ((lane >= 104) & (lane < 107))).astype(jnp.float32)
                kaug[head, rows, :] = (mxu(cells, pick_k) + ones).astype(jnp.bfloat16)
                ones = ((lane >= HD) & (lane < HD + 3)).astype(jnp.float32)
                vaug[head, rows, :] = (mxu(cells, pick_v) + ones).astype(jnp.bfloat16)
                one, two, three = split_three(mxu(cells, pick_q) * SCALE)
                query = jnp.where(lane < HD, one, jnp.where(lane < 2 * HD, two, three))
                other = (lane >= 96) & (lane < 96 + CLIPS + 1) & (lane - 96 != ids)
                query = query + jnp.where(other, -BIG, 0.0)
                lse = lse_ref[rows, 8 * head : 8 * head + 1]
                query = query + put(lane, 104, split_three(-lse))
                qaug[head, rows, :] = query.astype(jnp.bfloat16)
                d_out, out = mxu(do_ref[rows, :], pick_d), mxu(o_ref[rows, :], pick_d)
                delta = jnp.sum(d_out * out, axis=1, keepdims=True)
                d_out = d_out + put(lane, HD, split_three(-delta))
                daug[head, rows, :] = d_out.astype(jnp.bfloat16)
                return carry

            lax.fori_loop(0, n_pix // 512, prepare, 0)
            for start in range(0, n_pix, 512):
                kt[head, :, start : start + 512] = mxu(
                    pick_kt, x_ref[start : start + 512, :], NT
                ).astype(jnp.bfloat16)

    rows = pl.ds(pl.multiple_of(step * bk, bk), bk)
    for head in range(heads):
        key, value, key_t = kaug[head, rows, :], vaug[head, rows, :], kt[head, :, rows]
        d_value = jnp.zeros((bk, 128), jnp.float32)
        d_key = jnp.zeros((bk, 128), jnp.float32)
        for start in range(0, n_pix, bq):
            query = qaug[head, start : start + bq, :]
            d_out = daug[head, start : start + bq, :]
            probs = jnp.exp2(mxu(key, query, NT))
            d_scores = (probs * mxu(value, d_out, NT)).astype(jnp.bfloat16)
            d_value = d_value + mxu(probs.astype(jnp.bfloat16), d_out)
            d_key = d_key + mxu(d_scores, query)
            dqt[head, :, start : start + bq] += mxu(key_t, d_scores)
        base = 3 * HD * head
        d_key = (d_key[:, :HD] + d_key[:, HD : 2 * HD] + d_key[:, 2 * HD : 3 * HD]) * (1.0 / LOG2E)
        out_ref[rows, base + HD : base + 2 * HD] = d_key.astype(jnp.bfloat16)
        out_ref[rows, base + 2 * HD : base + 3 * HD] = d_value[:, :HD].astype(jnp.bfloat16)

    @pl.when(step == pl.num_programs(0) - 1)
    def _():
        for head in range(heads):
            for start in range(0, n_pix, 512):
                d_query = dqt[head, :, start : start + 512] * (HD**-0.5)
                out_ref[start : start + 512, 3 * HD * head : 3 * HD * head + HD] = (
                    d_query.T.astype(jnp.bfloat16)
                )


def attention_backward(heads_x, log_total, d_heads, out_heads, pixel_ids):
    n_pix, lanes = heads_x.shape
    heads = lanes // (3 * HD)
    bq, bk = min(1024, n_pix), min(1024, n_pix)
    operands = (heads_x, pixel_ids, d_heads, out_heads, log_total)
    return pl.pallas_call(
        functools.partial(backward_kernel, heads, bq, bk),
        grid=(n_pix // bk,),
        in_specs=[pl.BlockSpec(item.shape, lambda i: (0, 0)) for item in operands],
        out_specs=pl.BlockSpec((n_pix, lanes), lambda i: (0, 0)),
        out_shape=jax.ShapeDtypeStruct((n_pix, lanes), jnp.bfloat16),
        scratch_shapes=[pltpu.VMEM((heads, n_pix, 128), jnp.bfloat16)] * 4
        + [
            pltpu.VMEM((heads, HD, n_pix), jnp.bfloat16),
            pltpu.VMEM((heads, HD, n_pix), jnp.float32),
        ],
        compiler_params=pltpu.CompilerParams(vmem_limit_bytes=VMEM_LIMIT),
    )(*operands)


def body(
    clean_lat,
    noise_lat,
    column_ids,
    timesteps,
    clap_emb,
    conv_w,
    proj_w,
    film_w,
    skip_w,
    down_w,
    stem_w,
    head_w,
    gains,
    conv_m,
    proj_m,
    film_m,
    skip_m,
    down_m,
    stem_m,
    head_m,
    gains_m,
    conv_v,
    proj_v,
    film_v,
    skip_v,
    down_v,
    stem_v,
    head_v,
    gains_v,
):
    bf16 = jnp.bfloat16
    masters = (conv_w, proj_w, film_w, skip_w, down_w, stem_w, head_w, gains)
    firsts = (conv_m, proj_m, film_m, skip_m, down_m, stem_m, head_m, gains_m)
    seconds = (conv_v, proj_v, film_v, skip_v, down_v, stem_v, head_v, gains_v)
    shard_dims = (1, 1, 1, 1, 0, 1, 0, 1)
    conv_b, proj_b, film_b, skip_b, down_b, stem_b, head_b, gain_b = (
        lax.all_gather(conv_w.astype(bf16), "dp", axis=1, tiled=True),
        lax.all_gather(proj_w.astype(bf16), "dp", axis=1, tiled=True),
        lax.all_gather(film_w.astype(bf16), "dp", axis=1, tiled=True),
        lax.all_gather(skip_w.astype(bf16), "dp", axis=1, tiled=True),
        lax.all_gather(down_w.astype(bf16), "dp", axis=0, tiled=True),
        lax.all_gather(stem_w.astype(bf16), "dp", axis=1, tiled=True),
        lax.all_gather(head_w.astype(bf16), "dp", axis=0, tiled=True),
        lax.all_gather(gains.astype(bf16), "dp", axis=1, tiled=True),
    )
    gain_f = gain_b.astype(jnp.float32)
    clean_row = clean_lat[0]
    noise_row = noise_lat[0]
    ids_row = column_ids[0]
    height, n_cols, _ = clean_row.shape
    n_pix = height * n_cols
    section_size = lax.axis_size("section")
    edge_pad = jnp.full((1,), -1, jnp.int32)
    ids_rim = lax.dynamic_slice_in_dim(
        jnp.concatenate([edge_pad, ids_row, edge_pad]),
        lax.axis_index("section") * n_cols,
        n_cols + 2,
    )
    own_ids = ids_rim[1 : n_cols + 1]
    masks_all = [(ids_rim[offset : offset + n_cols] == own_ids).astype(bf16) for offset in range(3)]
    labels = jnp.arange(CLIPS + 1)
    onehot = (own_ids[:, None] == labels[None, :]).astype(jnp.float32)
    full_onehot = (ids_row[:, None] == labels[None, :]).astype(jnp.float32)
    counts = jnp.maximum(jnp.sum(full_onehot, axis=0) * (height * (C // GROUPS)), 1.0)[:, None]
    clip_hot = onehot[:, :CLIPS]
    valid_cols = jnp.sum(clip_hot, axis=1)
    cond_vec, alpha_clip, sigma_clip = clip_terms(timesteps[0], clap_emb[0])
    alpha_col = exact(clip_hot, alpha_clip[:, None])[:, 0][None, :, None]
    sigma_col = exact(clip_hot, sigma_clip[:, None])[:, 0][None, :, None]
    noisy_in = alpha_col * clean_row + sigma_col * noise_row
    target = alpha_col * noise_row - sigma_col * clean_row
    stem_cols, stem = conv_forward(noisy_in.astype(bf16), stem_b, masks_all)
    stem = stem.reshape(height, n_cols, C)
    norm_one, std_one = group_forward(stem, onehot, counts)
    first_act, silu_one = jax.vjp(jax.nn.silu, norm_one * gain_f[0] + gain_f[1])
    cols_one, inner_out = conv_forward(first_act.astype(bf16), conv_b[0], masks_all)
    inner_out = inner_out.reshape(height, n_cols, C)
    cond_act = jax.nn.silu(cond_vec).astype(bf16)
    film_col = exact(clip_hot, matmul(cond_act, film_b))
    norm_two, std_two = group_forward(inner_out, onehot, counts)
    affine_two = norm_two * gain_f[2] + gain_f[3]
    second, silu_two = jax.vjp(
        jax.nn.silu, affine_two * (1.0 + film_col[None, :, :C]) + film_col[None, :, C:]
    )
    cols_two, branch = conv_forward(second.astype(bf16), conv_b[1], masks_all)
    stem_rows = stem.reshape(n_pix, C)
    joined = jnp.concatenate([stem_rows + branch, stem_rows], axis=1).astype(bf16)
    base_rows = matmul(joined, skip_b)
    ln_one, normed_one, lstd_one = layer_forward(base_rows, gain_f[4], gain_f[5])
    ln_one_b = ln_one.astype(bf16)
    qkv_rows = matmul(ln_one_b, proj_b[:, : 3 * C]).astype(bf16)
    pixel_ids = jnp.broadcast_to(
        ids_row.reshape(section_size, 1, n_cols), (section_size, height, n_cols)
    ).reshape(-1)
    kept_heads = lax.all_to_all(
        qkv_rows.reshape(n_pix, section_size, HEADS // section_size, 3 * HD),
        "section",
        split_axis=1,
        concat_axis=0,
        tiled=True,
    ).reshape(section_size * n_pix, -1)
    pixel_ids = pixel_ids[:, None]
    out_heads, log_total = attention_forward(kept_heads, pixel_ids)
    attended = lax.all_to_all(
        out_heads, "section", split_axis=0, concat_axis=1, tiled=True
    ).reshape(n_pix, C)
    mid_rows = base_rows + matmul(attended, proj_b[:, 3 * C : 4 * C])
    ln_two, normed_two, lstd_two = layer_forward(mid_rows, gain_f[6], gain_f[7])
    ln_two_b = ln_two.astype(bf16)
    hidden = matmul(ln_two_b, proj_b[:, 4 * C :])
    act_out, gelu_pull = jax.vjp(jax.nn.gelu, hidden)
    act_b = act_out.astype(bf16)
    top_rows = mid_rows + matmul(act_b, down_b)
    head_cols, pred = conv_forward(
        top_rows.reshape(height, n_cols, C).astype(bf16), head_b, masks_all
    )
    residue = pred.reshape(height, n_cols, CIN) - target
    local_loss = jnp.sum(valid_cols[None, :, None] * residue * residue)
    local_count = jnp.sum(valid_cols) * (height * CIN)
    loss_sum, pix_count = lax.psum((local_loss, local_count), ("dp", "section"))
    d_pred = (2.0 * valid_cols[None, :, None] * residue / pix_count).astype(bf16)
    g_head = left_product(head_cols, d_pred.reshape(n_pix, CIN))
    d_top = conv_backward(d_pred, head_b, masks_all)
    d_top_b = d_top.astype(bf16)
    g_down = left_product(act_b, d_top_b)
    d_hidden = gelu_pull(matmul(d_top_b, down_b.T))[0].astype(bf16)
    g_up = left_product(ln_two_b, d_hidden)
    d_ln_two, g_ln2_g, g_ln2_b = layer_backward(
        matmul(d_hidden, proj_b[:, 4 * C :].T), normed_two, lstd_two, gain_f[6]
    )
    d_mid = d_top + d_ln_two
    d_mid_b = d_mid.astype(bf16)
    g_out = left_product(attended, d_mid_b)
    d_att = matmul(d_mid_b, proj_b[:, 3 * C : 4 * C].T).astype(bf16)
    d_heads = lax.all_to_all(
        d_att, "section", split_axis=1, concat_axis=0, tiled=True
    )
    d_qkv_heads = attention_backward(kept_heads, log_total, d_heads, out_heads, pixel_ids)
    d_qkv = lax.all_to_all(d_qkv_heads, "section", split_axis=0, concat_axis=1, tiled=True).reshape(
        n_pix, 3 * C
    )
    g_qkv = left_product(ln_one_b, d_qkv)
    d_ln_one, g_ln1_g, g_ln1_b = layer_backward(
        matmul(d_qkv, proj_b[:, : 3 * C].T), normed_one, lstd_one, gain_f[4]
    )
    d_base = (d_mid + d_ln_one).astype(bf16)
    g_skip = left_product(joined, d_base)
    d_joined = matmul(d_base, skip_b.T)
    d_branch = d_joined[:, :C].astype(bf16)
    g_conv_two = left_product(cols_two, d_branch)
    d_second = conv_backward(d_branch.reshape(height, n_cols, C), conv_b[1], masks_all).reshape(
        height, n_cols, C
    )
    d_pre_two = silu_two(d_second)[0]
    d_scale = jnp.sum(d_pre_two * affine_two, axis=0)
    d_shift = jnp.sum(d_pre_two, axis=0)
    d_film = exact(clip_hot.T, jnp.concatenate([d_scale, d_shift], axis=1))
    g_film = exact(cond_act.astype(jnp.float32).T, d_film)
    d_inner, g_gn2_g, g_gn2_b = group_backward(
        d_pre_two * (1.0 + film_col[None, :, :C]), norm_two, std_two, gain_f[2], onehot, counts
    )
    d_inner_b = d_inner.astype(bf16)
    g_conv_one = left_product(cols_one, d_inner_b.reshape(n_pix, C))
    d_first = conv_backward(d_inner_b, conv_b[0], masks_all).reshape(height, n_cols, C)
    d_stem_gn, g_gn1_g, g_gn1_b = group_backward(
        silu_one(d_first)[0], norm_one, std_one, gain_f[0], onehot, counts
    )
    d_stem = (d_stem_gn.reshape(n_pix, C) + d_joined[:, :C] + d_joined[:, C:]).astype(bf16)
    g_stem = left_product(stem_cols, d_stem)
    g_conv = jnp.stack([g_conv_one, g_conv_two])
    g_proj = jnp.concatenate([g_qkv, g_out, g_up], axis=1)
    g_gains = jnp.stack([g_gn1_g, g_gn1_b, g_gn2_g, g_gn2_b, g_ln1_g, g_ln1_b, g_ln2_g, g_ln2_b])
    totals = lax.psum(
        (g_conv, g_proj, g_film, g_skip, g_down, g_stem, g_head, g_gains), ("dp", "section")
    )
    squares = sum((jnp.sum(item * item) for item in totals))
    dp_size = lax.axis_size("dp")
    dp_place = lax.axis_index("dp")
    shards = tuple(
        (
            lax.dynamic_slice_in_dim(
                item, dp_place * (item.shape[dim] // dp_size), item.shape[dim] // dp_size, dim
            )
            for item, dim in zip(totals, shard_dims)
        )
    )
    grad_norm = jnp.sqrt(squares)
    factor = jnp.minimum(1.0, CLIP_NORM / grad_norm)
    new_w, new_m, new_v = ([], [], [])
    for weight, grad_one, m_old, v_old in zip(masters, shards, firsts, seconds):
        grad_one = grad_one * factor
        m_new = BETA_ONE * m_old + (1.0 - BETA_ONE) * grad_one
        v_new = BETA_TWO * v_old + (1.0 - BETA_TWO) * grad_one * grad_one
        step_dir = (
            m_new / (1.0 - BETA_ONE**STEP) / (jnp.sqrt(v_new / (1.0 - BETA_TWO**STEP)) + ADAM_EPS)
        )
        new_w.append(weight - RATE * (step_dir + DECAY * weight))
        new_m.append(m_new)
        new_v.append(v_new)
    return (
        new_w[0],
        new_w[1],
        new_w[2],
        new_w[3],
        new_w[4],
        new_w[5],
        new_w[6],
        new_w[7],
        new_m[0],
        new_m[1],
        new_m[2],
        new_m[3],
        new_m[4],
        new_m[5],
        new_m[6],
        new_m[7],
        new_v[0],
        new_v[1],
        new_v[2],
        new_v[3],
        new_v[4],
        new_v[5],
        new_v[6],
        new_v[7],
        grad_norm,
        loss_sum,
        pix_count,
    )


def solution(mesh):
    return jax.shard_map(
        body,
        mesh=mesh,
        in_specs=(
            P("dp", None, "section", None),
            P("dp", None, "section", None),
            P("dp", None),
            P("dp", None),
            P("dp", None, None),
            P(None, "dp", None),
            P(None, "dp"),
            P(None, "dp"),
            P(None, "dp"),
            P("dp", None),
            P(None, "dp"),
            P("dp", None),
            P(None, "dp"),
            P(None, "dp", None),
            P(None, "dp"),
            P(None, "dp"),
            P(None, "dp"),
            P("dp", None),
            P(None, "dp"),
            P("dp", None),
            P(None, "dp"),
            P(None, "dp", None),
            P(None, "dp"),
            P(None, "dp"),
            P(None, "dp"),
            P("dp", None),
            P(None, "dp"),
            P("dp", None),
            P(None, "dp"),
        ),
        out_specs=(
            P(None, "dp", None),
            P(None, "dp"),
            P(None, "dp"),
            P(None, "dp"),
            P("dp", None),
            P(None, "dp"),
            P("dp", None),
            P(None, "dp"),
            P(None, "dp", None),
            P(None, "dp"),
            P(None, "dp"),
            P(None, "dp"),
            P("dp", None),
            P(None, "dp"),
            P("dp", None),
            P(None, "dp"),
            P(None, "dp", None),
            P(None, "dp"),
            P(None, "dp"),
            P(None, "dp"),
            P("dp", None),
            P(None, "dp"),
            P("dp", None),
            P(None, "dp"),
            P(),
            P(),
            P(),
        ),
        check_vma=False,
    )
```

```python
import functools
import math

import jax
import jax.numpy as jnp
from jax import lax
from jax.experimental import pallas as pl
from jax.experimental.pallas import tpu as pltpu
from jax.sharding import PartitionSpec as P

CIN = 8
C = 256
HEADS = 8
HD = 32
COND = 512
GROUPS = 32
CLIPS = 4
STEP = 10


EPS_NORM = 1e-05
CLIP_NORM = 0.02
DP = ("a", "b")
RATE = 0.04
BETA_ONE = 0.9
BETA_TWO = 0.999
ADAM_EPS = 1e-08
DECAY = 0.1


def with_halo(cells, sides, width):
    for axis, dim in sides:
        count = lax.axis_size(axis)
        ends = count - 1
        head = lax.slice_in_dim(cells, 0, width, axis=dim)
        tail = lax.slice_in_dim(cells, cells.shape[dim] - width, cells.shape[dim], axis=dim)
        cells = jnp.concatenate(
            [
                lax.ppermute(tail, axis, [(i, (i + 1) % count) for i in range(ends)]),
                cells,
                lax.ppermute(head, axis, [((i + 1) % count, i) for i in range(ends)]),
            ],
            axis=dim,
        )
    return cells


def matmul(lhs_mat, rhs_mat):
    return jnp.dot(lhs_mat, rhs_mat, preferred_element_type=jnp.float32)


def left_product(lhs_mat, rhs_mat):
    return lax.dot_general(
        lhs_mat, rhs_mat, (((0,), (0,)), ((), ())), preferred_element_type=jnp.float32
    )


def exact(lhs_mat, rhs_mat):
    return jnp.dot(
        lhs_mat, rhs_mat, precision=lax.Precision.HIGHEST, preferred_element_type=jnp.float32
    )


def clip_terms(timesteps, clap_emb):
    half_cond = COND // 2
    frequency = jnp.exp(-math.log(10000.0) * jnp.arange(half_cond, dtype=jnp.float32) / half_cond)
    angles = timesteps.astype(jnp.float32)[:, None] * frequency[None]
    cond_vec = clap_emb + jnp.concatenate([jnp.sin(angles), jnp.cos(angles)], axis=1)
    theta_clip = 0.5 * math.pi * (timesteps.astype(jnp.float32) + 1.0) / 1001.0
    return (cond_vec, jnp.cos(theta_clip), jnp.sin(theta_clip))


def conv_forward(inputs, weight, masks_all):
    height, n_cols, n_in = inputs.shape
    widened = with_halo(inputs, (("s", 1),), 1)
    padded = jnp.pad(widened, ((1, 1), (0, 0), (0, 0)))
    taps = [
        padded[tap_row : tap_row + height, tap_col : tap_col + n_cols]
        * masks_all[tap_col][None, :, None]
        for tap_row in range(3)
        for tap_col in range(3)
    ]
    columns = jnp.concatenate(taps, axis=2).reshape(height * n_cols, 9 * n_in)
    return (columns, matmul(columns, weight))


def conv_backward(d_out, weight, masks_all):
    height, n_cols, n_out = d_out.shape
    widened = with_halo(d_out, (("s", 1),), 1)
    padded = jnp.pad(widened, ((1, 1), (0, 0), (0, 0)))
    taps = [
        padded[2 - tap_row : 2 - tap_row + height, 2 - tap_col : 2 - tap_col + n_cols]
        * masks_all[2 - tap_col][None, :, None]
        for tap_row in range(3)
        for tap_col in range(3)
    ]
    flipped = weight.reshape(9, -1, n_out).transpose(0, 2, 1).reshape(9 * n_out, -1)
    return matmul(jnp.concatenate(taps, axis=2).reshape(height * n_cols, 9 * n_out), flipped)


def group_forward(inputs, onehot, counts):
    per_group = inputs.shape[2] // GROUPS
    sum_one = exact(onehot.T, jnp.sum(inputs, axis=0)).reshape(-1, GROUPS, per_group).sum(axis=2)
    sum_two = (
        exact(onehot.T, jnp.sum(inputs * inputs, axis=0)).reshape(-1, GROUPS, per_group).sum(axis=2)
    )
    sum_one, sum_two = lax.psum((sum_one, sum_two), "s")
    mean_row = sum_one / counts
    inv_std = lax.rsqrt(sum_two / counts - mean_row * mean_row + EPS_NORM)
    mean_col = jnp.repeat(exact(onehot, mean_row), per_group, axis=1)
    std_col = jnp.repeat(exact(onehot, inv_std), per_group, axis=1)
    return ((inputs - mean_col[None]) * std_col[None], std_col)


def group_backward(d_out, normed, std_col, gain_row, onehot, counts):
    per_group = d_out.shape[2] // GROUPS
    scaled = d_out * gain_row
    sum_one = exact(onehot.T, jnp.sum(scaled, axis=0)).reshape(-1, GROUPS, per_group).sum(axis=2)
    sum_two = (
        exact(onehot.T, jnp.sum(scaled * normed, axis=0)).reshape(-1, GROUPS, per_group).sum(axis=2)
    )
    sum_one, sum_two = lax.psum((sum_one, sum_two), "s")
    mean_one = jnp.repeat(exact(onehot, sum_one / counts), per_group, axis=1)
    mean_two = jnp.repeat(exact(onehot, sum_two / counts), per_group, axis=1)
    d_in = std_col[None] * (scaled - mean_one[None] - normed * mean_two[None])
    return (d_in, jnp.sum(d_out * normed, axis=(0, 1)), jnp.sum(d_out, axis=(0, 1)))


def layer_forward(inputs, gain_row, bias_row):
    mean_row = jnp.mean(inputs, axis=1, keepdims=True)
    centered = inputs - mean_row
    inv_std = lax.rsqrt(jnp.mean(centered * centered, axis=1, keepdims=True) + EPS_NORM)
    normed = centered * inv_std
    return (normed * gain_row + bias_row, normed, inv_std)


def layer_backward(d_out, normed, inv_std, gain_row):
    scaled = d_out * gain_row
    d_in = inv_std * (
        scaled
        - jnp.mean(scaled, axis=1, keepdims=True)
        - normed * jnp.mean(scaled * normed, axis=1, keepdims=True)
    )
    return (d_in, jnp.sum(d_out * normed, axis=0), jnp.sum(d_out, axis=0))


BIG = 1e30
LOG2E = 1.4426950408889634
SCALE = HD**-0.5 * LOG2E
VMEM_LIMIT = 56 << 20
NN = (((1,), (0,)), ((), ()))
NT = (((1,), (1,)), ((), ()))


def mxu(lhs_mat, rhs_mat, dims=NN):
    return lax.dot_general(lhs_mat, rhs_mat, dims, preferred_element_type=jnp.float32)


def picker(rows, first, copies):
    row = lax.broadcasted_iota(jnp.int32, (rows, 128), 0) - first
    col = lax.broadcasted_iota(jnp.int32, (rows, 128), 1)
    hit = (row >= 0) & (row < HD) & (col < HD * copies) & ((col & (HD - 1)) == row)
    return hit.astype(jnp.bfloat16)


def picker_t(lanes, first):
    row = lax.broadcasted_iota(jnp.int32, (HD, lanes), 0)
    col = lax.broadcasted_iota(jnp.int32, (HD, lanes), 1) - first
    return (col == row).astype(jnp.bfloat16)


def split_three(value):
    high = value.astype(jnp.bfloat16).astype(jnp.float32)
    rest = value - high
    mid = rest.astype(jnp.bfloat16).astype(jnp.float32)
    return high, mid, rest - mid


def put(lane, first, parts):
    total = jnp.where(lane == first, parts[0], 0.0)
    for step, part in enumerate(parts[1:]):
        total = total + jnp.where(lane == first + 1 + step, part, 0.0)
    return total


def forward_kernel(heads, bq, bk, x_ref, ids_ref, out_ref, lse_ref, kaug, vt):
    n_pix, lanes = x_ref.shape
    step = pl.program_id(0)

    @pl.when(step == 0)
    def _():
        for head in range(heads):
            pick_k = picker(lanes, 3 * HD * head + HD, 1)
            pick_v = picker_t(lanes, 3 * HD * head + 2 * HD)
            for start in range(0, n_pix, 512):
                rows = x_ref[start : start + 512, :]
                lane = lax.broadcasted_iota(jnp.int32, (512, 128), 1)
                same = (lane - HD == ids_ref[start : start + 512, :]).astype(jnp.float32)
                kaug[head, start : start + 512, :] = (mxu(rows, pick_k) + same).astype(jnp.bfloat16)
                vt[head, :, start : start + 512] = mxu(pick_v, rows, NT).astype(jnp.bfloat16)

    block = pl.ds(pl.multiple_of(step * bq, bq), bq)
    own = x_ref[block, :]
    own_ids = ids_ref[block, :]
    lane = lax.broadcasted_iota(jnp.int32, (bq, 128), 1)
    other = (lane >= HD) & (lane < HD + CLIPS + 1) & (lane - HD != own_ids)
    tops, stats = [], []
    for head in range(heads):
        query = (mxu(own, picker(lanes, 3 * HD * head, 1)) + jnp.where(other, -BIG, 0.0)).astype(
            jnp.bfloat16
        )
        total = jnp.zeros((8, bq), jnp.float32)
        acc = jnp.zeros((HD, bq), jnp.float32)
        row_max = jnp.full((1, bq), -jnp.inf, jnp.float32)
        for start in range(0, n_pix, bk):
            scores = mxu(kaug[head, start : start + bk, :], query, NT)
            new_max = jnp.maximum(row_max, jnp.max(scores, axis=0, keepdims=True) * SCALE)
            probs = jnp.exp2(scores * SCALE - new_max)
            decay = jnp.exp2(row_max - new_max)
            total = total * decay + jnp.sum(probs.reshape(bk // 8, 8, bq), axis=0)
            acc = acc * decay + mxu(vt[head, :, start : start + bk], probs.astype(jnp.bfloat16))
            row_max = new_max
        total = jnp.sum(total, axis=0, keepdims=True)
        tops.append(acc / total)
        stats.append(jnp.broadcast_to(row_max + jnp.log2(total), (8, bq)))
    out_ref[...] = jnp.concatenate(tops, axis=0).T.astype(jnp.bfloat16)
    lse_ref[...] = jnp.concatenate(stats, axis=0).T


def attention_forward(heads_x, pixel_ids):
    n_pix, lanes = heads_x.shape
    heads = lanes // (3 * HD)
    bq, bk = min(2048, n_pix), min(512, n_pix)
    return pl.pallas_call(
        functools.partial(forward_kernel, heads, bq, bk),
        grid=(n_pix // bq,),
        in_specs=[
            pl.BlockSpec((n_pix, lanes), lambda i: (0, 0)),
            pl.BlockSpec((n_pix, 1), lambda i: (0, 0)),
        ],
        out_specs=[
            pl.BlockSpec((bq, heads * HD), lambda i: (i, 0)),
            pl.BlockSpec((bq, heads * 8), lambda i: (i, 0)),
        ],
        out_shape=[
            jax.ShapeDtypeStruct((n_pix, heads * HD), jnp.bfloat16),
            jax.ShapeDtypeStruct((n_pix, heads * 8), jnp.float32),
        ],
        scratch_shapes=[
            pltpu.VMEM((heads, n_pix, 128), jnp.bfloat16),
            pltpu.VMEM((heads, HD, n_pix), jnp.bfloat16),
        ],
        compiler_params=pltpu.CompilerParams(vmem_limit_bytes=VMEM_LIMIT),
    )(heads_x, pixel_ids)


def backward_kernel(
    heads, bq, bk, x_ref, ids_ref, do_ref, o_ref, lse_ref, out_ref, qaug, kaug, vaug, daug, kt, dqt
):
    n_pix, lanes = x_ref.shape
    step = pl.program_id(0)

    @pl.when(step == 0)
    def _():
        dqt[...] = jnp.zeros_like(dqt)
        for head in range(heads):
            base = 3 * HD * head
            pick_q, pick_k = picker(lanes, base, 3), picker(lanes, base + HD, 3)
            pick_v = picker(lanes, base + 2 * HD, 1)
            pick_d = picker(heads * HD, HD * head, 1)
            pick_kt = picker_t(lanes, base + HD)

            def prepare(part, carry):
                rows = pl.ds(pl.multiple_of(part * 512, 512), 512)
                cells, ids = x_ref[rows, :], ids_ref[rows, :]
                lane = lax.broadcasted_iota(jnp.int32, (512, 128), 1)
                ones = ((lane - 96 == ids) | ((lane >= 104) & (lane < 107))).astype(jnp.float32)
                kaug[head, rows, :] = (mxu(cells, pick_k) + ones).astype(jnp.bfloat16)
                ones = ((lane >= HD) & (lane < HD + 3)).astype(jnp.float32)
                vaug[head, rows, :] = (mxu(cells, pick_v) + ones).astype(jnp.bfloat16)
                one, two, three = split_three(mxu(cells, pick_q) * SCALE)
                query = jnp.where(lane < HD, one, jnp.where(lane < 2 * HD, two, three))
                other = (lane >= 96) & (lane < 96 + CLIPS + 1) & (lane - 96 != ids)
                query = query + jnp.where(other, -BIG, 0.0)
                lse = lse_ref[rows, 8 * head : 8 * head + 1]
                query = query + put(lane, 104, split_three(-lse))
                qaug[head, rows, :] = query.astype(jnp.bfloat16)
                d_out, out = mxu(do_ref[rows, :], pick_d), mxu(o_ref[rows, :], pick_d)
                delta = jnp.sum(d_out * out, axis=1, keepdims=True)
                d_out = d_out + put(lane, HD, split_three(-delta))
                daug[head, rows, :] = d_out.astype(jnp.bfloat16)
                return carry

            lax.fori_loop(0, n_pix // 512, prepare, 0)
            for start in range(0, n_pix, 512):
                kt[head, :, start : start + 512] = mxu(
                    pick_kt, x_ref[start : start + 512, :], NT
                ).astype(jnp.bfloat16)

    rows = pl.ds(pl.multiple_of(step * bk, bk), bk)
    for head in range(heads):
        key, value, key_t = kaug[head, rows, :], vaug[head, rows, :], kt[head, :, rows]
        d_value = jnp.zeros((bk, 128), jnp.float32)
        d_key = jnp.zeros((bk, 128), jnp.float32)
        for start in range(0, n_pix, bq):
            query = qaug[head, start : start + bq, :]
            d_out = daug[head, start : start + bq, :]
            probs = jnp.exp2(mxu(key, query, NT))
            d_scores = (probs * mxu(value, d_out, NT)).astype(jnp.bfloat16)
            d_value = d_value + mxu(probs.astype(jnp.bfloat16), d_out)
            d_key = d_key + mxu(d_scores, query)
            dqt[head, :, start : start + bq] += mxu(key_t, d_scores)
        base = 3 * HD * head
        d_key = (d_key[:, :HD] + d_key[:, HD : 2 * HD] + d_key[:, 2 * HD : 3 * HD]) * (1.0 / LOG2E)
        out_ref[rows, base + HD : base + 2 * HD] = d_key.astype(jnp.bfloat16)
        out_ref[rows, base + 2 * HD : base + 3 * HD] = d_value[:, :HD].astype(jnp.bfloat16)

    @pl.when(step == pl.num_programs(0) - 1)
    def _():
        for head in range(heads):
            for start in range(0, n_pix, 512):
                d_query = dqt[head, :, start : start + 512] * (HD**-0.5)
                out_ref[start : start + 512, 3 * HD * head : 3 * HD * head + HD] = (
                    d_query.T.astype(jnp.bfloat16)
                )


def attention_backward(heads_x, log_total, d_heads, out_heads, pixel_ids):
    n_pix, lanes = heads_x.shape
    heads = lanes // (3 * HD)
    bq, bk = min(1024, n_pix), min(1024, n_pix)
    operands = (heads_x, pixel_ids, d_heads, out_heads, log_total)
    return pl.pallas_call(
        functools.partial(backward_kernel, heads, bq, bk),
        grid=(n_pix // bk,),
        in_specs=[pl.BlockSpec(item.shape, lambda i: (0, 0)) for item in operands],
        out_specs=pl.BlockSpec((n_pix, lanes), lambda i: (0, 0)),
        out_shape=jax.ShapeDtypeStruct((n_pix, lanes), jnp.bfloat16),
        scratch_shapes=[pltpu.VMEM((heads, n_pix, 128), jnp.bfloat16)] * 4
        + [
            pltpu.VMEM((heads, HD, n_pix), jnp.bfloat16),
            pltpu.VMEM((heads, HD, n_pix), jnp.float32),
        ],
        compiler_params=pltpu.CompilerParams(vmem_limit_bytes=VMEM_LIMIT),
    )(*operands)


MESH = pl.DeviceIdType.MESH


def round_up(count, unit):
    return -(-count // unit) * unit


def greet(peers):
    barrier = pltpu.get_barrier_semaphore()
    for peer in peers:
        pl.semaphore_signal(barrier, inc=1, device_id=peer, device_id_type=MESH)
    pl.semaphore_wait(barrier, len(peers))


def push(src, dst, sems, slot, peer):
    copy = pltpu.make_async_remote_copy(
        src_ref=src,
        dst_ref=dst,
        send_sem=sems.at[0, slot],
        recv_sem=sems.at[1, slot],
        device_id=peer,
        device_id_type=MESH,
    )
    copy.start()
    return copy


def reduce_kernel(n_a, n_x, n_s, chunks, square_rows, *refs):
    n_in = sum(len(parts) for parts in chunks)
    n_chunk = len(chunks)
    ins = refs[:n_in]
    outs = refs[n_in : n_in + n_chunk]
    norm_ref = refs[n_in + n_chunk]
    scratch = list(refs[n_in + n_chunk + 1 :])
    halves = scratch[:n_in]
    accs, one_bufs, two_bufs, bit_bufs = (
        scratch[n_in + i * n_chunk : n_in + (i + 1) * n_chunk] for i in range(4)
    )
    squares, sems = scratch[n_in + 4 * n_chunk :]
    bits = n_s.bit_length() - 1
    my_a, my_b, my_s = lax.axis_index("a"), lax.axis_index("b"), lax.axis_index("s")
    core, my_x = lax.rem(my_b, 2), lax.div(my_b, 2)
    n_b = 2 * n_x
    n_d = n_a * n_b

    def dp_peer(off):
        place = lax.rem(my_a * n_b + my_b + off, n_d)
        return {"a": lax.div(place, n_b), "b": lax.rem(place, n_b)}

    def s_peer(bit):
        flipped = my_s + (1 << bit) - 2 * (1 << bit) * lax.rem(lax.div(my_s, 1 << bit), 2)
        return {"s": flipped}

    greet([dp_peer(off) for off in range(1, n_d)] + [s_peer(bit) for bit in range(bits)])
    slots = iter(range(sems.shape[1]))

    first_in = []
    at = 0
    for parts in chunks:
        first_in.append(at)
        at += len(parts)

    def core_send(c):
        copies = []
        for i in range(first_in[c], first_in[c] + len(chunks[c])):
            copies.append(
                push(ins[i].at[:, 1 - core], halves[i], sems, next(slots), {"b": my_b + 1 - 2 * core})
            )
        return copies

    def core_sum(c):
        acc = accs[c]
        row = 0
        for i in range(first_in[c], first_in[c] + len(chunks[c])):
            rows, lanes = ins[i].shape[2:]
            for lane in range(0, lanes, 256):
                for j in range(n_a * n_x):
                    acc[j // n_x, j % n_x, row : row + rows] = (
                        ins[i][j, core, :, lane : lane + 256] + halves[i][j, :, lane : lane + 256]
                    )
                row += rows
        if row < acc.shape[2]:
            for j in range(n_a * n_x):
                acc[j // n_x, j % n_x, row:] = jnp.zeros((acc.shape[2] - row, 256), jnp.float32)

    def plane_send(c, stage):
        over_x = (c + stage) % 2 == 0
        buf = (one_bufs, two_bufs)[stage][c]
        copies = []
        for off in range(1, n_x if over_x else n_a):
            if over_x:
                there = lax.rem(my_x + off, n_x)
                src = accs[c].at[:, there] if stage == 0 else accs[c].at[my_a, there]
                peer = {"b": 2 * there + core}
            else:
                there = lax.rem(my_a + off, n_a)
                src = accs[c].at[there] if stage == 0 else accs[c].at[there, my_x]
                peer = {"a": there}
            copies.append(push(src, buf.at[off - 1], sems, next(slots), peer))
        return copies

    def plane_sum(c, stage):
        over_x = (c + stage) % 2 == 0
        buf = (one_bufs, two_bufs)[stage][c]
        for off in range(1, n_x if over_x else n_a):
            if stage == 1:
                accs[c][my_a, my_x] += buf[off - 1]
            elif over_x:
                for j in range(n_a):
                    accs[c][j, my_x] += buf[off - 1, j]
            else:
                for j in range(n_x):
                    accs[c][my_a, j] += buf[off - 1, j]

    def span(c, level):
        length = accs[c].shape[2]
        start = 0
        for bit in range(level):
            length //= 2
            start = start + lax.rem(lax.div(my_s, 1 << bit), 2) * length
        return start, length

    def s_send(c, bit):
        start, length = span(c, bit)
        length //= 2
        mine = lax.rem(lax.div(my_s, 1 << bit), 2)
        rows = pl.ds(pl.multiple_of(start + (1 - mine) * length, 8), length)
        return [
            push(
                accs[c].at[my_a, my_x, rows],
                bit_bufs[c].at[bit, pl.ds(0, length)],
                sems,
                next(slots),
                s_peer(bit),
            )
        ]

    def s_sum(c, bit):
        start, length = span(c, bit + 1)
        rows = pl.ds(pl.multiple_of(start, 8), length)
        total = accs[c][my_a, my_x, rows] + bit_bufs[c][bit, :length]
        if bit == bits - 1:
            outs[c][rows] = total
        else:
            accs[c][my_a, my_x, rows] = total

    def up_send(c, bit):
        start, length = span(c, bit + 1)
        rows = pl.ds(pl.multiple_of(start, 8), length)
        return [push(outs[c].at[rows], outs[c].at[rows], sems, next(slots), s_peer(bit))]

    steps = [(core_send, core_sum, ())]
    steps += [(plane_send, plane_sum, (stage,)) for stage in range(2)]
    steps += [(s_send, s_sum, (bit,)) for bit in range(bits)]
    steps += [(up_send, None, (bit,)) for bit in reversed(range(bits))]
    flying = [None] * n_chunk
    for tick in range(n_chunk + len(steps)):
        for c in range(n_chunk):
            at = tick - c
            if at < 0 or at > len(steps):
                continue
            if at > 0:
                for copy in flying[c]:
                    copy.wait()
                if steps[at - 1][1] is not None:
                    steps[at - 1][1](c, *steps[at - 1][2])
            if at < len(steps):
                flying[c] = steps[at][0](c, *steps[at][2])

    lane = lax.broadcasted_iota(jnp.int32, (8, 256), 1)
    total = jnp.zeros((8, 256), jnp.float32)
    for c in range(n_chunk):
        rows = square_rows[c]
        total = total + jnp.sum((outs[c][:rows] * outs[c][:rows]).reshape(rows // 8, 8, 256), axis=0)
    total = jnp.sum(jnp.sum(total, axis=0, keepdims=True), axis=1, keepdims=True)
    last = square_rows[-1]
    squares[my_a * n_b + my_b] = jnp.where(lane == 1, total, outs[-1][last : last + 8])
    copies = []
    for off in range(1, n_d):
        place = squares.at[my_a * n_b + my_b]
        copies.append(push(place, place, sems, next(slots), dp_peer(off)))
    for copy in copies:
        copy.wait()
    total = squares[0]
    for place in range(1, n_d):
        total = total + squares[place]
    norm_ref[...] = total


def reduce_grads(chunks, square_rows, collective_id):
    n_a, n_b, n_s = lax.axis_size("a"), lax.axis_size("b"), lax.axis_size("s")
    n_x = n_b // 2
    bits = n_s.bit_length() - 1
    flat = [item for parts in chunks for item in parts]
    heights = [
        round_up(sum(item.shape[2] * item.shape[3] // 256 for item in parts), 8 * n_s)
        for parts in chunks
    ]
    f32 = jnp.float32
    one_shapes, two_shapes = [], []
    for c, rows in enumerate(heights):
        one_shapes.append((n_x - 1, n_a, rows, 256) if c % 2 == 0 else (n_a - 1, n_x, rows, 256))
        two_shapes.append((n_a - 1, rows, 256) if c % 2 == 0 else (n_x - 1, rows, 256))
    scratch = [(item.shape[0], *item.shape[2:]) for item in flat]
    scratch += [(n_a, n_x, rows, 256) for rows in heights]
    scratch += one_shapes + two_shapes
    scratch += [(bits, rows // 2, 256) for rows in heights]
    scratch += [(n_a * n_b, 8, 256)]
    n_copy = len(flat) + len(chunks) * (n_x - 1 + n_a - 1 + 2 * bits) + n_a * n_b - 1
    out = pl.pallas_call(
        functools.partial(reduce_kernel, n_a, n_x, n_s, [[None] * len(parts) for parts in chunks], square_rows),
        in_specs=[pl.BlockSpec(memory_space=pltpu.VMEM)] * len(flat),
        out_specs=[pl.BlockSpec(memory_space=pltpu.VMEM)] * (len(chunks) + 1),
        out_shape=[jax.ShapeDtypeStruct((rows, 256), f32) for rows in heights]
        + [jax.ShapeDtypeStruct((8, 256), f32)],
        scratch_shapes=[pltpu.VMEM(shape, f32) for shape in scratch]
        + [pltpu.SemaphoreType.DMA((2, n_copy))],
        compiler_params=pltpu.CompilerParams(
            collective_id=collective_id, has_side_effects=True, vmem_limit_bytes=VMEM_LIMIT
        ),
    )(*flat)
    return out[:-1], out[-1]


def body(
    clean_lat,
    noise_lat,
    column_ids,
    timesteps,
    clap_emb,
    conv_w,
    proj_w,
    film_w,
    skip_w,
    down_w,
    stem_w,
    head_w,
    gains,
    conv_m,
    proj_m,
    film_m,
    skip_m,
    down_m,
    stem_m,
    head_m,
    gains_m,
    conv_v,
    proj_v,
    film_v,
    skip_v,
    down_v,
    stem_v,
    head_v,
    gains_v,
):
    bf16 = jnp.bfloat16
    masters = (conv_w, proj_w, film_w, skip_w, down_w, stem_w, head_w, gains)
    firsts = (conv_m, proj_m, film_m, skip_m, down_m, stem_m, head_m, gains_m)
    seconds = (conv_v, proj_v, film_v, skip_v, down_v, stem_v, head_v, gains_v)
    shard_dims = (1, 1, 1, 1, 0, 1, 0, 1)
    conv_b, proj_b, film_b, skip_b, down_b, stem_b, head_b, gain_b = (
        lax.all_gather(conv_w.astype(bf16), DP, axis=1, tiled=True),
        lax.all_gather(proj_w.astype(bf16), DP, axis=1, tiled=True),
        lax.all_gather(film_w.astype(bf16), DP, axis=1, tiled=True),
        lax.all_gather(skip_w.astype(bf16), DP, axis=1, tiled=True),
        lax.all_gather(down_w.astype(bf16), DP, axis=0, tiled=True),
        lax.all_gather(stem_w.astype(bf16), DP, axis=1, tiled=True),
        lax.all_gather(head_w.astype(bf16), DP, axis=0, tiled=True),
        lax.all_gather(gains.astype(bf16), DP, axis=1, tiled=True),
    )
    gain_f = gain_b.astype(jnp.float32)
    clean_row = clean_lat[0]
    noise_row = noise_lat[0]
    ids_row = column_ids[0]
    height, n_cols, _ = clean_row.shape
    n_pix = height * n_cols
    section_size = lax.axis_size("s")
    edge_pad = jnp.full((1,), -1, jnp.int32)
    ids_rim = lax.dynamic_slice_in_dim(
        jnp.concatenate([edge_pad, ids_row, edge_pad]),
        lax.axis_index("s") * n_cols,
        n_cols + 2,
    )
    own_ids = ids_rim[1 : n_cols + 1]
    masks_all = [(ids_rim[offset : offset + n_cols] == own_ids).astype(bf16) for offset in range(3)]
    labels = jnp.arange(CLIPS + 1)
    onehot = (own_ids[:, None] == labels[None, :]).astype(jnp.float32)
    full_onehot = (ids_row[:, None] == labels[None, :]).astype(jnp.float32)
    counts = jnp.maximum(jnp.sum(full_onehot, axis=0) * (height * (C // GROUPS)), 1.0)[:, None]
    clip_hot = onehot[:, :CLIPS]
    pix_count = lax.psum(jnp.sum(full_onehot[:, :CLIPS]) * (height * CIN), DP)
    valid_cols = jnp.sum(clip_hot, axis=1)
    cond_vec, alpha_clip, sigma_clip = clip_terms(timesteps[0], clap_emb[0])
    alpha_col = exact(clip_hot, alpha_clip[:, None])[:, 0][None, :, None]
    sigma_col = exact(clip_hot, sigma_clip[:, None])[:, 0][None, :, None]
    noisy_in = alpha_col * clean_row + sigma_col * noise_row
    target = alpha_col * noise_row - sigma_col * clean_row
    stem_cols, stem = conv_forward(noisy_in.astype(bf16), stem_b, masks_all)
    stem = stem.reshape(height, n_cols, C)
    norm_one, std_one = group_forward(stem, onehot, counts)
    first_act, silu_one = jax.vjp(jax.nn.silu, norm_one * gain_f[0] + gain_f[1])
    cols_one, inner_out = conv_forward(first_act.astype(bf16), conv_b[0], masks_all)
    inner_out = inner_out.reshape(height, n_cols, C)
    cond_act = jax.nn.silu(cond_vec).astype(bf16)
    film_col = exact(clip_hot, matmul(cond_act, film_b))
    norm_two, std_two = group_forward(inner_out, onehot, counts)
    affine_two = norm_two * gain_f[2] + gain_f[3]
    second, silu_two = jax.vjp(
        jax.nn.silu, affine_two * (1.0 + film_col[None, :, :C]) + film_col[None, :, C:]
    )
    cols_two, branch = conv_forward(second.astype(bf16), conv_b[1], masks_all)
    stem_rows = stem.reshape(n_pix, C)
    joined = jnp.concatenate([stem_rows + branch, stem_rows], axis=1).astype(bf16)
    base_rows = matmul(joined, skip_b)
    ln_one, normed_one, lstd_one = layer_forward(base_rows, gain_f[4], gain_f[5])
    ln_one_b = ln_one.astype(bf16)
    qkv_rows = matmul(ln_one_b, proj_b[:, : 3 * C]).astype(bf16)
    pixel_ids = jnp.broadcast_to(
        ids_row.reshape(section_size, 1, n_cols), (section_size, height, n_cols)
    ).reshape(-1)
    kept_heads = lax.all_to_all(
        qkv_rows.reshape(n_pix, section_size, HEADS // section_size, 3 * HD),
        "s",
        split_axis=1,
        concat_axis=0,
        tiled=True,
    ).reshape(section_size * n_pix, -1)
    pixel_ids = pixel_ids[:, None]
    out_heads, log_total = attention_forward(kept_heads, pixel_ids)
    attended = lax.all_to_all(
        out_heads, "s", split_axis=0, concat_axis=1, tiled=True
    ).reshape(n_pix, C)
    mid_rows = base_rows + matmul(attended, proj_b[:, 3 * C : 4 * C])
    ln_two, normed_two, lstd_two = layer_forward(mid_rows, gain_f[6], gain_f[7])
    ln_two_b = ln_two.astype(bf16)
    hidden = matmul(ln_two_b, proj_b[:, 4 * C :])
    act_out, gelu_pull = jax.vjp(jax.nn.gelu, hidden)
    act_b = act_out.astype(bf16)
    top_rows = mid_rows + matmul(act_b, down_b)
    head_cols, pred = conv_forward(
        top_rows.reshape(height, n_cols, C).astype(bf16), head_b, masks_all
    )
    residue = pred.reshape(height, n_cols, CIN) - target
    local_loss = jnp.sum(valid_cols[None, :, None] * residue * residue)
    d_pred = (2.0 * valid_cols[None, :, None] * residue / pix_count).astype(bf16)
    g_head = left_product(head_cols, d_pred.reshape(n_pix, CIN))
    d_top = conv_backward(d_pred, head_b, masks_all)
    d_top_b = d_top.astype(bf16)
    g_down = left_product(act_b, d_top_b)
    d_hidden = gelu_pull(matmul(d_top_b, down_b.T))[0].astype(bf16)
    g_up = left_product(d_hidden, ln_two_b)
    d_ln_two, g_ln2_g, g_ln2_b = layer_backward(
        matmul(d_hidden, proj_b[:, 4 * C :].T), normed_two, lstd_two, gain_f[6]
    )
    d_mid = d_top + d_ln_two
    d_mid_b = d_mid.astype(bf16)
    g_out = left_product(d_mid_b, attended)
    d_att = matmul(d_mid_b, proj_b[:, 3 * C : 4 * C].T).astype(bf16)
    d_heads = lax.all_to_all(
        d_att, "s", split_axis=1, concat_axis=0, tiled=True
    )
    d_qkv_heads = attention_backward(kept_heads, log_total, d_heads, out_heads, pixel_ids)
    d_qkv = lax.all_to_all(d_qkv_heads, "s", split_axis=0, concat_axis=1, tiled=True).reshape(
        n_pix, 3 * C
    )
    g_qkv = left_product(d_qkv, ln_one_b)
    d_ln_one, g_ln1_g, g_ln1_b = layer_backward(
        matmul(d_qkv, proj_b[:, : 3 * C].T), normed_one, lstd_one, gain_f[4]
    )
    d_base = (d_mid + d_ln_one).astype(bf16)
    g_skip = left_product(d_base, joined)
    d_joined = matmul(d_base, skip_b.T)
    d_branch = d_joined[:, :C].astype(bf16)
    g_conv_two = left_product(cols_two, d_branch)
    d_second = conv_backward(d_branch.reshape(height, n_cols, C), conv_b[1], masks_all).reshape(
        height, n_cols, C
    )
    d_pre_two = silu_two(d_second)[0]
    d_scale = jnp.sum(d_pre_two * affine_two, axis=0)
    d_shift = jnp.sum(d_pre_two, axis=0)
    d_film = exact(clip_hot.T, jnp.concatenate([d_scale, d_shift], axis=1))
    g_film = exact(d_film.T, cond_act.astype(jnp.float32))
    d_inner, g_gn2_g, g_gn2_b = group_backward(
        d_pre_two * (1.0 + film_col[None, :, :C]), norm_two, std_two, gain_f[2], onehot, counts
    )
    d_inner_b = d_inner.astype(bf16)
    g_conv_one = left_product(cols_one, d_inner_b.reshape(n_pix, C))
    d_first = conv_backward(d_inner_b, conv_b[0], masks_all).reshape(height, n_cols, C)
    d_stem_gn, g_gn1_g, g_gn1_b = group_backward(
        silu_one(d_first)[0], norm_one, std_one, gain_f[0], onehot, counts
    )
    d_stem = (d_stem_gn.reshape(n_pix, C) + d_joined[:, :C] + d_joined[:, C:]).astype(bf16)
    g_stem = left_product(stem_cols, d_stem)
    n_dp = lax.axis_size(DP)
    pairs = n_dp // 2

    def shards_of(item):
        return item.reshape(pairs, 2, -1, item.shape[-1])

    def small_rows(item):
        flat = item.reshape(n_dp, -1)
        flat = jnp.pad(flat, ((0, 0), (0, round_up(flat.shape[1], 256) - flat.shape[1])))
        return flat.reshape(n_dp, -1, 256)

    g_gains = jnp.stack([g_gn1_g, g_gn1_b, g_gn2_g, g_gn2_b, g_ln1_g, g_ln1_b, g_ln2_g, g_ln2_b])
    smalls = [
        small_rows(g_head),
        small_rows(g_stem.reshape(-1, n_dp, C // n_dp).transpose(1, 0, 2)),
        small_rows(g_gains.reshape(-1, n_dp, C // n_dp).transpose(1, 0, 2)),
    ]
    small_at = [0]
    for item in smalls:
        small_at.append(small_at[-1] + item.shape[1])
    small_end = round_up(small_at[-1], 8)
    loss_rows = jnp.zeros((n_dp, 8 + small_end - small_at[-1], 256), jnp.float32)
    smalls.append(loss_rows.at[0, -8, 0].set(local_loss))
    small = jnp.concatenate(smalls, axis=1)
    g_proj = jnp.concatenate([g_qkv, g_out, g_up], axis=0)
    chunks = [
        [shards_of(g_conv_one)],
        [shards_of(g_conv_two)],
        [shards_of(g_proj)],
        [shards_of(g_film), shards_of(g_skip), shards_of(g_down), shards_of(small)],
    ]
    heights = [sum(item.shape[2] * item.shape[3] // 256 for item in parts) for parts in chunks]
    heights[3] -= 8
    shards, sums = reduce_grads(chunks, heights, 0)
    squares, loss_sum = sums[0, 1], sums[0, 0]
    grad_norm = jnp.sqrt(squares)
    factor = jnp.minimum(1.0, CLIP_NORM / grad_norm)
    conv_rows, film_cols = 9 * C // n_dp, 2 * C // n_dp
    skip_cols, down_rows = C // n_dp, 4 * C // n_dp
    last = shards[3]
    film_end, skip_end = 2 * film_cols, 2 * film_cols + 2 * skip_cols
    film_shard = jnp.concatenate([last[:film_cols], last[film_cols:film_end]], axis=1).T
    skip_shard = jnp.concatenate(
        [last[film_end : film_end + skip_cols], last[film_end + skip_cols : skip_end]], axis=1
    ).T
    small_shard = last[skip_end + down_rows :]

    def small_part(index, like):
        rows = small_shard[small_at[index] : small_at[index + 1]].reshape(-1)
        return rows[: like.size].reshape(like.shape)

    shards = (
        jnp.stack([shards[0][:conv_rows], shards[1][:conv_rows]]),
        shards[2][: proj_w.shape[1]].T,
        film_shard,
        skip_shard,
        last[skip_end : skip_end + down_rows],
        small_part(1, stem_w),
        small_part(0, head_w),
        small_part(2, gains),
    )
    new_w, new_m, new_v = ([], [], [])
    for weight, grad_one, m_old, v_old in zip(masters, shards, firsts, seconds):
        grad_one = grad_one * factor
        m_new = BETA_ONE * m_old + (1.0 - BETA_ONE) * grad_one
        v_new = BETA_TWO * v_old + (1.0 - BETA_TWO) * grad_one * grad_one
        step_dir = (
            m_new / (1.0 - BETA_ONE**STEP) / (jnp.sqrt(v_new / (1.0 - BETA_TWO**STEP)) + ADAM_EPS)
        )
        new_w.append(weight - RATE * (step_dir + DECAY * weight))
        new_m.append(m_new)
        new_v.append(v_new)
    return (
        new_w[0],
        new_w[1],
        new_w[2],
        new_w[3],
        new_w[4],
        new_w[5],
        new_w[6],
        new_w[7],
        new_m[0],
        new_m[1],
        new_m[2],
        new_m[3],
        new_m[4],
        new_m[5],
        new_m[6],
        new_m[7],
        new_v[0],
        new_v[1],
        new_v[2],
        new_v[3],
        new_v[4],
        new_v[5],
        new_v[6],
        new_v[7],
        grad_norm,
        loss_sum,
        pix_count,
    )


def solution(mesh):
    n_dp, n_s = mesh.shape["dp"], mesh.shape["section"]
    blocks = jax.sharding.Mesh(mesh.devices.reshape(n_dp // n_s, n_s, n_s), ("a", "b", "s"))
    return jax.shard_map(
        body,
        mesh=blocks,
        in_specs=(
            P(DP, None, "s", None),
            P(DP, None, "s", None),
            P(DP, None),
            P(DP, None),
            P(DP, None, None),
            P(None, DP, None),
            P(None, DP),
            P(None, DP),
            P(None, DP),
            P(DP, None),
            P(None, DP),
            P(DP, None),
            P(None, DP),
            P(None, DP, None),
            P(None, DP),
            P(None, DP),
            P(None, DP),
            P(DP, None),
            P(None, DP),
            P(DP, None),
            P(None, DP),
            P(None, DP, None),
            P(None, DP),
            P(None, DP),
            P(None, DP),
            P(DP, None),
            P(None, DP),
            P(DP, None),
            P(None, DP),
        ),
        out_specs=(
            P(None, DP, None),
            P(None, DP),
            P(None, DP),
            P(None, DP),
            P(DP, None),
            P(None, DP),
            P(DP, None),
            P(None, DP),
            P(None, DP, None),
            P(None, DP),
            P(None, DP),
            P(None, DP),
            P(DP, None),
            P(None, DP),
            P(DP, None),
            P(None, DP),
            P(None, DP, None),
            P(None, DP),
            P(None, DP),
            P(None, DP),
            P(DP, None),
            P(None, DP),
            P(DP, None),
            P(None, DP),
            P(),
            P(),
            P(),
        ),
        check_vma=False,
    )
```

```python
import functools
import math

import jax
import jax.numpy as jnp
from jax import lax
from jax.experimental import pallas as pl
from jax.experimental.pallas import tpu as pltpu
from jax.sharding import PartitionSpec as P

CIN = 8
C = 256
HEADS = 8
HD = 32
COND = 512
GROUPS = 32
CLIPS = 4
STEP = 10


EPS_NORM = 1e-05
CLIP_NORM = 0.02
DP = ("a", "b")
RATE = 0.04
BETA_ONE = 0.9
BETA_TWO = 0.999
ADAM_EPS = 1e-08
DECAY = 0.1


def matmul(lhs_mat, rhs_mat):
    return jnp.dot(lhs_mat, rhs_mat, preferred_element_type=jnp.float32)


def left_product(lhs_mat, rhs_mat):
    return lax.dot_general(
        lhs_mat, rhs_mat, (((0,), (0,)), ((), ())), preferred_element_type=jnp.float32
    )


def exact(lhs_mat, rhs_mat):
    return jnp.dot(
        lhs_mat, rhs_mat, precision=lax.Precision.HIGHEST, preferred_element_type=jnp.float32
    )


def contract(lhs_mat, rhs_mat, lhs_dim, rhs_dim):
    return lax.dot_general(
        lhs_mat, rhs_mat, (((lhs_dim,), (rhs_dim,)), ((), ())), preferred_element_type=jnp.float32
    )


def silu_pull(x, d_out):
    gate = jax.nn.sigmoid(x)
    return d_out * (gate + x * gate * (1.0 - gate))


def clip_terms(timesteps, clap_emb):
    half_cond = COND // 2
    frequency = jnp.exp(-math.log(10000.0) * jnp.arange(half_cond, dtype=jnp.float32) / half_cond)
    angles = timesteps.astype(jnp.float32)[:, None] * frequency[None]
    cond_vec = clap_emb + jnp.concatenate([jnp.sin(angles), jnp.cos(angles)], axis=1)
    theta_clip = 0.5 * math.pi * (timesteps.astype(jnp.float32) + 1.0) / 1001.0
    return (cond_vec, jnp.cos(theta_clip), jnp.sin(theta_clip))


def layer_forward(inputs, gain_row, bias_row):
    mean_row = jnp.mean(inputs, axis=1, keepdims=True)
    centered = inputs - mean_row
    inv_std = lax.rsqrt(jnp.mean(centered * centered, axis=1, keepdims=True) + EPS_NORM)
    normed = centered * inv_std
    return (normed * gain_row + bias_row, normed, inv_std)


def layer_backward(d_out, normed, inv_std, gain_row):
    scaled = d_out * gain_row
    d_in = inv_std * (
        scaled
        - jnp.mean(scaled, axis=1, keepdims=True)
        - normed * jnp.mean(scaled * normed, axis=1, keepdims=True)
    )
    return (d_in, jnp.sum(d_out * normed, axis=0), jnp.sum(d_out, axis=0))


BIG = 1e30
LOG2E = 1.4426950408889634
SCALE = HD**-0.5 * LOG2E
VMEM_LIMIT = 56 << 20
NN = (((1,), (0,)), ((), ()))
NT = (((1,), (1,)), ((), ()))


def mxu(lhs_mat, rhs_mat, dims=NN):
    return lax.dot_general(lhs_mat, rhs_mat, dims, preferred_element_type=jnp.float32)


def split_three(value):
    high = value.astype(jnp.bfloat16).astype(jnp.float32)
    rest = value - high
    mid = rest.astype(jnp.bfloat16).astype(jnp.float32)
    return high, mid, rest - mid


def rows_of(height, parts):
    row = lax.broadcasted_iota(jnp.int32, (height, parts[0].shape[1]), 0)
    total = jnp.zeros(row.shape, jnp.float32)
    for place, part in enumerate(parts):
        total = jnp.where(row == place, part, total)
    return total


def clip_rows(ids, hit, miss):
    return [jnp.where(ids == clip, hit, miss) for clip in range(CLIPS + 1)]


def forward_kernel(heads, bq, bk, x_ref, ids_ref, out_ref, lse_ref, keys):
    n_pix = x_ref.shape[1]
    step = pl.program_id(0)

    @pl.when(step == 0)
    def _():
        for head in range(heads):
            base = 3 * HD * head
            for start in range(0, n_pix, 512):
                cols = slice(start, start + 512)
                key = x_ref[base + HD : base + 2 * HD, cols].astype(jnp.float32)
                marks = rows_of(32, clip_rows(ids_ref[:, cols], 1.0, 0.0))
                stack = jnp.concatenate([key, marks, jnp.zeros((64, 512), jnp.float32)], axis=0)
                keys[head, cols, :] = stack.T.astype(jnp.bfloat16)

    block = pl.ds(pl.multiple_of(step * bq, bq), bq)
    marks = rows_of(32, clip_rows(ids_ref[:, block], 0.0, -BIG)).astype(jnp.bfloat16)
    for head in range(heads):
        base = 3 * HD * head
        query = jnp.concatenate([x_ref[base : base + HD, block], marks], axis=0)
        total = jnp.zeros((8, bq), jnp.float32)
        acc = jnp.zeros((HD, bq), jnp.float32)
        row_max = jnp.full((1, bq), -jnp.inf, jnp.float32)
        for start in range(0, n_pix, bk):
            scores = mxu(keys[head, start : start + bk, :64], query)
            new_max = jnp.maximum(row_max, jnp.max(scores, axis=0, keepdims=True) * SCALE)
            probs = jnp.exp2(scores * SCALE - new_max)
            decay = jnp.exp2(row_max - new_max)
            total = total * decay + jnp.sum(probs.reshape(bk // 8, 8, bq), axis=0)
            value = x_ref[base + 2 * HD : base + 3 * HD, start : start + bk]
            acc = acc * decay + mxu(value, probs.astype(jnp.bfloat16))
            row_max = new_max
        total = jnp.sum(total, axis=0, keepdims=True)
        out_ref[HD * head : HD * (head + 1), :] = (acc / total).astype(jnp.bfloat16)
        lse_ref[8 * head : 8 * (head + 1), :] = jnp.broadcast_to(row_max + jnp.log2(total), (8, bq))


def attention_forward(heads_x, pixel_ids):
    lanes, n_pix = heads_x.shape
    heads = lanes // (3 * HD)
    bq, bk = min(2048, n_pix), min(512, n_pix)
    return pl.pallas_call(
        functools.partial(forward_kernel, heads, bq, bk),
        grid=(n_pix // bq,),
        in_specs=[
            pl.BlockSpec((lanes, n_pix), lambda i: (0, 0)),
            pl.BlockSpec((1, n_pix), lambda i: (0, 0)),
        ],
        out_specs=[
            pl.BlockSpec((heads * HD, bq), lambda i: (0, i)),
            pl.BlockSpec((heads * 8, bq), lambda i: (0, i)),
        ],
        out_shape=[
            jax.ShapeDtypeStruct((heads * HD, n_pix), jnp.bfloat16),
            jax.ShapeDtypeStruct((heads * 8, n_pix), jnp.float32),
        ],
        scratch_shapes=[pltpu.VMEM((heads, n_pix, 128), jnp.bfloat16)],
        compiler_params=pltpu.CompilerParams(vmem_limit_bytes=VMEM_LIMIT),
    )(heads_x, pixel_ids)


def backward_kernel(
    heads, bq, bk, x_ref, ids_ref, do_ref, o_ref, lse_ref, out_ref,
    queries, keys, values, d_outs, d_query, query_rows, d_out_rows,
):
    n_pix = x_ref.shape[1]
    step = pl.program_id(0)

    @pl.when(step == 0)
    def _():
        d_query[...] = jnp.zeros_like(d_query)
        for head in range(heads):
            base = 3 * HD * head

            def prepare(part, carry):
                cols = pl.ds(pl.multiple_of(part * 512, 512), 512)
                ids = ids_ref[:, cols]
                one = jnp.ones((1, 512), jnp.float32)
                key = x_ref[base + HD : base + 2 * HD, cols].astype(jnp.float32)
                marks = rows_of(32, clip_rows(ids, 1.0, 0.0) + [one, one, one])
                stack = jnp.concatenate([key, key, key, marks], axis=0)
                keys[head, cols, :] = stack.T.astype(jnp.bfloat16)
                value = x_ref[base + 2 * HD : base + 3 * HD, cols].astype(jnp.float32)
                stack = jnp.concatenate(
                    [value, rows_of(32, [one, one, one]), jnp.zeros((64, 512), jnp.float32)], axis=0
                )
                values[head, cols, :] = stack.T.astype(jnp.bfloat16)
                query = x_ref[base : base + HD, cols].astype(jnp.float32) * SCALE
                lse = lse_ref[8 * head : 8 * head + 1, cols]
                marks = rows_of(32, clip_rows(ids, 0.0, -BIG) + list(split_three(-lse)))
                stack = jnp.concatenate([*split_three(query), marks], axis=0)
                queries[head, :, cols] = stack.astype(jnp.bfloat16)
                d_out = do_ref[HD * head : HD * (head + 1), cols].astype(jnp.float32)
                out = o_ref[HD * head : HD * (head + 1), cols].astype(jnp.float32)
                delta = jnp.sum(d_out * out, axis=0, keepdims=True)
                stack = jnp.concatenate([d_out, rows_of(32, split_three(-delta))], axis=0)
                d_outs[head, :, cols] = stack.astype(jnp.bfloat16)
                zero = jnp.zeros((96, 512), jnp.float32)
                query = x_ref[base : base + HD, cols].astype(jnp.float32)
                query_rows[head, cols, :] = jnp.concatenate([query, zero], 0).T.astype(jnp.bfloat16)
                d_out_rows[head, cols, :] = jnp.concatenate([d_out, zero], 0).T.astype(jnp.bfloat16)
                return carry

            lax.fori_loop(0, n_pix // 512, prepare, 0)

    block = pl.ds(pl.multiple_of(step * bk, bk), bk)
    for head in range(heads):
        base = 3 * HD * head
        key, value = keys[head, block, :], values[head, block, :64]
        key_t = x_ref[base + HD : base + 2 * HD, block]
        d_value = jnp.zeros((bk, 128), jnp.float32)
        d_key = jnp.zeros((bk, 128), jnp.float32)
        for start in range(0, n_pix, bq):
            cols = slice(start, start + bq)
            probs = jnp.exp2(mxu(key, queries[head, :, cols]))
            d_scores = (probs * mxu(value, d_outs[head, :, cols])).astype(jnp.bfloat16)
            probs = probs.astype(jnp.bfloat16)
            d_value += mxu(probs, d_out_rows[head, cols, :])
            d_key += mxu(d_scores, query_rows[head, cols, :])
            d_query[head, :, cols] += mxu(key_t, d_scores)
        d_key, d_value = d_key.T[:HD], d_value.T[:HD]
        out_ref[base + HD : base + 2 * HD, block] = (d_key * (HD**-0.5)).astype(jnp.bfloat16)
        out_ref[base + 2 * HD : base + 3 * HD, block] = d_value.astype(jnp.bfloat16)

    @pl.when(step == pl.num_programs(0) - 1)
    def _():
        for head in range(heads):
            base = 3 * HD * head
            out_ref[base : base + HD, :] = (d_query[head] * (HD**-0.5)).astype(jnp.bfloat16)


def attention_backward(heads_x, log_total, d_heads, out_heads, pixel_ids, bq=1024, bk=1024):
    lanes, n_pix = heads_x.shape
    heads = lanes // (3 * HD)
    bq, bk = min(bq, n_pix), min(bk, n_pix)
    operands = (heads_x, pixel_ids, d_heads, out_heads, log_total)
    return pl.pallas_call(
        functools.partial(backward_kernel, heads, bq, bk),
        grid=(n_pix // bk,),
        in_specs=[pl.BlockSpec(item.shape, lambda i: (0, 0)) for item in operands],
        out_specs=pl.BlockSpec((lanes, n_pix), lambda i: (0, 0)),
        out_shape=jax.ShapeDtypeStruct((lanes, n_pix), jnp.bfloat16),
        scratch_shapes=[
            pltpu.VMEM((heads, 128, n_pix), jnp.bfloat16),
            pltpu.VMEM((heads, n_pix, 128), jnp.bfloat16),
            pltpu.VMEM((heads, n_pix, 128), jnp.bfloat16),
            pltpu.VMEM((heads, 64, n_pix), jnp.bfloat16),
            pltpu.VMEM((heads, HD, n_pix), jnp.float32),
            pltpu.VMEM((heads, n_pix, 128), jnp.bfloat16),
            pltpu.VMEM((heads, n_pix, 128), jnp.bfloat16),
        ],
        compiler_params=pltpu.CompilerParams(vmem_limit_bytes=VMEM_LIMIT),
    )(*operands)


MESH = pl.DeviceIdType.MESH


def round_up(count, unit):
    return -(-count // unit) * unit


def greet(peers):
    barrier = pltpu.get_barrier_semaphore()
    for peer in peers:
        pl.semaphore_signal(barrier, inc=1, device_id=peer, device_id_type=MESH)
    pl.semaphore_wait(barrier, len(peers))


def push(src, dst, sems, slot, peer):
    copy = pltpu.make_async_remote_copy(
        src_ref=src,
        dst_ref=dst,
        send_sem=sems.at[0, slot],
        recv_sem=sems.at[1, slot],
        device_id=peer,
        device_id_type=MESH,
    )
    copy.start()
    return copy


def reduce_kernel(n_a, n_x, n_s, chunks, square_rows, *refs):
    n_in = sum(len(parts) for parts in chunks)
    n_chunk = len(chunks)
    ins = refs[:n_in]
    outs = refs[n_in : n_in + n_chunk]
    norm_ref = refs[n_in + n_chunk]
    scratch = list(refs[n_in + n_chunk + 1 :])
    halves = scratch[:n_in]
    accs = scratch[n_in : n_in + n_chunk]
    one_bufs = scratch[n_in + n_chunk : n_in + 3 * n_chunk]
    two_bufs = scratch[n_in + 3 * n_chunk : n_in + 5 * n_chunk]
    bit_bufs = scratch[n_in + 5 * n_chunk : n_in + 6 * n_chunk]
    squares, sems = scratch[n_in + 6 * n_chunk :]
    bits = n_s.bit_length() - 1
    my_a, my_b, my_s = lax.axis_index("a"), lax.axis_index("b"), lax.axis_index("s")
    core, my_x = lax.rem(my_b, 2), lax.div(my_b, 2)
    n_b = 2 * n_x
    n_d = n_a * n_b

    def dp_peer(off):
        place = lax.rem(my_a * n_b + my_b + off, n_d)
        return {"a": lax.div(place, n_b), "b": lax.rem(place, n_b)}

    def s_peer(bit):
        flipped = my_s + (1 << bit) - 2 * (1 << bit) * lax.rem(lax.div(my_s, 1 << bit), 2)
        return {"s": flipped}

    greet([dp_peer(off) for off in range(1, n_d)] + [s_peer(bit) for bit in range(bits)])
    slots = iter(range(sems.shape[1]))

    first_in = []
    at = 0
    for parts in chunks:
        first_in.append(at)
        at += len(parts)

    def core_send(c):
        copies = []
        for i in range(first_in[c], first_in[c] + len(chunks[c])):
            copies.append(
                push(ins[i].at[:, 1 - core], halves[i], sems, next(slots), {"b": my_b + 1 - 2 * core})
            )
        return copies

    def core_sum(c):
        acc = accs[c]
        row = 0
        for i in range(first_in[c], first_in[c] + len(chunks[c])):
            rows, lanes = ins[i].shape[2:]
            for lane in range(0, lanes, 256):
                for j in range(n_a * n_x):
                    acc[j // n_x, j % n_x, row : row + rows] = (
                        ins[i][j, core, :, lane : lane + 256] + halves[i][j, :, lane : lane + 256]
                    )
                row += rows
        if row < acc.shape[2]:
            for j in range(n_a * n_x):
                acc[j // n_x, j % n_x, row:] = jnp.zeros((acc.shape[2] - row, 256), jnp.float32)

    def plane_moves(c, stage):
        rows = accs[c].shape[2] // 2
        for half in range(2):
            over_x = (half + stage) % 2 == 0
            for off in range(1, n_x if over_x else n_a):
                yield half, over_x, off, pl.ds(half * rows, rows)

    def plane_buf(c, stage, half, off):
        return (one_bufs, two_bufs)[stage][2 * c + half].at[off - 1]

    def plane_send(c, stage):
        copies = []
        for half, over_x, off, rows in plane_moves(c, stage):
            acc = accs[c]
            if over_x:
                there = lax.rem(my_x + off, n_x)
                src = acc.at[:, there, rows] if stage == 0 else acc.at[my_a, there, rows]
                peer = {"b": 2 * there + core}
            else:
                there = lax.rem(my_a + off, n_a)
                src = acc.at[there, :, rows] if stage == 0 else acc.at[there, my_x, rows]
                peer = {"a": there}
            copies.append(push(src, plane_buf(c, stage, half, off), sems, next(slots), peer))
        return copies

    def plane_sum(c, stage):
        for half, over_x, off, rows in plane_moves(c, stage):
            buf = plane_buf(c, stage, half, off)
            if stage == 1:
                accs[c][my_a, my_x, rows] += buf[...]
            elif over_x:
                for j in range(n_a):
                    accs[c][j, my_x, rows] += buf[j]
            else:
                for j in range(n_x):
                    accs[c][my_a, j, rows] += buf[j]

    def span(c, level):
        length = accs[c].shape[2]
        start = 0
        for bit in range(level):
            length //= 2
            start = start + lax.rem(lax.div(my_s, 1 << bit), 2) * length
        return start, length

    def s_send(c, bit):
        start, length = span(c, bit)
        length //= 2
        mine = lax.rem(lax.div(my_s, 1 << bit), 2)
        rows = pl.ds(pl.multiple_of(start + (1 - mine) * length, 8), length)
        return [
            push(
                accs[c].at[my_a, my_x, rows],
                bit_bufs[c].at[bit, pl.ds(0, length)],
                sems,
                next(slots),
                s_peer(bit),
            )
        ]

    def s_sum(c, bit):
        start, length = span(c, bit + 1)
        rows = pl.ds(pl.multiple_of(start, 8), length)
        total = accs[c][my_a, my_x, rows] + bit_bufs[c][bit, :length]
        if bit == bits - 1:
            outs[c][rows] = total
        else:
            accs[c][my_a, my_x, rows] = total

    def up_send(c, bit):
        start, length = span(c, bit + 1)
        rows = pl.ds(pl.multiple_of(start, 8), length)
        return [push(outs[c].at[rows], outs[c].at[rows], sems, next(slots), s_peer(bit))]

    steps = [(core_send, core_sum, ())]
    steps += [(plane_send, plane_sum, (stage,)) for stage in range(2)]
    steps += [(s_send, s_sum, (bit,)) for bit in range(bits)]
    steps += [(up_send, None, (bit,)) for bit in reversed(range(bits))]
    flying = [None] * n_chunk
    for tick in range(n_chunk + len(steps)):
        for c in range(n_chunk):
            at = tick - c
            if at < 0 or at > len(steps):
                continue
            if at > 0:
                for copy in flying[c]:
                    copy.wait()
                if steps[at - 1][1] is not None:
                    steps[at - 1][1](c, *steps[at - 1][2])
            if at < len(steps):
                flying[c] = steps[at][0](c, *steps[at][2])

    lane = lax.broadcasted_iota(jnp.int32, (8, 256), 1)
    total = jnp.zeros((8, 256), jnp.float32)
    for c in range(n_chunk):
        rows = square_rows[c]
        total = total + jnp.sum((outs[c][:rows] * outs[c][:rows]).reshape(rows // 8, 8, 256), axis=0)
    total = jnp.sum(jnp.sum(total, axis=0, keepdims=True), axis=1, keepdims=True)
    last = square_rows[-1]
    squares[my_a * n_b + my_b] = jnp.where(lane == 1, total, outs[-1][last : last + 8])
    copies = []
    for off in range(1, n_d):
        place = squares.at[my_a * n_b + my_b]
        copies.append(push(place, place, sems, next(slots), dp_peer(off)))
    for copy in copies:
        copy.wait()
    total = squares[0]
    for place in range(1, n_d):
        total = total + squares[place]
    norm_ref[...] = total


def reduce_grads(chunks, square_rows, collective_id):
    n_a, n_b, n_s = lax.axis_size("a"), lax.axis_size("b"), lax.axis_size("s")
    n_x = n_b // 2
    bits = n_s.bit_length() - 1
    flat = [item for parts in chunks for item in parts]
    heights = [
        round_up(sum(item.shape[2] * item.shape[3] // 256 for item in parts), 16 * max(n_s // 2, 1))
        for parts in chunks
    ]
    f32 = jnp.float32
    one_shapes, two_shapes = [], []
    for rows in heights:
        half = rows // 2
        one_shapes += [(n_x - 1, n_a, half, 256), (n_a - 1, n_x, half, 256)]
        two_shapes += [(n_a - 1, half, 256), (n_x - 1, half, 256)]
    scratch = [(item.shape[0], *item.shape[2:]) for item in flat]
    scratch += [(n_a, n_x, rows, 256) for rows in heights]
    scratch += one_shapes + two_shapes
    scratch += [(bits, rows // 2, 256) for rows in heights]
    scratch += [(n_a * n_b, 8, 256)]
    n_copy = len(flat) + len(chunks) * 2 * (n_x - 1 + n_a - 1 + bits) + n_a * n_b - 1
    out = pl.pallas_call(
        functools.partial(reduce_kernel, n_a, n_x, n_s, [[None] * len(parts) for parts in chunks], square_rows),
        in_specs=[pl.BlockSpec(memory_space=pltpu.VMEM)] * len(flat),
        out_specs=[pl.BlockSpec(memory_space=pltpu.VMEM)] * (len(chunks) + 1),
        out_shape=[jax.ShapeDtypeStruct((rows, 256), f32) for rows in heights]
        + [jax.ShapeDtypeStruct((8, 256), f32)],
        scratch_shapes=[pltpu.VMEM(shape, f32) for shape in scratch]
        + [pltpu.SemaphoreType.DMA((2, n_copy))],
        compiler_params=pltpu.CompilerParams(
            collective_id=collective_id, has_side_effects=True, vmem_limit_bytes=VMEM_LIMIT
        ),
    )(*flat)
    return out[:-1], out[-1]


def exchange_kernel(n_b, has_stats, has_edges, *refs):
    refs = list(refs)
    take = lambda count: [refs.pop(0) for _ in range(count)]
    stats_in, edges_in = take(has_stats), take(2 * has_edges)
    stats_out, edges_out = take(has_stats), take(2 * has_edges)
    held = take(has_stats)
    (sems,) = refs
    me = lax.axis_index("b")
    peers = [{"b": lax.rem(me + off, n_b)} for off in range(1, n_b)]
    greet(peers)
    copies = []
    if has_edges:
        first, last = edges_in
        left, right = edges_out
        copies.append(push(last, left, sems, n_b - 1, {"b": lax.rem(me + 1, n_b)}))
        copies.append(push(first, right, sems, n_b, {"b": lax.rem(me + n_b - 1, n_b)}))
    if has_stats:
        held[0][me] = stats_in[0][...]
        for slot, peer in enumerate(peers):
            copies.append(push(stats_in[0], held[0].at[me], sems, slot, peer))
    for copy in copies:
        copy.wait()
    if has_stats:
        total = held[0][0]
        for place in range(1, n_b):
            total = total + held[0][place]
        stats_out[0][...] = total


def exchange(collective_id, stats=None, edges=None):
    n_b = lax.axis_size("b")
    operands = ([] if stats is None else [stats]) + ([] if edges is None else list(edges))
    shapes = [jax.ShapeDtypeStruct(item.shape, item.dtype) for item in operands]
    scratch = [] if stats is None else [pltpu.VMEM((n_b, *stats.shape), stats.dtype)]
    vmem = pl.BlockSpec(memory_space=pltpu.VMEM)
    return pl.pallas_call(
        functools.partial(exchange_kernel, n_b, int(stats is not None), int(edges is not None)),
        in_specs=[vmem] * len(operands),
        out_specs=[vmem] * len(operands),
        out_shape=shapes,
        scratch_shapes=scratch + [pltpu.SemaphoreType.DMA((2, n_b + 1))],
        compiler_params=pltpu.CompilerParams(collective_id=collective_id, has_side_effects=True),
    )(*operands)


def swap_kernel(n_b, spread, x_ref, out_ref, sems, own_sem):
    me = lax.axis_index("b")
    peers = [lax.rem(me + off, n_b) for off in range(1, n_b)]
    greet([{"b": peer} for peer in peers])
    rows = (x_ref if spread else out_ref).shape[0] // n_b
    cols = (out_ref if spread else x_ref).shape[1] // n_b

    def tall(ref, place):
        return ref.at[pl.ds(pl.multiple_of(place * rows, 16), rows)]

    def wide(ref, place):
        return ref.at[:, pl.ds(pl.multiple_of(place * cols, 128), cols)]

    source, target = (tall, wide) if spread else (wide, tall)
    copies = [
        push(source(x_ref, peer), target(out_ref, me), sems, slot, {"b": peer})
        for slot, peer in enumerate(peers)
    ]
    own = pltpu.make_async_copy(source(x_ref, me), target(out_ref, me), own_sem)
    own.start()
    for copy in copies:
        copy.wait()
    own.wait()


def swap(x, spread, collective_id):
    n_b = lax.axis_size("b")
    rows, cols = x.shape
    shape = (rows // n_b, cols * n_b) if spread else (rows * n_b, cols // n_b)
    return pl.pallas_call(
        functools.partial(swap_kernel, n_b, spread),
        in_specs=[pl.BlockSpec(memory_space=pl.ANY)],
        out_specs=pl.BlockSpec(memory_space=pl.ANY),
        out_shape=jax.ShapeDtypeStruct(shape, x.dtype),
        scratch_shapes=[pltpu.SemaphoreType.DMA((2, n_b - 1)), pltpu.SemaphoreType.DMA(())],
        compiler_params=pltpu.CompilerParams(collective_id=collective_id, has_side_effects=True),
    )(x)


def opening_kernel(n_a, n_b, n_gather, *refs):
    main, first, last = refs[:3]
    shards = refs[3 : 3 + n_gather]
    main_out, left, right = refs[3 + n_gather : 6 + n_gather]
    wholes = refs[6 + n_gather : 6 + 2 * n_gather]
    (sems,) = refs[6 + 2 * n_gather :]
    my_a, my_b, my_s = lax.axis_index("a"), lax.axis_index("b"), lax.axis_index("s")
    n_d = n_a * n_b
    place = my_a * n_b + my_b

    def at(b, s):
        return {"b": lax.rem(b + n_b, n_b), "s": lax.rem(s + n_b, n_b)}

    dp_peers = []
    for off in range(1, n_d):
        there = lax.rem(place + off, n_d)
        dp_peers.append({"a": lax.div(there, n_b), "b": lax.rem(there, n_b)})
    mirrored = my_b != my_s
    shift = jnp.where(mirrored, 0, 1)
    greet(
        dp_peers
        + [at(my_s + 1, my_b), at(my_s - 1, my_b), at(my_s, my_b + 1), at(my_s, my_b - 1)]
        + [at(my_s + shift, my_b + shift)]
    )

    @pl.when(mirrored)
    def _():
        push(main, main_out, sems, 0, at(my_s, my_b))

    @pl.when(jnp.logical_not(mirrored))
    def _():
        main_out[...] = main[...]

    copies = [
        push(last, left, sems, 1, at(my_s + 1, my_b)),
        push(first, right, sems, 2, at(my_s - 1, my_b)),
    ]
    slot = 3
    for shard, whole in zip(shards, wholes):
        rows = shard.shape[0]
        mine = pl.ds(pl.multiple_of(place * rows, 8), rows)
        for peer in dp_peers:
            copies.append(push(shard, whole.at[mine], sems, slot, peer))
            slot += 1
        whole[mine] = shard[...]
    for copy in copies:
        copy.wait()

    @pl.when(mirrored)
    def _():
        pltpu.make_async_remote_copy(
            src_ref=main,
            dst_ref=main_out,
            send_sem=sems.at[0, 0],
            recv_sem=sems.at[1, 0],
            device_id=at(my_s, my_b),
            device_id_type=MESH,
        ).wait()


def opening(main, first, last, shards, collective_id):
    n_a, n_b = lax.axis_size("a"), lax.axis_size("b")
    n_d = n_a * n_b
    operands = [main, first, last, *shards]
    shapes = [jax.ShapeDtypeStruct(item.shape, item.dtype) for item in operands[:3]]
    shapes += [jax.ShapeDtypeStruct((n_d * item.shape[0], item.shape[1]), item.dtype) for item in shards]
    vmem = pl.BlockSpec(memory_space=pltpu.VMEM)
    return pl.pallas_call(
        functools.partial(opening_kernel, n_a, n_b, len(shards)),
        in_specs=[vmem] * len(operands),
        out_specs=[vmem] * len(operands),
        out_shape=shapes,
        scratch_shapes=[pltpu.SemaphoreType.DMA((2, 3 + len(shards) * (n_d - 1)))],
        compiler_params=pltpu.CompilerParams(collective_id=collective_id, has_side_effects=True),
    )(*operands)


def conv_forward(widened, weight, masks_all):
    height, n_wide, n_in = widened.shape
    n_cols = n_wide - 2
    padded = jnp.pad(widened, ((1, 1), (0, 0), (0, 0)))
    taps = [
        padded[tap_row : tap_row + height, tap_col : tap_col + n_cols]
        * masks_all[tap_col][None, :, None]
        for tap_row in range(3)
        for tap_col in range(3)
    ]
    columns = jnp.concatenate(taps, axis=2).reshape(height * n_cols, 9 * n_in)
    return columns, weight(columns)


def conv_backward(widened, weight, masks_all):
    height, n_wide, n_out = widened.shape
    n_cols = n_wide - 2
    padded = jnp.pad(widened, ((1, 1), (0, 0), (0, 0)))
    taps = [
        padded[2 - tap_row : 2 - tap_row + height, 2 - tap_col : 2 - tap_col + n_cols]
        * masks_all[2 - tap_col][None, :, None]
        for tap_row in range(3)
        for tap_col in range(3)
    ]
    flipped = weight.reshape(9, -1, n_out).transpose(0, 2, 1).reshape(9 * n_out, -1)
    return matmul(jnp.concatenate(taps, axis=2).reshape(height * n_cols, 9 * n_out), flipped)


def group_sums(one, two, onehot):
    per_group = one.shape[2] // GROUPS

    def fold(item):
        return exact(onehot.T, jnp.sum(item, axis=0)).reshape(-1, GROUPS, per_group).sum(axis=2)

    sums = jnp.concatenate([fold(one), fold(two)], axis=1)
    return jnp.pad(sums, ((0, 8 - sums.shape[0]), (0, 128 - sums.shape[1])))


def group_rows(sums, counts):
    return sums[: CLIPS + 1, :GROUPS] / counts, sums[: CLIPS + 1, GROUPS : 2 * GROUPS] / counts


def per_column(onehot, values):
    return jnp.repeat(exact(onehot, values), C // GROUPS, axis=1)


def edges_of(item, width=1):
    count = item.shape[1]
    return item[:, :width].reshape(item.shape[0], -1), item[:, count - width :].reshape(
        item.shape[0], -1
    )


def widen(item, left, right):
    height, _, chans = item.shape
    left, right = (side.reshape(height, -1, chans) for side in (left, right))
    return jnp.concatenate([left, item, right], axis=1)


def group_forward(inputs, onehot, wide_hot, counts, collective_id):
    sums, left, right = exchange(
        collective_id, group_sums(inputs, inputs * inputs, onehot), edges_of(inputs)
    )
    mean_row, square_row = group_rows(sums, counts)
    inv_std = lax.rsqrt(square_row - mean_row * mean_row + EPS_NORM)
    mean_col, std_col = per_column(wide_hot, mean_row), per_column(wide_hot, inv_std)
    return (widen(inputs, left, right) - mean_col[None]) * std_col[None], std_col


def group_backward(d_out, normed, std_col, gain_row, onehot, wide_hot, counts, collective_id, wide):
    own = normed[:, 1:-1]
    scaled = d_out * gain_row
    sums = group_sums(scaled, scaled * own, onehot)
    if wide:
        sums, left, right = exchange(collective_id, sums, edges_of(scaled))
        scaled = widen(scaled, left, right)
        hot = wide_hot
    else:
        (sums,) = exchange(collective_id, sums)
        normed, std_col, hot = own, std_col[1:-1], onehot
    one_row, two_row = group_rows(sums, counts)
    mean_one, mean_two = per_column(hot, one_row), per_column(hot, two_row)
    d_in = std_col[None] * (scaled - mean_one[None] - normed * mean_two[None])
    return d_in, jnp.sum(d_out * own, axis=(0, 1)), jnp.sum(d_out, axis=(0, 1))


def body(
    clean_lat,
    noise_lat,
    column_ids,
    timesteps,
    clap_emb,
    conv_w,
    proj_w,
    film_w,
    skip_w,
    down_w,
    stem_w,
    head_w,
    gains,
    conv_m,
    proj_m,
    film_m,
    skip_m,
    down_m,
    stem_m,
    head_m,
    gains_m,
    conv_v,
    proj_v,
    film_v,
    skip_v,
    down_v,
    stem_v,
    head_v,
    gains_v,
):
    bf16, f32 = jnp.bfloat16, jnp.float32
    masters = (conv_w, proj_w, film_w, skip_w, down_w, stem_w, head_w, gains)
    firsts = (conv_m, proj_m, film_m, skip_m, down_m, stem_m, head_m, gains_m)
    seconds = (conv_v, proj_v, film_v, skip_v, down_v, stem_v, head_v, gains_v)
    n_dp, n_s = lax.axis_size(DP), lax.axis_size("s")
    conv_b = [lax.all_gather(conv_w[i].astype(bf16), DP, axis=0, tiled=True) for i in range(2)]
    head_size = head_w.size
    head_rows = round_up(round_up(head_size, 256) // 256, 16)
    head_flat = jnp.pad(head_w.reshape(-1), (0, head_rows * 256 - head_size)).reshape(-1, 256)
    late = jnp.concatenate([proj_w.T, down_w, head_flat], axis=0).astype(bf16)
    late = lax.all_gather(late, DP, axis=0, tiled=False)
    proj_cols, down_rows = proj_w.shape[1], down_w.shape[0]
    proj_t = late[:, :proj_cols].reshape(-1, C)
    down_b = late[:, proj_cols : proj_cols + down_rows].reshape(-1, C)
    head_b = late[:, proj_cols + down_rows :].reshape(n_dp, -1)[:, :head_size].reshape(-1, CIN)

    _, height, n_cols, _ = clean_lat.shape
    n_pix = height * n_cols
    wide = n_cols * CIN
    extra = jnp.concatenate(
        [column_ids[0].astype(f32), timesteps[0].astype(f32), clap_emb[0].reshape(-1)]
    )
    extra_rows = round_up(-(-extra.size // wide), 8)
    extra = jnp.pad(extra, (0, extra_rows * wide - extra.size)).reshape(-1, wide)
    both = jnp.concatenate([clean_lat[0], noise_lat[0]], axis=0)
    pack = jnp.concatenate([both.reshape(2 * height, wide), extra], axis=0)
    first, last = (
        jnp.pad(both[:, at], ((0, 0), (0, 128 - CIN))) for at in (0, n_cols - 1)
    )
    own_count = jnp.sum((column_ids < CLIPS).astype(f32)) * (height * CIN)
    stem_rows = stem_w.shape[0]
    front = jnp.concatenate([stem_w, gains], axis=0)
    front = jnp.pad(front, ((0, 128 - front.shape[0]), (0, 0))).T.astype(bf16)
    pack, left, right, film_t, skip_t, front, counts_all = opening(
        pack,
        first,
        last,
        [film_w.T.astype(bf16), skip_w.T.astype(bf16), front, jnp.full((8, 128), own_count)],
        0,
    )
    pix_count = jnp.sum(counts_all.reshape(n_dp, 8, 128)[:, 0, 0])
    stem_t = front[:, :stem_rows]
    gain_f = front[:, stem_rows : stem_rows + 8].T.astype(f32)
    both = pack[: 2 * height].reshape(2 * height, n_cols, CIN)
    both = jnp.concatenate([left[:, None, :CIN], both, right[:, None, :CIN]], axis=1)
    clean_row, noise_row = both[:height], both[height:]
    extra = pack[2 * height :].reshape(-1)
    row_cols = column_ids.shape[1]
    ids_row = extra[:row_cols].astype(jnp.int32)
    times = extra[row_cols : row_cols + CLIPS]
    emb = extra[row_cols + CLIPS : row_cols + CLIPS + CLIPS * COND].reshape(CLIPS, COND)

    edge_pad = jnp.full((2,), -1, jnp.int32)
    ids_rim = lax.dynamic_slice_in_dim(
        jnp.concatenate([edge_pad, ids_row, edge_pad]), lax.axis_index("b") * n_cols, n_cols + 4
    )
    own_ids, wide_ids = ids_rim[2:-2], ids_rim[1:-1]
    masks_all = [(ids_rim[1 + at : 1 + at + n_cols] == own_ids).astype(bf16) for at in range(3)]
    wide_masks = [(ids_rim[at : at + n_cols + 2] == wide_ids).astype(bf16) for at in range(3)]
    labels = jnp.arange(CLIPS + 1)
    wide_hot = (wide_ids[:, None] == labels[None, :]).astype(f32)
    onehot = wide_hot[1:-1]
    full_onehot = (ids_row[:, None] == labels[None, :]).astype(f32)
    counts = jnp.maximum(jnp.sum(full_onehot, axis=0) * (height * (C // GROUPS)), 1.0)[:, None]
    clip_hot = onehot[:, :CLIPS]
    wide_clips = wide_hot[:, :CLIPS]
    wide_valid = jnp.sum(wide_clips, axis=1)
    cond_vec, alpha_clip, sigma_clip = clip_terms(times, emb)
    alpha_col = exact(wide_clips, alpha_clip[:, None])[:, 0][None, :, None]
    sigma_col = exact(wide_clips, sigma_clip[:, None])[:, 0][None, :, None]
    noisy_in = alpha_col * clean_row + sigma_col * noise_row
    target = alpha_col * noise_row - sigma_col * clean_row
    stem_cols, stem = conv_forward(
        noisy_in.astype(bf16), lambda cols: mxu(cols, stem_t, NT), masks_all
    )
    stem = stem.reshape(height, n_cols, C)
    norm_one, std_one = group_forward(stem, onehot, wide_hot, counts, 1)
    act_one = norm_one * gain_f[0] + gain_f[1]
    first_act = jax.nn.silu(act_one).astype(bf16)
    cols_one, inner_out = conv_forward(first_act, lambda cols: matmul(cols, conv_b[0]), masks_all)
    inner_out = inner_out.reshape(height, n_cols, C)
    cond_act = jax.nn.silu(cond_vec).astype(bf16)
    film_col = exact(wide_clips, mxu(cond_act, film_t, NT))
    norm_two, std_two = group_forward(inner_out, onehot, wide_hot, counts, 2)
    affine_two = norm_two * gain_f[2] + gain_f[3]
    act_two = affine_two * (1.0 + film_col[None, :, :C]) + film_col[None, :, C:]
    second = jax.nn.silu(act_two).astype(bf16)
    cols_two, branch = conv_forward(second, lambda cols: matmul(cols, conv_b[1]), masks_all)
    stem_rows_f = stem.reshape(n_pix, C)
    joined = jnp.concatenate([stem_rows_f + branch, stem_rows_f], axis=1).astype(bf16)
    base_rows = mxu(joined, skip_t, NT)
    ln_one, normed_one, lstd_one = layer_forward(base_rows, gain_f[4], gain_f[5])
    ln_one_b = ln_one.astype(bf16)
    proj_qkv, proj_out, proj_up = proj_t[: 3 * C], proj_t[3 * C : 4 * C], proj_t[4 * C :]
    qkv_t = mxu(proj_qkv, ln_one_b, NT).astype(bf16)
    pixel_ids = jnp.broadcast_to(
        ids_row.reshape(n_s, 1, n_cols), (n_s, height, n_cols)
    ).reshape(1, -1)
    heads_x = swap(qkv_t, True, 3)
    out_heads, log_total = attention_forward(heads_x, pixel_ids)
    attended_t = swap(out_heads, False, 4)
    mid_rows = base_rows + contract(attended_t, proj_out, 0, 1)
    ln_two, normed_two, lstd_two = layer_forward(mid_rows, gain_f[6], gain_f[7])
    ln_two_b = ln_two.astype(bf16)
    hidden = mxu(ln_two_b, proj_up, NT)
    act_out, gelu_pull = jax.vjp(jax.nn.gelu, hidden)
    act_b = act_out.astype(bf16)
    top_rows = mid_rows + matmul(act_b, down_b)
    top_b = top_rows.reshape(height, n_cols, C).astype(bf16)
    left, right = exchange(5, None, edges_of(top_b, 2))
    head_cols, pred = conv_forward(
        widen(top_b, left, right), lambda cols: matmul(cols, head_b), wide_masks
    )
    residue = pred.reshape(height, n_cols + 2, CIN) - target
    weighted = wide_valid[None, :, None] * residue
    local_loss = jnp.sum((weighted * residue)[:, 1:-1])
    d_pred = (2.0 * weighted / pix_count).astype(bf16)
    d_own = jnp.pad(d_pred[:, 1:-1], ((0, 0), (1, 1), (0, 0)))
    g_head = left_product(head_cols, d_own.reshape(-1, CIN))
    d_top = conv_backward(d_pred, head_b, masks_all)
    d_top_b = d_top.astype(bf16)
    g_down = left_product(act_b, d_top_b)
    d_hidden = gelu_pull(matmul(d_top_b, down_b.T))[0].astype(bf16)
    g_up = left_product(d_hidden, ln_two_b)
    d_ln_two, g_ln2_g, g_ln2_b = layer_backward(
        matmul(d_hidden, proj_up), normed_two, lstd_two, gain_f[6]
    )
    d_mid = d_top + d_ln_two
    d_mid_b = d_mid.astype(bf16)
    g_out = contract(d_mid_b, attended_t, 0, 1)
    d_att_t = contract(proj_out, d_mid_b, 0, 1).astype(bf16)
    d_heads = swap(d_att_t, True, 6)
    d_heads_x = attention_backward(heads_x, log_total, d_heads, out_heads, pixel_ids)
    d_qkv_t = swap(d_heads_x, False, 7)
    g_qkv = matmul(d_qkv_t, ln_one_b)
    d_ln_one, g_ln1_g, g_ln1_b = layer_backward(
        contract(d_qkv_t, proj_qkv, 0, 0), normed_one, lstd_one, gain_f[4]
    )
    d_base = (d_mid + d_ln_one).astype(bf16)
    g_skip = left_product(d_base, joined)
    d_joined = matmul(d_base, skip_t)
    d_branch = d_joined[:, :C].astype(bf16)
    g_conv_two = left_product(cols_two, d_branch)
    d_branch = d_branch.reshape(height, n_cols, C)
    left, right = exchange(8, None, edges_of(d_branch))
    d_second = conv_backward(widen(d_branch, left, right), conv_b[1], masks_all).reshape(
        height, n_cols, C
    )
    d_pre_two = silu_pull(act_two[:, 1:-1], d_second)
    own_scale = film_col[1:-1, :C]
    d_scale = jnp.sum(d_pre_two * affine_two[:, 1:-1], axis=0)
    d_shift = jnp.sum(d_pre_two, axis=0)
    d_film = exact(clip_hot.T, jnp.concatenate([d_scale, d_shift], axis=1))
    g_film = exact(d_film.T, cond_act.astype(f32))
    d_inner, g_gn2_g, g_gn2_b = group_backward(
        d_pre_two * (1.0 + own_scale[None]),
        norm_two, std_two, gain_f[2], onehot, wide_hot, counts, 9, True,
    )
    d_inner_b = d_inner.astype(bf16)
    g_conv_one = left_product(cols_one, d_inner_b[:, 1:-1].reshape(n_pix, C))
    d_first = conv_backward(d_inner_b, conv_b[0], masks_all).reshape(height, n_cols, C)
    d_stem_gn, g_gn1_g, g_gn1_b = group_backward(
        silu_pull(act_one[:, 1:-1], d_first),
        norm_one, std_one, gain_f[0], onehot, wide_hot, counts, 10, False,
    )
    d_stem = (d_stem_gn.reshape(n_pix, C) + d_joined[:, :C] + d_joined[:, C:]).astype(bf16)
    g_stem = left_product(stem_cols, d_stem)
    pairs = n_dp // 2

    def shards_of(item):
        return item.reshape(pairs, 2, -1, item.shape[-1])

    def small_rows(item):
        flat = item.reshape(n_dp, -1)
        flat = jnp.pad(flat, ((0, 0), (0, round_up(flat.shape[1], 256) - flat.shape[1])))
        return flat.reshape(n_dp, -1, 256)

    g_gains = jnp.stack([g_gn1_g, g_gn1_b, g_gn2_g, g_gn2_b, g_ln1_g, g_ln1_b, g_ln2_g, g_ln2_b])
    smalls = [
        small_rows(g_head),
        small_rows(g_stem.reshape(-1, n_dp, C // n_dp).transpose(1, 0, 2)),
        small_rows(g_gains.reshape(-1, n_dp, C // n_dp).transpose(1, 0, 2)),
    ]
    small_at = [0]
    for item in smalls:
        small_at.append(small_at[-1] + item.shape[1])
    small_end = round_up(small_at[-1], 8)
    loss_rows = jnp.zeros((n_dp, 8 + small_end - small_at[-1], 256), jnp.float32)
    smalls.append(loss_rows.at[0, -8, 0].set(local_loss))
    small = jnp.concatenate(smalls, axis=1)
    g_proj = jnp.concatenate([g_qkv, g_out, g_up], axis=0)
    chunks = [
        [shards_of(g_conv_one)],
        [shards_of(g_conv_two)],
        [shards_of(g_proj)],
        [shards_of(g_film), shards_of(g_skip), shards_of(g_down), shards_of(small)],
    ]
    heights = [sum(item.shape[2] * item.shape[3] // 256 for item in parts) for parts in chunks]
    heights[3] -= 8
    shards, sums = reduce_grads(chunks, heights, 11)
    squares, loss_sum = sums[0, 1], sums[0, 0]
    grad_norm = jnp.sqrt(squares)
    factor = jnp.minimum(1.0, CLIP_NORM / grad_norm)
    conv_rows, film_cols = 9 * C // n_dp, 2 * C // n_dp
    skip_cols, down_rows = C // n_dp, 4 * C // n_dp
    last = shards[3]
    film_end, skip_end = 2 * film_cols, 2 * film_cols + 2 * skip_cols
    film_shard = jnp.concatenate([last[:film_cols], last[film_cols:film_end]], axis=1).T
    skip_shard = jnp.concatenate(
        [last[film_end : film_end + skip_cols], last[film_end + skip_cols : skip_end]], axis=1
    ).T
    small_shard = last[skip_end + down_rows :]

    def small_part(index, like):
        rows = small_shard[small_at[index] : small_at[index + 1]].reshape(-1)
        return rows[: like.size].reshape(like.shape)

    shards = (
        jnp.stack([shards[0][:conv_rows], shards[1][:conv_rows]]),
        shards[2][: proj_w.shape[1]].T,
        film_shard,
        skip_shard,
        last[skip_end : skip_end + down_rows],
        small_part(1, stem_w),
        small_part(0, head_w),
        small_part(2, gains),
    )
    new_w, new_m, new_v = ([], [], [])
    for weight, grad_one, m_old, v_old in zip(masters, shards, firsts, seconds):
        grad_one = grad_one * factor
        m_new = BETA_ONE * m_old + (1.0 - BETA_ONE) * grad_one
        v_new = BETA_TWO * v_old + (1.0 - BETA_TWO) * grad_one * grad_one
        step_dir = (
            m_new / (1.0 - BETA_ONE**STEP) / (jnp.sqrt(v_new / (1.0 - BETA_TWO**STEP)) + ADAM_EPS)
        )
        new_w.append(weight - RATE * (step_dir + DECAY * weight))
        new_m.append(m_new)
        new_v.append(v_new)
    return (
        new_w[0],
        new_w[1],
        new_w[2],
        new_w[3],
        new_w[4],
        new_w[5],
        new_w[6],
        new_w[7],
        new_m[0],
        new_m[1],
        new_m[2],
        new_m[3],
        new_m[4],
        new_m[5],
        new_m[6],
        new_m[7],
        new_v[0],
        new_v[1],
        new_v[2],
        new_v[3],
        new_v[4],
        new_v[5],
        new_v[6],
        new_v[7],
        grad_norm,
        loss_sum,
        pix_count,
    )


def solution(mesh):
    n_dp, n_s = mesh.shape["dp"], mesh.shape["section"]
    blocks = jax.sharding.Mesh(mesh.devices.reshape(n_dp // n_s, n_s, n_s), ("a", "b", "s"))
    return jax.shard_map(
        body,
        mesh=blocks,
        in_specs=(
            P(DP, None, "s", None),
            P(DP, None, "s", None),
            P(DP, None),
            P(DP, None),
            P(DP, None, None),
            P(None, DP, None),
            P(None, DP),
            P(None, DP),
            P(None, DP),
            P(DP, None),
            P(None, DP),
            P(DP, None),
            P(None, DP),
            P(None, DP, None),
            P(None, DP),
            P(None, DP),
            P(None, DP),
            P(DP, None),
            P(None, DP),
            P(DP, None),
            P(None, DP),
            P(None, DP, None),
            P(None, DP),
            P(None, DP),
            P(None, DP),
            P(DP, None),
            P(None, DP),
            P(DP, None),
            P(None, DP),
        ),
        out_specs=(
            P(None, DP, None),
            P(None, DP),
            P(None, DP),
            P(None, DP),
            P(DP, None),
            P(None, DP),
            P(DP, None),
            P(None, DP),
            P(None, DP, None),
            P(None, DP),
            P(None, DP),
            P(None, DP),
            P(DP, None),
            P(None, DP),
            P(DP, None),
            P(None, DP),
            P(None, DP, None),
            P(None, DP),
            P(None, DP),
            P(None, DP),
            P(DP, None),
            P(None, DP),
            P(DP, None),
            P(None, DP),
            P(),
            P(),
            P(),
        ),
        check_vma=False,
    )
```

```python
import functools
import math

import jax
import jax.numpy as jnp
from jax import lax
from jax.experimental import pallas as pl
from jax.experimental.pallas import tpu as pltpu
from jax.sharding import PartitionSpec as P

CIN = 8
C = 256
HEADS = 8
HD = 32
COND = 512
GROUPS = 32
CLIPS = 4
STEP = 10


EPS_NORM = 1e-05
CLIP_NORM = 0.02
DP = ("a", "b")
RATE = 0.04
BETA_ONE = 0.9
BETA_TWO = 0.999
ADAM_EPS = 1e-08
DECAY = 0.1


def matmul(lhs_mat, rhs_mat):
    return jnp.dot(lhs_mat, rhs_mat, preferred_element_type=jnp.float32)


def clip_terms(timesteps, clap_emb):
    half_cond = COND // 2
    frequency = jnp.exp(-math.log(10000.0) * jnp.arange(half_cond, dtype=jnp.float32) / half_cond)
    angles = timesteps.astype(jnp.float32)[:, None] * frequency[None]
    cond_vec = clap_emb + jnp.concatenate([jnp.sin(angles), jnp.cos(angles)], axis=1)
    theta_clip = 0.5 * math.pi * (timesteps.astype(jnp.float32) + 1.0) / 1001.0
    return (cond_vec, jnp.cos(theta_clip), jnp.sin(theta_clip))


BIG = 1e30
LOG2E = 1.4426950408889634
SCALE = HD**-0.5 * LOG2E
VMEM_LIMIT = 56 << 20
NN = (((1,), (0,)), ((), ()))
NT = (((1,), (1,)), ((), ()))


def mxu(lhs_mat, rhs_mat, dims=NN):
    return lax.dot_general(lhs_mat, rhs_mat, dims, preferred_element_type=jnp.float32)


def split_three(value):
    high = value.astype(jnp.bfloat16).astype(jnp.float32)
    rest = value - high
    mid = rest.astype(jnp.bfloat16).astype(jnp.float32)
    return high, mid, rest - mid


def rows_of(height, parts):
    row = lax.broadcasted_iota(jnp.int32, (height, parts[0].shape[1]), 0)
    total = jnp.zeros(row.shape, jnp.float32)
    for place, part in enumerate(parts):
        total = jnp.where(row == place, part, total)
    return total


def clip_rows(ids, hit, miss):
    return [jnp.where(ids == clip, hit, miss) for clip in range(CLIPS + 1)]


def forward_kernel(heads, bq, bk, x_ref, ids_ref, out_ref, lse_ref, keys):
    n_pix = x_ref.shape[1]
    step = pl.program_id(0)

    @pl.when(step == 0)
    def _():
        for head in range(heads):
            base = 3 * HD * head
            for start in range(0, n_pix, 512):
                cols = slice(start, start + 512)
                key = x_ref[base + HD : base + 2 * HD, cols].astype(jnp.float32)
                marks = rows_of(32, clip_rows(ids_ref[:, cols], 1.0, 0.0))
                stack = jnp.concatenate([key, marks, jnp.zeros((64, 512), jnp.float32)], axis=0)
                keys[head, cols, :] = stack.T.astype(jnp.bfloat16)

    block = pl.ds(pl.multiple_of(step * bq, bq), bq)
    marks = rows_of(32, clip_rows(ids_ref[:, block], 0.0, -BIG)).astype(jnp.bfloat16)
    for head in range(heads):
        base = 3 * HD * head
        query = jnp.concatenate([x_ref[base : base + HD, block], marks], axis=0)
        total = jnp.zeros((8, bq), jnp.float32)
        acc = jnp.zeros((HD, bq), jnp.float32)
        row_max = jnp.full((1, bq), -jnp.inf, jnp.float32)
        for start in range(0, n_pix, bk):
            scores = mxu(keys[head, start : start + bk, :64], query)
            new_max = jnp.maximum(row_max, jnp.max(scores, axis=0, keepdims=True) * SCALE)
            probs = jnp.exp2(scores * SCALE - new_max)
            decay = jnp.exp2(row_max - new_max)
            total = total * decay + jnp.sum(probs.reshape(bk // 8, 8, bq), axis=0)
            value = x_ref[base + 2 * HD : base + 3 * HD, start : start + bk]
            acc = acc * decay + mxu(value, probs.astype(jnp.bfloat16))
            row_max = new_max
        total = jnp.sum(total, axis=0, keepdims=True)
        out_ref[HD * head : HD * (head + 1), :] = (acc / total).astype(jnp.bfloat16)
        lse_ref[8 * head : 8 * (head + 1), :] = jnp.broadcast_to(row_max + jnp.log2(total), (8, bq))


def attention_forward(heads_x, pixel_ids):
    lanes, n_pix = heads_x.shape
    heads = lanes // (3 * HD)
    bq, bk = min(2048, n_pix), min(512, n_pix)
    return pl.pallas_call(
        functools.partial(forward_kernel, heads, bq, bk),
        grid=(n_pix // bq,),
        in_specs=[
            pl.BlockSpec((lanes, n_pix), lambda i: (0, 0)),
            pl.BlockSpec((1, n_pix), lambda i: (0, 0)),
        ],
        out_specs=[
            pl.BlockSpec((heads * HD, bq), lambda i: (0, i)),
            pl.BlockSpec((heads * 8, bq), lambda i: (0, i)),
        ],
        out_shape=[
            jax.ShapeDtypeStruct((heads * HD, n_pix), jnp.bfloat16),
            jax.ShapeDtypeStruct((heads * 8, n_pix), jnp.float32),
        ],
        scratch_shapes=[pltpu.VMEM((heads, n_pix, 128), jnp.bfloat16)],
        compiler_params=pltpu.CompilerParams(vmem_limit_bytes=VMEM_LIMIT),
    )(heads_x, pixel_ids)


def backward_kernel(
    heads, bq, bk, x_ref, ids_ref, do_ref, o_ref, lse_ref, out_ref,
    queries, keys, values, d_outs, d_query, query_rows, d_out_rows,
):
    n_pix = x_ref.shape[1]
    step = pl.program_id(0)

    @pl.when(step == 0)
    def _():
        d_query[...] = jnp.zeros_like(d_query)
        for head in range(heads):
            base = 3 * HD * head

            def prepare(part, carry):
                cols = pl.ds(pl.multiple_of(part * 512, 512), 512)
                ids = ids_ref[:, cols]
                one = jnp.ones((1, 512), jnp.float32)
                key = x_ref[base + HD : base + 2 * HD, cols].astype(jnp.float32)
                marks = rows_of(32, clip_rows(ids, 1.0, 0.0) + [one, one, one])
                stack = jnp.concatenate([key, key, key, marks], axis=0)
                keys[head, cols, :] = stack.T.astype(jnp.bfloat16)
                value = x_ref[base + 2 * HD : base + 3 * HD, cols].astype(jnp.float32)
                stack = jnp.concatenate(
                    [value, rows_of(32, [one, one, one]), jnp.zeros((64, 512), jnp.float32)], axis=0
                )
                values[head, cols, :] = stack.T.astype(jnp.bfloat16)
                query = x_ref[base : base + HD, cols].astype(jnp.float32) * SCALE
                lse = lse_ref[8 * head : 8 * head + 1, cols]
                marks = rows_of(32, clip_rows(ids, 0.0, -BIG) + list(split_three(-lse)))
                stack = jnp.concatenate([*split_three(query), marks], axis=0)
                queries[head, :, cols] = stack.astype(jnp.bfloat16)
                d_out = do_ref[HD * head : HD * (head + 1), cols].astype(jnp.float32)
                out = o_ref[HD * head : HD * (head + 1), cols].astype(jnp.float32)
                delta = jnp.sum(d_out * out, axis=0, keepdims=True)
                stack = jnp.concatenate([d_out, rows_of(32, split_three(-delta))], axis=0)
                d_outs[head, :, cols] = stack.astype(jnp.bfloat16)
                zero = jnp.zeros((96, 512), jnp.float32)
                query = x_ref[base : base + HD, cols].astype(jnp.float32)
                query_rows[head, cols, :] = jnp.concatenate([query, zero], 0).T.astype(jnp.bfloat16)
                d_out_rows[head, cols, :] = jnp.concatenate([d_out, zero], 0).T.astype(jnp.bfloat16)
                return carry

            lax.fori_loop(0, n_pix // 512, prepare, 0)

    block = pl.ds(pl.multiple_of(step * bk, bk), bk)
    for head in range(heads):
        base = 3 * HD * head
        key, value = keys[head, block, :], values[head, block, :64]
        key_t = x_ref[base + HD : base + 2 * HD, block]
        d_value = jnp.zeros((bk, 128), jnp.float32)
        d_key = jnp.zeros((bk, 128), jnp.float32)
        for start in range(0, n_pix, bq):
            cols = slice(start, start + bq)
            probs = jnp.exp2(mxu(key, queries[head, :, cols]))
            d_scores = (probs * mxu(value, d_outs[head, :, cols])).astype(jnp.bfloat16)
            probs = probs.astype(jnp.bfloat16)
            d_value += mxu(probs, d_out_rows[head, cols, :])
            d_key += mxu(d_scores, query_rows[head, cols, :])
            d_query[head, :, cols] += mxu(key_t, d_scores)
        d_key, d_value = d_key.T[:HD], d_value.T[:HD]
        out_ref[base + HD : base + 2 * HD, block] = (d_key * (HD**-0.5)).astype(jnp.bfloat16)
        out_ref[base + 2 * HD : base + 3 * HD, block] = d_value.astype(jnp.bfloat16)

    @pl.when(step == pl.num_programs(0) - 1)
    def _():
        for head in range(heads):
            base = 3 * HD * head
            out_ref[base : base + HD, :] = (d_query[head] * (HD**-0.5)).astype(jnp.bfloat16)


def attention_backward(heads_x, log_total, d_heads, out_heads, pixel_ids, bq=1024, bk=1024):
    lanes, n_pix = heads_x.shape
    heads = lanes // (3 * HD)
    bq, bk = min(bq, n_pix), min(bk, n_pix)
    operands = (heads_x, pixel_ids, d_heads, out_heads, log_total)
    return pl.pallas_call(
        functools.partial(backward_kernel, heads, bq, bk),
        grid=(n_pix // bk,),
        in_specs=[pl.BlockSpec(item.shape, lambda i: (0, 0)) for item in operands],
        out_specs=pl.BlockSpec((lanes, n_pix), lambda i: (0, 0)),
        out_shape=jax.ShapeDtypeStruct((lanes, n_pix), jnp.bfloat16),
        scratch_shapes=[
            pltpu.VMEM((heads, 128, n_pix), jnp.bfloat16),
            pltpu.VMEM((heads, n_pix, 128), jnp.bfloat16),
            pltpu.VMEM((heads, n_pix, 128), jnp.bfloat16),
            pltpu.VMEM((heads, 64, n_pix), jnp.bfloat16),
            pltpu.VMEM((heads, HD, n_pix), jnp.float32),
            pltpu.VMEM((heads, n_pix, 128), jnp.bfloat16),
            pltpu.VMEM((heads, n_pix, 128), jnp.bfloat16),
        ],
        compiler_params=pltpu.CompilerParams(vmem_limit_bytes=VMEM_LIMIT),
    )(*operands)


MESH = pl.DeviceIdType.MESH


def round_up(count, unit):
    return -(-count // unit) * unit


def greet(peers):
    barrier = pltpu.get_barrier_semaphore()
    for peer in peers:
        pl.semaphore_signal(barrier, inc=1, device_id=peer, device_id_type=MESH)
    pl.semaphore_wait(barrier, len(peers))


def push(src, dst, sems, slot, peer):
    copy = pltpu.make_async_remote_copy(
        src_ref=src,
        dst_ref=dst,
        send_sem=sems.at[0, slot],
        recv_sem=sems.at[1, slot],
        device_id=peer,
        device_id_type=MESH,
    )
    copy.start()
    return copy


def reduce_kernel(n_a, n_x, n_s, chunks, square_rows, *refs):
    n_in = sum(len(parts) for parts in chunks)
    n_chunk = len(chunks)
    ins = refs[:n_in]
    outs = refs[n_in : n_in + n_chunk]
    norm_ref = refs[n_in + n_chunk]
    scratch = list(refs[n_in + n_chunk + 1 :])
    halves = scratch[:n_in]
    accs = scratch[n_in : n_in + n_chunk]
    one_bufs = scratch[n_in + n_chunk : n_in + 3 * n_chunk]
    two_bufs = scratch[n_in + 3 * n_chunk : n_in + 5 * n_chunk]
    bit_bufs = scratch[n_in + 5 * n_chunk : n_in + 6 * n_chunk]
    squares, sems = scratch[n_in + 6 * n_chunk :]
    bits = n_s.bit_length() - 1
    my_a, my_b, my_s = lax.axis_index("a"), lax.axis_index("b"), lax.axis_index("s")
    core, my_x = lax.rem(my_b, 2), lax.div(my_b, 2)
    n_b = 2 * n_x
    n_d = n_a * n_b

    def dp_peer(off):
        place = lax.rem(my_a * n_b + my_b + off, n_d)
        return {"a": lax.div(place, n_b), "b": lax.rem(place, n_b)}

    def s_peer(bit):
        flipped = my_s + (1 << bit) - 2 * (1 << bit) * lax.rem(lax.div(my_s, 1 << bit), 2)
        return {"s": flipped}

    greet([dp_peer(off) for off in range(1, n_d)] + [s_peer(bit) for bit in range(bits)])
    slots = iter(range(sems.shape[1]))

    first_in = []
    at = 0
    for parts in chunks:
        first_in.append(at)
        at += len(parts)

    def core_send(c):
        copies = []
        for i in range(first_in[c], first_in[c] + len(chunks[c])):
            copies.append(
                push(ins[i].at[:, 1 - core], halves[i], sems, next(slots), {"b": my_b + 1 - 2 * core})
            )
        return copies

    def core_sum(c):
        acc = accs[c]
        row = 0
        for i in range(first_in[c], first_in[c] + len(chunks[c])):
            rows, lanes = ins[i].shape[2:]
            for lane in range(0, lanes, 256):
                for j in range(n_a * n_x):
                    acc[j // n_x, j % n_x, row : row + rows] = (
                        ins[i][j, core, :, lane : lane + 256] + halves[i][j, :, lane : lane + 256]
                    )
                row += rows
        if row < acc.shape[2]:
            for j in range(n_a * n_x):
                acc[j // n_x, j % n_x, row:] = jnp.zeros((acc.shape[2] - row, 256), jnp.float32)

    def plane_moves(c, stage):
        rows = accs[c].shape[2] // 2
        for half in range(2):
            over_x = (half + stage) % 2 == 0
            for off in range(1, n_x if over_x else n_a):
                yield half, over_x, off, pl.ds(half * rows, rows)

    def plane_buf(c, stage, half, off):
        return (one_bufs, two_bufs)[stage][2 * c + half].at[off - 1]

    def plane_send(c, stage):
        copies = []
        for half, over_x, off, rows in plane_moves(c, stage):
            acc = accs[c]
            if over_x:
                there = lax.rem(my_x + off, n_x)
                src = acc.at[:, there, rows] if stage == 0 else acc.at[my_a, there, rows]
                peer = {"b": 2 * there + core}
            else:
                there = lax.rem(my_a + off, n_a)
                src = acc.at[there, :, rows] if stage == 0 else acc.at[there, my_x, rows]
                peer = {"a": there}
            copies.append(push(src, plane_buf(c, stage, half, off), sems, next(slots), peer))
        return copies

    def plane_sum(c, stage):
        for half, over_x, off, rows in plane_moves(c, stage):
            buf = plane_buf(c, stage, half, off)
            if stage == 1:
                accs[c][my_a, my_x, rows] += buf[...]
            elif over_x:
                for j in range(n_a):
                    accs[c][j, my_x, rows] += buf[j]
            else:
                for j in range(n_x):
                    accs[c][my_a, j, rows] += buf[j]

    def span(c, level):
        length = accs[c].shape[2]
        start = 0
        for bit in range(level):
            length //= 2
            start = start + lax.rem(lax.div(my_s, 1 << bit), 2) * length
        return start, length

    def s_send(c, bit):
        start, length = span(c, bit)
        length //= 2
        mine = lax.rem(lax.div(my_s, 1 << bit), 2)
        rows = pl.ds(pl.multiple_of(start + (1 - mine) * length, 8), length)
        return [
            push(
                accs[c].at[my_a, my_x, rows],
                bit_bufs[c].at[bit, pl.ds(0, length)],
                sems,
                next(slots),
                s_peer(bit),
            )
        ]

    def s_sum(c, bit):
        start, length = span(c, bit + 1)
        rows = pl.ds(pl.multiple_of(start, 8), length)
        total = accs[c][my_a, my_x, rows] + bit_bufs[c][bit, :length]
        if bit == bits - 1:
            outs[c][rows] = total
        else:
            accs[c][my_a, my_x, rows] = total

    def up_send(c, bit):
        start, length = span(c, bit + 1)
        rows = pl.ds(pl.multiple_of(start, 8), length)
        return [push(outs[c].at[rows], outs[c].at[rows], sems, next(slots), s_peer(bit))]

    steps = [(core_send, core_sum, ())]
    steps += [(plane_send, plane_sum, (stage,)) for stage in range(2)]
    steps += [(s_send, s_sum, (bit,)) for bit in range(bits)]
    steps += [(up_send, None, (bit,)) for bit in reversed(range(bits))]
    flying = [None] * n_chunk
    for tick in range(n_chunk + len(steps)):
        for c in range(n_chunk):
            at = tick - c
            if at < 0 or at > len(steps):
                continue
            if at > 0:
                for copy in flying[c]:
                    copy.wait()
                if steps[at - 1][1] is not None:
                    steps[at - 1][1](c, *steps[at - 1][2])
            if at < len(steps):
                flying[c] = steps[at][0](c, *steps[at][2])

    lane = lax.broadcasted_iota(jnp.int32, (8, 256), 1)
    total = jnp.zeros((8, 256), jnp.float32)
    for c in range(n_chunk):
        rows = square_rows[c]
        total = total + jnp.sum((outs[c][:rows] * outs[c][:rows]).reshape(rows // 8, 8, 256), axis=0)
    total = jnp.sum(jnp.sum(total, axis=0, keepdims=True), axis=1, keepdims=True)
    last = square_rows[-1]
    squares[my_a * n_b + my_b] = jnp.where(lane == 1, total, outs[-1][last : last + 8])
    copies = []
    for off in range(1, n_d):
        place = squares.at[my_a * n_b + my_b]
        copies.append(push(place, place, sems, next(slots), dp_peer(off)))
    for copy in copies:
        copy.wait()
    total = squares[0]
    for place in range(1, n_d):
        total = total + squares[place]
    norm_ref[...] = total


def reduce_grads(chunks, square_rows, collective_id):
    n_a, n_b, n_s = lax.axis_size("a"), lax.axis_size("b"), lax.axis_size("s")
    n_x = n_b // 2
    bits = n_s.bit_length() - 1
    flat = [item for parts in chunks for item in parts]
    heights = [
        round_up(sum(item.shape[2] * item.shape[3] // 256 for item in parts), 16 * max(n_s // 2, 1))
        for parts in chunks
    ]
    f32 = jnp.float32
    one_shapes, two_shapes = [], []
    for rows in heights:
        half = rows // 2
        one_shapes += [(n_x - 1, n_a, half, 256), (n_a - 1, n_x, half, 256)]
        two_shapes += [(n_a - 1, half, 256), (n_x - 1, half, 256)]
    scratch = [(item.shape[0], *item.shape[2:]) for item in flat]
    scratch += [(n_a, n_x, rows, 256) for rows in heights]
    scratch += one_shapes + two_shapes
    scratch += [(bits, rows // 2, 256) for rows in heights]
    scratch += [(n_a * n_b, 8, 256)]
    n_copy = len(flat) + len(chunks) * 2 * (n_x - 1 + n_a - 1 + bits) + n_a * n_b - 1
    out = pl.pallas_call(
        functools.partial(reduce_kernel, n_a, n_x, n_s, [[None] * len(parts) for parts in chunks], square_rows),
        in_specs=[pl.BlockSpec(memory_space=pltpu.VMEM)] * len(flat),
        out_specs=[pl.BlockSpec(memory_space=pltpu.VMEM)] * (len(chunks) + 1),
        out_shape=[jax.ShapeDtypeStruct((rows, 256), f32) for rows in heights]
        + [jax.ShapeDtypeStruct((8, 256), f32)],
        scratch_shapes=[pltpu.VMEM(shape, f32) for shape in scratch]
        + [pltpu.SemaphoreType.DMA((2, n_copy))],
        compiler_params=pltpu.CompilerParams(
            collective_id=collective_id, has_side_effects=True, vmem_limit_bytes=VMEM_LIMIT
        ),
    )(*flat)
    return out[:-1], out[-1]


def swap_kernel(n_b, spread, x_ref, out_ref, sems, own_sem):
    me = lax.axis_index("b")
    peers = [lax.rem(me + off, n_b) for off in range(1, n_b)]
    greet([{"b": peer} for peer in peers])
    rows = (x_ref if spread else out_ref).shape[0] // n_b
    cols = (out_ref if spread else x_ref).shape[1] // n_b

    def tall(ref, place):
        return ref.at[pl.ds(pl.multiple_of(place * rows, 16), rows)]

    def wide(ref, place):
        return ref.at[:, pl.ds(pl.multiple_of(place * cols, 128), cols)]

    source, target = (tall, wide) if spread else (wide, tall)
    copies = [
        push(source(x_ref, peer), target(out_ref, me), sems, slot, {"b": peer})
        for slot, peer in enumerate(peers)
    ]
    own = pltpu.make_async_copy(source(x_ref, me), target(out_ref, me), own_sem)
    own.start()
    for copy in copies:
        copy.wait()
    own.wait()


def swap(x, spread, collective_id):
    n_b = lax.axis_size("b")
    rows, cols = x.shape
    shape = (rows // n_b, cols * n_b) if spread else (rows * n_b, cols // n_b)
    return pl.pallas_call(
        functools.partial(swap_kernel, n_b, spread),
        in_specs=[pl.BlockSpec(memory_space=pl.ANY)],
        out_specs=pl.BlockSpec(memory_space=pl.ANY),
        out_shape=jax.ShapeDtypeStruct(shape, x.dtype),
        scratch_shapes=[pltpu.SemaphoreType.DMA((2, n_b - 1)), pltpu.SemaphoreType.DMA(())],
        compiler_params=pltpu.CompilerParams(collective_id=collective_id, has_side_effects=True),
    )(x)


def opening_kernel(n_a, n_b, n_gather, *refs):
    main, first, last = refs[:3]
    shards = refs[3 : 3 + n_gather]
    main_out, left, right = refs[3 + n_gather : 6 + n_gather]
    wholes = refs[6 + n_gather : 6 + 2 * n_gather]
    (sems,) = refs[6 + 2 * n_gather :]
    my_a, my_b, my_s = lax.axis_index("a"), lax.axis_index("b"), lax.axis_index("s")
    n_d = n_a * n_b
    place = my_a * n_b + my_b

    def at(b, s):
        return {"b": lax.rem(b + n_b, n_b), "s": lax.rem(s + n_b, n_b)}

    dp_peers = []
    for off in range(1, n_d):
        there = lax.rem(place + off, n_d)
        dp_peers.append({"a": lax.div(there, n_b), "b": lax.rem(there, n_b)})
    mirrored = my_b != my_s
    shift = jnp.where(mirrored, 0, 1)
    greet(
        dp_peers
        + [at(my_s + 1, my_b), at(my_s - 1, my_b), at(my_s, my_b + 1), at(my_s, my_b - 1)]
        + [at(my_s + shift, my_b + shift)]
    )

    @pl.when(mirrored)
    def _():
        push(main, main_out, sems, 0, at(my_s, my_b))

    @pl.when(jnp.logical_not(mirrored))
    def _():
        main_out[...] = main[...]

    copies = [
        push(last, left, sems, 1, at(my_s + 1, my_b)),
        push(first, right, sems, 2, at(my_s - 1, my_b)),
    ]
    slot = 3
    for shard, whole in zip(shards, wholes):
        rows = shard.shape[0]
        mine = pl.ds(pl.multiple_of(place * rows, 8), rows)
        for peer in dp_peers:
            copies.append(push(shard, whole.at[mine], sems, slot, peer))
            slot += 1
        whole[mine] = shard[...]
    for copy in copies:
        copy.wait()

    @pl.when(mirrored)
    def _():
        pltpu.make_async_remote_copy(
            src_ref=main,
            dst_ref=main_out,
            send_sem=sems.at[0, 0],
            recv_sem=sems.at[1, 0],
            device_id=at(my_s, my_b),
            device_id_type=MESH,
        ).wait()


def opening(main, first, last, shards, collective_id):
    n_a, n_b = lax.axis_size("a"), lax.axis_size("b")
    n_d = n_a * n_b
    operands = [main, first, last, *shards]
    shapes = [jax.ShapeDtypeStruct(item.shape, item.dtype) for item in operands[:3]]
    shapes += [jax.ShapeDtypeStruct((n_d * item.shape[0], item.shape[1]), item.dtype) for item in shards]
    vmem = pl.BlockSpec(memory_space=pltpu.VMEM)
    return pl.pallas_call(
        functools.partial(opening_kernel, n_a, n_b, len(shards)),
        in_specs=[vmem] * len(operands),
        out_specs=[vmem] * len(operands),
        out_shape=shapes,
        scratch_shapes=[pltpu.SemaphoreType.DMA((2, 3 + len(shards) * (n_d - 1)))],
        compiler_params=pltpu.CompilerParams(collective_id=collective_id, has_side_effects=True),
    )(*operands)


FREQ = 16
PAD = 2 * FREQ
HIGH = lax.Precision.HIGHEST


def high(lhs_mat, rhs_mat, dims=NN):
    return lax.dot_general(
        lhs_mat, rhs_mat, dims, precision=HIGH, preferred_element_type=jnp.float32
    )


def low(value):
    return value.astype(jnp.bfloat16)


def frame_of(n_pix):
    return round_up(n_pix + 2 * PAD, 128)


def lane_taps(value, left, right, sign):
    n_lane = value.shape[1]
    freq = lax.broadcasted_iota(jnp.int32, value.shape, 1) & (FREQ - 1)
    parts = []
    for df in (-1, 0, 1):
        for dc in (-1, 0, 1):
            moved = sign * (FREQ * dc + df)
            part = value if moved == 0 else pltpu.roll(value, (-moved) % n_lane, 1)
            if sign * df < 0:
                part = jnp.where(freq > 0, part, 0.0)
            if sign * df > 0:
                part = jnp.where(freq < FREQ - 1, part, 0.0)
            if sign * dc < 0:
                part = part * left
            if sign * dc > 0:
                part = part * right
            parts.append(part)
    return jnp.concatenate(parts, axis=0)


def fill(value, rows):
    return jnp.concatenate(
        [value, jnp.zeros((rows - value.shape[0], value.shape[1]), value.dtype)], axis=0
    )


def silu(x):
    return x * jax.nn.sigmoid(x)


def table_parts(table):
    return low(fill(jnp.concatenate(split_three(table), axis=0), 128))


def group_table(sums, counts):
    size = C // GROUPS
    row = lax.broadcasted_iota(jnp.int32, (C, C), 0) & (C - size)
    col = lax.broadcasted_iota(jnp.int32, (C, C), 1) & (C - size)
    totals = high(sums, (row == col).astype(jnp.float32))
    return totals[:8] / counts, totals[8:] / counts


def clip_sums(hot_t, one, two):
    return jnp.concatenate([high(hot_t, one), high(hot_t, two)], axis=0)


def hot_rows(ids, rows):
    clip = lax.broadcasted_iota(jnp.int32, (rows, ids.shape[1]), 0)
    return ((clip & 7) == ids) & (clip < 24)


def row_shifts(value, keep):
    n_row = value.shape[0]
    freq = lax.broadcasted_iota(jnp.int32, value.shape, 0) & (FREQ - 1)
    keep[0] = low(jnp.where(freq > 0, pltpu.roll(value, 1, 0), 0.0))
    keep[1] = low(value)
    keep[2] = low(jnp.where(freq < FREQ - 1, pltpu.roll(value, n_row - 1, 0), 0.0))


def conv_rows(shifts, weight, left, right, n_pix):
    total = None
    for dc in range(3):
        part = None
        for df in range(3):
            tap = 3 * df + dc
            item = mxu(shifts[df, FREQ * dc : FREQ * dc + n_pix], weight[C * tap : C * (tap + 1)])
            part = item if part is None else part + item
        part = part if dc == 1 else part * (left if dc == 0 else right)
        total = part if total is None else total + part
    return total


def conv_pull(shifts, weight, act_t, grad, left, right, n_pix):
    total = None
    for df in range(3):
        for dc in range(3):
            tap = 3 * df + dc
            at = FREQ * (2 - dc)
            window = shifts[2 - df, at : at + n_pix]
            if dc != 1:
                window = window * (right if dc == 0 else left)
            grad[C * tap : C * (tap + 1)] = mxu(act_t, window)
            item = mxu(window, weight[C * tap : C * (tap + 1)], NT)
            total = item if total is None else total + item
    return total


def layer_parts(x):
    centered = x - jnp.mean(x, axis=1, keepdims=True)
    inv_std = lax.rsqrt(jnp.mean(centered * centered, axis=1, keepdims=True) + EPS_NORM)
    return centered * inv_std, inv_std


def layer_pull(d_out, normed, inv_std, gain):
    scaled = d_out * gain
    return inv_std * (
        scaled
        - jnp.mean(scaled, axis=1, keepdims=True)
        - normed * jnp.mean(scaled * normed, axis=1, keepdims=True)
    )


class Ring:
    def __init__(self, n_b, sems):
        self.n_b, self.sems = n_b, sems
        self.me = lax.axis_index("b")
        self.slots = iter(range(sems.shape[1]))
        self.peers = [{"b": lax.rem(self.me + off, n_b)} for off in range(1, n_b)]
        greet(self.peers)

    def edges(self, first, last, left, right):
        return [
            push(last, left, self.sems, next(self.slots), self.peers[0]),
            push(first, right, self.sems, next(self.slots), self.peers[-1]),
        ]

    def sums(self, mine, held):
        held[self.me] = mine
        place = held.at[self.me]
        return [push(place, place, self.sems, next(self.slots), peer) for peer in self.peers]

    def total(self, held):
        total = held[0]
        for place in range(1, self.n_b):
            total = total + held[place]
        return total


def stem_kernel(
    data, rows, ids_own, front, stem_out, sums_out, taps_out, target_out, hot_out
):
    n_pix = stem_out.shape[0]
    n_lane = data.shape[1]
    clean, noise = data[:8], data[8:16]
    ids, alpha, sigma = rows[0:1], rows[1:2], rows[2:3]
    left, right = rows[4:5], rows[5:6]
    noisy = low(alpha * clean + sigma * noise).astype(jnp.float32)
    target_out[...] = alpha * noise - sigma * clean
    taps = fill(lane_taps(noisy, left, right, 1), 128)
    taps_out[...] = low(taps[:80])
    taps = low(taps.T)
    stem = mxu(taps[PAD : PAD + n_pix], front[...], NT)
    stem_out[...] = stem
    hot_t = hot_rows(ids_own[...].astype(jnp.int32), 8).astype(jnp.float32)
    sums_out[...] = clip_sums(hot_t, stem, stem * stem)
    clip = lax.broadcasted_iota(jnp.int32, (128, n_lane), 0)
    hot = hot_rows(ids.astype(jnp.int32), 128).astype(jnp.float32)
    hot = hot + jnp.where(clip == 24, left, 0.0) + jnp.where(clip == 25, right, 0.0)
    hot_out[...] = low(hot.T)


def side_masks(hot, n_pix):
    own = hot[PAD : PAD + n_pix, :].astype(jnp.float32)
    return own[:, 24:25], own[:, 25:26]


def first_kernel(
    n_b, stem, sums, ids_own, hot, counts, gains, weight,
    inner_out, sums_out, wide_out, table_out, shifts, held, sems,
):
    n_pix = stem.shape[0]
    ring = Ring(n_b, sems)
    copies = ring.edges(
        stem.at[pl.ds(0, FREQ)],
        stem.at[pl.ds(n_pix - FREQ, FREQ)],
        wide_out.at[pl.ds(0, FREQ)],
        wide_out.at[pl.ds(n_pix + FREQ, FREQ)],
    )
    copies += ring.sums(sums[...], held)
    wide_out[FREQ : FREQ + n_pix] = stem[...]
    left, right = side_masks(hot, n_pix)
    for copy in copies:
        copy.wait()
    mean, square = group_table(ring.total(held), counts[...])
    inv_std = lax.rsqrt(square - mean * mean + EPS_NORM)
    table_out[:8] = mean
    table_out[8:] = inv_std
    wide_hot = hot[FREQ : 3 * FREQ + n_pix]
    normed = (wide_out[...] - mxu(wide_hot, table_parts(mean))) * mxu(wide_hot, table_parts(inv_std))
    act = low(silu(normed * gains[0:1] + gains[1:2])).astype(jnp.float32)
    row_shifts(act, shifts)
    inner = conv_rows(shifts, weight, left, right, n_pix)
    inner_out[...] = inner
    hot_t = hot_rows(ids_own[...].astype(jnp.int32), 8).astype(jnp.float32)
    sums_out[...] = clip_sums(hot_t, inner, inner * inner)


def second_kernel(
    n_b, inner, sums, hot, counts, gains, weight, stem, cond, film_t, skip_t, proj_t,
    qkv_out, joined_out, base_out, wide_out, table_out, film_out, shifts, held, sems,
):
    n_pix = inner.shape[0]
    ring = Ring(n_b, sems)
    copies = ring.edges(
        inner.at[pl.ds(0, FREQ)],
        inner.at[pl.ds(n_pix - FREQ, FREQ)],
        wide_out.at[pl.ds(0, FREQ)],
        wide_out.at[pl.ds(n_pix + FREQ, FREQ)],
    )
    copies += ring.sums(sums[...], held)
    wide_out[FREQ : FREQ + n_pix] = inner[...]
    left, right = side_masks(hot, n_pix)
    film = mxu(cond[...], film_t[...], NT)
    film_out[...] = film
    wide_hot = hot[FREQ : 3 * FREQ + n_pix]
    film_rows = mxu(wide_hot, table_parts(film))
    for copy in copies:
        copy.wait()
    mean, square = group_table(ring.total(held), counts[...])
    inv_std = lax.rsqrt(square - mean * mean + EPS_NORM)
    table_out[:8] = mean
    table_out[8:] = inv_std
    normed = (wide_out[...] - mxu(wide_hot, table_parts(mean))) * mxu(wide_hot, table_parts(inv_std))
    act = (normed * gains[2:3] + gains[3:4]) * (1.0 + film_rows[:, :C]) + film_rows[:, C:]
    row_shifts(low(silu(act)).astype(jnp.float32), shifts)
    branch = conv_rows(shifts, weight, left, right, n_pix)
    joined_out[:, :C] = low(stem[...] + branch)
    joined_out[:, C:] = low(stem[...])
    base = mxu(joined_out[...], skip_t[...], NT)
    base_out[...] = base
    normed, _ = layer_parts(base)
    normed = low(normed * gains[4:5] + gains[5:6])
    qkv_out[...] = low(mxu(proj_t[: 3 * C], normed, NT))


def middle_kernel(
    n_b, attended, base, proj_t, down, head, target, rows, gains, pix_count,
    d_mid_out, d_att_out, g_up, g_down, g_out, g_head, g_gains, loss_out,
    wide, act_t, pull_t, edge, sems,
):
    n_pix = base.shape[0]
    n_lane = target.shape[1]
    n_hid = down.shape[0]
    ring = Ring(n_b, sems)
    proj_out, proj_up = proj_t.at[pl.ds(3 * C, C)], proj_t.at[pl.ds(4 * C, n_hid)]
    mid = base[...] + mxu(low(attended[...].astype(jnp.float32).T), proj_out[...], NT)
    normed, inv_std = layer_parts(mid)
    ln_b = low(normed * gains[6:7] + gains[7:8])
    top_t = jnp.zeros((C, n_pix), jnp.float32)
    scale = math.sqrt(2.0 / math.pi)
    for start in range(0, n_hid, 256):
        part = slice(start, start + 256)
        hidden = mxu(proj_up[part], ln_b, NT)
        bend = jnp.tanh(scale * (hidden + 0.044715 * hidden * hidden * hidden))
        gate = 0.5 * (1.0 + bend)
        act = low(hidden * gate)
        act_t[part] = act
        pull_t[part] = gate + 0.5 * hidden * (1.0 - bend * bend) * scale * (
            1.0 + 3.0 * 0.044715 * hidden * hidden
        )
        top_t = top_t + mxu(low(down[part].astype(jnp.float32).T), act)
    top = low(mid + top_t.T)
    wide[PAD : PAD + n_pix] = top
    wide[2 * PAD + n_pix :] = jnp.zeros((n_lane - 2 * PAD - n_pix, C), jnp.bfloat16)
    edge[0] = top[:PAD]
    edge[1] = top[n_pix - PAD :]
    copies = ring.edges(
        edge.at[0], edge.at[1], wide.at[pl.ds(0, PAD)], wide.at[pl.ds(PAD + n_pix, PAD)]
    )
    for copy in copies:
        copy.wait()
    left, right, valid, own = rows[4:5], rows[5:6], rows[3:4], rows[6:7]
    products = mxu(head[...], wide[...], NT)
    freq = lax.broadcasted_iota(jnp.int32, (8, n_lane), 1) & (FREQ - 1)
    pred = jnp.zeros((8, n_lane), jnp.float32)
    for df in (-1, 0, 1):
        for dc in (-1, 0, 1):
            tap = 3 * (df + 1) + dc + 1
            moved = FREQ * dc + df
            part = products[8 * tap : 8 * (tap + 1)]
            part = part if moved == 0 else pltpu.roll(part, (-moved) % n_lane, 1)
            if df != 0:
                part = jnp.where(freq > 0 if df < 0 else freq < FREQ - 1, part, 0.0)
            if dc != 0:
                part = part * (left if dc < 0 else right)
            pred = pred + part
    residue = jnp.where(valid > 0.0, pred - target[...], 0.0)
    loss = jnp.sum(own * residue * residue, axis=0, keepdims=True)
    loss_out[...] = jnp.broadcast_to(jnp.sum(loss, axis=1, keepdims=True), (8, 128))
    d_pred = low(2.0 * residue / pix_count[0:1, 0:1]).astype(jnp.float32)
    taps = lane_taps(d_pred, left, right, -1) * own
    taps = fill(taps, 128)
    g_head[...] = mxu(low(taps[:80]), wide[...])
    d_top = mxu(low(taps.T)[PAD : PAD + n_pix], fill(head[...], 128))
    d_top_b = low(d_top)
    d_ln_t = jnp.zeros((C, n_pix), jnp.float32)
    for start in range(0, n_hid, 256):
        part = slice(start, start + 256)
        d_hidden = low(mxu(down[part], d_top_b, NT) * pull_t[part])
        g_up[part] = mxu(d_hidden, ln_b)
        g_down[part] = mxu(act_t[part], d_top_b)
        d_ln_t = d_ln_t + mxu(low(proj_up[part].astype(jnp.float32).T), d_hidden)
    d_ln = d_ln_t.T
    g_gains[...] = rows_of(
        8, [jnp.sum(d_ln * normed, axis=0, keepdims=True), jnp.sum(d_ln, axis=0, keepdims=True)]
    )
    d_mid = d_top + layer_pull(d_ln, normed, inv_std, gains[6:7])
    d_mid_out[...] = d_mid
    d_mid_b = low(d_mid)
    g_out[...] = mxu(attended[...], d_mid_b).T
    d_att_out[...] = low(mxu(low(proj_out[...].astype(jnp.float32).T), d_mid_b, NT))


def back_kernel(
    n_b, d_qkv, base, d_mid, joined, proj_t, skip_t, weight_one, weight_two, wide_one, wide_two,
    table_one, table_two, film, hot, ids_own, cond, gains, counts, taps,
    g_qkv, g_skip, g_one, g_two, g_film, g_stem, g_gains,
    shifts, wide, held, edge_b, edge_f, sems,
):
    n_pix = base.shape[0]
    ring = Ring(n_b, sems)
    own = slice(FREQ, FREQ + n_pix)
    normed, inv_std = layer_parts(base[...])
    ln_b = low(normed * gains[4:5] + gains[5:6])
    g_qkv[...] = mxu(d_qkv[...], ln_b)
    d_ln = mxu(low(proj_t[: 3 * C].astype(jnp.float32).T), d_qkv[...]).T
    sum_gain = [jnp.sum(d_ln * normed, axis=0, keepdims=True), jnp.sum(d_ln, axis=0, keepdims=True)]
    d_base = d_mid[...] + layer_pull(d_ln, normed, inv_std, gains[4:5])
    g_skip[...] = mxu(low(d_base.T), joined[...])
    d_joined = mxu(low(d_base), skip_t[...])
    d_branch = low(d_joined[:, :C])
    edge_b[0] = d_branch[:FREQ]
    edge_b[1] = d_branch[n_pix - FREQ :]
    copies = ring.edges(edge_b.at[0], edge_b.at[1], edge_b.at[2], edge_b.at[3])
    d_stem = d_joined[:, :C] + d_joined[:, C:]

    left, right = side_masks(hot, n_pix)
    left_b, right_b = low(left), low(right)
    hot_t = hot_rows(ids_own[...].astype(jnp.int32), 8).astype(jnp.float32)
    wide_hot = hot[FREQ : 3 * FREQ + n_pix]
    film_rows = mxu(wide_hot[own], table_parts(film[...]))
    inv_two = mxu(wide_hot, table_parts(table_two[8:]))
    norm_two = (wide_two[...] - mxu(wide_hot, table_parts(table_two[:8]))) * inv_two
    affine = norm_two[own] * gains[2:3] + gains[3:4]
    act = affine * (1.0 + film_rows[:, :C]) + film_rows[:, C:]
    gate = jax.nn.sigmoid(act)
    act_t = low((low(act * gate).astype(jnp.float32)).T)
    wide[own] = d_branch.astype(jnp.float32)
    for copy in copies:
        copy.wait()
    wide[:FREQ] = edge_b[2].astype(jnp.float32)
    wide[FREQ + n_pix :] = edge_b[3].astype(jnp.float32)
    row_shifts(wide[...], shifts)
    d_act = conv_pull(shifts, weight_two, act_t, g_two, left_b, right_b, n_pix)
    d_act = d_act * (gate + act * gate * (1.0 - gate))
    d_film = jnp.concatenate([high(hot_t, d_act * affine), high(hot_t, d_act)], axis=1)
    clip = lax.broadcasted_iota(jnp.int32, d_film.shape, 0)
    d_film = jnp.where(clip < CLIPS, d_film, 0.0)
    g_film[...] = high(d_film.T, cond[...].astype(jnp.float32))
    d_act = d_act * (1.0 + film_rows[:, :C])
    sum_two = [
        jnp.sum(d_act * norm_two[own], axis=0, keepdims=True),
        jnp.sum(d_act, axis=0, keepdims=True),
    ]
    scaled = d_act * gains[2:3]
    wide[own] = scaled
    edge_f[0] = scaled[:FREQ]
    edge_f[1] = scaled[n_pix - FREQ :]
    copies = ring.edges(edge_f.at[0], edge_f.at[1], edge_f.at[2], edge_f.at[3])
    copies += ring.sums(clip_sums(hot_t, scaled, scaled * norm_two[own]), held.at[0])
    inv_one = mxu(wide_hot[own], table_parts(table_one[8:]))
    norm_one = (wide_one[own] - mxu(wide_hot[own], table_parts(table_one[:8]))) * inv_one
    act = norm_one * gains[0:1] + gains[1:2]
    gate = jax.nn.sigmoid(act)
    act_t = low((low(act * gate).astype(jnp.float32)).T)
    for copy in copies:
        copy.wait()
    wide[:FREQ] = edge_f[2]
    wide[FREQ + n_pix :] = edge_f[3]
    mean, slope = group_table(ring.total(held.at[0]), counts[...])
    d_inner = inv_two * (
        wide[...] - mxu(wide_hot, table_parts(mean)) - norm_two * mxu(wide_hot, table_parts(slope))
    )
    row_shifts(low(d_inner).astype(jnp.float32), shifts)
    d_act = conv_pull(shifts, weight_one, act_t, g_one, left_b, right_b, n_pix)
    d_act = d_act * (gate + act * gate * (1.0 - gate))
    sum_one = [
        jnp.sum(d_act * norm_one, axis=0, keepdims=True),
        jnp.sum(d_act, axis=0, keepdims=True),
    ]
    g_gains[...] = rows_of(8, sum_one + sum_two + sum_gain)
    scaled = d_act * gains[0:1]
    copies = ring.sums(clip_sums(hot_t, scaled, scaled * norm_one), held.at[1])
    for copy in copies:
        copy.wait()
    mean, slope = group_table(ring.total(held.at[1]), counts[...])
    own_hot = wide_hot[own]
    d_stem = d_stem + inv_one * (
        scaled - mxu(own_hot, table_parts(mean)) - norm_one * mxu(own_hot, table_parts(slope))
    )
    n_lane = taps.shape[1]
    d_stem = jnp.concatenate(
        [
            jnp.zeros((PAD, C), jnp.bfloat16),
            low(d_stem),
            jnp.zeros((n_lane - n_pix - PAD, C), jnp.bfloat16),
        ],
        axis=0,
    )
    g_stem[...] = mxu(taps[...], d_stem)


def dense(kernel, operands, outs, scratch, collective_id=None):
    vmem = pl.BlockSpec(memory_space=pltpu.VMEM)
    params = dict(vmem_limit_bytes=VMEM_LIMIT)
    if collective_id is not None:
        params.update(collective_id=collective_id, has_side_effects=True)
    return pl.pallas_call(
        kernel,
        in_specs=[vmem] * len(operands),
        out_specs=[vmem] * len(outs),
        out_shape=[jax.ShapeDtypeStruct(shape, dtype) for shape, dtype in outs],
        scratch_shapes=scratch,
        compiler_params=pltpu.CompilerParams(**params),
    )(*operands)


def body(
    clean_lat,
    noise_lat,
    column_ids,
    timesteps,
    clap_emb,
    conv_w,
    proj_w,
    film_w,
    skip_w,
    down_w,
    stem_w,
    head_w,
    gains,
    conv_m,
    proj_m,
    film_m,
    skip_m,
    down_m,
    stem_m,
    head_m,
    gains_m,
    conv_v,
    proj_v,
    film_v,
    skip_v,
    down_v,
    stem_v,
    head_v,
    gains_v,
):
    bf16, f32 = jnp.bfloat16, jnp.float32
    masters = (conv_w, proj_w, film_w, skip_w, down_w, stem_w, head_w, gains)
    firsts = (conv_m, proj_m, film_m, skip_m, down_m, stem_m, head_m, gains_m)
    seconds = (conv_v, proj_v, film_v, skip_v, down_v, stem_v, head_v, gains_v)
    n_dp, n_s = lax.axis_size(DP), lax.axis_size("s")
    conv_b = [lax.all_gather(conv_w[i].astype(bf16), DP, axis=0, tiled=True) for i in range(2)]
    head_size = head_w.size
    head_rows = round_up(round_up(head_size, 256) // 256, 16)
    head_flat = jnp.pad(head_w.reshape(-1), (0, head_rows * 256 - head_size)).reshape(-1, 256)
    late = jnp.concatenate([proj_w.T, down_w, head_flat], axis=0).astype(bf16)
    late = lax.all_gather(late, DP, axis=0, tiled=False)
    proj_cols, down_rows = proj_w.shape[1], down_w.shape[0]
    proj_t = late[:, :proj_cols].reshape(-1, C)
    down_b = late[:, proj_cols : proj_cols + down_rows].reshape(-1, C)
    head_b = late[:, proj_cols + down_rows :].reshape(n_dp, -1)[:, :head_size]
    head_t = head_b.reshape(9, C, CIN).transpose(0, 2, 1).reshape(9 * CIN, C)
    head_t = jnp.pad(head_t, ((0, 80 - 9 * CIN), (0, 0)))

    _, height, n_cols, _ = clean_lat.shape
    n_pix = height * n_cols
    n_lane = frame_of(n_pix)
    extra = jnp.concatenate(
        [column_ids[0].astype(f32), timesteps[0].astype(f32), clap_emb[0].reshape(-1)]
    )
    extra_rows = round_up(-(-extra.size // n_pix), 8)
    extra = jnp.pad(extra, (0, extra_rows * n_pix - extra.size)).reshape(-1, n_pix)
    both = jnp.concatenate([clean_lat, noise_lat], axis=0).transpose(0, 3, 2, 1)
    both = both.reshape(2 * CIN, n_pix)
    pack = jnp.concatenate([both, extra], axis=0)
    first, last = (
        jnp.pad(both[:, at : at + height], ((0, 0), (0, 128 - height)))
        for at in (0, n_pix - height)
    )
    own_count = jnp.sum((column_ids < CLIPS).astype(f32)) * (height * CIN)
    stem_rows = stem_w.shape[0]
    front = jnp.concatenate([stem_w, gains], axis=0)
    front = jnp.pad(front, ((0, 128 - front.shape[0]), (0, 0))).T.astype(bf16)
    pack, left, right, film_t, skip_t, front, counts_all = opening(
        pack,
        first,
        last,
        [film_w.T.astype(bf16), skip_w.T.astype(bf16), front, jnp.full((8, 128), own_count)],
        0,
    )
    pix_count = jnp.sum(counts_all.reshape(n_dp, 8, 128)[:, 0, 0])
    gain_f = front[:, stem_rows : stem_rows + 8].T.astype(f32)
    data = jnp.concatenate(
        [
            jnp.zeros((2 * CIN, height), f32),
            left[:, :height],
            pack[: 2 * CIN],
            right[:, :height],
            jnp.zeros((2 * CIN, n_lane - n_pix - 3 * height), f32),
        ],
        axis=1,
    )
    extra = pack[2 * CIN :].reshape(-1)
    row_cols = column_ids.shape[1]
    ids_row = extra[:row_cols]
    times = extra[row_cols : row_cols + CLIPS]
    emb = extra[row_cols + CLIPS : row_cols + CLIPS + CLIPS * COND].reshape(CLIPS, COND)

    edge_pad = jnp.full((2,), -1.0, f32)
    ids_rim = lax.dynamic_slice_in_dim(
        jnp.concatenate([edge_pad, ids_row, edge_pad]), lax.axis_index("b") * n_cols, n_cols + 4
    )
    labels = jnp.arange(8, dtype=f32)
    clip_hot = (ids_rim[:, None] == labels[None, :CLIPS]).astype(f32)
    place = jnp.arange(n_cols + 4)
    inner = (place > 0) & (place < n_cols + 3)
    own = (place > 1) & (place < n_cols + 2)
    same = ids_rim[1:] == ids_rim[:-1]
    off = jnp.zeros((1,), bool)
    cond_vec, alpha_clip, sigma_clip = clip_terms(times, emb)
    rows = [
        ids_rim,
        jnp.sum(clip_hot * alpha_clip[None], axis=1),
        jnp.sum(clip_hot * sigma_clip[None], axis=1),
        jnp.sum(clip_hot, axis=1) * inner,
        jnp.concatenate([off, same]),
        jnp.concatenate([same, off]),
        own,
        own,
    ]
    rows = jnp.stack([item.astype(f32) for item in rows])
    rows = jnp.repeat(rows, height, axis=1)
    rows = jnp.pad(rows, ((0, 0), (0, n_lane - rows.shape[1])))
    ids_own = jnp.repeat(ids_rim[2:-2], height)[None]
    pixel_ids = jnp.repeat(ids_row.astype(jnp.int32), height)[None]
    counts = jnp.sum((ids_row[None] == labels[:, None]).astype(f32), axis=1) * (height * C // GROUPS)
    counts = jnp.broadcast_to(jnp.maximum(counts, 1.0)[:, None], (8, C))
    cond_act = jnp.pad(jax.nn.silu(cond_vec), ((0, 8 - CLIPS), (0, 0))).astype(bf16)
    n_b = lax.axis_size("b")
    n_wide = n_pix + PAD
    vmem = pltpu.VMEM

    def sems(count):
        return pltpu.SemaphoreType.DMA((2, count))

    stem, sums, taps, target, hot = dense(
        stem_kernel,
        [data, rows, ids_own, front],
        [
            ((n_pix, C), f32),
            ((16, C), f32),
            ((80, n_lane), bf16),
            ((8, n_lane), f32),
            ((n_lane, 128), bf16),
        ],
        [],
    )
    inner, sums, wide_one, table_one = dense(
        functools.partial(first_kernel, n_b),
        [stem, sums, ids_own, hot, counts, gain_f, conv_b[0]],
        [((n_pix, C), f32), ((16, C), f32), ((n_wide, C), f32), ((16, C), f32)],
        [vmem((3, n_wide, C), bf16), vmem((n_b, 16, C), f32), sems(n_b + 1)],
        1,
    )
    qkv_t, joined, base_rows, wide_two, table_two, film = dense(
        functools.partial(second_kernel, n_b),
        [inner, sums, hot, counts, gain_f, conv_b[1], stem, cond_act, film_t, skip_t, proj_t],
        [
            ((3 * C, n_pix), bf16),
            ((n_pix, 2 * C), bf16),
            ((n_pix, C), f32),
            ((n_wide, C), f32),
            ((16, C), f32),
            ((8, 2 * C), f32),
        ],
        [vmem((3, n_wide, C), bf16), vmem((n_b, 16, C), f32), sems(n_b + 1)],
        2,
    )
    heads_x = swap(qkv_t, True, 3)
    out_heads, log_total = attention_forward(heads_x, pixel_ids)
    attended_t = swap(out_heads, False, 4)
    n_hid = down_b.shape[0]
    d_mid, d_att_t, g_up, g_down, g_out, g_head, gain_mid, loss = dense(
        functools.partial(middle_kernel, n_b),
        [
            attended_t, base_rows, proj_t, down_b, head_t, target, rows, gain_f,
            jnp.full((8, 128), pix_count),
        ],
        [
            ((n_pix, C), f32),
            ((C, n_pix), bf16),
            ((n_hid, C), f32),
            ((n_hid, C), f32),
            ((C, C), f32),
            ((80, C), f32),
            ((8, C), f32),
            ((8, 128), f32),
        ],
        [
            vmem((n_lane, C), bf16),
            vmem((n_hid, n_pix), bf16),
            vmem((n_hid, n_pix), f32),
            vmem((2, PAD, C), bf16),
            sems(2),
        ],
        5,
    )
    local_loss = loss[0, 0]
    d_heads = swap(d_att_t, True, 6)
    d_heads_x = attention_backward(heads_x, log_total, d_heads, out_heads, pixel_ids)
    d_qkv_t = swap(d_heads_x, False, 7)
    g_qkv, g_skip, g_conv_one, g_conv_two, g_film, g_stem, gain_back = dense(
        functools.partial(back_kernel, n_b),
        [
            d_qkv_t, base_rows, d_mid, joined, proj_t, skip_t, conv_b[0], conv_b[1], wide_one,
            wide_two, table_one, table_two, film, hot, ids_own, cond_act, gain_f, counts, taps,
        ],
        [
            ((3 * C, C), f32),
            ((C, 2 * C), f32),
            ((9 * C, C), f32),
            ((9 * C, C), f32),
            ((2 * C, COND), f32),
            ((80, C), f32),
            ((8, C), f32),
        ],
        [
            vmem((3, n_wide, C), bf16),
            vmem((n_wide, C), f32),
            vmem((2, n_b, 16, C), f32),
            vmem((4, FREQ, C), bf16),
            vmem((4, FREQ, C), f32),
            sems(2 * n_b + 2),
        ],
        8,
    )
    g_head = g_head[:72].reshape(9, CIN, C).transpose(0, 2, 1)
    g_stem = g_stem[:stem_rows]
    g_gains = jnp.concatenate([gain_back[:6], gain_mid[:2]], axis=0)
    pairs = n_dp // 2

    def shards_of(item):
        return item.reshape(pairs, 2, -1, item.shape[-1])

    def small_rows(item):
        flat = item.reshape(n_dp, -1)
        flat = jnp.pad(flat, ((0, 0), (0, round_up(flat.shape[1], 256) - flat.shape[1])))
        return flat.reshape(n_dp, -1, 256)

    smalls = [
        small_rows(g_head),
        small_rows(g_stem.reshape(-1, n_dp, C // n_dp).transpose(1, 0, 2)),
        small_rows(g_gains.reshape(-1, n_dp, C // n_dp).transpose(1, 0, 2)),
    ]
    small_at = [0]
    for item in smalls:
        small_at.append(small_at[-1] + item.shape[1])
    small_end = round_up(small_at[-1], 8)
    loss_rows = jnp.zeros((n_dp, 8 + small_end - small_at[-1], 256), jnp.float32)
    smalls.append(loss_rows.at[0, -8, 0].set(local_loss))
    small = jnp.concatenate(smalls, axis=1)
    g_proj = jnp.concatenate([g_qkv, g_out, g_up], axis=0)
    chunks = [
        [shards_of(g_conv_one)],
        [shards_of(g_conv_two)],
        [shards_of(g_proj)],
        [shards_of(g_film), shards_of(g_skip), shards_of(g_down), shards_of(small)],
    ]
    heights = [sum(item.shape[2] * item.shape[3] // 256 for item in parts) for parts in chunks]
    heights[3] -= 8
    shards, sums = reduce_grads(chunks, heights, 11)
    squares, loss_sum = sums[0, 1], sums[0, 0]
    grad_norm = jnp.sqrt(squares)
    factor = jnp.minimum(1.0, CLIP_NORM / grad_norm)
    conv_rows, film_cols = 9 * C // n_dp, 2 * C // n_dp
    skip_cols, down_rows = C // n_dp, 4 * C // n_dp
    last = shards[3]
    film_end, skip_end = 2 * film_cols, 2 * film_cols + 2 * skip_cols
    film_shard = jnp.concatenate([last[:film_cols], last[film_cols:film_end]], axis=1).T
    skip_shard = jnp.concatenate(
        [last[film_end : film_end + skip_cols], last[film_end + skip_cols : skip_end]], axis=1
    ).T
    small_shard = last[skip_end + down_rows :]

    def small_part(index, like):
        rows = small_shard[small_at[index] : small_at[index + 1]].reshape(-1)
        return rows[: like.size].reshape(like.shape)

    shards = (
        jnp.stack([shards[0][:conv_rows], shards[1][:conv_rows]]),
        shards[2][: proj_w.shape[1]].T,
        film_shard,
        skip_shard,
        last[skip_end : skip_end + down_rows],
        small_part(1, stem_w),
        small_part(0, head_w),
        small_part(2, gains),
    )
    new_w, new_m, new_v = ([], [], [])
    for weight, grad_one, m_old, v_old in zip(masters, shards, firsts, seconds):
        grad_one = grad_one * factor
        m_new = BETA_ONE * m_old + (1.0 - BETA_ONE) * grad_one
        v_new = BETA_TWO * v_old + (1.0 - BETA_TWO) * grad_one * grad_one
        step_dir = (
            m_new / (1.0 - BETA_ONE**STEP) / (jnp.sqrt(v_new / (1.0 - BETA_TWO**STEP)) + ADAM_EPS)
        )
        new_w.append(weight - RATE * (step_dir + DECAY * weight))
        new_m.append(m_new)
        new_v.append(v_new)
    return (
        new_w[0],
        new_w[1],
        new_w[2],
        new_w[3],
        new_w[4],
        new_w[5],
        new_w[6],
        new_w[7],
        new_m[0],
        new_m[1],
        new_m[2],
        new_m[3],
        new_m[4],
        new_m[5],
        new_m[6],
        new_m[7],
        new_v[0],
        new_v[1],
        new_v[2],
        new_v[3],
        new_v[4],
        new_v[5],
        new_v[6],
        new_v[7],
        grad_norm,
        loss_sum,
        pix_count,
    )


def solution(mesh):
    n_dp, n_s = mesh.shape["dp"], mesh.shape["section"]
    blocks = jax.sharding.Mesh(mesh.devices.reshape(n_dp // n_s, n_s, n_s), ("a", "b", "s"))
    return jax.shard_map(
        body,
        mesh=blocks,
        in_specs=(
            P(DP, None, "s", None),
            P(DP, None, "s", None),
            P(DP, None),
            P(DP, None),
            P(DP, None, None),
            P(None, DP, None),
            P(None, DP),
            P(None, DP),
            P(None, DP),
            P(DP, None),
            P(None, DP),
            P(DP, None),
            P(None, DP),
            P(None, DP, None),
            P(None, DP),
            P(None, DP),
            P(None, DP),
            P(DP, None),
            P(None, DP),
            P(DP, None),
            P(None, DP),
            P(None, DP, None),
            P(None, DP),
            P(None, DP),
            P(None, DP),
            P(DP, None),
            P(None, DP),
            P(DP, None),
            P(None, DP),
        ),
        out_specs=(
            P(None, DP, None),
            P(None, DP),
            P(None, DP),
            P(None, DP),
            P(DP, None),
            P(None, DP),
            P(DP, None),
            P(None, DP),
            P(None, DP, None),
            P(None, DP),
            P(None, DP),
            P(None, DP),
            P(DP, None),
            P(None, DP),
            P(DP, None),
            P(None, DP),
            P(None, DP, None),
            P(None, DP),
            P(None, DP),
            P(None, DP),
            P(DP, None),
            P(None, DP),
            P(DP, None),
            P(None, DP),
            P(),
            P(),
            P(),
        ),
        check_vma=False,
    )
```

```python
import functools
import math

import jax
import jax.numpy as jnp
from jax import lax
from jax.experimental import pallas as pl
from jax.experimental.pallas import tpu as pltpu
from jax.sharding import PartitionSpec as P

CIN = 8
C = 256
HEADS = 8
HD = 32
COND = 512
GROUPS = 32
CLIPS = 4
STEP = 10


EPS_NORM = 1e-05
CLIP_NORM = 0.02
DP = ("a", "b")
GATHERED = ("front", "count", "film", "skip", "conv0", "conv1", "proj", "down", "head")
RATE = 0.04
BETA_ONE = 0.9
BETA_TWO = 0.999
ADAM_EPS = 1e-08
DECAY = 0.1


def matmul(lhs_mat, rhs_mat):
    return jnp.dot(lhs_mat, rhs_mat, preferred_element_type=jnp.float32)


def clip_terms(timesteps, clap_emb):
    half_cond = COND // 2
    frequency = jnp.exp(-math.log(10000.0) * jnp.arange(half_cond, dtype=jnp.float32) / half_cond)
    angles = timesteps.astype(jnp.float32)[:, None] * frequency[None]
    cond_vec = clap_emb + jnp.concatenate([jnp.sin(angles), jnp.cos(angles)], axis=1)
    theta_clip = 0.5 * math.pi * (timesteps.astype(jnp.float32) + 1.0) / 1001.0
    return (cond_vec, jnp.cos(theta_clip), jnp.sin(theta_clip))


BIG = 1e30
LOG2E = 1.4426950408889634
SCALE = HD**-0.5 * LOG2E
VMEM_LIMIT = 56 << 20
NN = (((1,), (0,)), ((), ()))
NT = (((1,), (1,)), ((), ()))


def mxu(lhs_mat, rhs_mat, dims=NN):
    return lax.dot_general(lhs_mat, rhs_mat, dims, preferred_element_type=jnp.float32)


def split_three(value):
    high = value.astype(jnp.bfloat16).astype(jnp.float32)
    rest = value - high
    mid = rest.astype(jnp.bfloat16).astype(jnp.float32)
    return high, mid, rest - mid


def rows_of(height, parts):
    row = lax.broadcasted_iota(jnp.int32, (height, parts[0].shape[1]), 0)
    total = jnp.zeros(row.shape, jnp.float32)
    for place, part in enumerate(parts):
        total = jnp.where(row == place, part, total)
    return total


def clip_rows(ids, hit, miss):
    return [jnp.where(ids == clip, hit, miss) for clip in range(CLIPS + 1)]


def forward_kernel(heads, bq, bk, x_ref, ids_ref, out_ref, lse_ref, keys):
    n_pix = x_ref.shape[1]
    step = pl.program_id(0)

    @pl.when(step == 0)
    def _():
        for head in range(heads):
            base = 3 * HD * head
            for start in range(0, n_pix, 512):
                cols = slice(start, start + 512)
                key = x_ref[base + HD : base + 2 * HD, cols].astype(jnp.float32)
                marks = rows_of(32, clip_rows(ids_ref[:, cols], 1.0, 0.0))
                stack = jnp.concatenate([key, marks, jnp.zeros((64, 512), jnp.float32)], axis=0)
                keys[head, cols, :] = stack.T.astype(jnp.bfloat16)

    block = pl.ds(pl.multiple_of(step * bq, bq), bq)
    marks = rows_of(32, clip_rows(ids_ref[:, block], 0.0, -BIG)).astype(jnp.bfloat16)
    for head in range(heads):
        base = 3 * HD * head
        query = jnp.concatenate([x_ref[base : base + HD, block], marks], axis=0)
        total = jnp.zeros((8, bq), jnp.float32)
        acc = jnp.zeros((HD, bq), jnp.float32)
        row_max = jnp.full((1, bq), -jnp.inf, jnp.float32)
        for start in range(0, n_pix, bk):
            scores = mxu(keys[head, start : start + bk, :64], query)
            new_max = jnp.maximum(row_max, jnp.max(scores, axis=0, keepdims=True) * SCALE)
            probs = jnp.exp2(scores * SCALE - new_max)
            decay = jnp.exp2(row_max - new_max)
            total = total * decay + jnp.sum(probs.reshape(bk // 8, 8, bq), axis=0)
            value = x_ref[base + 2 * HD : base + 3 * HD, start : start + bk]
            acc = acc * decay + mxu(value, probs.astype(jnp.bfloat16))
            row_max = new_max
        total = jnp.sum(total, axis=0, keepdims=True)
        out_ref[HD * head : HD * (head + 1), :] = (acc / total).astype(jnp.bfloat16)
        lse_ref[8 * head : 8 * (head + 1), :] = jnp.broadcast_to(row_max + jnp.log2(total), (8, bq))


def attention_forward(heads_x, pixel_ids):
    lanes, n_pix = heads_x.shape
    heads = lanes // (3 * HD)
    bq, bk = min(2048, n_pix), min(512, n_pix)
    return pl.pallas_call(
        functools.partial(forward_kernel, heads, bq, bk),
        grid=(n_pix // bq,),
        in_specs=[
            pl.BlockSpec((lanes, n_pix), lambda i: (0, 0)),
            pl.BlockSpec((1, n_pix), lambda i: (0, 0)),
        ],
        out_specs=[
            pl.BlockSpec((heads * HD, bq), lambda i: (0, i)),
            pl.BlockSpec((heads * 8, bq), lambda i: (0, i)),
        ],
        out_shape=[
            jax.ShapeDtypeStruct((heads * HD, n_pix), jnp.bfloat16),
            jax.ShapeDtypeStruct((heads * 8, n_pix), jnp.float32),
        ],
        scratch_shapes=[pltpu.VMEM((heads, n_pix, 128), jnp.bfloat16)],
        compiler_params=pltpu.CompilerParams(vmem_limit_bytes=VMEM_LIMIT),
    )(heads_x, pixel_ids)


def backward_kernel(
    heads, bq, bk, x_ref, ids_ref, do_ref, o_ref, lse_ref, out_ref,
    queries, keys, values, d_outs, d_query, query_rows, d_out_rows,
):
    n_pix = x_ref.shape[1]
    step = pl.program_id(0)

    @pl.when(step == 0)
    def _():
        d_query[...] = jnp.zeros_like(d_query)
        for head in range(heads):
            base = 3 * HD * head

            def prepare(part, carry):
                cols = pl.ds(pl.multiple_of(part * 512, 512), 512)
                ids = ids_ref[:, cols]
                one = jnp.ones((1, 512), jnp.float32)
                key = x_ref[base + HD : base + 2 * HD, cols].astype(jnp.float32)
                marks = rows_of(32, clip_rows(ids, 1.0, 0.0) + [one, one, one])
                stack = jnp.concatenate([key, key, key, marks], axis=0)
                keys[head, cols, :] = stack.T.astype(jnp.bfloat16)
                value = x_ref[base + 2 * HD : base + 3 * HD, cols].astype(jnp.float32)
                stack = jnp.concatenate(
                    [value, rows_of(32, [one, one, one]), jnp.zeros((64, 512), jnp.float32)], axis=0
                )
                values[head, cols, :] = stack.T.astype(jnp.bfloat16)
                query = x_ref[base : base + HD, cols].astype(jnp.float32) * SCALE
                lse = lse_ref[8 * head : 8 * head + 1, cols]
                marks = rows_of(32, clip_rows(ids, 0.0, -BIG) + list(split_three(-lse)))
                stack = jnp.concatenate([*split_three(query), marks], axis=0)
                queries[head, :, cols] = stack.astype(jnp.bfloat16)
                d_out = do_ref[HD * head : HD * (head + 1), cols].astype(jnp.float32)
                out = o_ref[HD * head : HD * (head + 1), cols].astype(jnp.float32)
                delta = jnp.sum(d_out * out, axis=0, keepdims=True)
                stack = jnp.concatenate([d_out, rows_of(32, split_three(-delta))], axis=0)
                d_outs[head, :, cols] = stack.astype(jnp.bfloat16)
                zero = jnp.zeros((96, 512), jnp.float32)
                query = x_ref[base : base + HD, cols].astype(jnp.float32)
                query_rows[head, cols, :] = jnp.concatenate([query, zero], 0).T.astype(jnp.bfloat16)
                d_out_rows[head, cols, :] = jnp.concatenate([d_out, zero], 0).T.astype(jnp.bfloat16)
                return carry

            lax.fori_loop(0, n_pix // 512, prepare, 0)

    block = pl.ds(pl.multiple_of(step * bk, bk), bk)
    for head in range(heads):
        base = 3 * HD * head
        key, value = keys[head, block, :], values[head, block, :64]
        key_t = x_ref[base + HD : base + 2 * HD, block]
        d_value = jnp.zeros((bk, 128), jnp.float32)
        d_key = jnp.zeros((bk, 128), jnp.float32)
        for start in range(0, n_pix, bq):
            cols = slice(start, start + bq)
            probs = jnp.exp2(mxu(key, queries[head, :, cols]))
            d_scores = (probs * mxu(value, d_outs[head, :, cols])).astype(jnp.bfloat16)
            probs = probs.astype(jnp.bfloat16)
            d_value += mxu(probs, d_out_rows[head, cols, :])
            d_key += mxu(d_scores, query_rows[head, cols, :])
            d_query[head, :, cols] += mxu(key_t, d_scores)
        d_key, d_value = d_key.T[:HD], d_value.T[:HD]
        out_ref[base + HD : base + 2 * HD, block] = (d_key * (HD**-0.5)).astype(jnp.bfloat16)
        out_ref[base + 2 * HD : base + 3 * HD, block] = d_value.astype(jnp.bfloat16)

    @pl.when(step == pl.num_programs(0) - 1)
    def _():
        for head in range(heads):
            base = 3 * HD * head
            out_ref[base : base + HD, :] = (d_query[head] * (HD**-0.5)).astype(jnp.bfloat16)


def attention_backward(heads_x, log_total, d_heads, out_heads, pixel_ids, bq=1024, bk=1024):
    lanes, n_pix = heads_x.shape
    heads = lanes // (3 * HD)
    bq, bk = min(bq, n_pix), min(bk, n_pix)
    operands = (heads_x, pixel_ids, d_heads, out_heads, log_total)
    return pl.pallas_call(
        functools.partial(backward_kernel, heads, bq, bk),
        grid=(n_pix // bk,),
        in_specs=[pl.BlockSpec(item.shape, lambda i: (0, 0)) for item in operands],
        out_specs=pl.BlockSpec((lanes, n_pix), lambda i: (0, 0)),
        out_shape=jax.ShapeDtypeStruct((lanes, n_pix), jnp.bfloat16),
        scratch_shapes=[
            pltpu.VMEM((heads, 128, n_pix), jnp.bfloat16),
            pltpu.VMEM((heads, n_pix, 128), jnp.bfloat16),
            pltpu.VMEM((heads, n_pix, 128), jnp.bfloat16),
            pltpu.VMEM((heads, 64, n_pix), jnp.bfloat16),
            pltpu.VMEM((heads, HD, n_pix), jnp.float32),
            pltpu.VMEM((heads, n_pix, 128), jnp.bfloat16),
            pltpu.VMEM((heads, n_pix, 128), jnp.bfloat16),
        ],
        compiler_params=pltpu.CompilerParams(vmem_limit_bytes=VMEM_LIMIT),
    )(*operands)


MESH = pl.DeviceIdType.MESH


def round_up(count, unit):
    return -(-count // unit) * unit


def greet(peers):
    barrier = pltpu.get_barrier_semaphore()
    for peer in peers:
        pl.semaphore_signal(barrier, inc=1, device_id=peer, device_id_type=MESH)
    pl.semaphore_wait(barrier, len(peers))


def push(src, dst, sems, slot, peer):
    copy = pltpu.make_async_remote_copy(
        src_ref=src,
        dst_ref=dst,
        send_sem=sems.at[0, slot],
        recv_sem=sems.at[1, slot],
        device_id=peer,
        device_id_type=MESH,
    )
    copy.start()
    return copy


def reduce_kernel(n_a, n_x, n_s, chunks, square_rows, *refs):
    n_in = sum(len(parts) for parts in chunks)
    n_chunk = len(chunks)
    ins = refs[:n_in]
    outs = refs[n_in : n_in + n_chunk]
    norm_ref = refs[n_in + n_chunk]
    scratch = list(refs[n_in + n_chunk + 1 :])
    halves = scratch[:n_in]
    accs = scratch[n_in : n_in + n_chunk]
    one_bufs = scratch[n_in + n_chunk : n_in + 3 * n_chunk]
    two_bufs = scratch[n_in + 3 * n_chunk : n_in + 5 * n_chunk]
    bit_bufs = scratch[n_in + 5 * n_chunk : n_in + 6 * n_chunk]
    squares, sems = scratch[n_in + 6 * n_chunk :]
    bits = n_s.bit_length() - 1
    my_a, my_b, my_s = lax.axis_index("a"), lax.axis_index("b"), lax.axis_index("s")
    core, my_x = lax.rem(my_b, 2), lax.div(my_b, 2)
    n_b = 2 * n_x
    n_d = n_a * n_b

    def dp_peer(off):
        place = lax.rem(my_a * n_b + my_b + off, n_d)
        return {"a": lax.div(place, n_b), "b": lax.rem(place, n_b)}

    def s_peer(bit):
        flipped = my_s + (1 << bit) - 2 * (1 << bit) * lax.rem(lax.div(my_s, 1 << bit), 2)
        return {"s": flipped}

    greet([dp_peer(off) for off in range(1, n_d)] + [s_peer(bit) for bit in range(bits)])
    slots = iter(range(sems.shape[1]))

    first_in = []
    at = 0
    for parts in chunks:
        first_in.append(at)
        at += len(parts)

    def core_send(c):
        copies = []
        for i in range(first_in[c], first_in[c] + len(chunks[c])):
            copies.append(
                push(ins[i].at[:, 1 - core], halves[i], sems, next(slots), {"b": my_b + 1 - 2 * core})
            )
        return copies

    def core_sum(c):
        acc = accs[c]
        row = 0
        for i in range(first_in[c], first_in[c] + len(chunks[c])):
            rows, lanes = ins[i].shape[2:]
            for lane in range(0, lanes, 256):
                for j in range(n_a * n_x):
                    acc[j // n_x, j % n_x, row : row + rows] = (
                        ins[i][j, core, :, lane : lane + 256] + halves[i][j, :, lane : lane + 256]
                    )
                row += rows
        if row < acc.shape[2]:
            for j in range(n_a * n_x):
                acc[j // n_x, j % n_x, row:] = jnp.zeros((acc.shape[2] - row, 256), jnp.float32)

    def plane_moves(c, stage):
        rows = accs[c].shape[2] // 2
        for half in range(2):
            over_x = (half + stage) % 2 == 0
            for off in range(1, n_x if over_x else n_a):
                yield half, over_x, off, pl.ds(half * rows, rows)

    def plane_buf(c, stage, half, off):
        return (one_bufs, two_bufs)[stage][2 * c + half].at[off - 1]

    def plane_send(c, stage):
        copies = []
        for half, over_x, off, rows in plane_moves(c, stage):
            acc = accs[c]
            if over_x:
                there = lax.rem(my_x + off, n_x)
                src = acc.at[:, there, rows] if stage == 0 else acc.at[my_a, there, rows]
                peer = {"b": 2 * there + core}
            else:
                there = lax.rem(my_a + off, n_a)
                src = acc.at[there, :, rows] if stage == 0 else acc.at[there, my_x, rows]
                peer = {"a": there}
            copies.append(push(src, plane_buf(c, stage, half, off), sems, next(slots), peer))
        return copies

    def plane_sum(c, stage):
        for half, over_x, off, rows in plane_moves(c, stage):
            buf = plane_buf(c, stage, half, off)
            if stage == 1:
                accs[c][my_a, my_x, rows] += buf[...]
            elif over_x:
                for j in range(n_a):
                    accs[c][j, my_x, rows] += buf[j]
            else:
                for j in range(n_x):
                    accs[c][my_a, j, rows] += buf[j]

    def span(c, level):
        length = accs[c].shape[2]
        start = 0
        for bit in range(level):
            length //= 2
            start = start + lax.rem(lax.div(my_s, 1 << bit), 2) * length
        return start, length

    def s_send(c, bit):
        start, length = span(c, bit)
        length //= 2
        mine = lax.rem(lax.div(my_s, 1 << bit), 2)
        rows = pl.ds(pl.multiple_of(start + (1 - mine) * length, 8), length)
        return [
            push(
                accs[c].at[my_a, my_x, rows],
                bit_bufs[c].at[bit, pl.ds(0, length)],
                sems,
                next(slots),
                s_peer(bit),
            )
        ]

    def s_sum(c, bit):
        start, length = span(c, bit + 1)
        rows = pl.ds(pl.multiple_of(start, 8), length)
        total = accs[c][my_a, my_x, rows] + bit_bufs[c][bit, :length]
        if bit == bits - 1:
            outs[c][rows] = total
        else:
            accs[c][my_a, my_x, rows] = total

    def up_send(c, bit):
        start, length = span(c, bit + 1)
        rows = pl.ds(pl.multiple_of(start, 8), length)
        return [push(outs[c].at[rows], outs[c].at[rows], sems, next(slots), s_peer(bit))]

    steps = [(core_send, core_sum, ())]
    steps += [(plane_send, plane_sum, (stage,)) for stage in range(2)]
    steps += [(s_send, s_sum, (bit,)) for bit in range(bits)]
    steps += [(up_send, None, (bit,)) for bit in reversed(range(bits))]
    flying = [None] * n_chunk
    for tick in range(n_chunk + len(steps)):
        for c in range(n_chunk):
            at = tick - c
            if at < 0 or at > len(steps):
                continue
            if at > 0:
                for copy in flying[c]:
                    copy.wait()
                if steps[at - 1][1] is not None:
                    steps[at - 1][1](c, *steps[at - 1][2])
            if at < len(steps):
                flying[c] = steps[at][0](c, *steps[at][2])

    lane = lax.broadcasted_iota(jnp.int32, (8, 256), 1)
    total = jnp.zeros((8, 256), jnp.float32)
    for c in range(n_chunk):
        rows = square_rows[c]
        total = total + jnp.sum((outs[c][:rows] * outs[c][:rows]).reshape(rows // 8, 8, 256), axis=0)
    total = jnp.sum(jnp.sum(total, axis=0, keepdims=True), axis=1, keepdims=True)
    last = square_rows[-1]
    squares[my_a * n_b + my_b] = jnp.where(lane == 1, total, outs[-1][last : last + 8])
    copies = []
    for off in range(1, n_d):
        place = squares.at[my_a * n_b + my_b]
        copies.append(push(place, place, sems, next(slots), dp_peer(off)))
    for copy in copies:
        copy.wait()
    total = squares[0]
    for place in range(1, n_d):
        total = total + squares[place]
    norm_ref[...] = total


def reduce_grads(chunks, square_rows, collective_id):
    n_a, n_b, n_s = lax.axis_size("a"), lax.axis_size("b"), lax.axis_size("s")
    n_x = n_b // 2
    bits = n_s.bit_length() - 1
    flat = [item for parts in chunks for item in parts]
    heights = [
        round_up(sum(item.shape[2] * item.shape[3] // 256 for item in parts), 16 * max(n_s // 2, 1))
        for parts in chunks
    ]
    f32 = jnp.float32
    one_shapes, two_shapes = [], []
    for rows in heights:
        half = rows // 2
        one_shapes += [(n_x - 1, n_a, half, 256), (n_a - 1, n_x, half, 256)]
        two_shapes += [(n_a - 1, half, 256), (n_x - 1, half, 256)]
    scratch = [(item.shape[0], *item.shape[2:]) for item in flat]
    scratch += [(n_a, n_x, rows, 256) for rows in heights]
    scratch += one_shapes + two_shapes
    scratch += [(bits, rows // 2, 256) for rows in heights]
    scratch += [(n_a * n_b, 8, 256)]
    n_copy = len(flat) + len(chunks) * 2 * (n_x - 1 + n_a - 1 + bits) + n_a * n_b - 1
    out = pl.pallas_call(
        functools.partial(reduce_kernel, n_a, n_x, n_s, [[None] * len(parts) for parts in chunks], square_rows),
        in_specs=[pl.BlockSpec(memory_space=pltpu.VMEM)] * len(flat),
        out_specs=[pl.BlockSpec(memory_space=pltpu.VMEM)] * (len(chunks) + 1),
        out_shape=[jax.ShapeDtypeStruct((rows, 256), f32) for rows in heights]
        + [jax.ShapeDtypeStruct((8, 256), f32)],
        scratch_shapes=[pltpu.VMEM(shape, f32) for shape in scratch]
        + [pltpu.SemaphoreType.DMA((2, n_copy))],
        compiler_params=pltpu.CompilerParams(
            collective_id=collective_id, has_side_effects=True, vmem_limit_bytes=VMEM_LIMIT
        ),
    )(*flat)
    return out[:-1], out[-1]


FREQ = 16
PAD = 2 * FREQ
HIGH = lax.Precision.HIGHEST


def high(lhs_mat, rhs_mat, dims=NN):
    return lax.dot_general(
        lhs_mat, rhs_mat, dims, precision=HIGH, preferred_element_type=jnp.float32
    )


def low(value):
    return value.astype(jnp.bfloat16)


def frame_of(n_pix):
    return round_up(n_pix + 2 * PAD, 128)


def lane_taps(value, left, right, sign):
    n_lane = value.shape[1]
    freq = lax.broadcasted_iota(jnp.int32, value.shape, 1) & (FREQ - 1)
    parts = []
    for df in (-1, 0, 1):
        for dc in (-1, 0, 1):
            moved = sign * (FREQ * dc + df)
            part = value if moved == 0 else pltpu.roll(value, (-moved) % n_lane, 1)
            if sign * df < 0:
                part = jnp.where(freq > 0, part, 0.0)
            if sign * df > 0:
                part = jnp.where(freq < FREQ - 1, part, 0.0)
            if sign * dc < 0:
                part = part * left
            if sign * dc > 0:
                part = part * right
            parts.append(part)
    return jnp.concatenate(parts, axis=0)


def fill(value, rows):
    return jnp.concatenate(
        [value, jnp.zeros((rows - value.shape[0], value.shape[1]), value.dtype)], axis=0
    )


def silu(x):
    return x * jax.nn.sigmoid(x)


def table_parts(table):
    return low(fill(jnp.concatenate(split_three(table), axis=0), 128))


def group_table(sums, counts):
    size = C // GROUPS
    row = lax.broadcasted_iota(jnp.int32, (C, C), 0) & (C - size)
    col = lax.broadcasted_iota(jnp.int32, (C, C), 1) & (C - size)
    totals = high(sums, (row == col).astype(jnp.float32))
    return totals[:8] / counts, totals[8:] / counts


def clip_sums(hot_t, one, two):
    return jnp.concatenate([high(hot_t, one), high(hot_t, two)], axis=0)


def hot_rows(ids, rows):
    clip = lax.broadcasted_iota(jnp.int32, (rows, ids.shape[1]), 0)
    return ((clip & 7) == ids) & (clip < 24)


def row_shifts(value, keep):
    n_row = value.shape[0]
    freq = lax.broadcasted_iota(jnp.int32, value.shape, 0) & (FREQ - 1)
    keep[0] = low(jnp.where(freq > 0, pltpu.roll(value, 1, 0), 0.0))
    keep[1] = low(value)
    keep[2] = low(jnp.where(freq < FREQ - 1, pltpu.roll(value, n_row - 1, 0), 0.0))


def conv_rows(shifts, weight, left, right, n_pix):
    total = None
    for dc in range(3):
        part = None
        for df in range(3):
            tap = 3 * df + dc
            item = mxu(shifts[df, FREQ * dc : FREQ * dc + n_pix], weight[C * tap : C * (tap + 1)])
            part = item if part is None else part + item
        part = part if dc == 1 else part * (left if dc == 0 else right)
        total = part if total is None else total + part
    return total


def conv_pull(shifts, weight, act_t, grad, left, right, n_pix):
    total = None
    for df in range(3):
        for dc in range(3):
            tap = 3 * df + dc
            at = FREQ * (2 - dc)
            window = shifts[2 - df, at : at + n_pix]
            if dc != 1:
                window = window * (right if dc == 0 else left)
            grad[C * tap : C * (tap + 1)] = mxu(act_t, window)
            item = mxu(window, weight[C * tap : C * (tap + 1)], NT)
            total = item if total is None else total + item
    return total


def layer_parts(x):
    centered = x - jnp.mean(x, axis=1, keepdims=True)
    inv_std = lax.rsqrt(jnp.mean(centered * centered, axis=1, keepdims=True) + EPS_NORM)
    return centered * inv_std, inv_std


def layer_pull(d_out, normed, inv_std, gain):
    scaled = d_out * gain
    return inv_std * (
        scaled
        - jnp.mean(scaled, axis=1, keepdims=True)
        - normed * jnp.mean(scaled * normed, axis=1, keepdims=True)
    )


class Ring:
    def __init__(self, n_b, sems, slots=None):
        self.n_b, self.sems = n_b, sems
        self.me = lax.axis_index("b")
        self.slots = iter(range(sems.shape[1])) if slots is None else slots
        self.places = [lax.rem(self.me + off, n_b) for off in range(1, n_b)]
        self.peers = [{"b": place} for place in self.places]

    def send(self, src, dst, peer):
        return push(src, dst, self.sems, next(self.slots), peer)

    def edges(self, first, last, left, right):
        return [self.send(last, left, self.peers[0]), self.send(first, right, self.peers[-1])]

    def sums(self, mine, held):
        held[self.me] = mine
        place = held.at[self.me]
        return [self.send(place, place, peer) for peer in self.peers]

    def total(self, held):
        total = held[0]
        for place in range(1, self.n_b):
            total = total + held[place]
        return total

    def rows_at(self, ref, place):
        count = ref.shape[0] // self.n_b
        return pl.ds(pl.multiple_of(place * count, 16), count)

    def cols_at(self, ref, place):
        count = ref.shape[1] // self.n_b
        return pl.ds(pl.multiple_of(place * count, 128), count)

    def spread(self, make, buf, out):
        copies = []
        for place, peer in zip(self.places, self.peers):
            rows = self.rows_at(buf, place)
            buf[rows] = make(rows)
            copies.append(self.send(buf.at[rows], out.at[:, self.cols_at(out, self.me)], peer))
        rows = self.rows_at(buf, self.me)
        out[:, self.cols_at(out, self.me)] = make(rows)
        return copies

    def collect(self, src, out):
        copies = []
        for place, peer in zip(self.places, self.peers):
            source = src.at[:, self.cols_at(src, place)]
            copies.append(self.send(source, out.at[self.rows_at(out, self.me)], peer))
        out[self.rows_at(out, self.me)] = src[:, self.cols_at(src, self.me)]
        return copies


def wait_all(copies):
    for copy in copies:
        copy.wait()


def own_hot(hot, n_pix):
    own = hot[PAD : PAD + n_pix].astype(jnp.float32)
    return own.T[:8], own[:, 24:25], own[:, 25:26]


def norm_wide(ring, held, wide, counts, hot, table_out):
    mean, square = group_table(ring.total(held), counts[...])
    inv_std = lax.rsqrt(square - mean * mean + EPS_NORM)
    table_out[:8] = mean
    table_out[8:] = inv_std
    return (wide[...] - mxu(hot, table_parts(mean))) * mxu(hot, table_parts(inv_std))


def front_kernel(n_a, n_b, *refs):
    n_move, n_gather = 4, len(GATHERED)
    refs = list(refs)
    moved_in, shards = refs[:n_move], refs[n_move : n_move + n_gather]
    refs = refs[n_move + n_gather :]
    moved, wholes = refs[:n_move], refs[n_move : n_move + n_gather]
    refs = refs[n_move + n_gather :]
    heads_out, joined_out, base_out, wide_one, table_one, wide_two, table_two, film_out = refs[:8]
    hot, taps_out, target_out, gains = refs[8:12]
    stem_buf, inner_buf, qkv_buf, shifts, held, sems = refs[12:]
    main_in, extra_in, first, last = moved_in
    main, extra, left_edge, right_edge = moved
    n_pix, n_lane = base_out.shape[0], main.shape[1]
    my_a, my_b, my_s = lax.axis_index("a"), lax.axis_index("b"), lax.axis_index("s")
    core, my_x = lax.rem(my_b, 2), lax.div(my_b, 2)
    n_x = n_b // 2
    n_d, n_j = n_a * n_b, n_a * n_x
    my_j = my_a * n_x + my_x
    slots = iter(range(sems.shape[1]))
    ring = Ring(n_b, sems, slots)

    def at(b, s):
        return {"b": lax.rem(b + n_b, n_b), "s": lax.rem(s + n_b, n_b)}

    dp_peers = []
    for off in range(1, n_d):
        there = lax.rem(my_a * n_b + my_b + off, n_d)
        dp_peers.append({"a": lax.div(there, n_b), "b": lax.rem(there, n_b)})
    mirrored = my_b != my_s
    shift = jnp.where(mirrored, 0, 1)
    greet(
        dp_peers
        + [at(my_s + 1, my_b), at(my_s - 1, my_b), at(my_s, my_b + 1), at(my_s, my_b - 1)]
        + [at(my_s + shift, my_b + shift)]
    )
    main_slot, extra_slot = next(slots), next(slots)

    @pl.when(mirrored)
    def _():
        push(main_in, main, sems, main_slot, at(my_s, my_b))
        push(extra_in, extra, sems, extra_slot, at(my_s, my_b))

    @pl.when(jnp.logical_not(mirrored))
    def _():
        main[...] = main_in[...]
        extra[...] = extra_in[...]

    copies = [
        push(last, left_edge, sems, next(slots), at(my_s + 1, my_b)),
        push(first, right_edge, sems, next(slots), at(my_s - 1, my_b)),
    ]

    def rows_of_shard(whole, j, of_core):
        count = whole.shape[0] // n_d
        return whole.at[pl.ds(pl.multiple_of((2 * j + of_core) * count, 8), count)]

    sibling = {"b": my_b + 1 - 2 * core}
    near, far = {}, {}
    for name, shard, whole in zip(GATHERED, shards, wholes):
        near[name] = []
        for off in range(1, n_j):
            there = lax.rem(my_j + off, n_j)
            peer = {"a": lax.div(there, n_x), "b": 2 * lax.rem(there, n_x) + core}
            near[name].append(
                push(shard, rows_of_shard(whole, my_j, core), sems, next(slots), peer)
            )
        place = rows_of_shard(whole, my_j, core)
        far[name] = [push(shard, place, sems, next(slots), sibling)]
        place[...] = shard[...]

    def forward(*names):
        for name in names:
            whole = wholes[GATHERED.index(name)]
            for off, copy in enumerate(near[name]):
                copy.wait()
                rows = rows_of_shard(whole, lax.rem(my_j + n_j - off - 1, n_j), core)
                far[name].append(push(rows, rows, sems, next(slots), sibling))

    def arrived(*names):
        for name in names:
            wait_all(far[name])

    part = dict(zip(GATHERED, wholes))
    forward("front", "count")
    wait_all(copies)

    @pl.when(mirrored)
    def _():
        for source, target, slot in ((main_in, main, main_slot), (extra_in, extra, extra_slot)):
            pltpu.make_async_remote_copy(
                src_ref=source,
                dst_ref=target,
                send_sem=sems.at[0, slot],
                recv_sem=sems.at[1, slot],
                device_id=at(my_s, my_b),
                device_id_type=MESH,
            ).wait()

    end = (PAD + n_pix) // 128 * 128
    main[:16, :128] += left_edge[...]
    main[:16, end : end + 128] += right_edge[...]
    rows = main[16:24]
    ids, left, right = rows[0:1], rows[4:5], rows[5:6]
    target_out[...] = main[8:16]
    taps = lane_taps(low(main[:8]).astype(jnp.float32), left, right, 1)
    taps = fill(taps, 128)
    taps_out[...] = low(taps[:80])
    clip = lax.broadcasted_iota(jnp.int32, (128, n_lane), 0)
    marks = hot_rows(ids.astype(jnp.int32), 128).astype(jnp.float32)
    marks = marks + jnp.where(clip == 24, left, 0.0) + jnp.where(clip == 25, right, 0.0)
    hot[...] = low(marks.T)
    hot_t, left, right = own_hot(hot, n_pix)
    wide_hot = hot[FREQ : 3 * FREQ + n_pix]
    taps = low(taps.T)[PAD : PAD + n_pix]
    arrived("front", "count")
    stem_w = part["front"][...]
    gains[...] = stem_w.astype(jnp.float32).T[72:80]
    stem = mxu(taps, stem_w, NT)
    stem_buf[...] = stem
    counts = extra.at[pl.ds(8, 8), pl.ds(0, C)]

    copies = ring.edges(
        stem_buf.at[pl.ds(0, FREQ)],
        stem_buf.at[pl.ds(n_pix - FREQ, FREQ)],
        wide_one.at[pl.ds(0, FREQ)],
        wide_one.at[pl.ds(n_pix + FREQ, FREQ)],
    )
    copies += ring.sums(clip_sums(hot_t, stem, stem * stem), held.at[0])
    wide_one[FREQ : FREQ + n_pix] = stem
    forward("film", "skip", "conv0")
    wait_all(copies)
    normed = norm_wide(ring, held.at[0], wide_one, counts, wide_hot, table_one)
    row_shifts(low(silu(normed * gains[0:1] + gains[1:2])).astype(jnp.float32), shifts)
    arrived("conv0")
    inner = conv_rows(shifts, part["conv0"], left, right, n_pix)
    inner_buf[...] = inner

    copies = ring.edges(
        inner_buf.at[pl.ds(0, FREQ)],
        inner_buf.at[pl.ds(n_pix - FREQ, FREQ)],
        wide_two.at[pl.ds(0, FREQ)],
        wide_two.at[pl.ds(n_pix + FREQ, FREQ)],
    )
    copies += ring.sums(clip_sums(hot_t, inner, inner * inner), held.at[1])
    wide_two[FREQ : FREQ + n_pix] = inner
    forward("conv1", "proj")
    arrived("film", "skip")
    film = mxu(low(extra[:8, : part["film"].shape[1]]), part["film"][...], NT)
    film_out[...] = film
    film_rows = mxu(wide_hot, table_parts(film))
    wait_all(copies)
    normed = norm_wide(ring, held.at[1], wide_two, counts, wide_hot, table_two)
    act = (normed * gains[2:3] + gains[3:4]) * (1.0 + film_rows[:, :C]) + film_rows[:, C:]
    row_shifts(low(silu(act)).astype(jnp.float32), shifts)
    arrived("conv1")
    branch = conv_rows(shifts, part["conv1"], left, right, n_pix)

    stem = stem_buf[...]
    joined_out[:, :C] = low(stem + branch)
    joined_out[:, C:] = low(stem)
    base = mxu(joined_out[...], part["skip"][...], NT)
    base_out[...] = base
    normed, _ = layer_parts(base)
    normed = low(normed * gains[4:5] + gains[5:6])
    forward("down", "head")
    arrived("proj")
    copies = ring.spread(lambda rows: low(mxu(part["proj"][rows], normed, NT)), qkv_buf, heads_out)
    arrived("down", "head")
    wait_all(copies)


def middle_kernel(
    n_b, heads, base, proj_t, down, head, target, main, gains, counts,
    d_mid_out, d_heads_out, g_up, g_down, g_out, g_head, g_gains, loss_out,
    attended, wide, act_t, pull_t, edge, d_att_buf, sems,
):
    n_pix = base.shape[0]
    n_lane = target.shape[1]
    n_hid = down.shape[0]
    ring = Ring(n_b, sems)
    greet(ring.peers)
    copies = ring.collect(heads, attended)
    rows = main[16:24]
    pix_count = jnp.sum(counts[:, 0:1], axis=0, keepdims=True) * 0.125
    wait_all(copies)
    proj_out, proj_up = proj_t.at[pl.ds(3 * C, C)], proj_t.at[pl.ds(4 * C, n_hid)]
    mid = base[...] + mxu(low(attended[...].astype(jnp.float32).T), proj_out[...], NT)
    normed, inv_std = layer_parts(mid)
    ln_b = low(normed * gains[6:7] + gains[7:8])
    top_t = jnp.zeros((C, n_pix), jnp.float32)
    scale = math.sqrt(2.0 / math.pi)
    for start in range(0, n_hid, 256):
        part = slice(start, start + 256)
        hidden = mxu(proj_up[part], ln_b, NT)
        bend = jnp.tanh(scale * (hidden + 0.044715 * hidden * hidden * hidden))
        gate = 0.5 * (1.0 + bend)
        act = low(hidden * gate)
        act_t[part] = act
        pull_t[part] = gate + 0.5 * hidden * (1.0 - bend * bend) * scale * (
            1.0 + 3.0 * 0.044715 * hidden * hidden
        )
        top_t = top_t + mxu(low(down[part].astype(jnp.float32).T), act)
    top = low(mid + top_t.T)
    wide[PAD : PAD + n_pix] = top
    wide[2 * PAD + n_pix :] = jnp.zeros((n_lane - 2 * PAD - n_pix, C), jnp.bfloat16)
    edge[0] = top[:PAD]
    edge[1] = top[n_pix - PAD :]
    copies = ring.edges(
        edge.at[0], edge.at[1], wide.at[pl.ds(0, PAD)], wide.at[pl.ds(PAD + n_pix, PAD)]
    )
    wait_all(copies)
    left, right, valid, own = rows[4:5], rows[5:6], rows[3:4], rows[6:7]
    products = mxu(head[...], wide[...], NT)
    freq = lax.broadcasted_iota(jnp.int32, (8, n_lane), 1) & (FREQ - 1)
    pred = jnp.zeros((8, n_lane), jnp.float32)
    for df in (-1, 0, 1):
        for dc in (-1, 0, 1):
            tap = 3 * (df + 1) + dc + 1
            moved = FREQ * dc + df
            part = products[8 * tap : 8 * (tap + 1)]
            part = part if moved == 0 else pltpu.roll(part, (-moved) % n_lane, 1)
            if df != 0:
                part = jnp.where(freq > 0 if df < 0 else freq < FREQ - 1, part, 0.0)
            if dc != 0:
                part = part * (left if dc < 0 else right)
            pred = pred + part
    residue = jnp.where(valid > 0.0, pred - target[...], 0.0)
    loss = jnp.sum(own * residue * residue, axis=0, keepdims=True)
    lane = lax.broadcasted_iota(jnp.int32, (8, 128), 1)
    loss_out[...] = jnp.where(lane == 1, pix_count, jnp.sum(loss, axis=1, keepdims=True))
    d_pred = low(2.0 * residue / pix_count).astype(jnp.float32)
    taps = lane_taps(d_pred, left, right, -1) * own
    taps = fill(taps, 128)
    g_head[...] = mxu(low(taps[:80]), wide[...])
    d_top = mxu(low(taps.T)[PAD : PAD + n_pix], fill(head[...], 128))
    d_top_b = low(d_top)
    d_ln_t = jnp.zeros((C, n_pix), jnp.float32)
    for start in range(0, n_hid, 256):
        part = slice(start, start + 256)
        d_hidden = low(mxu(down[part], d_top_b, NT) * pull_t[part])
        g_up[part] = mxu(d_hidden, ln_b)
        g_down[part] = mxu(act_t[part], d_top_b)
        d_ln_t = d_ln_t + mxu(low(proj_up[part].astype(jnp.float32).T), d_hidden)
    d_ln = d_ln_t.T
    g_gains[...] = rows_of(
        8, [jnp.sum(d_ln * normed, axis=0, keepdims=True), jnp.sum(d_ln, axis=0, keepdims=True)]
    )
    d_mid = d_top + layer_pull(d_ln, normed, inv_std, gains[6:7])
    d_mid_out[...] = d_mid
    d_mid_b = low(d_mid)
    g_out[...] = mxu(attended[...], d_mid_b).T
    d_att_buf[...] = low(mxu(low(proj_out[...].astype(jnp.float32).T), d_mid_b, NT))
    wait_all(ring.spread(lambda rows: d_att_buf[rows], d_att_buf, d_heads_out))


def back_kernel(
    n_b, d_heads, base, d_mid, joined, proj_t, skip_t, weight_one, weight_two, wide_one, wide_two,
    table_one, table_two, film, hot, extra, gains, taps,
    g_qkv, g_skip, g_one, g_two, g_film, g_stem, g_gains,
    d_qkv, shifts, wide, held, edge_b, edge_f, sems,
):
    n_pix = base.shape[0]
    ring = Ring(n_b, sems)
    greet(ring.peers)
    copies = ring.collect(d_heads, d_qkv)
    counts = extra.at[pl.ds(8, 8), pl.ds(0, C)]
    cond = extra[:8, : g_film.shape[1]]
    own = slice(FREQ, FREQ + n_pix)
    normed, inv_std = layer_parts(base[...])
    ln_b = low(normed * gains[4:5] + gains[5:6])
    wait_all(copies)
    g_qkv[...] = mxu(d_qkv[...], ln_b)
    d_ln = mxu(low(proj_t[: 3 * C].astype(jnp.float32).T), d_qkv[...]).T
    sum_gain = [jnp.sum(d_ln * normed, axis=0, keepdims=True), jnp.sum(d_ln, axis=0, keepdims=True)]
    d_base = d_mid[...] + layer_pull(d_ln, normed, inv_std, gains[4:5])
    g_skip[...] = mxu(low(d_base.T), joined[...])
    d_joined = mxu(low(d_base), skip_t[...])
    d_branch = low(d_joined[:, :C])
    edge_b[0] = d_branch[:FREQ]
    edge_b[1] = d_branch[n_pix - FREQ :]
    copies = ring.edges(edge_b.at[0], edge_b.at[1], edge_b.at[2], edge_b.at[3])
    d_stem = d_joined[:, :C] + d_joined[:, C:]

    hot_t, left, right = own_hot(hot, n_pix)
    left_b, right_b = low(left), low(right)
    wide_hot = hot[FREQ : 3 * FREQ + n_pix]
    film_rows = mxu(wide_hot[own], table_parts(film[...]))
    inv_two = mxu(wide_hot, table_parts(table_two[8:]))
    norm_two = (wide_two[...] - mxu(wide_hot, table_parts(table_two[:8]))) * inv_two
    affine = norm_two[own] * gains[2:3] + gains[3:4]
    act = affine * (1.0 + film_rows[:, :C]) + film_rows[:, C:]
    gate = jax.nn.sigmoid(act)
    act_t = low((low(act * gate).astype(jnp.float32)).T)
    wide[own] = d_branch.astype(jnp.float32)
    for copy in copies:
        copy.wait()
    wide[:FREQ] = edge_b[2].astype(jnp.float32)
    wide[FREQ + n_pix :] = edge_b[3].astype(jnp.float32)
    row_shifts(wide[...], shifts)
    d_act = conv_pull(shifts, weight_two, act_t, g_two, left_b, right_b, n_pix)
    d_act = d_act * (gate + act * gate * (1.0 - gate))
    d_film = jnp.concatenate([high(hot_t, d_act * affine), high(hot_t, d_act)], axis=1)
    clip = lax.broadcasted_iota(jnp.int32, d_film.shape, 0)
    d_film = jnp.where(clip < CLIPS, d_film, 0.0)
    g_film[...] = high(d_film.T, cond)
    d_act = d_act * (1.0 + film_rows[:, :C])
    sum_two = [
        jnp.sum(d_act * norm_two[own], axis=0, keepdims=True),
        jnp.sum(d_act, axis=0, keepdims=True),
    ]
    scaled = d_act * gains[2:3]
    wide[own] = scaled
    edge_f[0] = scaled[:FREQ]
    edge_f[1] = scaled[n_pix - FREQ :]
    copies = ring.edges(edge_f.at[0], edge_f.at[1], edge_f.at[2], edge_f.at[3])
    copies += ring.sums(clip_sums(hot_t, scaled, scaled * norm_two[own]), held.at[0])
    inv_one = mxu(wide_hot[own], table_parts(table_one[8:]))
    norm_one = (wide_one[own] - mxu(wide_hot[own], table_parts(table_one[:8]))) * inv_one
    act = norm_one * gains[0:1] + gains[1:2]
    gate = jax.nn.sigmoid(act)
    act_t = low((low(act * gate).astype(jnp.float32)).T)
    for copy in copies:
        copy.wait()
    wide[:FREQ] = edge_f[2]
    wide[FREQ + n_pix :] = edge_f[3]
    mean, slope = group_table(ring.total(held.at[0]), counts[...])
    d_inner = inv_two * (
        wide[...] - mxu(wide_hot, table_parts(mean)) - norm_two * mxu(wide_hot, table_parts(slope))
    )
    row_shifts(low(d_inner).astype(jnp.float32), shifts)
    d_act = conv_pull(shifts, weight_one, act_t, g_one, left_b, right_b, n_pix)
    d_act = d_act * (gate + act * gate * (1.0 - gate))
    sum_one = [
        jnp.sum(d_act * norm_one, axis=0, keepdims=True),
        jnp.sum(d_act, axis=0, keepdims=True),
    ]
    g_gains[...] = rows_of(8, sum_one + sum_two + sum_gain)
    scaled = d_act * gains[0:1]
    copies = ring.sums(clip_sums(hot_t, scaled, scaled * norm_one), held.at[1])
    for copy in copies:
        copy.wait()
    mean, slope = group_table(ring.total(held.at[1]), counts[...])
    hot_own = wide_hot[own]
    d_stem = d_stem + inv_one * (
        scaled - mxu(hot_own, table_parts(mean)) - norm_one * mxu(hot_own, table_parts(slope))
    )
    n_lane = taps.shape[1]
    d_stem = jnp.concatenate(
        [
            jnp.zeros((PAD, C), jnp.bfloat16),
            low(d_stem),
            jnp.zeros((n_lane - n_pix - PAD, C), jnp.bfloat16),
        ],
        axis=0,
    )
    g_stem[...] = mxu(taps[...], d_stem)


def dense(kernel, operands, outs, scratch, collective_id=None):
    vmem = pl.BlockSpec(memory_space=pltpu.VMEM)
    params = dict(vmem_limit_bytes=VMEM_LIMIT)
    if collective_id is not None:
        params.update(collective_id=collective_id, has_side_effects=True)
    return pl.pallas_call(
        kernel,
        in_specs=[vmem] * len(operands),
        out_specs=[vmem] * len(outs),
        out_shape=[jax.ShapeDtypeStruct(shape, dtype) for shape, dtype in outs],
        scratch_shapes=scratch,
        compiler_params=pltpu.CompilerParams(**params),
    )(*operands)


def body(
    clean_lat,
    noise_lat,
    column_ids,
    timesteps,
    clap_emb,
    conv_w,
    proj_w,
    film_w,
    skip_w,
    down_w,
    stem_w,
    head_w,
    gains,
    conv_m,
    proj_m,
    film_m,
    skip_m,
    down_m,
    stem_m,
    head_m,
    gains_m,
    conv_v,
    proj_v,
    film_v,
    skip_v,
    down_v,
    stem_v,
    head_v,
    gains_v,
):
    bf16, f32 = jnp.bfloat16, jnp.float32
    masters = (conv_w, proj_w, film_w, skip_w, down_w, stem_w, head_w, gains)
    firsts = (conv_m, proj_m, film_m, skip_m, down_m, stem_m, head_m, gains_m)
    seconds = (conv_v, proj_v, film_v, skip_v, down_v, stem_v, head_v, gains_v)
    n_dp, n_s = lax.axis_size(DP), lax.axis_size("s")
    n_a, n_b = lax.axis_size("a"), lax.axis_size("b")
    _, height, n_cols, _ = clean_lat.shape
    n_pix = height * n_cols
    n_lane = frame_of(n_pix)
    proj_cols, down_rows = proj_w.shape[1], down_w.shape[0]
    stem_rows = stem_w.shape[0]

    ids_row = column_ids[0]
    edge_pad = jnp.full((2,), -1, jnp.int32)
    ids_rim = lax.dynamic_slice_in_dim(
        jnp.concatenate([edge_pad, ids_row, edge_pad]), lax.axis_index("s") * n_cols, n_cols + 4
    )
    clip_hot = (ids_rim[:, None] == jnp.arange(CLIPS)[None, :]).astype(f32)
    place = jnp.arange(n_cols + 4)
    inner = (place > 0) & (place < n_cols + 3)
    own = (place > 1) & (place < n_cols + 2)
    same = ids_rim[1:] == ids_rim[:-1]
    off = jnp.zeros((1,), bool)
    cond_vec, alpha_clip, sigma_clip = clip_terms(timesteps[0], clap_emb[0])
    alpha_col = jnp.sum(clip_hot * alpha_clip[None], axis=1)
    sigma_col = jnp.sum(clip_hot * sigma_clip[None], axis=1)
    rows = [
        ids_rim,
        alpha_col,
        sigma_col,
        jnp.sum(clip_hot, axis=1) * inner,
        jnp.concatenate([off, same]),
        jnp.concatenate([same, off]),
        own,
        own,
    ]
    rows = jnp.stack([item.astype(f32) for item in rows])[:, :, None]
    clean, noise = (item[0].transpose(2, 1, 0) for item in (clean_lat, noise_lat))
    alpha, sigma = alpha_col[2:-2][None, :, None], sigma_col[2:-2][None, :, None]
    data = jnp.concatenate([alpha * clean + sigma * noise, alpha * noise - sigma * clean], axis=0)
    first, last = (
        jnp.pad(item, ((0, 0), (before, 128 - before - height)))
        for item, before in ((data[:, 0], PAD), (data[:, n_cols - 1], FREQ))
    )
    main = jnp.concatenate(
        [
            jnp.pad(data, ((0, 0), (2, 2), (0, 0))),
            jnp.broadcast_to(rows, (8, n_cols + 4, height)),
        ],
        axis=0,
    ).reshape(24, -1)
    main = jnp.pad(main, ((0, 0), (0, n_lane - main.shape[1])))
    labels = jnp.arange(8)
    counts = jnp.sum((ids_row[None] == labels[:, None]).astype(f32), axis=1) * (height * C // GROUPS)
    pixel_ids = jnp.repeat(ids_row.astype(f32), height).reshape(8, -1)
    lanes = max(COND, pixel_ids.shape[1])
    extra = [
        jnp.pad(jax.nn.silu(cond_vec).astype(bf16).astype(f32), ((0, 8 - CLIPS), (0, lanes - COND))),
        jnp.broadcast_to(jnp.maximum(counts, 1.0)[:, None], (8, lanes)),
        jnp.pad(pixel_ids, ((0, 0), (0, lanes - pixel_ids.shape[1]))),
    ]
    extra = jnp.concatenate(extra, axis=0)
    own_count = jnp.sum((ids_row < CLIPS).astype(f32)) * (height * CIN)
    front = jnp.concatenate([stem_w, gains], axis=0)
    front = jnp.pad(front, ((0, 128 - front.shape[0]), (0, 0))).T
    head_size = head_w.size
    head_rows = round_up(-(-head_size // 256), 16)
    head_flat = jnp.pad(head_w.reshape(-1), (0, head_rows * 256 - head_size)).reshape(-1, 256)
    shards = [
        front.astype(bf16),
        jnp.full((8, 128), own_count),
        film_w.T.astype(bf16),
        skip_w.T.astype(bf16),
        conv_w[0].astype(bf16),
        conv_w[1].astype(bf16),
        proj_w.T.astype(bf16),
        down_w.astype(bf16),
        head_flat.astype(bf16),
    ]
    n_wide = n_pix + PAD
    n_heads = 3 * C // n_b
    vmem = pltpu.VMEM

    def sems(count):
        return pltpu.SemaphoreType.DMA((2, count))

    moves = [main, extra, first, last]
    outs = dense(
        functools.partial(front_kernel, n_a, n_b),
        [*moves, *shards],
        [(item.shape, item.dtype) for item in moves]
        + [((n_dp * item.shape[0], item.shape[1]), item.dtype) for item in shards]
        + [
            ((n_heads, n_b * n_pix), bf16),
            ((n_pix, 2 * C), bf16),
            ((n_pix, C), f32),
            ((n_wide, C), f32),
            ((16, C), f32),
            ((n_wide, C), f32),
            ((16, C), f32),
            ((8, 2 * C), f32),
            ((n_lane, 128), bf16),
            ((80, n_lane), bf16),
            ((8, n_lane), f32),
            ((8, C), f32),
        ],
        [
            vmem((n_pix, C), f32),
            vmem((n_pix, C), f32),
            vmem((3 * C, n_pix), bf16),
            vmem((3, n_wide, C), bf16),
            vmem((2, n_b, 16, C), f32),
            sems(4 + len(shards) * (n_dp - 1) + 2 * (n_b + 1) + n_b - 1),
        ],
        0,
    )
    main, extra, _, _ = outs[:4]
    _, counts_all, film_t, skip_t, conv_one, conv_two, proj_t, down_b, head_b = outs[4:13]
    heads_x, joined, base_rows, wide_one, table_one, wide_two, table_two, film = outs[13:21]
    hot, taps, target, gain_f = outs[21:]
    pixel_ids = extra[16:, : pixel_ids.shape[1]].reshape(1, -1).astype(jnp.int32)
    head_b = head_b.reshape(n_dp, -1)[:, :head_size]
    head_t = head_b.reshape(9, C, CIN).transpose(0, 2, 1).reshape(9 * CIN, C)
    head_t = jnp.pad(head_t, ((0, 80 - 9 * CIN), (0, 0)))
    out_heads, log_total = attention_forward(heads_x, pixel_ids)
    n_hid = down_b.shape[0]
    d_mid, d_heads, g_up, g_down, g_out, g_head, gain_mid, loss = dense(
        functools.partial(middle_kernel, n_b),
        [out_heads, base_rows, proj_t, down_b, head_t, target, main, gain_f, counts_all],
        [
            ((n_pix, C), f32),
            ((C // n_b, n_b * n_pix), bf16),
            ((n_hid, C), f32),
            ((n_hid, C), f32),
            ((C, C), f32),
            ((80, C), f32),
            ((8, C), f32),
            ((8, 128), f32),
        ],
        [
            vmem((C, n_pix), bf16),
            vmem((n_lane, C), bf16),
            vmem((n_hid, n_pix), bf16),
            vmem((n_hid, n_pix), f32),
            vmem((2, PAD, C), bf16),
            vmem((C, n_pix), bf16),
            sems(2 * n_b),
        ],
        1,
    )
    local_loss, pix_count = loss[0, 0], loss[0, 1]
    d_heads_x = attention_backward(heads_x, log_total, d_heads, out_heads, pixel_ids)
    g_qkv, g_skip, g_conv_one, g_conv_two, g_film, g_stem, gain_back = dense(
        functools.partial(back_kernel, n_b),
        [
            d_heads_x, base_rows, d_mid, joined, proj_t, skip_t, conv_one, conv_two, wide_one,
            wide_two, table_one, table_two, film, hot, extra, gain_f, taps,
        ],
        [
            ((3 * C, C), f32),
            ((C, 2 * C), f32),
            ((9 * C, C), f32),
            ((9 * C, C), f32),
            ((2 * C, COND), f32),
            ((80, C), f32),
            ((8, C), f32),
        ],
        [
            vmem((3 * C, n_pix), bf16),
            vmem((3, n_wide, C), bf16),
            vmem((n_wide, C), f32),
            vmem((2, n_b, 16, C), f32),
            vmem((4, FREQ, C), bf16),
            vmem((4, FREQ, C), f32),
            sems(3 * n_b + 1),
        ],
        2,
    )
    g_head = g_head[:72].reshape(9, CIN, C).transpose(0, 2, 1)
    g_stem = g_stem[:stem_rows]
    g_gains = jnp.concatenate([gain_back[:6], gain_mid[:2]], axis=0)
    pairs = n_dp // 2

    def shards_of(item):
        return item.reshape(pairs, 2, -1, item.shape[-1])

    def small_rows(item):
        flat = item.reshape(n_dp, -1)
        flat = jnp.pad(flat, ((0, 0), (0, round_up(flat.shape[1], 256) - flat.shape[1])))
        return flat.reshape(n_dp, -1, 256)

    smalls = [
        small_rows(g_head),
        small_rows(g_stem.reshape(-1, n_dp, C // n_dp).transpose(1, 0, 2)),
        small_rows(g_gains.reshape(-1, n_dp, C // n_dp).transpose(1, 0, 2)),
    ]
    small_at = [0]
    for item in smalls:
        small_at.append(small_at[-1] + item.shape[1])
    small_end = round_up(small_at[-1], 8)
    loss_rows = jnp.zeros((n_dp, 8 + small_end - small_at[-1], 256), jnp.float32)
    smalls.append(loss_rows.at[0, -8, 0].set(local_loss))
    small = jnp.concatenate(smalls, axis=1)
    g_proj = jnp.concatenate([g_qkv, g_out, g_up], axis=0)
    chunks = [
        [shards_of(g_conv_one)],
        [shards_of(g_conv_two)],
        [shards_of(g_proj)],
        [shards_of(g_film), shards_of(g_skip), shards_of(g_down), shards_of(small)],
    ]
    heights = [sum(item.shape[2] * item.shape[3] // 256 for item in parts) for parts in chunks]
    heights[3] -= 8
    shards, sums = reduce_grads(chunks, heights, 3)
    squares, loss_sum = sums[0, 1], sums[0, 0]
    grad_norm = jnp.sqrt(squares)
    factor = jnp.minimum(1.0, CLIP_NORM / grad_norm)
    conv_rows, film_cols = 9 * C // n_dp, 2 * C // n_dp
    skip_cols, down_rows = C // n_dp, 4 * C // n_dp
    last = shards[3]
    film_end, skip_end = 2 * film_cols, 2 * film_cols + 2 * skip_cols
    film_shard = jnp.concatenate([last[:film_cols], last[film_cols:film_end]], axis=1).T
    skip_shard = jnp.concatenate(
        [last[film_end : film_end + skip_cols], last[film_end + skip_cols : skip_end]], axis=1
    ).T
    small_shard = last[skip_end + down_rows :]

    def small_part(index, like):
        rows = small_shard[small_at[index] : small_at[index + 1]].reshape(-1)
        return rows[: like.size].reshape(like.shape)

    shards = (
        jnp.stack([shards[0][:conv_rows], shards[1][:conv_rows]]),
        shards[2][: proj_w.shape[1]].T,
        film_shard,
        skip_shard,
        last[skip_end : skip_end + down_rows],
        small_part(1, stem_w),
        small_part(0, head_w),
        small_part(2, gains),
    )
    new_w, new_m, new_v = ([], [], [])
    for weight, grad_one, m_old, v_old in zip(masters, shards, firsts, seconds):
        grad_one = grad_one * factor
        m_new = BETA_ONE * m_old + (1.0 - BETA_ONE) * grad_one
        v_new = BETA_TWO * v_old + (1.0 - BETA_TWO) * grad_one * grad_one
        step_dir = (
            m_new / (1.0 - BETA_ONE**STEP) / (jnp.sqrt(v_new / (1.0 - BETA_TWO**STEP)) + ADAM_EPS)
        )
        new_w.append(weight - RATE * (step_dir + DECAY * weight))
        new_m.append(m_new)
        new_v.append(v_new)
    return (
        new_w[0],
        new_w[1],
        new_w[2],
        new_w[3],
        new_w[4],
        new_w[5],
        new_w[6],
        new_w[7],
        new_m[0],
        new_m[1],
        new_m[2],
        new_m[3],
        new_m[4],
        new_m[5],
        new_m[6],
        new_m[7],
        new_v[0],
        new_v[1],
        new_v[2],
        new_v[3],
        new_v[4],
        new_v[5],
        new_v[6],
        new_v[7],
        grad_norm,
        loss_sum,
        pix_count,
    )


def solution(mesh):
    n_dp, n_s = mesh.shape["dp"], mesh.shape["section"]
    blocks = jax.sharding.Mesh(mesh.devices.reshape(n_dp // n_s, n_s, n_s), ("a", "b", "s"))
    return jax.shard_map(
        body,
        mesh=blocks,
        in_specs=(
            P(DP, None, "s", None),
            P(DP, None, "s", None),
            P(DP, None),
            P(DP, None),
            P(DP, None, None),
            P(None, DP, None),
            P(None, DP),
            P(None, DP),
            P(None, DP),
            P(DP, None),
            P(None, DP),
            P(DP, None),
            P(None, DP),
            P(None, DP, None),
            P(None, DP),
            P(None, DP),
            P(None, DP),
            P(DP, None),
            P(None, DP),
            P(DP, None),
            P(None, DP),
            P(None, DP, None),
            P(None, DP),
            P(None, DP),
            P(None, DP),
            P(DP, None),
            P(None, DP),
            P(DP, None),
            P(None, DP),
        ),
        out_specs=(
            P(None, DP, None),
            P(None, DP),
            P(None, DP),
            P(None, DP),
            P(DP, None),
            P(None, DP),
            P(DP, None),
            P(None, DP),
            P(None, DP, None),
            P(None, DP),
            P(None, DP),
            P(None, DP),
            P(DP, None),
            P(None, DP),
            P(DP, None),
            P(None, DP),
            P(None, DP, None),
            P(None, DP),
            P(None, DP),
            P(None, DP),
            P(DP, None),
            P(None, DP),
            P(DP, None),
            P(None, DP),
            P(),
            P(),
            P(),
        ),
        check_vma=False,
    )
```

```python
import functools
import math

import jax
import jax.numpy as jnp
from jax import lax
from jax.experimental import pallas as pl
from jax.experimental.pallas import tpu as pltpu
from jax.sharding import PartitionSpec as P

CIN = 8
C = 256
HEADS = 8
HD = 32
COND = 512
GROUPS = 32
CLIPS = 4
STEP = 10


EPS_NORM = 1e-05
CLIP_NORM = 0.02
DP = ("a", "b")
STATES = ("conv", "proj", "film", "skip", "down")
GATHERED = ("front", "count", "film", "skip", "conv0", "conv1", "proj", "down", "head")
RATE = 0.04
BETA_ONE = 0.9
BETA_TWO = 0.999
ADAM_EPS = 1e-08
DECAY = 0.1


def matmul(lhs_mat, rhs_mat):
    return jnp.dot(lhs_mat, rhs_mat, preferred_element_type=jnp.float32)


def clip_terms(timesteps, clap_emb):
    half_cond = COND // 2
    frequency = jnp.exp(-math.log(10000.0) * jnp.arange(half_cond, dtype=jnp.float32) / half_cond)
    angles = timesteps.astype(jnp.float32)[:, None] * frequency[None]
    cond_vec = clap_emb + jnp.concatenate([jnp.sin(angles), jnp.cos(angles)], axis=1)
    theta_clip = 0.5 * math.pi * (timesteps.astype(jnp.float32) + 1.0) / 1001.0
    return (cond_vec, jnp.cos(theta_clip), jnp.sin(theta_clip))


BIG = 1e30
LOG2E = 1.4426950408889634
SCALE = HD**-0.5 * LOG2E
VMEM_LIMIT = 56 << 20
NN = (((1,), (0,)), ((), ()))
NT = (((1,), (1,)), ((), ()))


def mxu(lhs_mat, rhs_mat, dims=NN):
    return lax.dot_general(lhs_mat, rhs_mat, dims, preferred_element_type=jnp.float32)


def split_three(value):
    high = value.astype(jnp.bfloat16).astype(jnp.float32)
    rest = value - high
    mid = rest.astype(jnp.bfloat16).astype(jnp.float32)
    return high, mid, rest - mid


def rows_of(height, parts):
    row = lax.broadcasted_iota(jnp.int32, (height, parts[0].shape[1]), 0)
    total = jnp.zeros(row.shape, jnp.float32)
    for place, part in enumerate(parts):
        total = jnp.where(row == place, part, total)
    return total


def clip_rows(ids, hit, miss):
    return [jnp.where(ids == clip, hit, miss) for clip in range(CLIPS + 1)]


def forward_kernel(heads, bq, bk, x_ref, ids_ref, out_ref, lse_ref, keys):
    n_pix = x_ref.shape[1]
    step = pl.program_id(0)

    @pl.when(step == 0)
    def _():
        for head in range(heads):
            base = 3 * HD * head
            for start in range(0, n_pix, 512):
                cols = slice(start, start + 512)
                key = x_ref[base + HD : base + 2 * HD, cols].astype(jnp.float32)
                marks = rows_of(32, clip_rows(ids_ref[:, cols], 1.0, 0.0))
                stack = jnp.concatenate([key, marks, jnp.zeros((64, 512), jnp.float32)], axis=0)
                keys[head, cols, :] = stack.T.astype(jnp.bfloat16)

    block = pl.ds(pl.multiple_of(step * bq, bq), bq)
    marks = rows_of(32, clip_rows(ids_ref[:, block], 0.0, -BIG)).astype(jnp.bfloat16)
    for head in range(heads):
        base = 3 * HD * head
        query = jnp.concatenate([x_ref[base : base + HD, block], marks], axis=0)
        total = jnp.zeros((8, bq), jnp.float32)
        acc = jnp.zeros((HD, bq), jnp.float32)
        row_max = jnp.full((1, bq), -jnp.inf, jnp.float32)
        for start in range(0, n_pix, bk):
            scores = mxu(keys[head, start : start + bk, :64], query)
            new_max = jnp.maximum(row_max, jnp.max(scores, axis=0, keepdims=True) * SCALE)
            probs = jnp.exp2(scores * SCALE - new_max)
            decay = jnp.exp2(row_max - new_max)
            total = total * decay + jnp.sum(probs.reshape(bk // 8, 8, bq), axis=0)
            value = x_ref[base + 2 * HD : base + 3 * HD, start : start + bk]
            acc = acc * decay + mxu(value, probs.astype(jnp.bfloat16))
            row_max = new_max
        total = jnp.sum(total, axis=0, keepdims=True)
        out_ref[HD * head : HD * (head + 1), :] = (acc / total).astype(jnp.bfloat16)
        lse_ref[8 * head : 8 * (head + 1), :] = jnp.broadcast_to(row_max + jnp.log2(total), (8, bq))


def attention_forward(heads_x, pixel_ids):
    lanes, n_pix = heads_x.shape
    heads = lanes // (3 * HD)
    bq, bk = min(2048, n_pix), min(512, n_pix)
    return pl.pallas_call(
        functools.partial(forward_kernel, heads, bq, bk),
        grid=(n_pix // bq,),
        in_specs=[
            pl.BlockSpec((lanes, n_pix), lambda i: (0, 0)),
            pl.BlockSpec((1, n_pix), lambda i: (0, 0)),
        ],
        out_specs=[
            pl.BlockSpec((heads * HD, bq), lambda i: (0, i)),
            pl.BlockSpec((heads * 8, bq), lambda i: (0, i)),
        ],
        out_shape=[
            jax.ShapeDtypeStruct((heads * HD, n_pix), jnp.bfloat16),
            jax.ShapeDtypeStruct((heads * 8, n_pix), jnp.float32),
        ],
        scratch_shapes=[pltpu.VMEM((heads, n_pix, 128), jnp.bfloat16)],
        compiler_params=pltpu.CompilerParams(vmem_limit_bytes=VMEM_LIMIT),
    )(heads_x, pixel_ids)


def backward_kernel(
    heads, bq, bk, x_ref, ids_ref, do_ref, o_ref, lse_ref, out_ref,
    queries, keys, values, d_outs, d_query, query_rows, d_out_rows,
):
    n_pix = x_ref.shape[1]
    step = pl.program_id(0)

    @pl.when(step == 0)
    def _():
        d_query[...] = jnp.zeros_like(d_query)
        for head in range(heads):
            base = 3 * HD * head

            def prepare(part, carry):
                cols = pl.ds(pl.multiple_of(part * 512, 512), 512)
                ids = ids_ref[:, cols]
                one = jnp.ones((1, 512), jnp.float32)
                key = x_ref[base + HD : base + 2 * HD, cols].astype(jnp.float32)
                marks = rows_of(32, clip_rows(ids, 1.0, 0.0) + [one, one, one])
                stack = jnp.concatenate([key, key, key, marks], axis=0)
                keys[head, cols, :] = stack.T.astype(jnp.bfloat16)
                value = x_ref[base + 2 * HD : base + 3 * HD, cols].astype(jnp.float32)
                stack = jnp.concatenate(
                    [value, rows_of(32, [one, one, one]), jnp.zeros((64, 512), jnp.float32)], axis=0
                )
                values[head, cols, :] = stack.T.astype(jnp.bfloat16)
                query = x_ref[base : base + HD, cols].astype(jnp.float32) * SCALE
                lse = lse_ref[8 * head : 8 * head + 1, cols]
                marks = rows_of(32, clip_rows(ids, 0.0, -BIG) + list(split_three(-lse)))
                stack = jnp.concatenate([*split_three(query), marks], axis=0)
                queries[head, :, cols] = stack.astype(jnp.bfloat16)
                d_out = do_ref[HD * head : HD * (head + 1), cols].astype(jnp.float32)
                out = o_ref[HD * head : HD * (head + 1), cols].astype(jnp.float32)
                delta = jnp.sum(d_out * out, axis=0, keepdims=True)
                stack = jnp.concatenate([d_out, rows_of(32, split_three(-delta))], axis=0)
                d_outs[head, :, cols] = stack.astype(jnp.bfloat16)
                zero = jnp.zeros((96, 512), jnp.float32)
                query = x_ref[base : base + HD, cols].astype(jnp.float32)
                query_rows[head, cols, :] = jnp.concatenate([query, zero], 0).T.astype(jnp.bfloat16)
                d_out_rows[head, cols, :] = jnp.concatenate([d_out, zero], 0).T.astype(jnp.bfloat16)
                return carry

            lax.fori_loop(0, n_pix // 512, prepare, 0)

    block = pl.ds(pl.multiple_of(step * bk, bk), bk)
    for head in range(heads):
        base = 3 * HD * head
        key, value = keys[head, block, :], values[head, block, :64]
        key_t = x_ref[base + HD : base + 2 * HD, block]
        d_value = jnp.zeros((bk, 128), jnp.float32)
        d_key = jnp.zeros((bk, 128), jnp.float32)
        for start in range(0, n_pix, bq):
            cols = slice(start, start + bq)
            probs = jnp.exp2(mxu(key, queries[head, :, cols]))
            d_scores = (probs * mxu(value, d_outs[head, :, cols])).astype(jnp.bfloat16)
            probs = probs.astype(jnp.bfloat16)
            d_value += mxu(probs, d_out_rows[head, cols, :])
            d_key += mxu(d_scores, query_rows[head, cols, :])
            d_query[head, :, cols] += mxu(key_t, d_scores)
        d_key, d_value = d_key.T[:HD], d_value.T[:HD]
        out_ref[base + HD : base + 2 * HD, block] = (d_key * (HD**-0.5)).astype(jnp.bfloat16)
        out_ref[base + 2 * HD : base + 3 * HD, block] = d_value.astype(jnp.bfloat16)

    @pl.when(step == pl.num_programs(0) - 1)
    def _():
        for head in range(heads):
            base = 3 * HD * head
            out_ref[base : base + HD, :] = (d_query[head] * (HD**-0.5)).astype(jnp.bfloat16)


def attention_backward(heads_x, log_total, d_heads, out_heads, pixel_ids, bq=1024, bk=1024):
    lanes, n_pix = heads_x.shape
    heads = lanes // (3 * HD)
    bq, bk = min(bq, n_pix), min(bk, n_pix)
    operands = (heads_x, pixel_ids, d_heads, out_heads, log_total)
    return pl.pallas_call(
        functools.partial(backward_kernel, heads, bq, bk),
        grid=(n_pix // bk,),
        in_specs=[pl.BlockSpec(item.shape, lambda i: (0, 0)) for item in operands],
        out_specs=pl.BlockSpec((lanes, n_pix), lambda i: (0, 0)),
        out_shape=jax.ShapeDtypeStruct((lanes, n_pix), jnp.bfloat16),
        scratch_shapes=[
            pltpu.VMEM((heads, 128, n_pix), jnp.bfloat16),
            pltpu.VMEM((heads, n_pix, 128), jnp.bfloat16),
            pltpu.VMEM((heads, n_pix, 128), jnp.bfloat16),
            pltpu.VMEM((heads, 64, n_pix), jnp.bfloat16),
            pltpu.VMEM((heads, HD, n_pix), jnp.float32),
            pltpu.VMEM((heads, n_pix, 128), jnp.bfloat16),
            pltpu.VMEM((heads, n_pix, 128), jnp.bfloat16),
        ],
        compiler_params=pltpu.CompilerParams(vmem_limit_bytes=VMEM_LIMIT),
    )(*operands)


MESH = pl.DeviceIdType.MESH


def round_up(count, unit):
    return -(-count // unit) * unit


def greet(peers):
    barrier = pltpu.get_barrier_semaphore()
    for peer in peers:
        pl.semaphore_signal(barrier, inc=1, device_id=peer, device_id_type=MESH)
    pl.semaphore_wait(barrier, len(peers))


def push(src, dst, sems, slot, peer):
    copy = pltpu.make_async_remote_copy(
        src_ref=src,
        dst_ref=dst,
        send_sem=sems.at[0, slot],
        recv_sem=sems.at[1, slot],
        device_id=peer,
        device_id_type=MESH,
    )
    copy.start()
    return copy


FREQ = 16
PAD = 2 * FREQ
HIGH = lax.Precision.HIGHEST


def high(lhs_mat, rhs_mat, dims=NN):
    return lax.dot_general(
        lhs_mat, rhs_mat, dims, precision=HIGH, preferred_element_type=jnp.float32
    )


def low(value):
    return value.astype(jnp.bfloat16)


def frame_of(n_pix):
    return round_up(n_pix + 2 * PAD, 128)


def lane_taps(value, left, right, sign):
    n_lane = value.shape[1]
    freq = lax.broadcasted_iota(jnp.int32, value.shape, 1) & (FREQ - 1)
    parts = []
    for df in (-1, 0, 1):
        for dc in (-1, 0, 1):
            moved = sign * (FREQ * dc + df)
            part = value if moved == 0 else pltpu.roll(value, (-moved) % n_lane, 1)
            if sign * df < 0:
                part = jnp.where(freq > 0, part, 0.0)
            if sign * df > 0:
                part = jnp.where(freq < FREQ - 1, part, 0.0)
            if sign * dc < 0:
                part = part * left
            if sign * dc > 0:
                part = part * right
            parts.append(part)
    return jnp.concatenate(parts, axis=0)


def fill(value, rows):
    return jnp.concatenate(
        [value, jnp.zeros((rows - value.shape[0], value.shape[1]), value.dtype)], axis=0
    )


def silu(x):
    return x * jax.nn.sigmoid(x)


def table_parts(table):
    return low(fill(jnp.concatenate(split_three(table), axis=0), 128))


def group_table(sums, counts):
    size = C // GROUPS
    row = lax.broadcasted_iota(jnp.int32, (C, C), 0) & (C - size)
    col = lax.broadcasted_iota(jnp.int32, (C, C), 1) & (C - size)
    totals = high(sums, (row == col).astype(jnp.float32))
    return totals[:8] / counts, totals[8:] / counts


def clip_sums(hot_t, one, two):
    return jnp.concatenate([high(hot_t, one), high(hot_t, two)], axis=0)


def hot_rows(ids, rows):
    clip = lax.broadcasted_iota(jnp.int32, (rows, ids.shape[1]), 0)
    return ((clip & 7) == ids) & (clip < 24)


def row_shifts(value, keep):
    n_row = value.shape[0]
    freq = lax.broadcasted_iota(jnp.int32, value.shape, 0) & (FREQ - 1)
    keep[0] = low(jnp.where(freq > 0, pltpu.roll(value, 1, 0), 0.0))
    keep[1] = low(value)
    keep[2] = low(jnp.where(freq < FREQ - 1, pltpu.roll(value, n_row - 1, 0), 0.0))


def conv_rows(shifts, weight, left, right, n_pix):
    total = None
    for dc in range(3):
        part = None
        for df in range(3):
            tap = 3 * df + dc
            item = mxu(shifts[df, FREQ * dc : FREQ * dc + n_pix], weight[C * tap : C * (tap + 1)])
            part = item if part is None else part + item
        part = part if dc == 1 else part * (left if dc == 0 else right)
        total = part if total is None else total + part
    return total


def conv_pull(shifts, weight, act_t, grad, left, right, n_pix):
    total = None
    for df in range(3):
        for dc in range(3):
            tap = 3 * df + dc
            at = FREQ * (2 - dc)
            window = shifts[2 - df, at : at + n_pix]
            if dc != 1:
                window = window * (right if dc == 0 else left)
            put_rows(grad, C * tap, mxu(act_t, window))
            item = mxu(window, weight[C * tap : C * (tap + 1)], NT)
            total = item if total is None else total + item
    return total


def layer_parts(x):
    centered = x - jnp.mean(x, axis=1, keepdims=True)
    inv_std = lax.rsqrt(jnp.mean(centered * centered, axis=1, keepdims=True) + EPS_NORM)
    return centered * inv_std, inv_std


def layer_pull(d_out, normed, inv_std, gain):
    scaled = d_out * gain
    return inv_std * (
        scaled
        - jnp.mean(scaled, axis=1, keepdims=True)
        - normed * jnp.mean(scaled * normed, axis=1, keepdims=True)
    )


class Ring:
    def __init__(self, n_b, sems, slots=None):
        self.n_b, self.sems = n_b, sems
        self.me = lax.axis_index("b")
        self.slots = iter(range(sems.shape[1])) if slots is None else slots
        self.places = [lax.rem(self.me + off, n_b) for off in range(1, n_b)]
        self.peers = [{"b": place} for place in self.places]

    def send(self, src, dst, peer):
        return push(src, dst, self.sems, next(self.slots), peer)

    def edges(self, first, last, left, right):
        return [self.send(last, left, self.peers[0]), self.send(first, right, self.peers[-1])]

    def sums(self, mine, held):
        held[self.me] = mine
        place = held.at[self.me]
        return [self.send(place, place, peer) for peer in self.peers]

    def total(self, held):
        total = held[0]
        for place in range(1, self.n_b):
            total = total + held[place]
        return total

    def rows_at(self, ref, place):
        count = ref.shape[0] // self.n_b
        return pl.ds(pl.multiple_of(place * count, 16), count)

    def cols_at(self, ref, place):
        count = ref.shape[1] // self.n_b
        return pl.ds(pl.multiple_of(place * count, 128), count)

    def spread(self, make, buf, out):
        copies = []
        for place, peer in zip(self.places, self.peers):
            rows = self.rows_at(buf, place)
            buf[rows] = make(rows)
            copies.append(self.send(buf.at[rows], out.at[:, self.cols_at(out, self.me)], peer))
        rows = self.rows_at(buf, self.me)
        out[:, self.cols_at(out, self.me)] = make(rows)
        return copies

    def collect(self, src, out):
        copies = []
        for place, peer in zip(self.places, self.peers):
            source = src.at[:, self.cols_at(src, place)]
            copies.append(self.send(source, out.at[self.rows_at(out, self.me)], peer))
        out[self.rows_at(out, self.me)] = src[:, self.cols_at(src, self.me)]
        return copies


def wait_all(copies):
    for copy in copies:
        copy.wait()


def own_hot(hot, n_pix):
    own = hot[PAD : PAD + n_pix].astype(jnp.float32)
    return own.T[:8], own[:, 24:25], own[:, 25:26]


def norm_wide(ring, held, wide, counts, hot, table_out):
    mean, square = group_table(ring.total(held), counts[...])
    inv_std = lax.rsqrt(square - mean * mean + EPS_NORM)
    table_out[:8] = mean
    table_out[8:] = inv_std
    return (wide[...] - mxu(hot, table_parts(mean))) * mxu(hot, table_parts(inv_std))


def front_kernel(n_a, n_b, *refs):
    n_move, n_gather = 4, len(GATHERED)
    refs = list(refs)
    moved_in, shards = refs[:n_move], refs[n_move : n_move + n_gather]
    refs = refs[n_move + n_gather :]
    moved, wholes = refs[:n_move], refs[n_move : n_move + n_gather]
    refs = refs[n_move + n_gather :]
    heads_out, joined_out, base_out, wide_one, table_one, wide_two, table_two, film_out = refs[:8]
    hot, taps_out, target_out, gains = refs[8:12]
    stem_buf, inner_buf, qkv_buf, shifts, held, sems = refs[12:]
    main_in, extra_in, first, last = moved_in
    main, extra, left_edge, right_edge = moved
    n_pix, n_lane = base_out.shape[0], main.shape[1]
    my_a, my_b, my_s = lax.axis_index("a"), lax.axis_index("b"), lax.axis_index("s")
    core, my_x = lax.rem(my_b, 2), lax.div(my_b, 2)
    n_x = n_b // 2
    n_d, n_j = n_a * n_b, n_a * n_x
    my_j = my_a * n_x + my_x
    slots = iter(range(sems.shape[1]))
    ring = Ring(n_b, sems, slots)

    def at(b, s):
        return {"b": lax.rem(b + n_b, n_b), "s": lax.rem(s + n_b, n_b)}

    dp_peers = []
    for off in range(1, n_d):
        there = lax.rem(my_a * n_b + my_b + off, n_d)
        dp_peers.append({"a": lax.div(there, n_b), "b": lax.rem(there, n_b)})
    mirrored = my_b != my_s
    shift = jnp.where(mirrored, 0, 1)
    greet(
        dp_peers
        + [at(my_s + 1, my_b), at(my_s - 1, my_b), at(my_s, my_b + 1), at(my_s, my_b - 1)]
        + [at(my_s + shift, my_b + shift)]
    )
    main_slot, extra_slot = next(slots), next(slots)

    @pl.when(mirrored)
    def _():
        push(main_in, main, sems, main_slot, at(my_s, my_b))
        push(extra_in, extra, sems, extra_slot, at(my_s, my_b))

    @pl.when(jnp.logical_not(mirrored))
    def _():
        main[...] = main_in[...]
        extra[...] = extra_in[...]

    copies = [
        push(last, left_edge, sems, next(slots), at(my_s + 1, my_b)),
        push(first, right_edge, sems, next(slots), at(my_s - 1, my_b)),
    ]

    def rows_of_shard(whole, j, of_core):
        count = whole.shape[0] // n_d
        return whole.at[pl.ds(pl.multiple_of((2 * j + of_core) * count, 8), count)]

    sibling = {"b": my_b + 1 - 2 * core}
    near, far = {}, {}
    for name, shard, whole in zip(GATHERED, shards, wholes):
        near[name] = []
        for off in range(1, n_j):
            there = lax.rem(my_j + off, n_j)
            peer = {"a": lax.div(there, n_x), "b": 2 * lax.rem(there, n_x) + core}
            near[name].append(
                push(shard, rows_of_shard(whole, my_j, core), sems, next(slots), peer)
            )
        place = rows_of_shard(whole, my_j, core)
        far[name] = [push(shard, place, sems, next(slots), sibling)]
        place[...] = shard[...]

    def forward(*names):
        for name in names:
            whole = wholes[GATHERED.index(name)]
            for off, copy in enumerate(near[name]):
                copy.wait()
                rows = rows_of_shard(whole, lax.rem(my_j + n_j - off - 1, n_j), core)
                far[name].append(push(rows, rows, sems, next(slots), sibling))

    def arrived(*names):
        for name in names:
            wait_all(far[name])

    part = dict(zip(GATHERED, wholes))
    forward("front", "count")
    wait_all(copies)

    @pl.when(mirrored)
    def _():
        for source, target, slot in ((main_in, main, main_slot), (extra_in, extra, extra_slot)):
            pltpu.make_async_remote_copy(
                src_ref=source,
                dst_ref=target,
                send_sem=sems.at[0, slot],
                recv_sem=sems.at[1, slot],
                device_id=at(my_s, my_b),
                device_id_type=MESH,
            ).wait()

    end = (PAD + n_pix) // 128 * 128
    main[:16, :128] += left_edge[...]
    main[:16, end : end + 128] += right_edge[...]
    rows = main[16:24]
    ids, left, right = rows[0:1], rows[4:5], rows[5:6]
    target_out[...] = main[8:16]
    taps = lane_taps(low(main[:8]).astype(jnp.float32), left, right, 1)
    taps = fill(taps, 128)
    taps_out[...] = low(taps[:80])
    clip = lax.broadcasted_iota(jnp.int32, (128, n_lane), 0)
    marks = hot_rows(ids.astype(jnp.int32), 128).astype(jnp.float32)
    marks = marks + jnp.where(clip == 24, left, 0.0) + jnp.where(clip == 25, right, 0.0)
    hot[...] = low(marks.T)
    hot_t, left, right = own_hot(hot, n_pix)
    wide_hot = hot[FREQ : 3 * FREQ + n_pix]
    taps = low(taps.T)[PAD : PAD + n_pix]
    arrived("front", "count")
    stem_w = part["front"][...]
    gains[...] = stem_w.astype(jnp.float32).T[72:80]
    stem = mxu(taps, stem_w, NT)
    stem_buf[...] = stem
    counts = extra.at[pl.ds(8, 8), pl.ds(0, C)]

    copies = ring.edges(
        stem_buf.at[pl.ds(0, FREQ)],
        stem_buf.at[pl.ds(n_pix - FREQ, FREQ)],
        wide_one.at[pl.ds(0, FREQ)],
        wide_one.at[pl.ds(n_pix + FREQ, FREQ)],
    )
    copies += ring.sums(clip_sums(hot_t, stem, stem * stem), held.at[0])
    wide_one[FREQ : FREQ + n_pix] = stem
    forward("film", "skip", "conv0")
    wait_all(copies)
    normed = norm_wide(ring, held.at[0], wide_one, counts, wide_hot, table_one)
    row_shifts(low(silu(normed * gains[0:1] + gains[1:2])).astype(jnp.float32), shifts)
    arrived("conv0")
    inner = conv_rows(shifts, part["conv0"], left, right, n_pix)
    inner_buf[...] = inner

    copies = ring.edges(
        inner_buf.at[pl.ds(0, FREQ)],
        inner_buf.at[pl.ds(n_pix - FREQ, FREQ)],
        wide_two.at[pl.ds(0, FREQ)],
        wide_two.at[pl.ds(n_pix + FREQ, FREQ)],
    )
    copies += ring.sums(clip_sums(hot_t, inner, inner * inner), held.at[1])
    wide_two[FREQ : FREQ + n_pix] = inner
    forward("conv1", "proj")
    arrived("film", "skip")
    film = mxu(low(extra[:8, : part["film"].shape[1]]), part["film"][...], NT)
    film_out[...] = film
    film_rows = mxu(wide_hot, table_parts(film))
    wait_all(copies)
    normed = norm_wide(ring, held.at[1], wide_two, counts, wide_hot, table_two)
    act = (normed * gains[2:3] + gains[3:4]) * (1.0 + film_rows[:, :C]) + film_rows[:, C:]
    row_shifts(low(silu(act)).astype(jnp.float32), shifts)
    arrived("conv1")
    branch = conv_rows(shifts, part["conv1"], left, right, n_pix)

    stem = stem_buf[...]
    joined_out[:, :C] = low(stem + branch)
    joined_out[:, C:] = low(stem)
    base = mxu(joined_out[...], part["skip"][...], NT)
    base_out[...] = base
    normed, _ = layer_parts(base)
    normed = low(normed * gains[4:5] + gains[5:6])
    forward("down", "head")
    arrived("proj")
    copies = ring.spread(lambda rows: low(mxu(part["proj"][rows], normed, NT)), qkv_buf, heads_out)
    arrived("down", "head")
    wait_all(copies)


def middle_kernel(
    n_b, heads, base, proj_t, down, head, target, main, gains, counts,
    d_mid_out, d_heads_out, g_up, g_down, g_out, g_head, g_gains, loss_out,
    attended, wide, act_t, pull_t, edge, d_att_buf, sems,
):
    n_pix = base.shape[0]
    n_lane = target.shape[1]
    n_hid = down.shape[0]
    ring = Ring(n_b, sems)
    greet(ring.peers)
    copies = ring.collect(heads, attended)
    rows = main[16:24]
    pix_count = jnp.sum(counts[:, 0:1], axis=0, keepdims=True) * 0.125
    wait_all(copies)
    proj_out, proj_up = proj_t.at[pl.ds(3 * C, C)], proj_t.at[pl.ds(4 * C, n_hid)]
    mid = base[...] + mxu(low(attended[...].astype(jnp.float32).T), proj_out[...], NT)
    normed, inv_std = layer_parts(mid)
    ln_b = low(normed * gains[6:7] + gains[7:8])
    top_t = jnp.zeros((C, n_pix), jnp.float32)
    scale = math.sqrt(2.0 / math.pi)
    for start in range(0, n_hid, 256):
        part = slice(start, start + 256)
        hidden = mxu(proj_up[part], ln_b, NT)
        bend = jnp.tanh(scale * (hidden + 0.044715 * hidden * hidden * hidden))
        gate = 0.5 * (1.0 + bend)
        act = low(hidden * gate)
        act_t[part] = act
        pull_t[part] = gate + 0.5 * hidden * (1.0 - bend * bend) * scale * (
            1.0 + 3.0 * 0.044715 * hidden * hidden
        )
        top_t = top_t + mxu(low(down[part].astype(jnp.float32).T), act)
    top = low(mid + top_t.T)
    wide[PAD : PAD + n_pix] = top
    wide[2 * PAD + n_pix :] = jnp.zeros((n_lane - 2 * PAD - n_pix, C), jnp.bfloat16)
    edge[0] = top[:PAD]
    edge[1] = top[n_pix - PAD :]
    copies = ring.edges(
        edge.at[0], edge.at[1], wide.at[pl.ds(0, PAD)], wide.at[pl.ds(PAD + n_pix, PAD)]
    )
    wait_all(copies)
    left, right, valid, own = rows[4:5], rows[5:6], rows[3:4], rows[6:7]
    products = mxu(head[...], wide[...], NT)
    freq = lax.broadcasted_iota(jnp.int32, (8, n_lane), 1) & (FREQ - 1)
    pred = jnp.zeros((8, n_lane), jnp.float32)
    for df in (-1, 0, 1):
        for dc in (-1, 0, 1):
            tap = 3 * (df + 1) + dc + 1
            moved = FREQ * dc + df
            part = products[8 * tap : 8 * (tap + 1)]
            part = part if moved == 0 else pltpu.roll(part, (-moved) % n_lane, 1)
            if df != 0:
                part = jnp.where(freq > 0 if df < 0 else freq < FREQ - 1, part, 0.0)
            if dc != 0:
                part = part * (left if dc < 0 else right)
            pred = pred + part
    residue = jnp.where(valid > 0.0, pred - target[...], 0.0)
    loss = jnp.sum(own * residue * residue, axis=0, keepdims=True)
    lane = lax.broadcasted_iota(jnp.int32, (8, 128), 1)
    loss_out[...] = jnp.where(lane == 1, pix_count, jnp.sum(loss, axis=1, keepdims=True))
    d_pred = low(2.0 * residue / pix_count).astype(jnp.float32)
    taps = lane_taps(d_pred, left, right, -1) * own
    taps = fill(taps, 128)
    g_head[...] = mxu(low(taps[:80]), wide[...])
    d_top = mxu(low(taps.T)[PAD : PAD + n_pix], fill(head[...], 128))
    d_top_b = low(d_top)
    d_ln_t = jnp.zeros((C, n_pix), jnp.float32)
    for start in range(0, n_hid, 256):
        part = slice(start, start + 256)
        d_hidden = low(mxu(down[part], d_top_b, NT) * pull_t[part])
        g_up[part] = mxu(d_hidden, ln_b)
        g_down[part] = mxu(act_t[part], d_top_b)
        d_ln_t = d_ln_t + mxu(low(proj_up[part].astype(jnp.float32).T), d_hidden)
    d_ln = d_ln_t.T
    g_gains[...] = rows_of(
        8, [jnp.sum(d_ln * normed, axis=0, keepdims=True), jnp.sum(d_ln, axis=0, keepdims=True)]
    )
    d_mid = d_top + layer_pull(d_ln, normed, inv_std, gains[6:7])
    d_mid_out[...] = d_mid
    d_mid_b = low(d_mid)
    g_out[...] = mxu(attended[...], d_mid_b).T
    d_att_buf[...] = low(mxu(low(proj_out[...].astype(jnp.float32).T), d_mid_b, NT))
    wait_all(ring.spread(lambda rows: d_att_buf[rows], d_att_buf, d_heads_out))


def put_rows(ref, start, value):
    height = ref.shape[2]
    at = 0
    while at < value.shape[0]:
        shard, row = divmod(start + at, height)
        count = min(height - row, value.shape[0] - at)
        ref[shard // 2, shard % 2, row : row + count] = value[at : at + count]
        at += count


class Reducer:
    def __init__(self, n_a, n_b, n_s, chunks, scratch, outs, sems):
        self.n_a, self.n_b, self.n_x, self.n_s = n_a, n_b, n_b // 2, n_s
        self.bits = n_s.bit_length() - 1
        self.chunks, self.outs, self.sems = chunks, outs, sems
        self.slots = iter(range(sems.shape[1]))
        scratch = list(scratch)
        self.halves, self.accs, self.one, self.two, self.bit = [], [], [], [], []
        for parts in chunks:
            self.halves.append([scratch.pop(0) for _ in parts])
            self.accs.append(scratch.pop(0))
            self.one.append([scratch.pop(0) for _ in range(2)])
            self.two.append([scratch.pop(0) for _ in range(2)])
            self.bit.append(scratch.pop(0))
        self.my_a, self.my_b, self.my_s = (lax.axis_index(axis) for axis in ("a", "b", "s"))
        self.core, self.my_x = lax.rem(self.my_b, 2), lax.div(self.my_b, 2)
        self.place = self.my_a * n_b + self.my_b
        self.n_d = n_a * n_b
        self.steps = [(self.core_send, self.core_sum, 0)]
        self.steps += [(self.plane_send, self.plane_sum, stage) for stage in range(2)]
        self.steps += [(self.s_send, self.s_sum, bit) for bit in range(self.bits)]
        self.steps += [(self.up_send, None, bit) for bit in reversed(range(self.bits))]
        self.at = [0] * len(chunks)
        self.flying = [None] * len(chunks)

    @staticmethod
    def heights(shapes, n_s):
        return [
            round_up(sum(shape[2] * shape[3] // 256 for shape in parts), 8 * max(n_s, 2))
            for parts in shapes
        ]

    @staticmethod
    def scratch(shapes, n_a, n_b, n_s):
        n_x, bits = n_b // 2, n_s.bit_length() - 1
        result = []
        for parts, rows in zip(shapes, Reducer.heights(shapes, n_s)):
            half = rows // 2
            result += [(shape[0], *shape[2:]) for shape in parts]
            result += [(n_a, n_x, rows, 256)]
            result += [(n_x - 1, n_a, half, 256), (n_a - 1, n_x, half, 256)]
            result += [(n_a - 1, half, 256), (n_x - 1, half, 256)]
            result += [(bits, half, 256)]
        return result

    @staticmethod
    def copies(shapes, n_a, n_b, n_s):
        each = 2 * (n_b // 2 - 1 + n_a - 1 + n_s.bit_length() - 1)
        return sum(len(parts) + each for parts in shapes)

    def send(self, src, dst, peer):
        return push(src, dst, self.sems, next(self.slots), peer)

    def dp_peers(self):
        peers = []
        for off in range(1, self.n_d):
            there = lax.rem(self.place + off, self.n_d)
            peers.append({"a": lax.div(there, self.n_b), "b": lax.rem(there, self.n_b)})
        return peers

    def digit(self, bit):
        return lax.rem(lax.div(self.my_s, 1 << bit), 2)

    def s_peer(self, bit):
        return {"s": self.my_s + (1 << bit) - 2 * (1 << bit) * self.digit(bit)}

    def tick(self, *names):
        for c in names:
            at = self.at[c]
            if at > len(self.steps):
                continue
            if at > 0:
                wait_all(self.flying[c])
                _, then, arg = self.steps[at - 1]
                if then is not None:
                    then(c, arg)
            if at < len(self.steps):
                send, _, arg = self.steps[at]
                self.flying[c] = send(c, arg)
            self.at[c] += 1

    def drain(self):
        while any(at <= len(self.steps) for at in self.at):
            self.tick(*range(len(self.chunks)))

    def core_send(self, c, _):
        peer = {"b": self.my_b + 1 - 2 * self.core}
        return [
            self.send(item.at[:, 1 - self.core], half, peer)
            for item, half in zip(self.chunks[c], self.halves[c])
        ]

    def core_sum(self, c, _):
        acc, row, n_x = self.accs[c], 0, self.n_x
        for item, half in zip(self.chunks[c], self.halves[c]):
            rows, lanes = item.shape[2:]
            for lane in range(0, lanes, 256):
                cols = slice(lane, lane + 256)
                for j in range(self.n_a * n_x):
                    acc[j // n_x, j % n_x, row : row + rows] = (
                        item[j, self.core, :, cols] + half[j, :, cols]
                    )
                row += rows
        if row < acc.shape[2]:
            for j in range(self.n_a * n_x):
                acc[j // n_x, j % n_x, row:] = jnp.zeros((acc.shape[2] - row, 256), jnp.float32)

    def plane_moves(self, c, stage):
        rows = self.accs[c].shape[2] // 2
        for half in range(2):
            over_x = (half + stage) % 2 == 0
            for off in range(1, self.n_x if over_x else self.n_a):
                buf = (self.one, self.two)[stage][c][half].at[off - 1]
                yield over_x, off, pl.ds(half * rows, rows), buf

    def plane_send(self, c, stage):
        acc, copies = self.accs[c], []
        for over_x, off, rows, buf in self.plane_moves(c, stage):
            if over_x:
                there = lax.rem(self.my_x + off, self.n_x)
                src = acc.at[:, there, rows] if stage == 0 else acc.at[self.my_a, there, rows]
                peer = {"b": 2 * there + self.core}
            else:
                there = lax.rem(self.my_a + off, self.n_a)
                src = acc.at[there, :, rows] if stage == 0 else acc.at[there, self.my_x, rows]
                peer = {"a": there}
            copies.append(self.send(src, buf, peer))
        return copies

    def plane_sum(self, c, stage):
        acc, my_a, my_x = self.accs[c], self.my_a, self.my_x
        for over_x, _, rows, buf in self.plane_moves(c, stage):
            if stage == 1:
                acc[my_a, my_x, rows] += buf[...]
            elif over_x:
                for j in range(self.n_a):
                    acc[j, my_x, rows] += buf[j]
            else:
                for j in range(self.n_x):
                    acc[my_a, j, rows] += buf[j]

    def span(self, c, level):
        length, start = self.accs[c].shape[2], 0
        for bit in range(level):
            length //= 2
            start = start + self.digit(bit) * length
        return start, length

    def s_send(self, c, bit):
        start, length = self.span(c, bit)
        length //= 2
        rows = pl.ds(pl.multiple_of(start + (1 - self.digit(bit)) * length, 8), length)
        source = self.accs[c].at[self.my_a, self.my_x, rows]
        return [self.send(source, self.bit[c].at[bit, pl.ds(0, length)], self.s_peer(bit))]

    def s_sum(self, c, bit):
        start, length = self.span(c, bit + 1)
        rows = pl.ds(pl.multiple_of(start, 8), length)
        total = self.accs[c][self.my_a, self.my_x, rows] + self.bit[c][bit, :length]
        if bit == self.bits - 1:
            self.outs[c][rows] = total
        else:
            self.accs[c][self.my_a, self.my_x, rows] = total

    def up_send(self, c, bit):
        start, length = self.span(c, bit + 1)
        rows = self.outs[c].at[pl.ds(pl.multiple_of(start, 8), length)]
        return [self.send(rows, rows, self.s_peer(bit))]


def square_sum(value):
    return jnp.sum((value * value).reshape(value.shape[0] // 8, 8, 256), axis=0)


def adam(grad, state, outs):
    weight, m_old, v_old = (ref[...] for ref in state)
    m_new = BETA_ONE * m_old + (1.0 - BETA_ONE) * grad
    v_new = BETA_TWO * v_old + (1.0 - BETA_TWO) * grad * grad
    step_dir = (
        m_new / (1.0 - BETA_ONE**STEP) / (jnp.sqrt(v_new / (1.0 - BETA_TWO**STEP)) + ADAM_EPS)
    )
    outs[0][...] = weight - RATE * (step_dir + DECAY * weight)
    outs[1][...] = m_new
    outs[2][...] = v_new


def back_kernel(
    n_a, n_b, n_s, d_heads, base, d_mid, joined, proj_t, skip_t, weight_one, weight_two, wide_one, wide_two,
    table_one, table_two, film, hot, extra, gains, taps,
    g_up, g_out, g_down, g_head, gain_mid, loss, *refs,
):
    n_state = 3 * len(STATES)
    state, refs = refs[:n_state], refs[n_state:]
    new_state, (small_out, norm_out), refs = refs[:n_state], refs[n_state : n_state + 2], refs[n_state + 2 :]
    d_qkv, shifts, wide, held, edge_b, edge_f, sems, red_sems, blocks = refs[:9]
    g_proj, g_two, g_skip, g_film, g_one, g_small = refs[9:15]
    n_chunk = 6
    shards, scratch = refs[15 : 15 + n_chunk], refs[15 + n_chunk :]
    chunks = [[g_down], [g_proj], [g_two], [g_skip, g_film], [g_one], [g_small]]
    reducer = Reducer(n_a, n_b, n_s, chunks, scratch, shards, red_sems)
    n_pix = base.shape[0]
    ring = Ring(n_b, sems)
    greet(reducer.dp_peers() + [reducer.s_peer(bit) for bit in range(reducer.bits)])
    copies = ring.collect(d_heads, d_qkv)
    reducer.tick(0)
    put_rows(g_proj, 3 * C, g_out[...])
    put_rows(g_proj, 4 * C, g_up[...])
    counts = extra.at[pl.ds(8, 8), pl.ds(0, C)]
    cond = extra[:8, : g_film.shape[3]]
    own = slice(FREQ, FREQ + n_pix)
    normed, inv_std = layer_parts(base[...])
    ln_b = low(normed * gains[4:5] + gains[5:6])
    reducer.tick(0)
    wait_all(copies)
    put_rows(g_proj, 0, mxu(d_qkv[...], ln_b))
    reducer.tick(1, 0)
    d_ln = mxu(low(proj_t[: 3 * C].astype(jnp.float32).T), d_qkv[...]).T
    sum_gain = [jnp.sum(d_ln * normed, axis=0, keepdims=True), jnp.sum(d_ln, axis=0, keepdims=True)]
    d_base = d_mid[...] + layer_pull(d_ln, normed, inv_std, gains[4:5])
    put_rows(g_skip, 0, mxu(low(d_base.T), joined[...]))
    d_joined = mxu(low(d_base), skip_t[...])
    d_branch = low(d_joined[:, :C])
    edge_b[0] = d_branch[:FREQ]
    edge_b[1] = d_branch[n_pix - FREQ :]
    copies = ring.edges(edge_b.at[0], edge_b.at[1], edge_b.at[2], edge_b.at[3])
    d_stem = d_joined[:, :C] + d_joined[:, C:]
    reducer.tick(1, 0)

    hot_t, left, right = own_hot(hot, n_pix)
    left_b, right_b = low(left), low(right)
    wide_hot = hot[FREQ : 3 * FREQ + n_pix]
    film_rows = mxu(wide_hot[own], table_parts(film[...]))
    inv_two = mxu(wide_hot, table_parts(table_two[8:]))
    norm_two = (wide_two[...] - mxu(wide_hot, table_parts(table_two[:8]))) * inv_two
    affine = norm_two[own] * gains[2:3] + gains[3:4]
    act = affine * (1.0 + film_rows[:, :C]) + film_rows[:, C:]
    gate = jax.nn.sigmoid(act)
    act_t = low((low(act * gate).astype(jnp.float32)).T)
    wide[own] = d_branch.astype(jnp.float32)
    wait_all(copies)
    wide[:FREQ] = edge_b[2].astype(jnp.float32)
    wide[FREQ + n_pix :] = edge_b[3].astype(jnp.float32)
    row_shifts(wide[...], shifts)
    d_act = conv_pull(shifts, weight_two, act_t, g_two, left_b, right_b, n_pix)
    reducer.tick(2, 1, 0)
    d_act = d_act * (gate + act * gate * (1.0 - gate))
    d_film = jnp.concatenate([high(hot_t, d_act * affine), high(hot_t, d_act)], axis=1)
    clip = lax.broadcasted_iota(jnp.int32, d_film.shape, 0)
    d_film = jnp.where(clip < CLIPS, d_film, 0.0)
    put_rows(g_film, 0, high(d_film.T, cond))
    reducer.tick(3)
    d_act = d_act * (1.0 + film_rows[:, :C])
    sum_two = [
        jnp.sum(d_act * norm_two[own], axis=0, keepdims=True),
        jnp.sum(d_act, axis=0, keepdims=True),
    ]
    scaled = d_act * gains[2:3]
    wide[own] = scaled
    edge_f[0] = scaled[:FREQ]
    edge_f[1] = scaled[n_pix - FREQ :]
    copies = ring.edges(edge_f.at[0], edge_f.at[1], edge_f.at[2], edge_f.at[3])
    copies += ring.sums(clip_sums(hot_t, scaled, scaled * norm_two[own]), held.at[0])
    inv_one = mxu(wide_hot[own], table_parts(table_one[8:]))
    norm_one = (wide_one[own] - mxu(wide_hot[own], table_parts(table_one[:8]))) * inv_one
    act = norm_one * gains[0:1] + gains[1:2]
    gate = jax.nn.sigmoid(act)
    act_t = low((low(act * gate).astype(jnp.float32)).T)
    wait_all(copies)
    reducer.tick(2, 1, 0, 3)
    wide[:FREQ] = edge_f[2]
    wide[FREQ + n_pix :] = edge_f[3]
    mean, slope = group_table(ring.total(held.at[0]), counts[...])
    d_inner = inv_two * (
        wide[...] - mxu(wide_hot, table_parts(mean)) - norm_two * mxu(wide_hot, table_parts(slope))
    )
    row_shifts(low(d_inner).astype(jnp.float32), shifts)
    reducer.tick(2)
    d_act = conv_pull(shifts, weight_one, act_t, g_one, left_b, right_b, n_pix)
    reducer.tick(4, 3, 2, 1, 0)
    d_act = d_act * (gate + act * gate * (1.0 - gate))
    sum_one = [
        jnp.sum(d_act * norm_one, axis=0, keepdims=True),
        jnp.sum(d_act, axis=0, keepdims=True),
    ]
    gain_rows = rows_of(8, sum_one + sum_two + sum_gain)
    scaled = d_act * gains[0:1]
    copies = ring.sums(clip_sums(hot_t, scaled, scaled * norm_one), held.at[1])
    wait_all(copies)
    mean, slope = group_table(ring.total(held.at[1]), counts[...])
    hot_own = wide_hot[own]
    d_stem = d_stem + inv_one * (
        scaled - mxu(hot_own, table_parts(mean)) - norm_one * mxu(hot_own, table_parts(slope))
    )
    n_lane = taps.shape[1]
    d_stem = jnp.concatenate(
        [
            jnp.zeros((PAD, C), jnp.bfloat16),
            low(d_stem),
            jnp.zeros((n_lane - n_pix - PAD, C), jnp.bfloat16),
        ],
        axis=0,
    )
    clip = lax.broadcasted_iota(jnp.int32, (8, C), 0)
    gain_rows = jnp.where(clip < 6, gain_rows, pltpu.roll(gain_mid[...], 6, 0))
    lane = lax.broadcasted_iota(jnp.int32, (8, 256), 1)
    first = (clip == 0) & (lane == 0)
    small = [g_head[...], mxu(taps[...], d_stem), gain_rows, jnp.where(first, loss[0:1, 0:1], 0.0)]
    small = jnp.concatenate(small, axis=0)
    put_rows(g_small, 0, fill(small, 2 * g_small.shape[0] * g_small.shape[2]))
    reducer.tick(5)
    reducer.drain()

    total = jnp.zeros((8, 256), jnp.float32)
    for shard in shards[:-1]:
        total = total + square_sum(shard[...])
    count = g_small.shape[2]
    own_small = shards[-1][:count]
    row = lax.broadcasted_iota(jnp.int32, (count, 256), 0) + reducer.place * count
    total = total + square_sum(jnp.where(row < 168, own_small, 0.0))
    total = jnp.sum(jnp.sum(total, axis=0, keepdims=True), axis=1, keepdims=True)
    blocks[reducer.place, :count] = own_small
    blocks[reducer.place, count:] = jnp.broadcast_to(total, (8, 256))
    here = blocks.at[reducer.place]
    wait_all([reducer.send(here, here, peer) for peer in reducer.dp_peers()])
    total = blocks[0, count:]
    small_out[:count] = blocks[0, :count]
    for place in range(1, reducer.n_d):
        total = total + blocks[place, count:]
        small_out[count * place : count * (place + 1)] = blocks[place, :count]
    norm = jnp.sqrt(total)
    norm_out[...] = norm
    factor = jnp.minimum(1.0, CLIP_NORM / norm)[0:1, 0:1]

    def update(name, grad, part=None):
        first = 3 * STATES.index(name)
        item, new = state[first : first + 3], new_state[first : first + 3]
        if part is not None:
            item, new = ([ref.at[part] for ref in refs] for refs in (item, new))
        adam(grad * factor, item, new)

    conv_height = state[0].shape[1]
    update("conv", shards[4][:conv_height], 0)
    update("conv", shards[2][:conv_height], 1)
    update("proj", shards[1][: g_proj.shape[2]].T)
    update("down", shards[0][: g_down.shape[2]])
    skip_rows, film_rows = g_skip.shape[2], g_film.shape[2]
    for name, start, rows in (("skip", 0, skip_rows), ("film", 2 * skip_rows, film_rows)):
        grads = shards[3][start : start + rows], shards[3][start + rows : start + 2 * rows]
        update(name, jnp.concatenate(grads, axis=1))


def dense(kernel, operands, outs, scratch, collective_id=None):
    vmem = pl.BlockSpec(memory_space=pltpu.VMEM)
    params = dict(vmem_limit_bytes=61 << 20)
    if collective_id is not None:
        params.update(collective_id=collective_id, has_side_effects=True)
    return pl.pallas_call(
        kernel,
        in_specs=[vmem] * len(operands),
        out_specs=[vmem] * len(outs),
        out_shape=[jax.ShapeDtypeStruct(shape, dtype) for shape, dtype in outs],
        scratch_shapes=scratch,
        compiler_params=pltpu.CompilerParams(**params),
    )(*operands)


def body(
    clean_lat,
    noise_lat,
    column_ids,
    timesteps,
    clap_emb,
    conv_w,
    proj_w,
    film_w,
    skip_w,
    down_w,
    stem_w,
    head_w,
    gains,
    conv_m,
    proj_m,
    film_m,
    skip_m,
    down_m,
    stem_m,
    head_m,
    gains_m,
    conv_v,
    proj_v,
    film_v,
    skip_v,
    down_v,
    stem_v,
    head_v,
    gains_v,
):
    bf16, f32 = jnp.bfloat16, jnp.float32
    masters = (conv_w, proj_w, film_w, skip_w, down_w, stem_w, head_w, gains)
    firsts = (conv_m, proj_m, film_m, skip_m, down_m, stem_m, head_m, gains_m)
    seconds = (conv_v, proj_v, film_v, skip_v, down_v, stem_v, head_v, gains_v)
    n_dp, n_s = lax.axis_size(DP), lax.axis_size("s")
    n_a, n_b = lax.axis_size("a"), lax.axis_size("b")
    _, height, n_cols, _ = clean_lat.shape
    n_pix = height * n_cols
    n_lane = frame_of(n_pix)
    proj_cols, down_rows = proj_w.shape[1], down_w.shape[0]
    stem_rows = stem_w.shape[0]

    ids_row = column_ids[0]
    edge_pad = jnp.full((2,), -1, jnp.int32)
    ids_rim = lax.dynamic_slice_in_dim(
        jnp.concatenate([edge_pad, ids_row, edge_pad]), lax.axis_index("s") * n_cols, n_cols + 4
    )
    clip_hot = (ids_rim[:, None] == jnp.arange(CLIPS)[None, :]).astype(f32)
    place = jnp.arange(n_cols + 4)
    inner = (place > 0) & (place < n_cols + 3)
    own = (place > 1) & (place < n_cols + 2)
    same = ids_rim[1:] == ids_rim[:-1]
    off = jnp.zeros((1,), bool)
    cond_vec, alpha_clip, sigma_clip = clip_terms(timesteps[0], clap_emb[0])
    alpha_col = jnp.sum(clip_hot * alpha_clip[None], axis=1)
    sigma_col = jnp.sum(clip_hot * sigma_clip[None], axis=1)
    rows = [
        ids_rim,
        alpha_col,
        sigma_col,
        jnp.sum(clip_hot, axis=1) * inner,
        jnp.concatenate([off, same]),
        jnp.concatenate([same, off]),
        own,
        own,
    ]
    rows = jnp.stack([item.astype(f32) for item in rows])[:, :, None]
    clean, noise = (item[0].transpose(2, 1, 0) for item in (clean_lat, noise_lat))
    alpha, sigma = alpha_col[2:-2][None, :, None], sigma_col[2:-2][None, :, None]
    data = jnp.concatenate([alpha * clean + sigma * noise, alpha * noise - sigma * clean], axis=0)
    first, last = (
        jnp.pad(item, ((0, 0), (before, 128 - before - height)))
        for item, before in ((data[:, 0], PAD), (data[:, n_cols - 1], FREQ))
    )
    main = jnp.concatenate(
        [
            jnp.pad(data, ((0, 0), (2, 2), (0, 0))),
            jnp.broadcast_to(rows, (8, n_cols + 4, height)),
        ],
        axis=0,
    ).reshape(24, -1)
    main = jnp.pad(main, ((0, 0), (0, n_lane - main.shape[1])))
    labels = jnp.arange(8)
    counts = jnp.sum((ids_row[None] == labels[:, None]).astype(f32), axis=1) * (height * C // GROUPS)
    pixel_ids = jnp.repeat(ids_row.astype(f32), height).reshape(8, -1)
    lanes = max(COND, pixel_ids.shape[1])
    extra = [
        jnp.pad(jax.nn.silu(cond_vec).astype(bf16).astype(f32), ((0, 8 - CLIPS), (0, lanes - COND))),
        jnp.broadcast_to(jnp.maximum(counts, 1.0)[:, None], (8, lanes)),
        jnp.pad(pixel_ids, ((0, 0), (0, lanes - pixel_ids.shape[1]))),
    ]
    extra = jnp.concatenate(extra, axis=0)
    own_count = jnp.sum((ids_row < CLIPS).astype(f32)) * (height * CIN)
    front = jnp.concatenate([stem_w, gains], axis=0)
    front = jnp.pad(front, ((0, 128 - front.shape[0]), (0, 0))).T
    head_size = head_w.size
    head_rows = round_up(-(-head_size // 256), 16)
    head_flat = jnp.pad(head_w.reshape(-1), (0, head_rows * 256 - head_size)).reshape(-1, 256)
    shards = [
        front.astype(bf16),
        jnp.full((8, 128), own_count),
        film_w.T.astype(bf16),
        skip_w.T.astype(bf16),
        conv_w[0].astype(bf16),
        conv_w[1].astype(bf16),
        proj_w.T.astype(bf16),
        down_w.astype(bf16),
        head_flat.astype(bf16),
    ]
    n_wide = n_pix + PAD
    n_heads = 3 * C // n_b
    vmem = pltpu.VMEM

    def sems(count):
        return pltpu.SemaphoreType.DMA((2, count))

    moves = [main, extra, first, last]
    outs = dense(
        functools.partial(front_kernel, n_a, n_b),
        [*moves, *shards],
        [(item.shape, item.dtype) for item in moves]
        + [((n_dp * item.shape[0], item.shape[1]), item.dtype) for item in shards]
        + [
            ((n_heads, n_b * n_pix), bf16),
            ((n_pix, 2 * C), bf16),
            ((n_pix, C), f32),
            ((n_wide, C), f32),
            ((16, C), f32),
            ((n_wide, C), f32),
            ((16, C), f32),
            ((8, 2 * C), f32),
            ((n_lane, 128), bf16),
            ((80, n_lane), bf16),
            ((8, n_lane), f32),
            ((8, C), f32),
        ],
        [
            vmem((n_pix, C), f32),
            vmem((n_pix, C), f32),
            vmem((3 * C, n_pix), bf16),
            vmem((3, n_wide, C), bf16),
            vmem((2, n_b, 16, C), f32),
            sems(4 + len(shards) * (n_dp - 1) + 2 * (n_b + 1) + n_b - 1),
        ],
        0,
    )
    main, extra, _, _ = outs[:4]
    _, counts_all, film_t, skip_t, conv_one, conv_two, proj_t, down_b, head_b = outs[4:13]
    heads_x, joined, base_rows, wide_one, table_one, wide_two, table_two, film = outs[13:21]
    hot, taps, target, gain_f = outs[21:]
    pixel_ids = extra[16:, : pixel_ids.shape[1]].reshape(1, -1).astype(jnp.int32)
    head_b = head_b.reshape(n_dp, -1)[:, :head_size]
    head_t = head_b.reshape(9, C, CIN).transpose(0, 2, 1).reshape(9 * CIN, C)
    head_t = jnp.pad(head_t, ((0, 80 - 9 * CIN), (0, 0)))
    out_heads, log_total = attention_forward(heads_x, pixel_ids)
    n_hid = down_b.shape[0]
    d_mid, d_heads, g_up, g_down, g_out, g_head, gain_mid, loss = dense(
        functools.partial(middle_kernel, n_b),
        [out_heads, base_rows, proj_t, down_b, head_t, target, main, gain_f, counts_all],
        [
            ((n_pix, C), f32),
            ((C // n_b, n_b * n_pix), bf16),
            ((n_hid, C), f32),
            ((n_hid, C), f32),
            ((C, C), f32),
            ((80, C), f32),
            ((8, C), f32),
            ((8, 128), f32),
        ],
        [
            vmem((C, n_pix), bf16),
            vmem((n_lane, C), bf16),
            vmem((n_hid, n_pix), bf16),
            vmem((n_hid, n_pix), f32),
            vmem((2, PAD, C), bf16),
            vmem((C, n_pix), bf16),
            sems(2 * n_b),
        ],
        1,
    )
    local_loss, pix_count = loss[0, 0], loss[0, 1]
    d_heads_x = attention_backward(heads_x, log_total, d_heads, out_heads, pixel_ids)
    pairs = n_dp // 2
    proj_rows, skip_rows, film_rows = proj_w.shape[1], skip_w.shape[1], film_w.shape[1]
    small_rows = round_up(-(-176 // n_dp), 8)
    grads = [
        [(pairs, 2, down_rows, C)],
        [(pairs, 2, proj_rows, C)],
        [(pairs, 2, conv_w.shape[1], C)],
        [(pairs, 2, skip_rows, 2 * C), (pairs, 2, film_rows, COND)],
        [(pairs, 2, conv_w.shape[1], C)],
        [(pairs, 2, small_rows, 256)],
    ]
    heights = Reducer.heights(grads, n_s)
    turn = {"film", "skip"}
    state = []
    for name in STATES:
        index = ("conv", "proj", "film", "skip", "down").index(name)
        for group in (masters, firsts, seconds):
            state.append(group[index].T if name in turn else group[index])
    outs = dense(
        functools.partial(back_kernel, n_a, n_b, n_s),
        [
            d_heads_x, base_rows, d_mid, joined, proj_t, skip_t, conv_one, conv_two, wide_one,
            wide_two, table_one, table_two, film, hot, extra, gain_f, taps,
            g_up, g_out, g_down.reshape(grads[0][0]), g_head, gain_mid, loss, *state,
        ],
        [(item.shape, f32) for item in state]
        + [((n_dp * small_rows, 256), f32), ((8, 256), f32)],
        [
            vmem((3 * C, n_pix), bf16),
            vmem((3, n_wide, C), bf16),
            vmem((n_wide, C), f32),
            vmem((2, n_b, 16, C), f32),
            vmem((4, FREQ, C), bf16),
            vmem((4, FREQ, C), f32),
            sems(3 * n_b + 1),
            sems(Reducer.copies(grads, n_a, n_b, n_s) + n_dp - 1),
            vmem((n_dp, small_rows + 8, 256), f32),
        ]
        + [vmem(shape, f32) for parts in grads[1:] for shape in parts]
        + [vmem((rows, 256), f32) for rows in heights]
        + [vmem(shape, f32) for shape in Reducer.scratch(grads, n_a, n_b, n_s)],
        2,
    )
    new_state, (small, norm) = outs[: len(state)], outs[len(state) :]
    new_w, new_m, new_v = {}, {}, {}
    for place, name in enumerate(STATES):
        for kind, group in enumerate((new_w, new_m, new_v)):
            item = new_state[3 * place + kind]
            group[name] = item.T if name in turn else item
    grad_norm, loss_sum = norm[0, 0], small[168, 0]
    factor = jnp.minimum(1.0, CLIP_NORM / grad_norm)
    dp_place = lax.axis_index(DP)
    g_head = small[:72].reshape(9, CIN, C).transpose(0, 2, 1).reshape(9 * C, CIN)
    cols = stem_w.shape[1]
    smalls = {
        "stem": lax.dynamic_slice_in_dim(small[80 : 80 + stem_rows], dp_place * cols, cols, 1),
        "head": lax.dynamic_slice_in_dim(g_head, dp_place * head_w.shape[0], head_w.shape[0], 0),
        "gains": lax.dynamic_slice_in_dim(small[160:168], dp_place * cols, cols, 1),
    }
    for name, index in (("stem", 5), ("head", 6), ("gains", 7)):
        weight, m_old, v_old = masters[index], firsts[index], seconds[index]
        grad_one = smalls[name] * factor
        m_new = BETA_ONE * m_old + (1.0 - BETA_ONE) * grad_one
        v_new = BETA_TWO * v_old + (1.0 - BETA_TWO) * grad_one * grad_one
        step_dir = (
            m_new / (1.0 - BETA_ONE**STEP) / (jnp.sqrt(v_new / (1.0 - BETA_TWO**STEP)) + ADAM_EPS)
        )
        new_w[name] = weight - RATE * (step_dir + DECAY * weight)
        new_m[name], new_v[name] = m_new, v_new
    order = ("conv", "proj", "film", "skip", "down", "stem", "head", "gains")
    return (
        *[new_w[name] for name in order],
        *[new_m[name] for name in order],
        *[new_v[name] for name in order],
        grad_norm,
        loss_sum,
        pix_count,
    )


def solution(mesh):
    n_dp, n_s = mesh.shape["dp"], mesh.shape["section"]
    blocks = jax.sharding.Mesh(mesh.devices.reshape(n_dp // n_s, n_s, n_s), ("a", "b", "s"))
    return jax.shard_map(
        body,
        mesh=blocks,
        in_specs=(
            P(DP, None, "s", None),
            P(DP, None, "s", None),
            P(DP, None),
            P(DP, None),
            P(DP, None, None),
            P(None, DP, None),
            P(None, DP),
            P(None, DP),
            P(None, DP),
            P(DP, None),
            P(None, DP),
            P(DP, None),
            P(None, DP),
            P(None, DP, None),
            P(None, DP),
            P(None, DP),
            P(None, DP),
            P(DP, None),
            P(None, DP),
            P(DP, None),
            P(None, DP),
            P(None, DP, None),
            P(None, DP),
            P(None, DP),
            P(None, DP),
            P(DP, None),
            P(None, DP),
            P(DP, None),
            P(None, DP),
        ),
        out_specs=(
            P(None, DP, None),
            P(None, DP),
            P(None, DP),
            P(None, DP),
            P(DP, None),
            P(None, DP),
            P(DP, None),
            P(None, DP),
            P(None, DP, None),
            P(None, DP),
            P(None, DP),
            P(None, DP),
            P(DP, None),
            P(None, DP),
            P(DP, None),
            P(None, DP),
            P(None, DP, None),
            P(None, DP),
            P(None, DP),
            P(None, DP),
            P(DP, None),
            P(None, DP),
            P(DP, None),
            P(None, DP),
            P(),
            P(),
            P(),
        ),
        check_vma=False,
    )
```

```python
import functools
import math

import jax
import jax.numpy as jnp
from jax import lax
from jax.experimental import pallas as pl
from jax.experimental.pallas import tpu as pltpu
from jax.sharding import PartitionSpec as P

CIN = 8
C = 256
HEADS = 8
HD = 32
COND = 512
GROUPS = 32
CLIPS = 4
STEP = 10


EPS_NORM = 1e-05
CLIP_NORM = 0.02
DP = ("a", "b")
STATES = ("conv", "proj", "film", "skip", "down", "stem", "head", "gains")
GATHERED = ("front", "count", "film", "skip", "conv0", "conv1", "proj", "down", "head")
RATE = 0.04
BETA_ONE = 0.9
BETA_TWO = 0.999
ADAM_EPS = 1e-08
DECAY = 0.1


def matmul(lhs_mat, rhs_mat):
    return jnp.dot(lhs_mat, rhs_mat, preferred_element_type=jnp.float32)


def clip_terms(timesteps, clap_emb):
    half_cond = COND // 2
    frequency = jnp.exp(-math.log(10000.0) * jnp.arange(half_cond, dtype=jnp.float32) / half_cond)
    angles = timesteps.astype(jnp.float32)[:, None] * frequency[None]
    cond_vec = clap_emb + jnp.concatenate([jnp.sin(angles), jnp.cos(angles)], axis=1)
    theta_clip = 0.5 * math.pi * (timesteps.astype(jnp.float32) + 1.0) / 1001.0
    return (cond_vec, jnp.cos(theta_clip), jnp.sin(theta_clip))


BIG = 1e30
LOG2E = 1.4426950408889634
SCALE = HD**-0.5 * LOG2E
VMEM_LIMIT = 56 << 20
NN = (((1,), (0,)), ((), ()))
NT = (((1,), (1,)), ((), ()))


def mxu(lhs_mat, rhs_mat, dims=NN):
    return lax.dot_general(lhs_mat, rhs_mat, dims, preferred_element_type=jnp.float32)


def split_three(value):
    high = value.astype(jnp.bfloat16).astype(jnp.float32)
    rest = value - high
    mid = rest.astype(jnp.bfloat16).astype(jnp.float32)
    return high, mid, rest - mid


def rows_of(height, parts):
    row = lax.broadcasted_iota(jnp.int32, (height, parts[0].shape[1]), 0)
    total = jnp.zeros(row.shape, jnp.float32)
    for place, part in enumerate(parts):
        total = jnp.where(row == place, part, total)
    return total


def clip_rows(ids, hit, miss):
    return [jnp.where(ids == clip, hit, miss) for clip in range(CLIPS + 1)]


def forward_kernel(bq, bk, x_ref, ids_ref, out_ref, lse_ref, keys, values):
    n_pix = x_ref.shape[1]
    step = pl.program_id(1)

    @pl.when(step == 0)
    def _():
        def prepare(part, carry):
            cols = pl.ds(pl.multiple_of(part * 512, 512), 512)
            key = x_ref[HD : 2 * HD, cols].astype(jnp.float32)
            marks = rows_of(32, clip_rows(ids_ref[:, cols], 1.0, 0.0))
            stack = jnp.concatenate([key, key, key, marks], axis=0)
            keys[cols, :] = stack.T.astype(jnp.bfloat16)
            ones = jnp.ones((16, 512), jnp.bfloat16)
            values[:, cols] = jnp.concatenate([x_ref[2 * HD : 3 * HD, cols], ones], axis=0)
            return carry

        lax.fori_loop(0, n_pix // 512, prepare, 0)

    block = pl.ds(pl.multiple_of(step * bq, bq), bq)
    marks = rows_of(32, clip_rows(ids_ref[:, block], 0.0, -BIG))
    query = split_three(x_ref[:HD, block].astype(jnp.float32) * SCALE)
    query = jnp.concatenate([*query, marks], axis=0).astype(jnp.bfloat16)
    acc = jnp.zeros((HD + 16, bq), jnp.float32)
    row_max = jnp.full((1, bq), -jnp.inf, jnp.float32)
    for start in range(0, n_pix, bk):
        scores = mxu(keys[start : start + bk, :], query)
        new_max = jnp.maximum(row_max, jnp.max(scores, axis=0, keepdims=True))
        probs = jnp.exp2(scores - new_max).astype(jnp.bfloat16)
        acc = acc * jnp.exp2(row_max - new_max) + mxu(values[:, start : start + bk], probs)
        row_max = new_max
    total = acc[HD : HD + 1]
    out_ref[...] = (acc[:HD] / total).astype(jnp.bfloat16)
    lse_ref[...] = jnp.broadcast_to(row_max + jnp.log2(total), (8, bq))


def attention_forward(heads_x, pixel_ids, bq=2048, bk=256):
    lanes, n_pix = heads_x.shape
    heads = lanes // (3 * HD)
    bq, bk = min(bq, n_pix), min(bk, n_pix)
    return pl.pallas_call(
        functools.partial(forward_kernel, bq, bk),
        grid=(heads, n_pix // bq),
        in_specs=[
            pl.BlockSpec((3 * HD, n_pix), lambda h, i: (h, 0)),
            pl.BlockSpec((1, n_pix), lambda h, i: (0, 0)),
        ],
        out_specs=[
            pl.BlockSpec((HD, bq), lambda h, i: (h, i)),
            pl.BlockSpec((8, bq), lambda h, i: (h, i)),
        ],
        out_shape=[
            jax.ShapeDtypeStruct((heads * HD, n_pix), jnp.bfloat16),
            jax.ShapeDtypeStruct((heads * 8, n_pix), jnp.float32),
        ],
        scratch_shapes=[
            pltpu.VMEM((n_pix, 128), jnp.bfloat16),
            pltpu.VMEM((HD + 16, n_pix), jnp.bfloat16),
        ],
        compiler_params=pltpu.CompilerParams(vmem_limit_bytes=VMEM_LIMIT),
    )(heads_x, pixel_ids)


def backward_kernel(
    bq, bk, x_ref, ids_ref, do_ref, o_ref, lse_ref, out_ref,
    queries, keys, values, d_outs, d_query, pair_rows,
):
    n_pix = x_ref.shape[1]
    step = pl.program_id(1)

    @pl.when(step == 0)
    def _():
        d_query[...] = jnp.zeros_like(d_query)

        def prepare(part, carry):
            cols = pl.ds(pl.multiple_of(part * 512, 512), 512)
            ids = ids_ref[:, cols]
            one = jnp.ones((1, 512), jnp.float32)
            zero = jnp.zeros((64, 512), jnp.float32)
            key = x_ref[HD : 2 * HD, cols].astype(jnp.float32)
            marks = rows_of(32, clip_rows(ids, 1.0, 0.0) + [one, one, one])
            stack = jnp.concatenate([key, key, key, marks], axis=0)
            keys[cols, :] = stack.T.astype(jnp.bfloat16)
            value = x_ref[2 * HD : 3 * HD, cols].astype(jnp.float32)
            stack = jnp.concatenate([value, rows_of(32, [one, one, one]), zero], axis=0)
            values[cols, :] = stack.T.astype(jnp.bfloat16)
            query = x_ref[:HD, cols].astype(jnp.float32)
            d_out = do_ref[:, cols].astype(jnp.float32)
            marks = rows_of(32, clip_rows(ids, 0.0, -BIG) + list(split_three(-lse_ref[0:1, cols])))
            stack = jnp.concatenate([*split_three(query * SCALE), marks], axis=0)
            queries[:, cols] = stack.astype(jnp.bfloat16)
            delta = jnp.sum(d_out * o_ref[:, cols].astype(jnp.float32), axis=0, keepdims=True)
            stack = jnp.concatenate([d_out, rows_of(32, split_three(-delta))], axis=0)
            d_outs[:, cols] = stack.astype(jnp.bfloat16)
            stack = jnp.concatenate([query, d_out, zero], axis=0).T.astype(jnp.bfloat16)
            pair_rows[cols, :] = stack
            return carry

        lax.fori_loop(0, n_pix // 512, prepare, 0)

    block = pl.ds(pl.multiple_of(step * bk, bk), bk)
    key, value = keys[block, :], values[block, :64]
    key_t = x_ref[HD : 2 * HD, block]
    d_value = jnp.zeros((bk, 128), jnp.float32)
    d_key = jnp.zeros((bk, 128), jnp.float32)
    for start in range(0, n_pix, bq):
        cols = slice(start, start + bq)
        probs = jnp.exp2(mxu(key, queries[:, cols]))
        d_scores = (probs * mxu(value, d_outs[:, cols])).astype(jnp.bfloat16)
        probs = probs.astype(jnp.bfloat16)
        d_value += mxu(probs, pair_rows[cols, :])
        d_key += mxu(d_scores, pair_rows[cols, :])
        d_query[:, cols] += mxu(key_t, d_scores)
    d_key, d_value = d_key.T[:HD], d_value.T[HD : 2 * HD]
    out_ref[HD : 2 * HD, block] = (d_key * (HD**-0.5)).astype(jnp.bfloat16)
    out_ref[2 * HD : 3 * HD, block] = d_value.astype(jnp.bfloat16)

    @pl.when(step == pl.num_programs(1) - 1)
    def _():
        out_ref[:HD, :] = (d_query[...] * (HD**-0.5)).astype(jnp.bfloat16)


def attention_backward(heads_x, log_total, d_heads, out_heads, pixel_ids, bq=1024, bk=1024):
    lanes, n_pix = heads_x.shape
    heads = lanes // (3 * HD)
    bq, bk = min(bq, n_pix), min(bk, n_pix)

    def rows(count):
        return pl.BlockSpec((count, n_pix), lambda h, i: (h, 0))

    return pl.pallas_call(
        functools.partial(backward_kernel, bq, bk),
        grid=(heads, n_pix // bk),
        in_specs=[
            rows(3 * HD),
            pl.BlockSpec((1, n_pix), lambda h, i: (0, 0)),
            rows(HD),
            rows(HD),
            rows(8),
        ],
        out_specs=rows(3 * HD),
        out_shape=jax.ShapeDtypeStruct((lanes, n_pix), jnp.bfloat16),
        scratch_shapes=[
            pltpu.VMEM((128, n_pix), jnp.bfloat16),
            pltpu.VMEM((n_pix, 128), jnp.bfloat16),
            pltpu.VMEM((n_pix, 128), jnp.bfloat16),
            pltpu.VMEM((64, n_pix), jnp.bfloat16),
            pltpu.VMEM((HD, n_pix), jnp.float32),
            pltpu.VMEM((n_pix, 128), jnp.bfloat16),
        ],
        compiler_params=pltpu.CompilerParams(vmem_limit_bytes=VMEM_LIMIT),
    )(heads_x, pixel_ids, d_heads, out_heads, log_total)


MESH = pl.DeviceIdType.MESH


def round_up(count, unit):
    return -(-count // unit) * unit


def greet(peers):
    barrier = pltpu.get_barrier_semaphore()
    for peer in peers:
        pl.semaphore_signal(barrier, inc=1, device_id=peer, device_id_type=MESH)
    pl.semaphore_wait(barrier, len(peers))


def push(src, dst, sems, slot, peer):
    copy = pltpu.make_async_remote_copy(
        src_ref=src,
        dst_ref=dst,
        send_sem=sems.at[0, slot],
        recv_sem=sems.at[1, slot],
        device_id=peer,
        device_id_type=MESH,
    )
    copy.start()
    return copy


FREQ = 16
PAD = 2 * FREQ
HIGH = lax.Precision.HIGHEST


def high(lhs_mat, rhs_mat, dims=NN):
    return lax.dot_general(
        lhs_mat, rhs_mat, dims, precision=HIGH, preferred_element_type=jnp.float32
    )


def low(value):
    return value.astype(jnp.bfloat16)


def frame_of(n_pix):
    return round_up(n_pix + 2 * PAD, 128)


def lane_taps(value, left, right, sign):
    n_lane = value.shape[1]
    freq = lax.broadcasted_iota(jnp.int32, value.shape, 1) & (FREQ - 1)
    parts = []
    for df in (-1, 0, 1):
        for dc in (-1, 0, 1):
            moved = sign * (FREQ * dc + df)
            part = value if moved == 0 else pltpu.roll(value, (-moved) % n_lane, 1)
            if sign * df < 0:
                part = jnp.where(freq > 0, part, 0.0)
            if sign * df > 0:
                part = jnp.where(freq < FREQ - 1, part, 0.0)
            if sign * dc < 0:
                part = part * left
            if sign * dc > 0:
                part = part * right
            parts.append(part)
    return jnp.concatenate(parts, axis=0)


def fill(value, rows):
    return jnp.concatenate(
        [value, jnp.zeros((rows - value.shape[0], value.shape[1]), value.dtype)], axis=0
    )


def silu(x):
    return x * jax.nn.sigmoid(x)


def table_parts(table):
    return low(fill(jnp.concatenate(split_three(table), axis=0), 128))


def group_table(sums, counts):
    size = C // GROUPS
    row = lax.broadcasted_iota(jnp.int32, (C, C), 0) & (C - size)
    col = lax.broadcasted_iota(jnp.int32, (C, C), 1) & (C - size)
    totals = high(sums, (row == col).astype(jnp.float32))
    return totals[:8] / counts, totals[8:] / counts


def clip_sums(hot_t, one, two):
    return jnp.concatenate([high(hot_t, one), high(hot_t, two)], axis=0)


def hot_rows(ids, rows):
    clip = lax.broadcasted_iota(jnp.int32, (rows, ids.shape[1]), 0)
    return ((clip & 7) == ids) & (clip < 24)


def row_shifts(value, keep):
    n_row = value.shape[0]
    freq = lax.broadcasted_iota(jnp.int32, value.shape, 0) & (FREQ - 1)
    keep[0] = low(jnp.where(freq > 0, pltpu.roll(value, 1, 0), 0.0))
    keep[1] = low(value)
    keep[2] = low(jnp.where(freq < FREQ - 1, pltpu.roll(value, n_row - 1, 0), 0.0))


def conv_rows(shifts, weight, left, right, n_pix):
    total = None
    for dc in range(3):
        part = None
        for df in range(3):
            tap = 3 * df + dc
            item = mxu(shifts[df, FREQ * dc : FREQ * dc + n_pix], weight[C * tap : C * (tap + 1)])
            part = item if part is None else part + item
        part = part if dc == 1 else part * (left if dc == 0 else right)
        total = part if total is None else total + part
    return total


def conv_pull(shifts, weight, act_t, grad, left, right, n_pix):
    total = None
    for df in range(3):
        for dc in range(3):
            tap = 3 * df + dc
            at = FREQ * (2 - dc)
            window = shifts[2 - df, at : at + n_pix]
            if dc != 1:
                window = window * (right if dc == 0 else left)
            put_rows(grad, C * tap, mxu(act_t, window))
            item = mxu(window, weight[C * tap : C * (tap + 1)], NT)
            total = item if total is None else total + item
    return total


def layer_parts(x):
    centered = x - jnp.mean(x, axis=1, keepdims=True)
    inv_std = lax.rsqrt(jnp.mean(centered * centered, axis=1, keepdims=True) + EPS_NORM)
    return centered * inv_std, inv_std


def layer_pull(d_out, normed, inv_std, gain):
    scaled = d_out * gain
    return inv_std * (
        scaled
        - jnp.mean(scaled, axis=1, keepdims=True)
        - normed * jnp.mean(scaled * normed, axis=1, keepdims=True)
    )


class Ring:
    def __init__(self, n_b, sems, slots=None):
        self.n_b, self.sems = n_b, sems
        self.me = lax.axis_index("b")
        self.slots = iter(range(sems.shape[1])) if slots is None else slots
        self.places = [lax.rem(self.me + off, n_b) for off in range(1, n_b)]
        self.peers = [{"b": place} for place in self.places]

    def send(self, src, dst, peer):
        return push(src, dst, self.sems, next(self.slots), peer)

    def edges(self, first, last, left, right):
        return [self.send(last, left, self.peers[0]), self.send(first, right, self.peers[-1])]

    def sums(self, mine, held):
        held[self.me] = mine
        place = held.at[self.me]
        return [self.send(place, place, peer) for peer in self.peers]

    def total(self, held):
        total = held[0]
        for place in range(1, self.n_b):
            total = total + held[place]
        return total

    def rows_at(self, ref, place):
        count = ref.shape[0] // self.n_b
        return pl.ds(pl.multiple_of(place * count, 16), count)

    def cols_at(self, ref, place):
        count = ref.shape[1] // self.n_b
        return pl.ds(pl.multiple_of(place * count, 128), count)

    def spread(self, make, buf, out):
        copies = []
        for place, peer in zip(self.places, self.peers):
            rows = self.rows_at(buf, place)
            buf[rows] = make(rows)
            copies.append(self.send(buf.at[rows], out.at[:, self.cols_at(out, self.me)], peer))
        rows = self.rows_at(buf, self.me)
        out[:, self.cols_at(out, self.me)] = make(rows)
        return copies

    def collect(self, src, out):
        copies = []
        for place, peer in zip(self.places, self.peers):
            source = src.at[:, self.cols_at(src, place)]
            copies.append(self.send(source, out.at[self.rows_at(out, self.me)], peer))
        out[self.rows_at(out, self.me)] = src[:, self.cols_at(src, self.me)]
        return copies


def wait_all(copies):
    for copy in copies:
        copy.wait()


def own_hot(hot, n_pix):
    own = hot[PAD : PAD + n_pix].astype(jnp.float32)
    return own.T[:8], own[:, 24:25], own[:, 25:26]


def norm_wide(ring, held, wide, counts, hot, table_out):
    mean, square = group_table(ring.total(held), counts[...])
    inv_std = lax.rsqrt(square - mean * mean + EPS_NORM)
    table_out[:8] = mean
    table_out[8:] = inv_std
    return (wide[...] - mxu(hot, table_parts(mean))) * mxu(hot, table_parts(inv_std))


def front_kernel(n_a, n_b, *refs):
    n_move, n_gather = 4, len(GATHERED)
    refs = list(refs)
    moved_in, shards = refs[:n_move], refs[n_move : n_move + n_gather - 1]
    at_conv = GATHERED.index("conv0")
    both = shards.pop(at_conv)
    shards[at_conv:at_conv] = [both.at[0], both.at[1]]
    refs = refs[n_move + n_gather - 1 :]
    moved, wholes = refs[:n_move], refs[n_move : n_move + n_gather]
    refs = refs[n_move + n_gather :]
    heads_out, joined_out, base_out, wide_one, table_one, wide_two, table_two, film_out = refs[:8]
    hot, taps_out, target_out, gains = refs[8:12]
    stem_buf, inner_buf, qkv_buf, shifts, held, sems = refs[12:]
    main_in, extra_in, first, last = moved_in
    main, extra, left_edge, right_edge = moved
    n_pix, n_lane = base_out.shape[0], main.shape[1]
    my_a, my_b, my_s = lax.axis_index("a"), lax.axis_index("b"), lax.axis_index("s")
    core, my_x = lax.rem(my_b, 2), lax.div(my_b, 2)
    n_x = n_b // 2
    n_d, n_j = n_a * n_b, n_a * n_x
    my_j = my_a * n_x + my_x
    slots = iter(range(sems.shape[1]))
    ring = Ring(n_b, sems, slots)

    def at(b, s):
        return {"b": lax.rem(b + n_b, n_b), "s": lax.rem(s + n_b, n_b)}

    dp_peers = []
    for off in range(1, n_d):
        there = lax.rem(my_a * n_b + my_b + off, n_d)
        dp_peers.append({"a": lax.div(there, n_b), "b": lax.rem(there, n_b)})
    mirrored = my_b != my_s
    shift = jnp.where(mirrored, 0, 1)
    greet(
        dp_peers
        + [at(my_s + 1, my_b), at(my_s - 1, my_b), at(my_s, my_b + 1), at(my_s, my_b - 1)]
        + [at(my_s + shift, my_b + shift)]
    )
    main_slot, extra_slot = next(slots), next(slots)

    @pl.when(mirrored)
    def _():
        push(main_in, main, sems, main_slot, at(my_s, my_b))
        push(extra_in, extra, sems, extra_slot, at(my_s, my_b))

    @pl.when(jnp.logical_not(mirrored))
    def _():
        main[...] = main_in[...]
        extra[...] = extra_in[...]

    copies = [
        push(last, left_edge, sems, next(slots), at(my_s + 1, my_b)),
        push(first, right_edge, sems, next(slots), at(my_s - 1, my_b)),
    ]

    def rows_of_shard(whole, j, of_core):
        count = whole.shape[0] // n_d
        return whole.at[pl.ds(pl.multiple_of((2 * j + of_core) * count, 8), count)]

    sibling = {"b": my_b + 1 - 2 * core}
    near, far = {}, {}
    for name, shard, whole in zip(GATHERED, shards, wholes):
        near[name] = []
        place = rows_of_shard(whole, my_j, core)
        own = shard[...]
        place[...] = (own.T if name == "proj" else own).astype(place.dtype)
        for off in range(1, n_j):
            there = lax.rem(my_j + off, n_j)
            peer = {"a": lax.div(there, n_x), "b": 2 * lax.rem(there, n_x) + core}
            near[name].append(
                push(place, place, sems, next(slots), peer)
            )
        far[name] = [push(place, place, sems, next(slots), sibling)]

    def forward(*names):
        for name in names:
            whole = wholes[GATHERED.index(name)]
            for off, copy in enumerate(near[name]):
                copy.wait()
                rows = rows_of_shard(whole, lax.rem(my_j + n_j - off - 1, n_j), core)
                far[name].append(push(rows, rows, sems, next(slots), sibling))

    def arrived(*names):
        for name in names:
            wait_all(far[name])

    part = dict(zip(GATHERED, wholes))
    forward("front", "count")
    wait_all(copies)

    @pl.when(mirrored)
    def _():
        for source, target, slot in ((main_in, main, main_slot), (extra_in, extra, extra_slot)):
            pltpu.make_async_remote_copy(
                src_ref=source,
                dst_ref=target,
                send_sem=sems.at[0, slot],
                recv_sem=sems.at[1, slot],
                device_id=at(my_s, my_b),
                device_id_type=MESH,
            ).wait()

    end = (PAD + n_pix) // 128 * 128
    main[:16, :128] += left_edge[...]
    main[:16, end : end + 128] += right_edge[...]
    rows = main[16:24]
    ids, left, right = rows[0:1], rows[4:5], rows[5:6]
    target_out[...] = main[8:16]
    taps = lane_taps(low(main[:8]).astype(jnp.float32), left, right, 1)
    taps = fill(taps, 128)
    taps_out[...] = low(taps[:80])
    clip = lax.broadcasted_iota(jnp.int32, (128, n_lane), 0)
    marks = hot_rows(ids.astype(jnp.int32), 128).astype(jnp.float32)
    marks = marks + jnp.where(clip == 24, left, 0.0) + jnp.where(clip == 25, right, 0.0)
    hot[...] = low(marks.T)
    hot_t, left, right = own_hot(hot, n_pix)
    wide_hot = hot[FREQ : 3 * FREQ + n_pix]
    taps = low(taps.T)[PAD : PAD + n_pix]
    arrived("front", "count")
    stem_w = part["front"][...]
    gains[...] = stem_w.astype(jnp.float32).T[72:80]
    stem = mxu(taps, stem_w, NT)
    stem_buf[...] = stem
    counts = extra.at[pl.ds(8, 8), pl.ds(0, C)]

    copies = ring.edges(
        stem_buf.at[pl.ds(0, FREQ)],
        stem_buf.at[pl.ds(n_pix - FREQ, FREQ)],
        wide_one.at[pl.ds(0, FREQ)],
        wide_one.at[pl.ds(n_pix + FREQ, FREQ)],
    )
    copies += ring.sums(clip_sums(hot_t, stem, stem * stem), held.at[0])
    wide_one[FREQ : FREQ + n_pix] = stem
    forward("film", "skip", "conv0")
    wait_all(copies)
    normed = norm_wide(ring, held.at[0], wide_one, counts, wide_hot, table_one)
    row_shifts(low(silu(normed * gains[0:1] + gains[1:2])).astype(jnp.float32), shifts)
    arrived("conv0")
    inner = conv_rows(shifts, part["conv0"], left, right, n_pix)
    inner_buf[...] = inner

    copies = ring.edges(
        inner_buf.at[pl.ds(0, FREQ)],
        inner_buf.at[pl.ds(n_pix - FREQ, FREQ)],
        wide_two.at[pl.ds(0, FREQ)],
        wide_two.at[pl.ds(n_pix + FREQ, FREQ)],
    )
    copies += ring.sums(clip_sums(hot_t, inner, inner * inner), held.at[1])
    wide_two[FREQ : FREQ + n_pix] = inner
    forward("conv1", "proj")
    arrived("film", "skip")
    film = mxu(low(extra[:8, : part["film"].shape[1]]), part["film"][...], NT)
    film_out[...] = film
    film_rows = mxu(wide_hot, table_parts(film))
    wait_all(copies)
    normed = norm_wide(ring, held.at[1], wide_two, counts, wide_hot, table_two)
    act = (normed * gains[2:3] + gains[3:4]) * (1.0 + film_rows[:, :C]) + film_rows[:, C:]
    row_shifts(low(silu(act)).astype(jnp.float32), shifts)
    arrived("conv1")
    branch = conv_rows(shifts, part["conv1"], left, right, n_pix)

    stem = stem_buf[...]
    joined_out[:, :C] = low(stem + branch)
    joined_out[:, C:] = low(stem)
    base = mxu(joined_out[...], part["skip"][...], NT)
    base_out[...] = base
    normed, _ = layer_parts(base)
    normed = low(normed * gains[4:5] + gains[5:6])
    forward("down", "head")
    arrived("proj")
    copies = ring.spread(lambda rows: low(mxu(part["proj"][rows], normed, NT)), qkv_buf, heads_out)
    arrived("down", "head")
    wait_all(copies)


def middle_kernel(
    n_b, heads, base, proj_t, down, head, target, main, gains, counts,
    d_mid_out, d_heads_out, g_up, g_down, g_out, g_head, g_gains, loss_out,
    attended, wide, act_t, pull_t, edge, d_att_buf, sems,
):
    n_pix = base.shape[0]
    n_lane = target.shape[1]
    n_hid = down.shape[0]
    ring = Ring(n_b, sems)
    greet(ring.peers)
    copies = ring.collect(heads, attended)
    rows = main[16:24]
    pix_count = jnp.sum(counts[:, 0:1], axis=0, keepdims=True) * 0.125
    wait_all(copies)
    proj_out, proj_up = proj_t.at[pl.ds(3 * C, C)], proj_t.at[pl.ds(4 * C, n_hid)]
    mid = base[...] + mxu(low(attended[...].astype(jnp.float32).T), proj_out[...], NT)
    normed, inv_std = layer_parts(mid)
    ln_b = low(normed * gains[6:7] + gains[7:8])
    top_t = jnp.zeros((C, n_pix), jnp.float32)
    scale = math.sqrt(2.0 / math.pi)
    for start in range(0, n_hid, 256):
        part = slice(start, start + 256)
        hidden = mxu(proj_up[part], ln_b, NT)
        bend = jnp.tanh(scale * (hidden + 0.044715 * hidden * hidden * hidden))
        gate = 0.5 * (1.0 + bend)
        act = low(hidden * gate)
        act_t[part] = act
        pull_t[part] = gate + 0.5 * hidden * (1.0 - bend * bend) * scale * (
            1.0 + 3.0 * 0.044715 * hidden * hidden
        )
        top_t = top_t + mxu(low(down[part].astype(jnp.float32).T), act)
    top = low(mid + top_t.T)
    wide[PAD : PAD + n_pix] = top
    wide[2 * PAD + n_pix :] = jnp.zeros((n_lane - 2 * PAD - n_pix, C), jnp.bfloat16)
    edge[0] = top[:PAD]
    edge[1] = top[n_pix - PAD :]
    copies = ring.edges(
        edge.at[0], edge.at[1], wide.at[pl.ds(0, PAD)], wide.at[pl.ds(PAD + n_pix, PAD)]
    )
    wait_all(copies)
    left, right, valid, own = rows[4:5], rows[5:6], rows[3:4], rows[6:7]
    products = mxu(head[...], wide[...], NT)
    freq = lax.broadcasted_iota(jnp.int32, (8, n_lane), 1) & (FREQ - 1)
    pred = jnp.zeros((8, n_lane), jnp.float32)
    for df in (-1, 0, 1):
        for dc in (-1, 0, 1):
            tap = 3 * (df + 1) + dc + 1
            moved = FREQ * dc + df
            part = products[8 * tap : 8 * (tap + 1)]
            part = part if moved == 0 else pltpu.roll(part, (-moved) % n_lane, 1)
            if df != 0:
                part = jnp.where(freq > 0 if df < 0 else freq < FREQ - 1, part, 0.0)
            if dc != 0:
                part = part * (left if dc < 0 else right)
            pred = pred + part
    residue = jnp.where(valid > 0.0, pred - target[...], 0.0)
    loss = jnp.sum(own * residue * residue, axis=0, keepdims=True)
    lane = lax.broadcasted_iota(jnp.int32, (8, 128), 1)
    loss_out[...] = jnp.where(lane == 1, pix_count, jnp.sum(loss, axis=1, keepdims=True))
    d_pred = low(2.0 * residue / pix_count).astype(jnp.float32)
    taps = lane_taps(d_pred, left, right, -1) * own
    taps = fill(taps, 128)
    g_head[...] = mxu(low(taps[:80]), wide[...])
    d_top = mxu(low(taps.T)[PAD : PAD + n_pix], fill(head[...], 128))
    d_top_b = low(d_top)
    d_ln_t = jnp.zeros((C, n_pix), jnp.float32)
    for start in range(0, n_hid, 256):
        part = slice(start, start + 256)
        d_hidden = low(mxu(down[part], d_top_b, NT) * pull_t[part])
        g_up[part] = mxu(d_hidden, ln_b)
        g_down[part] = mxu(act_t[part], d_top_b)
        d_ln_t = d_ln_t + mxu(low(proj_up[part].astype(jnp.float32).T), d_hidden)
    d_ln = d_ln_t.T
    g_gains[...] = rows_of(
        8, [jnp.sum(d_ln * normed, axis=0, keepdims=True), jnp.sum(d_ln, axis=0, keepdims=True)]
    )
    d_mid = d_top + layer_pull(d_ln, normed, inv_std, gains[6:7])
    d_mid_out[...] = d_mid
    d_mid_b = low(d_mid)
    g_out[...] = mxu(attended[...], d_mid_b).T
    d_att_buf[...] = low(mxu(low(proj_out[...].astype(jnp.float32).T), d_mid_b, NT))
    wait_all(ring.spread(lambda rows: d_att_buf[rows], d_att_buf, d_heads_out))


def put_rows(ref, start, value):
    height = ref.shape[2]
    at = 0
    while at < value.shape[0]:
        shard, row = divmod(start + at, height)
        count = min(height - row, value.shape[0] - at)
        ref[shard // 2, shard % 2, row : row + count] = value[at : at + count]
        at += count


class Reducer:
    def __init__(self, n_a, n_b, n_s, chunks, scratch, outs, sems):
        self.n_a, self.n_b, self.n_x, self.n_s = n_a, n_b, n_b // 2, n_s
        self.bits = n_s.bit_length() - 1
        self.chunks, self.outs, self.sems = chunks, outs, sems
        self.slots = iter(range(sems.shape[1]))
        scratch = list(scratch)
        self.halves, self.accs, self.one, self.two, self.bit = [], [], [], [], []
        for parts in chunks:
            self.halves.append([scratch.pop(0) for _ in parts])
            self.accs.append(scratch.pop(0))
            self.one.append([scratch.pop(0) for _ in range(2)])
            self.two.append([scratch.pop(0) for _ in range(2)])
            self.bit.append(scratch.pop(0))
        self.my_a, self.my_b, self.my_s = (lax.axis_index(axis) for axis in ("a", "b", "s"))
        self.core, self.my_x = lax.rem(self.my_b, 2), lax.div(self.my_b, 2)
        self.place = self.my_a * n_b + self.my_b
        self.n_d = n_a * n_b
        self.steps = [(self.core_send, self.core_sum, 0)]
        self.steps += [(self.plane_send, self.plane_sum, stage) for stage in range(2)]
        self.steps += [(self.s_send, self.s_sum, bit) for bit in range(self.bits)]
        self.steps += [(self.up_send, None, bit) for bit in reversed(range(self.bits))]
        self.at = [0] * len(chunks)
        self.flying = [None] * len(chunks)

    @staticmethod
    def heights(shapes, n_s):
        return [
            round_up(sum(shape[2] * shape[3] // 256 for shape in parts), 8 * max(n_s, 2))
            for parts in shapes
        ]

    @staticmethod
    def scratch(shapes, n_a, n_b, n_s):
        n_x, bits = n_b // 2, n_s.bit_length() - 1
        result = []
        for parts, rows in zip(shapes, Reducer.heights(shapes, n_s)):
            half = rows // 2
            result += [(shape[0], *shape[2:]) for shape in parts]
            result += [(n_a, n_x, rows, 256)]
            result += [(n_x - 1, n_a, half, 256), (n_a - 1, n_x, half, 256)]
            result += [(n_a - 1, half, 256), (n_x - 1, half, 256)]
            result += [(bits, half, 256)]
        return result

    @staticmethod
    def copies(shapes, n_a, n_b, n_s):
        each = 2 * (n_b // 2 - 1 + n_a - 1 + n_s.bit_length() - 1)
        return sum(len(parts) + each for parts in shapes)

    def send(self, src, dst, peer):
        return push(src, dst, self.sems, next(self.slots), peer)

    def dp_peers(self):
        peers = []
        for off in range(1, self.n_d):
            there = lax.rem(self.place + off, self.n_d)
            peers.append({"a": lax.div(there, self.n_b), "b": lax.rem(there, self.n_b)})
        return peers

    def digit(self, bit):
        return lax.rem(lax.div(self.my_s, 1 << bit), 2)

    def s_peer(self, bit):
        return {"s": self.my_s + (1 << bit) - 2 * (1 << bit) * self.digit(bit)}

    def tick(self, *names):
        for c in names:
            at = self.at[c]
            if at > len(self.steps):
                continue
            if at > 0:
                wait_all(self.flying[c])
                _, then, arg = self.steps[at - 1]
                if then is not None:
                    then(c, arg)
            if at < len(self.steps):
                send, _, arg = self.steps[at]
                self.flying[c] = send(c, arg)
            self.at[c] += 1

    def drain(self):
        while any(at <= len(self.steps) for at in self.at):
            self.tick(*range(len(self.chunks)))

    def core_send(self, c, _):
        peer = {"b": self.my_b + 1 - 2 * self.core}
        return [
            self.send(item.at[:, 1 - self.core], half, peer)
            for item, half in zip(self.chunks[c], self.halves[c])
        ]

    def core_sum(self, c, _):
        acc, row, n_x = self.accs[c], 0, self.n_x
        for item, half in zip(self.chunks[c], self.halves[c]):
            rows, lanes = item.shape[2:]
            for lane in range(0, lanes, 256):
                cols = slice(lane, lane + 256)
                for j in range(self.n_a * n_x):
                    acc[j // n_x, j % n_x, row : row + rows] = (
                        item[j, self.core, :, cols] + half[j, :, cols]
                    )
                row += rows
        if row < acc.shape[2]:
            for j in range(self.n_a * n_x):
                acc[j // n_x, j % n_x, row:] = jnp.zeros((acc.shape[2] - row, 256), jnp.float32)

    def plane_moves(self, c, stage):
        rows = self.accs[c].shape[2] // 2
        for half in range(2):
            over_x = (half + stage) % 2 == 0
            for off in range(1, self.n_x if over_x else self.n_a):
                buf = (self.one, self.two)[stage][c][half].at[off - 1]
                yield over_x, off, pl.ds(half * rows, rows), buf

    def plane_send(self, c, stage):
        acc, copies = self.accs[c], []
        for over_x, off, rows, buf in self.plane_moves(c, stage):
            if over_x:
                there = lax.rem(self.my_x + off, self.n_x)
                src = acc.at[:, there, rows] if stage == 0 else acc.at[self.my_a, there, rows]
                peer = {"b": 2 * there + self.core}
            else:
                there = lax.rem(self.my_a + off, self.n_a)
                src = acc.at[there, :, rows] if stage == 0 else acc.at[there, self.my_x, rows]
                peer = {"a": there}
            copies.append(self.send(src, buf, peer))
        return copies

    def plane_sum(self, c, stage):
        acc, my_a, my_x = self.accs[c], self.my_a, self.my_x
        for over_x, _, rows, buf in self.plane_moves(c, stage):
            if stage == 1:
                acc[my_a, my_x, rows] += buf[...]
            elif over_x:
                for j in range(self.n_a):
                    acc[j, my_x, rows] += buf[j]
            else:
                for j in range(self.n_x):
                    acc[my_a, j, rows] += buf[j]

    def span(self, c, level):
        length, start = self.accs[c].shape[2], 0
        for bit in range(level):
            length //= 2
            start = start + self.digit(bit) * length
        return start, length

    def s_send(self, c, bit):
        start, length = self.span(c, bit)
        length //= 2
        rows = pl.ds(pl.multiple_of(start + (1 - self.digit(bit)) * length, 8), length)
        source = self.accs[c].at[self.my_a, self.my_x, rows]
        return [self.send(source, self.bit[c].at[bit, pl.ds(0, length)], self.s_peer(bit))]

    def s_sum(self, c, bit):
        start, length = self.span(c, bit + 1)
        rows = pl.ds(pl.multiple_of(start, 8), length)
        total = self.accs[c][self.my_a, self.my_x, rows] + self.bit[c][bit, :length]
        if bit == self.bits - 1:
            self.outs[c][rows] = total
        else:
            self.accs[c][self.my_a, self.my_x, rows] = total

    def up_send(self, c, bit):
        start, length = self.span(c, bit + 1)
        rows = self.outs[c].at[pl.ds(pl.multiple_of(start, 8), length)]
        return [self.send(rows, rows, self.s_peer(bit))]


def square_sum(value):
    return jnp.sum((value * value).reshape(value.shape[0] // 8, 8, 256), axis=0)


def adam(grad, state, outs):
    weight, m_old, v_old = (ref[...] for ref in state)
    m_new = BETA_ONE * m_old + (1.0 - BETA_ONE) * grad
    v_new = BETA_TWO * v_old + (1.0 - BETA_TWO) * grad * grad
    step_dir = (
        m_new / (1.0 - BETA_ONE**STEP) / (jnp.sqrt(v_new / (1.0 - BETA_TWO**STEP)) + ADAM_EPS)
    )
    outs[0][...] = weight - RATE * (step_dir + DECAY * weight)
    outs[1][...] = m_new
    outs[2][...] = v_new


def back_kernel(
    n_a, n_b, n_s, d_heads, base, d_mid, joined, proj_t, skip_t, weight_one, weight_two, wide_one, wide_two,
    table_one, table_two, film, hot, extra, gains, taps,
    g_up, g_out, g_down, g_head, gain_mid, loss, *refs,
):
    n_chunk = 6
    shards, (small_out, norm_out) = refs[:n_chunk], refs[n_chunk : n_chunk + 2]
    refs = refs[n_chunk + 2 :]
    d_qkv, shifts, wide, held, edge_b, edge_f, sems, red_sems, blocks = refs[:9]
    g_proj, g_two, g_skip, g_film, g_one, g_small = refs[9:15]
    scratch = refs[15:]
    chunks = [[g_down], [g_proj], [g_two], [g_skip, g_film], [g_one], [g_small]]
    reducer = Reducer(n_a, n_b, n_s, chunks, scratch, shards, red_sems)
    n_pix = base.shape[0]
    ring = Ring(n_b, sems)
    greet(reducer.dp_peers() + [reducer.s_peer(bit) for bit in range(reducer.bits)])
    copies = ring.collect(d_heads, d_qkv)
    reducer.tick(0)
    put_rows(g_proj, 3 * C, g_out[...])
    put_rows(g_proj, 4 * C, g_up[...])
    counts = extra.at[pl.ds(8, 8), pl.ds(0, C)]
    cond = extra[:8, : g_film.shape[3]]
    own = slice(FREQ, FREQ + n_pix)
    normed, inv_std = layer_parts(base[...])
    ln_b = low(normed * gains[4:5] + gains[5:6])
    reducer.tick(0)
    wait_all(copies)
    put_rows(g_proj, 0, mxu(d_qkv[...], ln_b))
    reducer.tick(1, 0)
    d_ln = mxu(low(proj_t[: 3 * C].astype(jnp.float32).T), d_qkv[...]).T
    sum_gain = [jnp.sum(d_ln * normed, axis=0, keepdims=True), jnp.sum(d_ln, axis=0, keepdims=True)]
    d_base = d_mid[...] + layer_pull(d_ln, normed, inv_std, gains[4:5])
    put_rows(g_skip, 0, mxu(low(d_base.T), joined[...]))
    d_joined = mxu(low(d_base), skip_t[...])
    d_branch = low(d_joined[:, :C])
    edge_b[0] = d_branch[:FREQ]
    edge_b[1] = d_branch[n_pix - FREQ :]
    copies = ring.edges(edge_b.at[0], edge_b.at[1], edge_b.at[2], edge_b.at[3])
    d_stem = d_joined[:, :C] + d_joined[:, C:]
    reducer.tick(1, 0)

    hot_t, left, right = own_hot(hot, n_pix)
    left_b, right_b = low(left), low(right)
    wide_hot = hot[FREQ : 3 * FREQ + n_pix]
    film_rows = mxu(wide_hot[own], table_parts(film[...]))
    inv_two = mxu(wide_hot, table_parts(table_two[8:]))
    norm_two = (wide_two[...] - mxu(wide_hot, table_parts(table_two[:8]))) * inv_two
    affine = norm_two[own] * gains[2:3] + gains[3:4]
    act = affine * (1.0 + film_rows[:, :C]) + film_rows[:, C:]
    gate = jax.nn.sigmoid(act)
    act_t = low((low(act * gate).astype(jnp.float32)).T)
    wide[own] = d_branch.astype(jnp.float32)
    wait_all(copies)
    wide[:FREQ] = edge_b[2].astype(jnp.float32)
    wide[FREQ + n_pix :] = edge_b[3].astype(jnp.float32)
    row_shifts(wide[...], shifts)
    d_act = conv_pull(shifts, weight_two, act_t, g_two, left_b, right_b, n_pix)
    reducer.tick(2, 1, 0)
    d_act = d_act * (gate + act * gate * (1.0 - gate))
    d_film = jnp.concatenate([high(hot_t, d_act * affine), high(hot_t, d_act)], axis=1)
    clip = lax.broadcasted_iota(jnp.int32, d_film.shape, 0)
    d_film = jnp.where(clip < CLIPS, d_film, 0.0)
    put_rows(g_film, 0, high(d_film.T, cond))
    reducer.tick(3)
    d_act = d_act * (1.0 + film_rows[:, :C])
    sum_two = [
        jnp.sum(d_act * norm_two[own], axis=0, keepdims=True),
        jnp.sum(d_act, axis=0, keepdims=True),
    ]
    scaled = d_act * gains[2:3]
    wide[own] = scaled
    edge_f[0] = scaled[:FREQ]
    edge_f[1] = scaled[n_pix - FREQ :]
    copies = ring.edges(edge_f.at[0], edge_f.at[1], edge_f.at[2], edge_f.at[3])
    copies += ring.sums(clip_sums(hot_t, scaled, scaled * norm_two[own]), held.at[0])
    inv_one = mxu(wide_hot[own], table_parts(table_one[8:]))
    norm_one = (wide_one[own] - mxu(wide_hot[own], table_parts(table_one[:8]))) * inv_one
    act = norm_one * gains[0:1] + gains[1:2]
    gate = jax.nn.sigmoid(act)
    act_t = low((low(act * gate).astype(jnp.float32)).T)
    wait_all(copies)
    reducer.tick(2, 1, 0, 3)
    wide[:FREQ] = edge_f[2]
    wide[FREQ + n_pix :] = edge_f[3]
    mean, slope = group_table(ring.total(held.at[0]), counts[...])
    d_inner = inv_two * (
        wide[...] - mxu(wide_hot, table_parts(mean)) - norm_two * mxu(wide_hot, table_parts(slope))
    )
    row_shifts(low(d_inner).astype(jnp.float32), shifts)
    reducer.tick(2)
    d_act = conv_pull(shifts, weight_one, act_t, g_one, left_b, right_b, n_pix)
    reducer.tick(4, 3, 2, 1, 0)
    d_act = d_act * (gate + act * gate * (1.0 - gate))
    sum_one = [
        jnp.sum(d_act * norm_one, axis=0, keepdims=True),
        jnp.sum(d_act, axis=0, keepdims=True),
    ]
    gain_rows = rows_of(8, sum_one + sum_two + sum_gain)
    scaled = d_act * gains[0:1]
    copies = ring.sums(clip_sums(hot_t, scaled, scaled * norm_one), held.at[1])
    wait_all(copies)
    mean, slope = group_table(ring.total(held.at[1]), counts[...])
    hot_own = wide_hot[own]
    d_stem = d_stem + inv_one * (
        scaled - mxu(hot_own, table_parts(mean)) - norm_one * mxu(hot_own, table_parts(slope))
    )
    n_lane = taps.shape[1]
    d_stem = jnp.concatenate(
        [
            jnp.zeros((PAD, C), jnp.bfloat16),
            low(d_stem),
            jnp.zeros((n_lane - n_pix - PAD, C), jnp.bfloat16),
        ],
        axis=0,
    )
    clip = lax.broadcasted_iota(jnp.int32, (8, C), 0)
    gain_rows = jnp.where(clip < 6, gain_rows, pltpu.roll(gain_mid[...], 6, 0))
    lane = lax.broadcasted_iota(jnp.int32, (8, 256), 1)
    first = (clip == 0) & (lane == 0)
    small = [g_head[...], mxu(taps[...], d_stem), gain_rows, jnp.where(first, loss[0:1, 0:1], 0.0)]
    small = jnp.concatenate(small, axis=0)
    put_rows(g_small, 0, fill(small, 2 * g_small.shape[0] * g_small.shape[2]))
    reducer.tick(5)
    reducer.drain()

    total = jnp.zeros((8, 256), jnp.float32)
    for shard in shards[:-1]:
        total = total + square_sum(shard[...])
    count = g_small.shape[2]
    own_small = shards[-1][:count]
    row = lax.broadcasted_iota(jnp.int32, (count, 256), 0) + reducer.place * count
    total = total + square_sum(jnp.where(row < 168, own_small, 0.0))
    total = jnp.sum(jnp.sum(total, axis=0, keepdims=True), axis=1, keepdims=True)
    blocks[reducer.place, :count] = own_small
    blocks[reducer.place, count:] = jnp.broadcast_to(total, (8, 256))
    here = blocks.at[reducer.place]
    wait_all([reducer.send(here, here, peer) for peer in reducer.dp_peers()])
    total = blocks[0, count:]
    small_out[:count] = blocks[0, :count]
    for place in range(1, reducer.n_d):
        total = total + blocks[place, count:]
        small_out[count * place : count * (place + 1)] = blocks[place, :count]
    norm_out[...] = jnp.sqrt(total)


def update_kernel(n_b, *refs):
    shards, (small, norm), refs = refs[:5], refs[5:7], refs[7:]
    n_state = 3 * len(STATES)
    state, new_state = refs[:n_state], refs[n_state:]
    place = lax.axis_index("a") * n_b + lax.axis_index("b")
    factor = jnp.minimum(1.0, CLIP_NORM / norm[0:1, 0:1])

    def update(name, grad, part=None):
        first = 3 * STATES.index(name)
        item, new = state[first : first + 3], new_state[first : first + 3]
        if part is not None:
            item, new = [ref.at[part] for ref in item], [ref.at[part] for ref in new]
        adam(grad * factor, item, new)

    def shape(name):
        return state[3 * STATES.index(name)].shape

    def own_lanes(value, count):
        return pltpu.roll(value, (value.shape[1] - place * count) % value.shape[1], 1)[:, :count]

    for part, shard in ((0, shards[4]), (1, shards[2])):
        update("conv", shard[: shape("conv")[1]], part)
    update("proj", shards[1][: shape("proj")[1]].T)
    update("down", shards[0][: shape("down")[0]])
    start = 0
    for name in ("skip", "film"):
        rows = shape(name)[0]
        grads = shards[3][start : start + rows], shards[3][start + rows : start + 2 * rows]
        update(name, jnp.concatenate(grads, axis=1))
        start += 2 * rows
    count = shape("gains")[1]
    update("gains", own_lanes(small[160:168], count))
    stem = jnp.concatenate([small[80:160], jnp.zeros((48, C), jnp.float32)], axis=0)
    stem = own_lanes(stem, count)
    update("stem", stem.T[:, : shape("stem")[1]])
    head = [small[8 * tap : 8 * (tap + 1)] for tap in range(9)]
    update("head", own_lanes(jnp.concatenate(head, axis=1), shape("head")[1]))


def dense(kernel, operands, outs, scratch, collective_id=None):
    vmem = pl.BlockSpec(memory_space=pltpu.VMEM)
    params = dict(vmem_limit_bytes=61 << 20)
    if collective_id is not None:
        params.update(collective_id=collective_id, has_side_effects=True)
    return pl.pallas_call(
        kernel,
        in_specs=[vmem] * len(operands),
        out_specs=[vmem] * len(outs),
        out_shape=[jax.ShapeDtypeStruct(shape, dtype) for shape, dtype in outs],
        scratch_shapes=scratch,
        compiler_params=pltpu.CompilerParams(**params),
    )(*operands)


def body(
    clean_lat,
    noise_lat,
    column_ids,
    timesteps,
    clap_emb,
    conv_w,
    proj_w,
    film_w,
    skip_w,
    down_w,
    stem_w,
    head_w,
    gains,
    conv_m,
    proj_m,
    film_m,
    skip_m,
    down_m,
    stem_m,
    head_m,
    gains_m,
    conv_v,
    proj_v,
    film_v,
    skip_v,
    down_v,
    stem_v,
    head_v,
    gains_v,
):
    bf16, f32 = jnp.bfloat16, jnp.float32
    masters = (conv_w, proj_w, film_w, skip_w, down_w, stem_w, head_w, gains)
    firsts = (conv_m, proj_m, film_m, skip_m, down_m, stem_m, head_m, gains_m)
    seconds = (conv_v, proj_v, film_v, skip_v, down_v, stem_v, head_v, gains_v)
    n_dp, n_s = lax.axis_size(DP), lax.axis_size("s")
    n_a, n_b = lax.axis_size("a"), lax.axis_size("b")
    _, height, n_cols, _ = clean_lat.shape
    n_pix = height * n_cols
    n_lane = frame_of(n_pix)
    proj_cols, down_rows = proj_w.shape[1], down_w.shape[0]
    stem_rows = stem_w.shape[0]

    ids_row = column_ids[0]
    edge_pad = jnp.full((2,), -1, jnp.int32)
    ids_rim = lax.dynamic_slice_in_dim(
        jnp.concatenate([edge_pad, ids_row, edge_pad]), lax.axis_index("s") * n_cols, n_cols + 4
    )
    clip_hot = (ids_rim[:, None] == jnp.arange(CLIPS)[None, :]).astype(f32)
    place = jnp.arange(n_cols + 4)
    inner = (place > 0) & (place < n_cols + 3)
    own = (place > 1) & (place < n_cols + 2)
    same = ids_rim[1:] == ids_rim[:-1]
    off = jnp.zeros((1,), bool)
    cond_vec, alpha_clip, sigma_clip = clip_terms(timesteps[0], clap_emb[0])
    alpha_col = jnp.sum(clip_hot * alpha_clip[None], axis=1)
    sigma_col = jnp.sum(clip_hot * sigma_clip[None], axis=1)
    rows = [
        ids_rim,
        alpha_col,
        sigma_col,
        jnp.sum(clip_hot, axis=1) * inner,
        jnp.concatenate([off, same]),
        jnp.concatenate([same, off]),
        own,
        own,
    ]
    rows = jnp.stack([item.astype(f32) for item in rows])[:, :, None]
    clean, noise = (item[0].transpose(2, 1, 0) for item in (clean_lat, noise_lat))
    alpha, sigma = alpha_col[2:-2][None, :, None], sigma_col[2:-2][None, :, None]
    data = jnp.concatenate([alpha * clean + sigma * noise, alpha * noise - sigma * clean], axis=0)
    first, last = (
        jnp.pad(item, ((0, 0), (before, 128 - before - height)))
        for item, before in ((data[:, 0], PAD), (data[:, n_cols - 1], FREQ))
    )
    main = jnp.concatenate(
        [
            jnp.pad(data, ((0, 0), (2, 2), (0, 0))),
            jnp.broadcast_to(rows, (8, n_cols + 4, height)),
        ],
        axis=0,
    ).reshape(24, -1)
    main = jnp.pad(main, ((0, 0), (0, n_lane - main.shape[1])))
    labels = jnp.arange(8)
    counts = jnp.sum((ids_row[None] == labels[:, None]).astype(f32), axis=1) * (height * C // GROUPS)
    pixel_ids = jnp.repeat(ids_row.astype(f32), height).reshape(8, -1)
    lanes = max(COND, pixel_ids.shape[1])
    extra = [
        jnp.pad(jax.nn.silu(cond_vec).astype(bf16).astype(f32), ((0, 8 - CLIPS), (0, lanes - COND))),
        jnp.broadcast_to(jnp.maximum(counts, 1.0)[:, None], (8, lanes)),
        jnp.pad(pixel_ids, ((0, 0), (0, lanes - pixel_ids.shape[1]))),
    ]
    extra = jnp.concatenate(extra, axis=0)
    own_count = jnp.sum((ids_row < CLIPS).astype(f32)) * (height * CIN)
    front = jnp.concatenate([stem_w, gains], axis=0)
    front = jnp.pad(front, ((0, 128 - front.shape[0]), (0, 0))).T
    head_size = head_w.size
    head_rows = round_up(-(-head_size // 256), 16)
    head_flat = jnp.pad(head_w.reshape(-1), (0, head_rows * 256 - head_size)).reshape(-1, 256)
    shards = [
        front,
        jnp.full((8, 128), own_count),
        film_w.T,
        skip_w.T,
        conv_w,
        proj_w,
        down_w,
        head_flat,
    ]
    wholes = [(rows.shape, bf16) for rows in shards]
    wholes[1] = (shards[1].shape, f32)
    wholes[4:5] = [(conv_w.shape[1:], bf16)] * 2
    wholes[6] = (proj_w.shape[::-1], bf16)
    wholes = [((n_dp * shape[0], shape[1]), dtype) for shape, dtype in wholes]
    n_wide = n_pix + PAD
    n_heads = 3 * C // n_b
    vmem = pltpu.VMEM

    def sems(count):
        return pltpu.SemaphoreType.DMA((2, count))

    moves = [main, extra, first, last]
    outs = dense(
        functools.partial(front_kernel, n_a, n_b),
        [*moves, *shards],
        [(item.shape, item.dtype) for item in moves]
        + wholes
        + [
            ((n_heads, n_b * n_pix), bf16),
            ((n_pix, 2 * C), bf16),
            ((n_pix, C), f32),
            ((n_wide, C), f32),
            ((16, C), f32),
            ((n_wide, C), f32),
            ((16, C), f32),
            ((8, 2 * C), f32),
            ((n_lane, 128), bf16),
            ((80, n_lane), bf16),
            ((8, n_lane), f32),
            ((8, C), f32),
        ],
        [
            vmem((n_pix, C), f32),
            vmem((n_pix, C), f32),
            vmem((3 * C, n_pix), bf16),
            vmem((3, n_wide, C), bf16),
            vmem((2, n_b, 16, C), f32),
            sems(4 + len(wholes) * (n_dp - 1) + 2 * (n_b + 1) + n_b - 1),
        ],
        0,
    )
    main, extra, _, _ = outs[:4]
    _, counts_all, film_t, skip_t, conv_one, conv_two, proj_t, down_b, head_b = outs[4:13]
    heads_x, joined, base_rows, wide_one, table_one, wide_two, table_two, film = outs[13:21]
    hot, taps, target, gain_f = outs[21:]
    pixel_ids = extra[16:, : pixel_ids.shape[1]].reshape(1, -1).astype(jnp.int32)
    head_b = head_b.reshape(n_dp, -1)[:, :head_size]
    head_t = head_b.reshape(9, C, CIN).transpose(0, 2, 1).reshape(9 * CIN, C)
    head_t = jnp.pad(head_t, ((0, 80 - 9 * CIN), (0, 0)))
    out_heads, log_total = attention_forward(heads_x, pixel_ids)
    n_hid = down_b.shape[0]
    d_mid, d_heads, g_up, g_down, g_out, g_head, gain_mid, loss = dense(
        functools.partial(middle_kernel, n_b),
        [out_heads, base_rows, proj_t, down_b, head_t, target, main, gain_f, counts_all],
        [
            ((n_pix, C), f32),
            ((C // n_b, n_b * n_pix), bf16),
            ((n_hid, C), f32),
            ((n_hid, C), f32),
            ((C, C), f32),
            ((80, C), f32),
            ((8, C), f32),
            ((8, 128), f32),
        ],
        [
            vmem((C, n_pix), bf16),
            vmem((n_lane, C), bf16),
            vmem((n_hid, n_pix), bf16),
            vmem((n_hid, n_pix), f32),
            vmem((2, PAD, C), bf16),
            vmem((C, n_pix), bf16),
            sems(2 * n_b),
        ],
        1,
    )
    local_loss, pix_count = loss[0, 0], loss[0, 1]
    d_heads_x = attention_backward(heads_x, log_total, d_heads, out_heads, pixel_ids)
    pairs = n_dp // 2
    proj_rows, skip_rows, film_rows = proj_w.shape[1], skip_w.shape[1], film_w.shape[1]
    small_rows = round_up(-(-176 // n_dp), 8)
    grads = [
        [(pairs, 2, down_rows, C)],
        [(pairs, 2, proj_rows, C)],
        [(pairs, 2, conv_w.shape[1], C)],
        [(pairs, 2, skip_rows, 2 * C), (pairs, 2, film_rows, COND)],
        [(pairs, 2, conv_w.shape[1], C)],
        [(pairs, 2, small_rows, 256)],
    ]
    heights = Reducer.heights(grads, n_s)
    turn = {"film", "skip", "stem", "head"}
    state = []
    for index, name in enumerate(STATES):
        for group in (masters, firsts, seconds):
            state.append(group[index].T if name in turn else group[index])
    outs = dense(
        functools.partial(back_kernel, n_a, n_b, n_s),
        [
            d_heads_x, base_rows, d_mid, joined, proj_t, skip_t, conv_one, conv_two, wide_one,
            wide_two, table_one, table_two, film, hot, extra, gain_f, taps,
            g_up, g_out, g_down.reshape(grads[0][0]), g_head, gain_mid, loss,
        ],
        [((rows, 256), f32) for rows in heights]
        + [((n_dp * small_rows, 256), f32), ((8, 256), f32)],
        [
            vmem((3 * C, n_pix), bf16),
            vmem((3, n_wide, C), bf16),
            vmem((n_wide, C), f32),
            vmem((2, n_b, 16, C), f32),
            vmem((4, FREQ, C), bf16),
            vmem((4, FREQ, C), f32),
            sems(3 * n_b + 1),
            sems(Reducer.copies(grads, n_a, n_b, n_s) + n_dp - 1),
            vmem((n_dp, small_rows + 8, 256), f32),
        ]
        + [vmem(shape, f32) for parts in grads[1:] for shape in parts]
        + [vmem(shape, f32) for shape in Reducer.scratch(grads, n_a, n_b, n_s)],
        2,
    )
    *grad_shards, small, norm = outs
    new_state = dense(
        functools.partial(update_kernel, n_b),
        [*grad_shards[:5], small, norm, *state],
        [(item.shape, f32) for item in state],
        [],
    )
    new_w, new_m, new_v = {}, {}, {}
    for place, name in enumerate(STATES):
        for kind, group in enumerate((new_w, new_m, new_v)):
            item = new_state[3 * place + kind]
            group[name] = item.T if name in turn else item
    grad_norm, loss_sum = norm[0, 0], small[168, 0]
    return (
        *[new_w[name] for name in STATES],
        *[new_m[name] for name in STATES],
        *[new_v[name] for name in STATES],
        grad_norm,
        loss_sum,
        pix_count,
    )


def solution(mesh):
    n_dp, n_s = mesh.shape["dp"], mesh.shape["section"]
    blocks = jax.sharding.Mesh(mesh.devices.reshape(n_dp // n_s, n_s, n_s), ("a", "b", "s"))
    return jax.shard_map(
        body,
        mesh=blocks,
        in_specs=(
            P(DP, None, "s", None),
            P(DP, None, "s", None),
            P(DP, None),
            P(DP, None),
            P(DP, None, None),
            P(None, DP, None),
            P(None, DP),
            P(None, DP),
            P(None, DP),
            P(DP, None),
            P(None, DP),
            P(DP, None),
            P(None, DP),
            P(None, DP, None),
            P(None, DP),
            P(None, DP),
            P(None, DP),
            P(DP, None),
            P(None, DP),
            P(DP, None),
            P(None, DP),
            P(None, DP, None),
            P(None, DP),
            P(None, DP),
            P(None, DP),
            P(DP, None),
            P(None, DP),
            P(DP, None),
            P(None, DP),
        ),
        out_specs=(
            P(None, DP, None),
            P(None, DP),
            P(None, DP),
            P(None, DP),
            P(DP, None),
            P(None, DP),
            P(DP, None),
            P(None, DP),
            P(None, DP, None),
            P(None, DP),
            P(None, DP),
            P(None, DP),
            P(DP, None),
            P(None, DP),
            P(DP, None),
            P(None, DP),
            P(None, DP, None),
            P(None, DP),
            P(None, DP),
            P(None, DP),
            P(DP, None),
            P(None, DP),
            P(DP, None),
            P(None, DP),
            P(),
            P(),
            P(),
        ),
        check_vma=False,
    )
```

```python
import functools
import math

import jax
import jax.numpy as jnp
from jax import lax
from jax.experimental import pallas as pl
from jax.experimental.pallas import tpu as pltpu
from jax.sharding import PartitionSpec as P

CIN = 8
C = 256
HEADS = 8
HD = 32
COND = 512
GROUPS = 32
CLIPS = 4
STEP = 10


EPS_NORM = 1e-05
CLIP_NORM = 0.02
DP = ("a", "b")
STATES = ("conv", "proj", "film", "skip", "down", "stem", "head", "gains")
GATHERED = ("front", "count", "film", "skip", "conv0", "conv1", "proj", "down", "head")
RATE = 0.04
BETA_ONE = 0.9
BETA_TWO = 0.999
ADAM_EPS = 1e-08
DECAY = 0.1


def matmul(lhs_mat, rhs_mat):
    return jnp.dot(lhs_mat, rhs_mat, preferred_element_type=jnp.float32)


def clip_terms(timesteps, clap_emb):
    half_cond = COND // 2
    frequency = jnp.exp(-math.log(10000.0) * jnp.arange(half_cond, dtype=jnp.float32) / half_cond)
    angles = timesteps.astype(jnp.float32)[:, None] * frequency[None]
    cond_vec = clap_emb + jnp.concatenate([jnp.sin(angles), jnp.cos(angles)], axis=1)
    theta_clip = 0.5 * math.pi * (timesteps.astype(jnp.float32) + 1.0) / 1001.0
    return (cond_vec, jnp.cos(theta_clip), jnp.sin(theta_clip))


BIG = 1e30
LOG2E = 1.4426950408889634
SCALE = HD**-0.5 * LOG2E
VMEM_LIMIT = 56 << 20
NN = (((1,), (0,)), ((), ()))
NT = (((1,), (1,)), ((), ()))


def mxu(lhs_mat, rhs_mat, dims=NN):
    return lax.dot_general(lhs_mat, rhs_mat, dims, preferred_element_type=jnp.float32)


def split_three(value):
    high = value.astype(jnp.bfloat16).astype(jnp.float32)
    rest = value - high
    mid = rest.astype(jnp.bfloat16).astype(jnp.float32)
    return high, mid, rest - mid


def rows_of(height, parts):
    row = lax.broadcasted_iota(jnp.int32, (height, parts[0].shape[1]), 0)
    total = jnp.zeros(row.shape, jnp.float32)
    for place, part in enumerate(parts):
        total = jnp.where(row == place, part, total)
    return total


def clip_rows(ids, hit, miss):
    return [jnp.where(ids == clip, hit, miss) for clip in range(CLIPS + 1)]


def forward_kernel(bq, bk, x_ref, ids_ref, out_ref, lse_ref, keys, values):
    n_pix = x_ref.shape[1]
    step = pl.program_id(1)

    @pl.when(step == 0)
    def _():
        def prepare(part, carry):
            cols = pl.ds(pl.multiple_of(part * 512, 512), 512)
            key = x_ref[HD : 2 * HD, cols].astype(jnp.float32)
            marks = rows_of(32, clip_rows(ids_ref[:, cols], 1.0, 0.0))
            stack = jnp.concatenate([key, key, key, marks], axis=0)
            keys[cols, :] = stack.T.astype(jnp.bfloat16)
            ones = jnp.ones((16, 512), jnp.bfloat16)
            values[:, cols] = jnp.concatenate([x_ref[2 * HD : 3 * HD, cols], ones], axis=0)
            return carry

        lax.fori_loop(0, n_pix // 512, prepare, 0)

    block = pl.ds(pl.multiple_of(step * bq, bq), bq)
    marks = rows_of(32, clip_rows(ids_ref[:, block], 0.0, -BIG))
    query = split_three(x_ref[:HD, block].astype(jnp.float32) * SCALE)
    query = jnp.concatenate([*query, marks], axis=0).astype(jnp.bfloat16)
    acc = jnp.zeros((HD + 16, bq), jnp.float32)
    row_max = jnp.full((1, bq), -jnp.inf, jnp.float32)
    for start in range(0, n_pix, bk):
        scores = mxu(keys[start : start + bk, :], query)
        new_max = jnp.maximum(row_max, jnp.max(scores, axis=0, keepdims=True))
        probs = jnp.exp2(scores - new_max).astype(jnp.bfloat16)
        acc = acc * jnp.exp2(row_max - new_max) + mxu(values[:, start : start + bk], probs)
        row_max = new_max
    total = acc[HD : HD + 1]
    out_ref[...] = (acc[:HD] / total).astype(jnp.bfloat16)
    lse_ref[...] = jnp.broadcast_to(row_max + jnp.log2(total), (8, bq))


def attention_forward(heads_x, pixel_ids, bq=2048, bk=256):
    lanes, n_pix = heads_x.shape
    heads = lanes // (3 * HD)
    bq, bk = min(bq, n_pix), min(bk, n_pix)
    return pl.pallas_call(
        functools.partial(forward_kernel, bq, bk),
        grid=(heads, n_pix // bq),
        in_specs=[
            pl.BlockSpec((3 * HD, n_pix), lambda h, i: (h, 0)),
            pl.BlockSpec((1, n_pix), lambda h, i: (0, 0)),
        ],
        out_specs=[
            pl.BlockSpec((HD, bq), lambda h, i: (h, i)),
            pl.BlockSpec((8, bq), lambda h, i: (h, i)),
        ],
        out_shape=[
            jax.ShapeDtypeStruct((heads * HD, n_pix), jnp.bfloat16),
            jax.ShapeDtypeStruct((heads * 8, n_pix), jnp.float32),
        ],
        scratch_shapes=[
            pltpu.VMEM((n_pix, 128), jnp.bfloat16),
            pltpu.VMEM((HD + 16, n_pix), jnp.bfloat16),
        ],
        compiler_params=pltpu.CompilerParams(vmem_limit_bytes=VMEM_LIMIT),
    )(heads_x, pixel_ids)


def backward_kernel(
    bq, bk, x_ref, ids_ref, do_ref, o_ref, lse_ref, out_ref,
    queries, keys, values, d_outs, d_query, pair_rows,
):
    n_pix = x_ref.shape[1]
    step = pl.program_id(1)

    @pl.when(step == 0)
    def _():
        d_query[...] = jnp.zeros_like(d_query)

        def prepare(part, carry):
            cols = pl.ds(pl.multiple_of(part * 512, 512), 512)
            ids = ids_ref[:, cols]
            one = jnp.ones((1, 512), jnp.float32)
            zero = jnp.zeros((64, 512), jnp.float32)
            key = x_ref[HD : 2 * HD, cols].astype(jnp.float32)
            marks = rows_of(32, clip_rows(ids, 1.0, 0.0) + [one, one, one])
            stack = jnp.concatenate([key, key, key, marks], axis=0)
            keys[cols, :] = stack.T.astype(jnp.bfloat16)
            value = x_ref[2 * HD : 3 * HD, cols].astype(jnp.float32)
            stack = jnp.concatenate([value, rows_of(32, [one, one, one]), zero], axis=0)
            values[cols, :] = stack.T.astype(jnp.bfloat16)
            query = x_ref[:HD, cols].astype(jnp.float32)
            d_out = do_ref[:, cols].astype(jnp.float32)
            marks = rows_of(32, clip_rows(ids, 0.0, -BIG) + list(split_three(-lse_ref[0:1, cols])))
            stack = jnp.concatenate([*split_three(query * SCALE), marks], axis=0)
            queries[:, cols] = stack.astype(jnp.bfloat16)
            delta = jnp.sum(d_out * o_ref[:, cols].astype(jnp.float32), axis=0, keepdims=True)
            stack = jnp.concatenate([d_out, rows_of(32, split_three(-delta))], axis=0)
            d_outs[:, cols] = stack.astype(jnp.bfloat16)
            stack = jnp.concatenate([query, d_out, zero], axis=0).T.astype(jnp.bfloat16)
            pair_rows[cols, :] = stack
            return carry

        lax.fori_loop(0, n_pix // 512, prepare, 0)

    block = pl.ds(pl.multiple_of(step * bk, bk), bk)
    key, value = keys[block, :], values[block, :64]
    key_t = x_ref[HD : 2 * HD, block]
    d_value = jnp.zeros((bk, 128), jnp.float32)
    d_key = jnp.zeros((bk, 128), jnp.float32)
    for start in range(0, n_pix, bq):
        cols = slice(start, start + bq)
        probs = jnp.exp2(mxu(key, queries[:, cols]))
        d_scores = (probs * mxu(value, d_outs[:, cols])).astype(jnp.bfloat16)
        probs = probs.astype(jnp.bfloat16)
        d_value += mxu(probs, pair_rows[cols, :])
        d_key += mxu(d_scores, pair_rows[cols, :])
        d_query[:, cols] += mxu(key_t, d_scores)
    d_key, d_value = d_key.T[:HD], d_value.T[HD : 2 * HD]
    out_ref[HD : 2 * HD, block] = (d_key * (HD**-0.5)).astype(jnp.bfloat16)
    out_ref[2 * HD : 3 * HD, block] = d_value.astype(jnp.bfloat16)

    @pl.when(step == pl.num_programs(1) - 1)
    def _():
        out_ref[:HD, :] = (d_query[...] * (HD**-0.5)).astype(jnp.bfloat16)


def attention_backward(heads_x, log_total, d_heads, out_heads, pixel_ids, bq=1024, bk=1024):
    lanes, n_pix = heads_x.shape
    heads = lanes // (3 * HD)
    bq, bk = min(bq, n_pix), min(bk, n_pix)

    def rows(count):
        return pl.BlockSpec((count, n_pix), lambda h, i: (h, 0))

    return pl.pallas_call(
        functools.partial(backward_kernel, bq, bk),
        grid=(heads, n_pix // bk),
        in_specs=[
            rows(3 * HD),
            pl.BlockSpec((1, n_pix), lambda h, i: (0, 0)),
            rows(HD),
            rows(HD),
            rows(8),
        ],
        out_specs=rows(3 * HD),
        out_shape=jax.ShapeDtypeStruct((lanes, n_pix), jnp.bfloat16),
        scratch_shapes=[
            pltpu.VMEM((128, n_pix), jnp.bfloat16),
            pltpu.VMEM((n_pix, 128), jnp.bfloat16),
            pltpu.VMEM((n_pix, 128), jnp.bfloat16),
            pltpu.VMEM((64, n_pix), jnp.bfloat16),
            pltpu.VMEM((HD, n_pix), jnp.float32),
            pltpu.VMEM((n_pix, 128), jnp.bfloat16),
        ],
        compiler_params=pltpu.CompilerParams(vmem_limit_bytes=VMEM_LIMIT),
    )(heads_x, pixel_ids, d_heads, out_heads, log_total)


MESH = pl.DeviceIdType.MESH


def round_up(count, unit):
    return -(-count // unit) * unit


def greet(peers):
    barrier = pltpu.get_barrier_semaphore()
    for peer in peers:
        pl.semaphore_signal(barrier, inc=1, device_id=peer, device_id_type=MESH)
    pl.semaphore_wait(barrier, len(peers))


def push(src, dst, sems, slot, peer):
    copy = pltpu.make_async_remote_copy(
        src_ref=src,
        dst_ref=dst,
        send_sem=sems.at[0, slot],
        recv_sem=sems.at[1, slot],
        device_id=peer,
        device_id_type=MESH,
    )
    copy.start()
    return copy


FREQ = 16
PAD = 2 * FREQ
HIGH = lax.Precision.HIGHEST


def high(lhs_mat, rhs_mat, dims=NN):
    return lax.dot_general(
        lhs_mat, rhs_mat, dims, precision=HIGH, preferred_element_type=jnp.float32
    )


def low(value):
    return value.astype(jnp.bfloat16)


def frame_of(n_pix):
    return round_up(n_pix + 2 * PAD, 128)


def lane_taps(value, left, right, sign):
    n_lane = value.shape[1]
    freq = lax.broadcasted_iota(jnp.int32, value.shape, 1) & (FREQ - 1)
    parts = []
    for df in (-1, 0, 1):
        for dc in (-1, 0, 1):
            moved = sign * (FREQ * dc + df)
            part = value if moved == 0 else pltpu.roll(value, (-moved) % n_lane, 1)
            if sign * df < 0:
                part = jnp.where(freq > 0, part, 0.0)
            if sign * df > 0:
                part = jnp.where(freq < FREQ - 1, part, 0.0)
            if sign * dc < 0:
                part = part * left
            if sign * dc > 0:
                part = part * right
            parts.append(part)
    return jnp.concatenate(parts, axis=0)


def fill(value, rows):
    return jnp.concatenate(
        [value, jnp.zeros((rows - value.shape[0], value.shape[1]), value.dtype)], axis=0
    )


def silu(x):
    return x * jax.nn.sigmoid(x)


def table_parts(table):
    return low(fill(jnp.concatenate(split_three(table), axis=0), 128))


def group_table(sums, counts):
    size = C // GROUPS
    row = lax.broadcasted_iota(jnp.int32, (C, C), 0) & (C - size)
    col = lax.broadcasted_iota(jnp.int32, (C, C), 1) & (C - size)
    totals = high(sums, (row == col).astype(jnp.float32))
    return totals[:8] / counts, totals[8:] / counts


def clip_sums(hot_t, one, two):
    return jnp.concatenate([high(hot_t, one), high(hot_t, two)], axis=0)


def hot_rows(ids, rows):
    clip = lax.broadcasted_iota(jnp.int32, (rows, ids.shape[1]), 0)
    return ((clip & 7) == ids) & (clip < 24)


def row_shifts(value, keep):
    n_row = value.shape[0]
    freq = lax.broadcasted_iota(jnp.int32, value.shape, 0) & (FREQ - 1)
    keep[0] = low(jnp.where(freq > 0, pltpu.roll(value, 1, 0), 0.0))
    keep[1] = low(value)
    keep[2] = low(jnp.where(freq < FREQ - 1, pltpu.roll(value, n_row - 1, 0), 0.0))


def conv_rows(shifts, weight, left, right, n_pix):
    total = None
    for dc in range(3):
        part = None
        for df in range(3):
            tap = 3 * df + dc
            item = mxu(shifts[df, FREQ * dc : FREQ * dc + n_pix], weight[C * tap : C * (tap + 1)])
            part = item if part is None else part + item
        part = part if dc == 1 else part * (left if dc == 0 else right)
        total = part if total is None else total + part
    return total


def pull_windows(shifts, left, right, n_pix):
    for df in range(3):
        for dc in range(3):
            at = FREQ * (2 - dc)
            window = shifts[2 - df, at : at + n_pix]
            yield 3 * df + dc, window if dc == 1 else window * (right if dc == 0 else left)


def conv_weight_pull(shifts, act_t, grad, left, right, n_pix):
    for tap, window in pull_windows(shifts, left, right, n_pix):
        put_rows(grad, C * tap, mxu(act_t, window))


def conv_data_pull(shifts, weight, left, right, n_pix):
    total = None
    for tap, window in pull_windows(shifts, left, right, n_pix):
        item = mxu(window, weight[C * tap : C * (tap + 1)], NT)
        total = item if total is None else total + item
    return total


def layer_parts(x):
    centered = x - jnp.mean(x, axis=1, keepdims=True)
    inv_std = lax.rsqrt(jnp.mean(centered * centered, axis=1, keepdims=True) + EPS_NORM)
    return centered * inv_std, inv_std


def layer_pull(d_out, normed, inv_std, gain):
    scaled = d_out * gain
    return inv_std * (
        scaled
        - jnp.mean(scaled, axis=1, keepdims=True)
        - normed * jnp.mean(scaled * normed, axis=1, keepdims=True)
    )


class Ring:
    def __init__(self, n_b, sems, slots=None):
        self.n_b, self.sems = n_b, sems
        self.me = lax.axis_index("b")
        self.slots = iter(range(sems.shape[1])) if slots is None else slots
        self.places = [lax.rem(self.me + off, n_b) for off in range(1, n_b)]
        self.peers = [{"b": place} for place in self.places]

    def send(self, src, dst, peer):
        return push(src, dst, self.sems, next(self.slots), peer)

    def edges(self, first, last, left, right):
        return [self.send(last, left, self.peers[0]), self.send(first, right, self.peers[-1])]

    def sums(self, mine, held):
        held[self.me] = mine
        place = held.at[self.me]
        return [self.send(place, place, peer) for peer in self.peers]

    def total(self, held):
        total = held[0]
        for place in range(1, self.n_b):
            total = total + held[place]
        return total

    def rows_at(self, ref, place):
        count = ref.shape[0] // self.n_b
        return pl.ds(pl.multiple_of(place * count, 16), count)

    def cols_at(self, ref, place):
        count = ref.shape[1] // self.n_b
        return pl.ds(pl.multiple_of(place * count, 128), count)

    def spread(self, make, buf, out):
        copies = []
        for place, peer in zip(self.places, self.peers):
            rows = self.rows_at(buf, place)
            buf[rows] = make(rows)
            copies.append(self.send(buf.at[rows], out.at[:, self.cols_at(out, self.me)], peer))
        rows = self.rows_at(buf, self.me)
        out[:, self.cols_at(out, self.me)] = make(rows)
        return copies

    def collect(self, src, out):
        copies = []
        for place, peer in zip(self.places, self.peers):
            source = src.at[:, self.cols_at(src, place)]
            copies.append(self.send(source, out.at[self.rows_at(out, self.me)], peer))
        out[self.rows_at(out, self.me)] = src[:, self.cols_at(src, self.me)]
        return copies


def wait_all(copies):
    for copy in copies:
        copy.wait()


def own_hot(hot, n_pix):
    own = hot[PAD : PAD + n_pix].astype(jnp.float32)
    return own.T[:8], own[:, 24:25], own[:, 25:26]


def norm_wide(ring, held, wide, counts, hot, table_out):
    mean, square = group_table(ring.total(held), counts[...])
    inv_std = lax.rsqrt(square - mean * mean + EPS_NORM)
    table_out[:8] = mean
    table_out[8:] = inv_std
    return (wide[...] - mxu(hot, table_parts(mean))) * mxu(hot, table_parts(inv_std))


def front_kernel(n_a, n_b, *refs):
    n_move, n_gather = 2, len(GATHERED)
    refs = list(refs)
    moved_in, shards = refs[:n_move], refs[n_move : n_move + n_gather - 1]
    at_conv = GATHERED.index("conv0")
    both = shards.pop(at_conv)
    shards[at_conv:at_conv] = [both.at[0], both.at[1]]
    refs = refs[n_move + n_gather - 1 :]
    moved, wholes = refs[: n_move + 2], refs[n_move + 2 : n_move + 2 + n_gather]
    refs = refs[n_move + 2 + n_gather :]
    heads_out, joined_out, base_out, wide_one, table_one, wide_two, table_two, film_out = refs[:8]
    hot, taps_out, target_out, gains, pixel_ids = refs[8:13]
    stem_buf, inner_buf, qkv_buf, shifts, held, sems = refs[13:]
    main_in, extra_in = moved_in
    main, extra, left_edge, right_edge = moved
    n_pix, n_lane = base_out.shape[0], main.shape[1]
    my_a, my_b, my_s = lax.axis_index("a"), lax.axis_index("b"), lax.axis_index("s")
    core, my_x = lax.rem(my_b, 2), lax.div(my_b, 2)
    n_x = n_b // 2
    n_d, n_j = n_a * n_b, n_a * n_x
    my_j = my_a * n_x + my_x
    slots = iter(range(sems.shape[1]))
    ring = Ring(n_b, sems, slots)

    def at(b, s):
        return {"b": lax.rem(b + n_b, n_b), "s": lax.rem(s + n_b, n_b)}

    dp_peers = []
    for off in range(1, n_d):
        there = lax.rem(my_a * n_b + my_b + off, n_d)
        dp_peers.append({"a": lax.div(there, n_b), "b": lax.rem(there, n_b)})
    mirrored = my_b != my_s
    shift = jnp.where(mirrored, 0, 1)
    greet(
        dp_peers
        + [at(my_s + 1, my_b), at(my_s - 1, my_b), at(my_s, my_b + 1), at(my_s, my_b - 1)]
        + [at(my_s + shift, my_b + shift)]
    )
    main_slot, extra_slot = next(slots), next(slots)

    @pl.when(mirrored)
    def _():
        push(main_in, main, sems, main_slot, at(my_s, my_b))
        push(extra_in, extra, sems, extra_slot, at(my_s, my_b))

    @pl.when(jnp.logical_not(mirrored))
    def _():
        main[...] = main_in[...]
        extra[...] = extra_in[...]

    end = (PAD + n_pix) // 128 * 128
    first, last = (main_in.at[pl.ds(0, 16), pl.ds(start, 128)] for start in (0, end))
    copies = [
        push(last, left_edge, sems, next(slots), at(my_s + 1, my_b)),
        push(first, right_edge, sems, next(slots), at(my_s - 1, my_b)),
    ]

    def rows_of_shard(whole, j, of_core):
        count = whole.shape[0] // n_d
        return whole.at[pl.ds(pl.multiple_of((2 * j + of_core) * count, 8), count)]

    sibling = {"b": my_b + 1 - 2 * core}
    near, far = {}, {}

    def launch(*names):
        for name in names:
            index = GATHERED.index(name)
            place = rows_of_shard(wholes[index], my_j, core)
            own = shards[index][...]
            place[...] = (own.T if name == "proj" else own).astype(place.dtype)
            near[name] = []
            for off in range(1, n_j):
                there = lax.rem(my_j + off, n_j)
                peer = {"a": lax.div(there, n_x), "b": 2 * lax.rem(there, n_x) + core}
                near[name].append(push(place, place, sems, next(slots), peer))
            far[name] = [push(place, place, sems, next(slots), sibling)]

    def forward(*names):
        for name in names:
            whole = wholes[GATHERED.index(name)]
            for off, copy in enumerate(near[name]):
                copy.wait()
                rows = rows_of_shard(whole, lax.rem(my_j + n_j - off - 1, n_j), core)
                far[name].append(push(rows, rows, sems, next(slots), sibling))

    def arrived(*names):
        for name in names:
            wait_all(far[name])

    part = dict(zip(GATHERED, wholes))
    launch("front", "count", "conv0", "film")
    forward("front", "count")
    wait_all(copies)

    @pl.when(mirrored)
    def _():
        for source, target, slot in ((main_in, main, main_slot), (extra_in, extra, extra_slot)):
            pltpu.make_async_remote_copy(
                src_ref=source,
                dst_ref=target,
                send_sem=sems.at[0, slot],
                recv_sem=sems.at[1, slot],
                device_id=at(my_s, my_b),
                device_id_type=MESH,
            ).wait()

    lane = lax.broadcasted_iota(jnp.int32, (16, 128), 1)
    is_left, is_right = (lane >= FREQ) & (lane < PAD), (lane >= PAD) & (lane < PAD + FREQ)
    main[:16, :128] = jnp.where(is_left, left_edge[...], main[:16, :128])
    main[:16, end : end + 128] = jnp.where(is_right, right_edge[...], main[:16, end : end + 128])
    rows = main[16:24]
    ids, left, right = rows[0:1], rows[4:5], rows[5:6]
    target_out[...] = main[8:16]
    n_id = pixel_ids.shape[1] // 8
    for row in range(8):
        line = extra[16 + row : 17 + row, :n_id]
        pixel_ids[:, n_id * row : n_id * (row + 1)] = line.astype(jnp.int32)
    taps = lane_taps(low(main[:8]).astype(jnp.float32), left, right, 1)
    taps = fill(taps, 128)
    taps_out[...] = low(taps[:80])
    clip = lax.broadcasted_iota(jnp.int32, (128, n_lane), 0)
    marks = hot_rows(ids.astype(jnp.int32), 128).astype(jnp.float32)
    marks = marks + jnp.where(clip == 24, left, 0.0) + jnp.where(clip == 25, right, 0.0)
    hot[...] = low(marks.T)
    hot_t, left, right = own_hot(hot, n_pix)
    wide_hot = hot[FREQ : 3 * FREQ + n_pix]
    taps = low(taps.T)[PAD : PAD + n_pix]
    arrived("front", "count")
    stem_w = part["front"][...]
    gains[...] = stem_w.astype(jnp.float32).T[72:80]
    stem = mxu(taps, stem_w, NT)
    stem_buf[...] = stem
    counts = extra.at[pl.ds(8, 8), pl.ds(0, C)]

    copies = ring.edges(
        stem_buf.at[pl.ds(0, FREQ)],
        stem_buf.at[pl.ds(n_pix - FREQ, FREQ)],
        wide_one.at[pl.ds(0, FREQ)],
        wide_one.at[pl.ds(n_pix + FREQ, FREQ)],
    )
    copies += ring.sums(clip_sums(hot_t, stem, stem * stem), held.at[0])
    wide_one[FREQ : FREQ + n_pix] = stem
    forward("conv0", "film")
    wait_all(copies)
    launch("conv1", "skip")
    normed = norm_wide(ring, held.at[0], wide_one, counts, wide_hot, table_one)
    row_shifts(low(silu(normed * gains[0:1] + gains[1:2])).astype(jnp.float32), shifts)
    arrived("conv0")
    inner = conv_rows(shifts, part["conv0"], left, right, n_pix)
    inner_buf[...] = inner

    copies = ring.edges(
        inner_buf.at[pl.ds(0, FREQ)],
        inner_buf.at[pl.ds(n_pix - FREQ, FREQ)],
        wide_two.at[pl.ds(0, FREQ)],
        wide_two.at[pl.ds(n_pix + FREQ, FREQ)],
    )
    copies += ring.sums(clip_sums(hot_t, inner, inner * inner), held.at[1])
    wide_two[FREQ : FREQ + n_pix] = inner
    forward("conv1", "skip")
    arrived("film")
    film = mxu(low(extra[:8, : part["film"].shape[1]]), part["film"][...], NT)
    film_out[...] = film
    film_rows = mxu(wide_hot, table_parts(film))
    wait_all(copies)
    launch("proj", "down", "head")
    normed = norm_wide(ring, held.at[1], wide_two, counts, wide_hot, table_two)
    act = (normed * gains[2:3] + gains[3:4]) * (1.0 + film_rows[:, :C]) + film_rows[:, C:]
    row_shifts(low(silu(act)).astype(jnp.float32), shifts)
    arrived("conv1", "skip")
    branch = conv_rows(shifts, part["conv1"], left, right, n_pix)

    forward("proj")
    stem = stem_buf[...]
    joined_out[:, :C] = low(stem + branch)
    joined_out[:, C:] = low(stem)
    base = mxu(joined_out[...], part["skip"][...], NT)
    base_out[...] = base
    normed, _ = layer_parts(base)
    normed = low(normed * gains[4:5] + gains[5:6])
    arrived("proj")
    forward("down", "head")
    copies = ring.spread(lambda rows: low(mxu(part["proj"][rows], normed, NT)), qkv_buf, heads_out)
    arrived("down", "head")
    wait_all(copies)


def middle_kernel(
    n_b, heads, base, proj_t, down, head, target, main, gains, counts,
    d_mid_out, d_heads_out, g_up, g_down, g_out, g_head, g_gains, loss_out,
    attended, wide, act_t, pull_t, edge, d_att_buf, sems,
):
    n_pix = base.shape[0]
    n_lane = target.shape[1]
    n_hid = down.shape[0]
    ring = Ring(n_b, sems)
    greet(ring.peers)
    copies = ring.collect(heads, attended)
    rows = main[16:24]
    pix_count = jnp.sum(counts[:, 0:1], axis=0, keepdims=True) * 0.125
    wait_all(copies)
    proj_out, proj_up = proj_t.at[pl.ds(3 * C, C)], proj_t.at[pl.ds(4 * C, n_hid)]
    mid = base[...] + mxu(low(attended[...].astype(jnp.float32).T), proj_out[...], NT)
    normed, inv_std = layer_parts(mid)
    ln_b = low(normed * gains[6:7] + gains[7:8])
    top_t = jnp.zeros((C, n_pix), jnp.float32)
    scale = math.sqrt(2.0 / math.pi)
    for start in range(0, n_hid, 256):
        part = slice(start, start + 256)
        hidden = mxu(proj_up[part], ln_b, NT)
        bend = jnp.tanh(scale * (hidden + 0.044715 * hidden * hidden * hidden))
        gate = 0.5 * (1.0 + bend)
        act = low(hidden * gate)
        act_t[part] = act
        pull_t[part] = gate + 0.5 * hidden * (1.0 - bend * bend) * scale * (
            1.0 + 3.0 * 0.044715 * hidden * hidden
        )
        top_t = top_t + mxu(low(down[part].astype(jnp.float32).T), act)
    top = low(mid + top_t.T)
    wide[PAD : PAD + n_pix] = top
    wide[2 * PAD + n_pix :] = jnp.zeros((n_lane - 2 * PAD - n_pix, C), jnp.bfloat16)
    edge[0] = top[:PAD]
    edge[1] = top[n_pix - PAD :]
    copies = ring.edges(
        edge.at[0], edge.at[1], wide.at[pl.ds(0, PAD)], wide.at[pl.ds(PAD + n_pix, PAD)]
    )
    wait_all(copies)
    left, right, valid, own = rows[4:5], rows[5:6], rows[3:4], rows[6:7]
    products = mxu(head[...], wide[...], NT)
    freq = lax.broadcasted_iota(jnp.int32, (8, n_lane), 1) & (FREQ - 1)
    pred = jnp.zeros((8, n_lane), jnp.float32)
    for df in (-1, 0, 1):
        for dc in (-1, 0, 1):
            tap = 3 * (df + 1) + dc + 1
            moved = FREQ * dc + df
            part = products[8 * tap : 8 * (tap + 1)]
            part = part if moved == 0 else pltpu.roll(part, (-moved) % n_lane, 1)
            if df != 0:
                part = jnp.where(freq > 0 if df < 0 else freq < FREQ - 1, part, 0.0)
            if dc != 0:
                part = part * (left if dc < 0 else right)
            pred = pred + part
    residue = jnp.where(valid > 0.0, pred - target[...], 0.0)
    loss = jnp.sum(own * residue * residue, axis=0, keepdims=True)
    lane = lax.broadcasted_iota(jnp.int32, (8, 128), 1)
    loss_out[...] = jnp.where(lane == 1, pix_count, jnp.sum(loss, axis=1, keepdims=True))
    d_pred = low(2.0 * residue / pix_count).astype(jnp.float32)
    taps = lane_taps(d_pred, left, right, -1) * own
    taps = fill(taps, 128)
    g_head[...] = mxu(low(taps[:80]), wide[...])
    d_top = mxu(low(taps.T)[PAD : PAD + n_pix], fill(head[...], 128))
    d_top_b = low(d_top)
    d_ln_t = jnp.zeros((C, n_pix), jnp.float32)
    for start in range(0, n_hid, 256):
        part = slice(start, start + 256)
        d_hidden = low(mxu(down[part], d_top_b, NT) * pull_t[part])
        g_up[part] = mxu(d_hidden, ln_b)
        g_down[part] = mxu(act_t[part], d_top_b)
        d_ln_t = d_ln_t + mxu(low(proj_up[part].astype(jnp.float32).T), d_hidden)
    d_ln = d_ln_t.T
    g_gains[...] = rows_of(
        8, [jnp.sum(d_ln * normed, axis=0, keepdims=True), jnp.sum(d_ln, axis=0, keepdims=True)]
    )
    d_mid = d_top + layer_pull(d_ln, normed, inv_std, gains[6:7])
    d_mid_out[...] = d_mid
    d_mid_b = low(d_mid)
    g_out[...] = mxu(attended[...], d_mid_b).T
    d_att_buf[...] = low(mxu(low(proj_out[...].astype(jnp.float32).T), d_mid_b, NT))
    wait_all(ring.spread(lambda rows: d_att_buf[rows], d_att_buf, d_heads_out))


def put_rows(ref, start, value):
    height = ref.shape[2]
    at = 0
    while at < value.shape[0]:
        shard, row = divmod(start + at, height)
        count = min(height - row, value.shape[0] - at)
        ref[shard // 2, shard % 2, row : row + count] = value[at : at + count]
        at += count


class Reducer:
    def __init__(self, n_a, n_b, n_s, chunks, scratch, outs, sems):
        self.n_a, self.n_b, self.n_x, self.n_s = n_a, n_b, n_b // 2, n_s
        self.bits = n_s.bit_length() - 1
        self.chunks, self.outs, self.sems = chunks, outs, sems
        self.slots = iter(range(sems.shape[1]))
        scratch = list(scratch)
        self.halves, self.accs, self.one, self.two, self.bit, self.halved = [], [], [], [], [], []
        for parts in chunks:
            self.halves.append([scratch.pop(0) for _ in parts])
            self.accs.append(scratch.pop(0))
            self.one.append([scratch.pop(0) for _ in range(2)])
            self.two.append([scratch.pop(0) for _ in range(2)])
            self.bit.append(scratch[0])
            self.halved.append(scratch.pop(0))
        self.my_a, self.my_b, self.my_s = (lax.axis_index(axis) for axis in ("a", "b", "s"))
        self.core, self.my_x = lax.rem(self.my_b, 2), lax.div(self.my_b, 2)
        self.place = self.my_a * n_b + self.my_b
        self.n_d = n_a * n_b
        plane = [(self.core_send, self.core_sum, 0)]
        plane += [(self.plane_send, self.plane_sum, stage) for stage in range(2)]
        halving = [(self.bit_send, self.bit_sum, bit) for bit in range(self.bits)]
        halving += [(self.bit_up, None, bit) for bit in reversed(range(self.bits))]
        direct = [(self.s_send, self.s_sum, 0), (self.up_send, None, 0)]
        self.steps = [plane + halving for _ in chunks[1:]] + [plane + direct]
        self.at = [0] * len(chunks)
        self.flying = [None] * len(chunks)

    @staticmethod
    def heights(shapes, n_s):
        return [
            round_up(sum(shape[2] * shape[3] // 256 for shape in parts), 8 * max(n_s, 2))
            for parts in shapes
        ]

    @staticmethod
    def scratch(shapes, n_a, n_b, n_s):
        n_x = n_b // 2
        result = []
        for parts, rows in zip(shapes, Reducer.heights(shapes, n_s)):
            half = rows // 2
            result += [(shape[0], *shape[2:]) for shape in parts]
            result += [(n_a, n_x, rows, 256)]
            result += [(n_x - 1, n_a, half, 256), (n_a - 1, n_x, half, 256)]
            result += [(n_a - 1, half, 256), (n_x - 1, half, 256)]
            if parts is shapes[-1]:
                result += [(n_s - 1, rows // n_s, 256)]
            else:
                result += [(n_s.bit_length() - 1, half, 256)]
        return result

    @staticmethod
    def copies(shapes, n_a, n_b, n_s):
        each = 2 * (n_b // 2 - 1 + n_a - 1 + n_s - 1)
        return sum(len(parts) + each for parts in shapes)

    def send(self, src, dst, peer):
        return push(src, dst, self.sems, next(self.slots), peer)

    def dp_peers(self):
        peers = []
        for off in range(1, self.n_d):
            there = lax.rem(self.place + off, self.n_d)
            peers.append({"a": lax.div(there, self.n_b), "b": lax.rem(there, self.n_b)})
        return peers

    def s_place(self, off):
        return lax.rem(self.my_s + off, self.n_s)

    def s_peers(self):
        return [{"s": self.s_place(off)} for off in range(1, self.n_s)]

    def spread_small(self, grads, held):
        copies = []
        for slot, peer in enumerate(self.dp_peers()):
            there = lax.rem(self.place + slot + 1, self.n_d)
            source = grads.at[lax.div(there, 2), lax.rem(there, 2)]
            copies.append(self.send(source, held.at[slot], peer))
        return copies

    def tick(self, *names):
        for c in names:
            at = self.at[c]
            if at > len(self.steps[c]):
                continue
            if at > 0:
                wait_all(self.flying[c])
                _, then, arg = self.steps[c][at - 1]
                if then is not None:
                    then(c, arg)
            if at < len(self.steps[c]):
                send, _, arg = self.steps[c][at]
                self.flying[c] = send(c, arg)
            self.at[c] += 1

    def drain(self):
        while any(at <= len(steps) for at, steps in zip(self.at, self.steps)):
            self.tick(*reversed(range(len(self.chunks))))

    def core_send(self, c, _):
        peer = {"b": self.my_b + 1 - 2 * self.core}
        return [
            self.send(item.at[:, 1 - self.core], half, peer)
            for item, half in zip(self.chunks[c], self.halves[c])
        ]

    def core_sum(self, c, _):
        acc, row, n_x = self.accs[c], 0, self.n_x
        for item, half in zip(self.chunks[c], self.halves[c]):
            rows, lanes = item.shape[2:]
            for lane in range(0, lanes, 256):
                cols = slice(lane, lane + 256)
                for j in range(self.n_a * n_x):
                    acc[j // n_x, j % n_x, row : row + rows] = (
                        item[j, self.core, :, cols] + half[j, :, cols]
                    )
                row += rows
        if row < acc.shape[2]:
            for j in range(self.n_a * n_x):
                acc[j // n_x, j % n_x, row:] = jnp.zeros((acc.shape[2] - row, 256), jnp.float32)

    def plane_moves(self, c, stage):
        rows = self.accs[c].shape[2] // 2
        for half in range(2):
            over_x = (half + stage) % 2 == 0
            for off in range(1, self.n_x if over_x else self.n_a):
                buf = (self.one, self.two)[stage][c][half].at[off - 1]
                yield over_x, off, pl.ds(half * rows, rows), buf

    def plane_send(self, c, stage):
        acc, copies = self.accs[c], []
        for over_x, off, rows, buf in self.plane_moves(c, stage):
            if over_x:
                there = lax.rem(self.my_x + off, self.n_x)
                src = acc.at[:, there, rows] if stage == 0 else acc.at[self.my_a, there, rows]
                peer = {"b": 2 * there + self.core}
            else:
                there = lax.rem(self.my_a + off, self.n_a)
                src = acc.at[there, :, rows] if stage == 0 else acc.at[there, self.my_x, rows]
                peer = {"a": there}
            copies.append(self.send(src, buf, peer))
        return copies

    def plane_sum(self, c, stage):
        acc, my_a, my_x = self.accs[c], self.my_a, self.my_x
        for over_x, _, rows, buf in self.plane_moves(c, stage):
            if stage == 1:
                acc[my_a, my_x, rows] += buf[...]
            elif over_x:
                for j in range(self.n_a):
                    acc[j, my_x, rows] += buf[j]
            else:
                for j in range(self.n_x):
                    acc[my_a, j, rows] += buf[j]

    def digit(self, bit):
        return lax.rem(lax.div(self.my_s, 1 << bit), 2)

    def bit_peer(self, bit):
        return {"s": self.my_s + (1 << bit) - 2 * (1 << bit) * self.digit(bit)}

    def span(self, c, level):
        length, start = self.accs[c].shape[2], 0
        for bit in range(level):
            length //= 2
            start = start + self.digit(bit) * length
        return start, length

    def bit_send(self, c, bit):
        start, length = self.span(c, bit)
        length //= 2
        rows = pl.ds(pl.multiple_of(start + (1 - self.digit(bit)) * length, 8), length)
        source = self.accs[c].at[self.my_a, self.my_x, rows]
        return [self.send(source, self.halved[c].at[bit, pl.ds(0, length)], self.bit_peer(bit))]

    def bit_sum(self, c, bit):
        start, length = self.span(c, bit + 1)
        rows = pl.ds(pl.multiple_of(start, 8), length)
        total = self.accs[c][self.my_a, self.my_x, rows] + self.halved[c][bit, :length]
        if bit == self.bits - 1:
            self.outs[c][rows] = total
        else:
            self.accs[c][self.my_a, self.my_x, rows] = total

    def bit_up(self, c, bit):
        start, length = self.span(c, bit + 1)
        rows = self.outs[c].at[pl.ds(pl.multiple_of(start, 8), length)]
        return [self.send(rows, rows, self.bit_peer(bit))]

    def piece(self, c, place):
        length = self.accs[c].shape[2] // self.n_s
        return pl.ds(pl.multiple_of(place * length, 8), length)

    def s_send(self, c, _):
        mine = self.accs[c].at[self.my_a, self.my_x]
        return [
            self.send(mine.at[self.piece(c, self.s_place(slot + 1))], self.bit[c].at[slot], peer)
            for slot, peer in enumerate(self.s_peers())
        ]

    def s_sum(self, c, _):
        rows = self.piece(c, self.my_s)
        total = self.accs[c][self.my_a, self.my_x, rows]
        for slot in range(self.n_s - 1):
            total = total + self.bit[c][slot]
        self.outs[c][rows] = total

    def up_send(self, c, _):
        rows = self.outs[c].at[self.piece(c, self.my_s)]
        return [self.send(rows, rows, peer) for peer in self.s_peers()]


def square_sum(value):
    return jnp.sum((value * value).reshape(value.shape[0] // 8, 8, 256), axis=0)


def adam(grad, state, outs):
    weight, m_old, v_old = (ref[...] for ref in state)
    m_new = BETA_ONE * m_old + (1.0 - BETA_ONE) * grad
    v_new = BETA_TWO * v_old + (1.0 - BETA_TWO) * grad * grad
    step_dir = (
        m_new / (1.0 - BETA_ONE**STEP) / (jnp.sqrt(v_new / (1.0 - BETA_TWO**STEP)) + ADAM_EPS)
    )
    outs[0][...] = weight - RATE * (step_dir + DECAY * weight)
    outs[1][...] = m_new
    outs[2][...] = v_new


def back_kernel(
    n_a, n_b, n_s, d_heads, base, d_mid, joined, proj_t, skip_t, weight_one, weight_two, wide_one, wide_two,
    table_one, table_two, film, hot, extra, gains, taps,
    g_up, g_out, g_down, g_head, gain_mid, loss, *refs,
):
    n_chunk = 5
    shards, (small_out, norm_out) = refs[:n_chunk], refs[n_chunk : n_chunk + 2]
    refs = refs[n_chunk + 2 :]
    d_qkv, shifts, wide, held, edge_b, edge_f, sems, red_sems, blocks = refs[:9]
    g_proj, g_two, g_skip, g_film, g_one, g_small, small_in, small_z = refs[9:17]
    scratch = refs[17:]
    chunks = [[g_down], [g_proj], [g_two], [g_skip, g_film], [g_one]]
    reducer = Reducer(n_a, n_b, n_s, chunks, scratch, shards, red_sems)
    n_pix = base.shape[0]
    ring = Ring(n_b, sems)
    greet(reducer.dp_peers() + reducer.s_peers())
    copies = ring.collect(d_heads, d_qkv)
    reducer.tick(0)
    put_rows(g_proj, 3 * C, g_out[...])
    put_rows(g_proj, 4 * C, g_up[...])
    counts = extra.at[pl.ds(8, 8), pl.ds(0, C)]
    cond = extra[:8, : g_film.shape[3]]
    own = slice(FREQ, FREQ + n_pix)
    normed, inv_std = layer_parts(base[...])
    ln_b = low(normed * gains[4:5] + gains[5:6])
    wait_all(copies)
    put_rows(g_proj, 0, mxu(d_qkv[...], ln_b))
    reducer.tick(1, 0)
    d_ln = mxu(low(proj_t[: 3 * C].astype(jnp.float32).T), d_qkv[...]).T
    sum_gain = [jnp.sum(d_ln * normed, axis=0, keepdims=True), jnp.sum(d_ln, axis=0, keepdims=True)]
    d_base = d_mid[...] + layer_pull(d_ln, normed, inv_std, gains[4:5])
    put_rows(g_skip, 0, mxu(low(d_base.T), joined[...]))
    d_joined = mxu(low(d_base), skip_t[...])
    d_branch = low(d_joined[:, :C])
    edge_b[0] = d_branch[:FREQ]
    edge_b[1] = d_branch[n_pix - FREQ :]
    copies = ring.edges(edge_b.at[0], edge_b.at[1], edge_b.at[2], edge_b.at[3])
    d_stem = d_joined[:, :C] + d_joined[:, C:]

    hot_t, left, right = own_hot(hot, n_pix)
    left_b, right_b = low(left), low(right)
    wide_hot = hot[FREQ : 3 * FREQ + n_pix]
    film_rows = mxu(wide_hot[own], table_parts(film[...]))
    inv_two = mxu(wide_hot, table_parts(table_two[8:]))
    norm_two = (wide_two[...] - mxu(wide_hot, table_parts(table_two[:8]))) * inv_two
    affine = norm_two[own] * gains[2:3] + gains[3:4]
    act = affine * (1.0 + film_rows[:, :C]) + film_rows[:, C:]
    gate = jax.nn.sigmoid(act)
    act_t = low((low(act * gate).astype(jnp.float32)).T)
    wide[own] = d_branch.astype(jnp.float32)
    wait_all(copies)
    reducer.tick(1, 0)
    wide[:FREQ] = edge_b[2].astype(jnp.float32)
    wide[FREQ + n_pix :] = edge_b[3].astype(jnp.float32)
    row_shifts(wide[...], shifts)
    conv_weight_pull(shifts, act_t, g_two, left_b, right_b, n_pix)
    reducer.tick(2, 1, 0)
    d_act = conv_data_pull(shifts, weight_two, left_b, right_b, n_pix)
    d_act = d_act * (gate + act * gate * (1.0 - gate))
    d_film = jnp.concatenate([high(hot_t, d_act * affine), high(hot_t, d_act)], axis=1)
    clip = lax.broadcasted_iota(jnp.int32, d_film.shape, 0)
    d_film = jnp.where(clip < CLIPS, d_film, 0.0)
    put_rows(g_film, 0, high(d_film.T, cond))
    reducer.tick(3, 2, 1, 0)
    d_act = d_act * (1.0 + film_rows[:, :C])
    sum_two = [
        jnp.sum(d_act * norm_two[own], axis=0, keepdims=True),
        jnp.sum(d_act, axis=0, keepdims=True),
    ]
    scaled = d_act * gains[2:3]
    wide[own] = scaled
    edge_f[0] = scaled[:FREQ]
    edge_f[1] = scaled[n_pix - FREQ :]
    copies = ring.edges(edge_f.at[0], edge_f.at[1], edge_f.at[2], edge_f.at[3])
    copies += ring.sums(clip_sums(hot_t, scaled, scaled * norm_two[own]), held.at[0])
    inv_one = mxu(wide_hot[own], table_parts(table_one[8:]))
    norm_one = (wide_one[own] - mxu(wide_hot[own], table_parts(table_one[:8]))) * inv_one
    act = norm_one * gains[0:1] + gains[1:2]
    gate = jax.nn.sigmoid(act)
    act_t = low((low(act * gate).astype(jnp.float32)).T)
    wait_all(copies)
    wide[:FREQ] = edge_f[2]
    wide[FREQ + n_pix :] = edge_f[3]
    mean, slope = group_table(ring.total(held.at[0]), counts[...])
    d_inner = inv_two * (
        wide[...] - mxu(wide_hot, table_parts(mean)) - norm_two * mxu(wide_hot, table_parts(slope))
    )
    row_shifts(low(d_inner).astype(jnp.float32), shifts)
    reducer.tick(3, 2, 1, 0)
    conv_weight_pull(shifts, act_t, g_one, left_b, right_b, n_pix)
    reducer.tick(4, 3, 2, 1, 0)
    d_act = conv_data_pull(shifts, weight_one, left_b, right_b, n_pix)
    d_act = d_act * (gate + act * gate * (1.0 - gate))
    sum_one = [
        jnp.sum(d_act * norm_one, axis=0, keepdims=True),
        jnp.sum(d_act, axis=0, keepdims=True),
    ]
    gain_rows = rows_of(8, sum_one + sum_two + sum_gain)
    scaled = d_act * gains[0:1]
    copies = ring.sums(clip_sums(hot_t, scaled, scaled * norm_one), held.at[1])
    reducer.tick(4, 3, 2, 1, 0)
    wait_all(copies)
    mean, slope = group_table(ring.total(held.at[1]), counts[...])
    hot_own = wide_hot[own]
    d_stem = d_stem + inv_one * (
        scaled - mxu(hot_own, table_parts(mean)) - norm_one * mxu(hot_own, table_parts(slope))
    )
    n_lane = taps.shape[1]
    d_stem = jnp.concatenate(
        [
            jnp.zeros((PAD, C), jnp.bfloat16),
            low(d_stem),
            jnp.zeros((n_lane - n_pix - PAD, C), jnp.bfloat16),
        ],
        axis=0,
    )
    clip = lax.broadcasted_iota(jnp.int32, (8, C), 0)
    gain_rows = jnp.where(clip < 6, gain_rows, pltpu.roll(gain_mid[...], 6, 0))
    lane = lax.broadcasted_iota(jnp.int32, (8, 256), 1)
    first = (clip == 0) & (lane == 0)
    small = [g_head[...], mxu(taps[...], d_stem), gain_rows, jnp.where(first, loss[0:1, 0:1], 0.0)]
    small = jnp.concatenate(small, axis=0)
    put_rows(g_small, 0, fill(small, 2 * g_small.shape[0] * g_small.shape[2]))
    copies = reducer.spread_small(g_small, small_in)
    reducer.tick(4, 3, 2)
    wait_all(copies)
    own_small = g_small[lax.div(reducer.place, 2), lax.rem(reducer.place, 2)]
    for slot in range(reducer.n_d - 1):
        own_small = own_small + small_in[slot]
    small_z[reducer.my_s] = own_small
    here = small_z.at[reducer.my_s]
    copies = [reducer.send(here, here, peer) for peer in reducer.s_peers()]
    reducer.tick(4, 3, 2)
    wait_all(copies)
    own_small = small_z[0]
    for slot in range(1, n_s):
        own_small = own_small + small_z[slot]
    reducer.drain()

    total = jnp.zeros((8, 256), jnp.float32)
    for shard in shards:
        total = total + square_sum(shard[...])
    count = g_small.shape[2]
    row = lax.broadcasted_iota(jnp.int32, (count, 256), 0) + reducer.place * count
    total = total + square_sum(jnp.where(row < 168, own_small, 0.0))
    total = jnp.sum(jnp.sum(total, axis=0, keepdims=True), axis=1, keepdims=True)
    blocks[reducer.place, :count] = own_small
    blocks[reducer.place, count:] = jnp.broadcast_to(total, (8, 256))
    here = blocks.at[reducer.place]
    wait_all([reducer.send(here, here, peer) for peer in reducer.dp_peers()])
    total = blocks[0, count:]
    small_out[:count] = blocks[0, :count]
    for place in range(1, reducer.n_d):
        total = total + blocks[place, count:]
        small_out[count * place : count * (place + 1)] = blocks[place, :count]
    norm_out[...] = jnp.sqrt(total)


def update_kernel(n_b, *refs):
    shards, (small, norm, sums), refs = refs[:5], refs[5:8], refs[8:]
    n_state = 3 * len(STATES)
    state, new_state, scalars = refs[:n_state], refs[n_state : 2 * n_state], refs[2 * n_state :]
    place = lax.axis_index("a") * n_b + lax.axis_index("b")
    factor = jnp.minimum(1.0, CLIP_NORM / norm[0:1, 0:1])
    scalars[0][...] = norm[0:1, 0:1]
    scalars[1][...] = small[168:169, 0:1]
    scalars[2][...] = sums[0:1, 1:2]

    def update(name, grad, part=None):
        first = 3 * STATES.index(name)
        item, new = state[first : first + 3], new_state[first : first + 3]
        if part is not None:
            item, new = [ref.at[part] for ref in item], [ref.at[part] for ref in new]
        adam(grad * factor, item, new)

    def shape(name):
        return state[3 * STATES.index(name)].shape

    def own_lanes(value, count):
        return pltpu.roll(value, (value.shape[1] - place * count) % value.shape[1], 1)[:, :count]

    for part, shard in ((0, shards[4]), (1, shards[2])):
        update("conv", shard[: shape("conv")[1]], part)
    update("proj", shards[1][: shape("proj")[1]].T)
    update("down", shards[0][: shape("down")[0]])
    start = 0
    for name in ("skip", "film"):
        rows = shape(name)[0]
        grads = shards[3][start : start + rows], shards[3][start + rows : start + 2 * rows]
        update(name, jnp.concatenate(grads, axis=1))
        start += 2 * rows
    count = shape("gains")[1]
    update("gains", own_lanes(small[160:168], count))
    stem = jnp.concatenate([small[80:160], jnp.zeros((48, C), jnp.float32)], axis=0)
    stem = own_lanes(stem, count)
    update("stem", stem.T[:, : shape("stem")[1]])
    head = [small[8 * tap : 8 * (tap + 1)] for tap in range(9)]
    update("head", own_lanes(jnp.concatenate(head, axis=1), shape("head")[1]))


def dense(kernel, operands, outs, scratch, collective_id=None):
    vmem = pl.BlockSpec(memory_space=pltpu.VMEM)
    params = dict(vmem_limit_bytes=61 << 20)
    if collective_id is not None:
        params.update(collective_id=collective_id, has_side_effects=True)
    return pl.pallas_call(
        kernel,
        in_specs=[vmem] * len(operands),
        out_specs=[vmem] * len(outs),
        out_shape=[jax.ShapeDtypeStruct(shape, dtype) for shape, dtype in outs],
        scratch_shapes=scratch,
        compiler_params=pltpu.CompilerParams(**params),
    )(*operands)


def body(
    clean_lat,
    noise_lat,
    column_ids,
    timesteps,
    clap_emb,
    conv_w,
    proj_w,
    film_w,
    skip_w,
    down_w,
    stem_w,
    head_w,
    gains,
    conv_m,
    proj_m,
    film_m,
    skip_m,
    down_m,
    stem_m,
    head_m,
    gains_m,
    conv_v,
    proj_v,
    film_v,
    skip_v,
    down_v,
    stem_v,
    head_v,
    gains_v,
):
    bf16, f32 = jnp.bfloat16, jnp.float32
    masters = (conv_w, proj_w, film_w, skip_w, down_w, stem_w, head_w, gains)
    firsts = (conv_m, proj_m, film_m, skip_m, down_m, stem_m, head_m, gains_m)
    seconds = (conv_v, proj_v, film_v, skip_v, down_v, stem_v, head_v, gains_v)
    n_dp, n_s = lax.axis_size(DP), lax.axis_size("s")
    n_a, n_b = lax.axis_size("a"), lax.axis_size("b")
    _, height, n_cols, _ = clean_lat.shape
    n_pix = height * n_cols
    n_lane = frame_of(n_pix)
    proj_cols, down_rows = proj_w.shape[1], down_w.shape[0]
    stem_rows = stem_w.shape[0]

    ids_row = column_ids[0]
    edge_pad = jnp.full((2,), -1, jnp.int32)
    ids_rim = lax.dynamic_slice_in_dim(
        jnp.concatenate([edge_pad, ids_row, edge_pad]), lax.axis_index("s") * n_cols, n_cols + 4
    )
    clip_hot = (ids_rim[:, None] == jnp.arange(CLIPS)[None, :]).astype(f32)
    place = jnp.arange(n_cols + 4)
    inner = (place > 0) & (place < n_cols + 3)
    own = (place > 1) & (place < n_cols + 2)
    same = ids_rim[1:] == ids_rim[:-1]
    off = jnp.zeros((1,), bool)
    cond_vec, alpha_clip, sigma_clip = clip_terms(timesteps[0], clap_emb[0])
    alpha_col = jnp.sum(clip_hot * alpha_clip[None], axis=1)
    sigma_col = jnp.sum(clip_hot * sigma_clip[None], axis=1)
    rows = [
        ids_rim,
        alpha_col,
        sigma_col,
        jnp.sum(clip_hot, axis=1) * inner,
        jnp.concatenate([off, same]),
        jnp.concatenate([same, off]),
        own,
        own,
    ]
    rows = jnp.stack([item.astype(f32) for item in rows])[:, :, None]
    clean, noise = (item[0].transpose(2, 1, 0) for item in (clean_lat, noise_lat))
    alpha, sigma = alpha_col[2:-2][None, :, None], sigma_col[2:-2][None, :, None]
    data = jnp.concatenate([alpha * clean + sigma * noise, alpha * noise - sigma * clean], axis=0)
    main = jnp.concatenate(
        [
            jnp.pad(data, ((0, 0), (2, 2), (0, 0))),
            jnp.broadcast_to(rows, (8, n_cols + 4, height)),
        ],
        axis=0,
    ).reshape(24, -1)
    main = jnp.pad(main, ((0, 0), (0, n_lane - main.shape[1])))
    labels = jnp.arange(8)
    counts = jnp.sum((ids_row[None] == labels[:, None]).astype(f32), axis=1) * (height * C // GROUPS)
    pixel_ids = jnp.repeat(ids_row.astype(f32), height).reshape(8, -1)
    lanes = max(COND, pixel_ids.shape[1])
    extra = [
        jnp.pad(jax.nn.silu(cond_vec).astype(bf16).astype(f32), ((0, 8 - CLIPS), (0, lanes - COND))),
        jnp.broadcast_to(jnp.maximum(counts, 1.0)[:, None], (8, lanes)),
        jnp.pad(pixel_ids, ((0, 0), (0, lanes - pixel_ids.shape[1]))),
    ]
    extra = jnp.concatenate(extra, axis=0)
    own_count = jnp.sum((ids_row < CLIPS).astype(f32)) * (height * CIN)
    front = jnp.concatenate([stem_w, gains], axis=0)
    front = jnp.pad(front, ((0, 128 - front.shape[0]), (0, 0))).T
    head_size = head_w.size
    head_rows = round_up(-(-head_size // 256), 16)
    head_flat = jnp.pad(head_w.reshape(-1), (0, head_rows * 256 - head_size)).reshape(-1, 256)
    shards = [
        front,
        jnp.full((8, 128), own_count),
        film_w.T,
        skip_w.T,
        conv_w,
        proj_w,
        down_w,
        head_flat,
    ]
    wholes = [(rows.shape, bf16) for rows in shards]
    wholes[1] = (shards[1].shape, f32)
    wholes[4:5] = [(conv_w.shape[1:], bf16)] * 2
    wholes[6] = (proj_w.shape[::-1], bf16)
    wholes = [((n_dp * shape[0], shape[1]), dtype) for shape, dtype in wholes]
    n_wide = n_pix + PAD
    n_heads = 3 * C // n_b
    vmem = pltpu.VMEM

    def sems(count):
        return pltpu.SemaphoreType.DMA((2, count))

    moves = [main, extra]
    edge = ((2 * CIN, 128), f32)
    outs = dense(
        functools.partial(front_kernel, n_a, n_b),
        [*moves, *shards],
        [(item.shape, item.dtype) for item in moves]
        + [edge, edge]
        + wholes
        + [
            ((n_heads, n_b * n_pix), bf16),
            ((n_pix, 2 * C), bf16),
            ((n_pix, C), f32),
            ((n_wide, C), f32),
            ((16, C), f32),
            ((n_wide, C), f32),
            ((16, C), f32),
            ((8, 2 * C), f32),
            ((n_lane, 128), bf16),
            ((80, n_lane), bf16),
            ((8, n_lane), f32),
            ((8, C), f32),
            ((1, n_b * n_pix), jnp.int32),
        ],
        [
            vmem((n_pix, C), f32),
            vmem((n_pix, C), f32),
            vmem((3 * C, n_pix), bf16),
            vmem((3, n_wide, C), bf16),
            vmem((2, n_b, 16, C), f32),
            sems(4 + len(wholes) * (n_dp - 1) + 2 * (n_b + 1) + n_b - 1),
        ],
        0,
    )
    main, extra, _, _ = outs[:4]
    _, counts_all, film_t, skip_t, conv_one, conv_two, proj_t, down_b, head_b = outs[4:13]
    heads_x, joined, base_rows, wide_one, table_one, wide_two, table_two, film = outs[13:21]
    hot, taps, target, gain_f, pixel_ids = outs[21:]
    head_b = head_b.reshape(n_dp, -1)[:, :head_size]
    head_t = head_b.reshape(9, C, CIN).transpose(0, 2, 1).reshape(9 * CIN, C)
    head_t = jnp.pad(head_t, ((0, 80 - 9 * CIN), (0, 0)))
    out_heads, log_total = attention_forward(heads_x, pixel_ids)
    n_hid = down_b.shape[0]
    d_mid, d_heads, g_up, g_down, g_out, g_head, gain_mid, loss = dense(
        functools.partial(middle_kernel, n_b),
        [out_heads, base_rows, proj_t, down_b, head_t, target, main, gain_f, counts_all],
        [
            ((n_pix, C), f32),
            ((C // n_b, n_b * n_pix), bf16),
            ((n_hid, C), f32),
            ((n_hid, C), f32),
            ((C, C), f32),
            ((80, C), f32),
            ((8, C), f32),
            ((8, 128), f32),
        ],
        [
            vmem((C, n_pix), bf16),
            vmem((n_lane, C), bf16),
            vmem((n_hid, n_pix), bf16),
            vmem((n_hid, n_pix), f32),
            vmem((2, PAD, C), bf16),
            vmem((C, n_pix), bf16),
            sems(2 * n_b),
        ],
        1,
    )
    d_heads_x = attention_backward(heads_x, log_total, d_heads, out_heads, pixel_ids)
    pairs = n_dp // 2
    proj_rows, skip_rows, film_rows = proj_w.shape[1], skip_w.shape[1], film_w.shape[1]
    small_rows = round_up(-(-176 // n_dp), 8)
    grads = [
        [(pairs, 2, down_rows, C)],
        [(pairs, 2, proj_rows, C)],
        [(pairs, 2, conv_w.shape[1], C)],
        [(pairs, 2, skip_rows, 2 * C), (pairs, 2, film_rows, COND)],
        [(pairs, 2, conv_w.shape[1], C)],
    ]
    small_shape = (pairs, 2, small_rows, 256)
    heights = Reducer.heights(grads, n_s)
    turn = {"film", "skip", "stem", "head"}
    state = []
    for index, name in enumerate(STATES):
        for group in (masters, firsts, seconds):
            state.append(group[index].T if name in turn else group[index])
    outs = dense(
        functools.partial(back_kernel, n_a, n_b, n_s),
        [
            d_heads_x, base_rows, d_mid, joined, proj_t, skip_t, conv_one, conv_two, wide_one,
            wide_two, table_one, table_two, film, hot, extra, gain_f, taps,
            g_up, g_out, g_down.reshape(grads[0][0]), g_head, gain_mid, loss,
        ],
        [((rows, 256), f32) for rows in heights]
        + [((n_dp * small_rows, 256), f32), ((8, 256), f32)],
        [
            vmem((3 * C, n_pix), bf16),
            vmem((3, n_wide, C), bf16),
            vmem((n_wide, C), f32),
            vmem((2, n_b, 16, C), f32),
            vmem((4, FREQ, C), bf16),
            vmem((4, FREQ, C), f32),
            sems(3 * n_b + 1),
            sems(Reducer.copies(grads, n_a, n_b, n_s) + 2 * (n_dp - 1) + n_s - 1),
            vmem((n_dp, small_rows + 8, 256), f32),
        ]
        + [vmem(shape, f32) for parts in grads[1:] for shape in parts]
        + [vmem(small_shape, f32)]
        + [vmem((count, small_rows, 256), f32) for count in (n_dp - 1, n_s)]
        + [vmem(shape, f32) for shape in Reducer.scratch(grads, n_a, n_b, n_s)],
        2,
    )
    *grad_shards, small, norm = outs
    new_state = dense(
        functools.partial(update_kernel, n_b),
        [*grad_shards, small, norm, loss, *state],
        [(item.shape, f32) for item in state] + [((1, 1), f32)] * 3,
        [],
    )
    new_w, new_m, new_v = {}, {}, {}
    for place, name in enumerate(STATES):
        for kind, group in enumerate((new_w, new_m, new_v)):
            item = new_state[3 * place + kind]
            group[name] = item.T if name in turn else item
    grad_norm, loss_sum, pix_count = (item[0, 0] for item in new_state[3 * len(STATES) :])
    return (
        *[new_w[name] for name in STATES],
        *[new_m[name] for name in STATES],
        *[new_v[name] for name in STATES],
        grad_norm,
        loss_sum,
        pix_count,
    )


def solution(mesh):
    n_dp, n_s = mesh.shape["dp"], mesh.shape["section"]
    blocks = jax.sharding.Mesh(mesh.devices.reshape(n_dp // n_s, n_s, n_s), ("a", "b", "s"))
    return jax.shard_map(
        body,
        mesh=blocks,
        in_specs=(
            P(DP, None, "s", None),
            P(DP, None, "s", None),
            P(DP, None),
            P(DP, None),
            P(DP, None, None),
            P(None, DP, None),
            P(None, DP),
            P(None, DP),
            P(None, DP),
            P(DP, None),
            P(None, DP),
            P(DP, None),
            P(None, DP),
            P(None, DP, None),
            P(None, DP),
            P(None, DP),
            P(None, DP),
            P(DP, None),
            P(None, DP),
            P(DP, None),
            P(None, DP),
            P(None, DP, None),
            P(None, DP),
            P(None, DP),
            P(None, DP),
            P(DP, None),
            P(None, DP),
            P(DP, None),
            P(None, DP),
        ),
        out_specs=(
            P(None, DP, None),
            P(None, DP),
            P(None, DP),
            P(None, DP),
            P(DP, None),
            P(None, DP),
            P(DP, None),
            P(None, DP),
            P(None, DP, None),
            P(None, DP),
            P(None, DP),
            P(None, DP),
            P(DP, None),
            P(None, DP),
            P(DP, None),
            P(None, DP),
            P(None, DP, None),
            P(None, DP),
            P(None, DP),
            P(None, DP),
            P(DP, None),
            P(None, DP),
            P(DP, None),
            P(None, DP),
            P(),
            P(),
            P(),
        ),
        check_vma=False,
    )
```

```python
import functools
import math

import jax
import jax.numpy as jnp
from jax import lax
from jax.experimental import pallas as pl
from jax.experimental.pallas import tpu as pltpu
from jax.sharding import PartitionSpec as P

CIN = 8
C = 256
HEADS = 8
HD = 32
COND = 512
GROUPS = 32
CLIPS = 4
STEP = 10


EPS_NORM = 1e-05
CLIP_NORM = 0.02
DP = ("a", "b")
STATES = ("conv", "proj", "film", "skip", "down", "stem", "head", "gains")
GATHERED = ("front", "count", "film", "skip", "conv0", "conv1", "proj", "down", "head")
RATE = 0.04
BETA_ONE = 0.9
BETA_TWO = 0.999
ADAM_EPS = 1e-08
DECAY = 0.1


def matmul(lhs_mat, rhs_mat):
    return jnp.dot(lhs_mat, rhs_mat, preferred_element_type=jnp.float32)


def clip_terms(timesteps, clap_emb):
    half_cond = COND // 2
    frequency = jnp.exp(-math.log(10000.0) * jnp.arange(half_cond, dtype=jnp.float32) / half_cond)
    angles = timesteps.astype(jnp.float32)[:, None] * frequency[None]
    cond_vec = clap_emb + jnp.concatenate([jnp.sin(angles), jnp.cos(angles)], axis=1)
    theta_clip = 0.5 * math.pi * (timesteps.astype(jnp.float32) + 1.0) / 1001.0
    return (cond_vec, jnp.cos(theta_clip), jnp.sin(theta_clip))


BIG = 1e30
LOG2E = 1.4426950408889634
SCALE = HD**-0.5 * LOG2E
VMEM_LIMIT = 56 << 20
NN = (((1,), (0,)), ((), ()))
NT = (((1,), (1,)), ((), ()))


def mxu(lhs_mat, rhs_mat, dims=NN):
    return lax.dot_general(lhs_mat, rhs_mat, dims, preferred_element_type=jnp.float32)


def split_three(value):
    high = value.astype(jnp.bfloat16).astype(jnp.float32)
    rest = value - high
    mid = rest.astype(jnp.bfloat16).astype(jnp.float32)
    return high, mid, rest - mid


def rows_of(height, parts):
    row = lax.broadcasted_iota(jnp.int32, (height, parts[0].shape[1]), 0)
    total = jnp.zeros(row.shape, jnp.float32)
    for place, part in enumerate(parts):
        total = jnp.where(row == place, part, total)
    return total


def clip_rows(ids, hit, miss):
    return [jnp.where(ids == clip, hit, miss) for clip in range(CLIPS + 1)]


def forward_kernel(bq, bk, x_ref, ids_ref, out_ref, lse_ref, keys, values):
    n_pix = x_ref.shape[1]
    step = pl.program_id(1)

    @pl.when(step == 0)
    def _():
        def prepare(part, carry):
            cols = pl.ds(pl.multiple_of(part * 512, 512), 512)
            key = x_ref[HD : 2 * HD, cols].astype(jnp.float32)
            marks = rows_of(32, clip_rows(ids_ref[:, cols], 1.0, 0.0))
            stack = jnp.concatenate([key, key, key, marks], axis=0)
            keys[cols, :] = stack.T.astype(jnp.bfloat16)
            ones = jnp.ones((16, 512), jnp.bfloat16)
            values[:, cols] = jnp.concatenate([x_ref[2 * HD : 3 * HD, cols], ones], axis=0)
            return carry

        lax.fori_loop(0, n_pix // 512, prepare, 0)

    block = pl.ds(pl.multiple_of(step * bq, bq), bq)
    marks = rows_of(32, clip_rows(ids_ref[:, block], 0.0, -BIG))
    query = split_three(x_ref[:HD, block].astype(jnp.float32) * SCALE)
    query = jnp.concatenate([*query, marks], axis=0).astype(jnp.bfloat16)
    acc = jnp.zeros((HD + 16, bq), jnp.float32)
    row_max = jnp.full((1, bq), -jnp.inf, jnp.float32)
    for start in range(0, n_pix, bk):
        scores = mxu(keys[start : start + bk, :], query)
        new_max = jnp.maximum(row_max, jnp.max(scores, axis=0, keepdims=True))
        probs = jnp.exp2(scores - new_max).astype(jnp.bfloat16)
        acc = acc * jnp.exp2(row_max - new_max) + mxu(values[:, start : start + bk], probs)
        row_max = new_max
    total = acc[HD : HD + 1]
    out_ref[...] = (acc[:HD] / total).astype(jnp.bfloat16)
    lse_ref[...] = jnp.broadcast_to(row_max + jnp.log2(total), (8, bq))


def attention_forward(heads_x, pixel_ids, bq=2048, bk=256):
    lanes, n_pix = heads_x.shape
    heads = lanes // (3 * HD)
    bq, bk = min(bq, n_pix), min(bk, n_pix)
    return pl.pallas_call(
        functools.partial(forward_kernel, bq, bk),
        grid=(heads, n_pix // bq),
        in_specs=[
            pl.BlockSpec((3 * HD, n_pix), lambda h, i: (h, 0)),
            pl.BlockSpec((1, n_pix), lambda h, i: (0, 0)),
        ],
        out_specs=[
            pl.BlockSpec((HD, bq), lambda h, i: (h, i)),
            pl.BlockSpec((8, bq), lambda h, i: (h, i)),
        ],
        out_shape=[
            jax.ShapeDtypeStruct((heads * HD, n_pix), jnp.bfloat16),
            jax.ShapeDtypeStruct((heads * 8, n_pix), jnp.float32),
        ],
        scratch_shapes=[
            pltpu.VMEM((n_pix, 128), jnp.bfloat16),
            pltpu.VMEM((HD + 16, n_pix), jnp.bfloat16),
        ],
        compiler_params=pltpu.CompilerParams(vmem_limit_bytes=VMEM_LIMIT),
    )(heads_x, pixel_ids)


def backward_kernel(
    bq, bk, x_ref, ids_ref, do_ref, o_ref, lse_ref, out_ref,
    queries, keys, values, d_outs, d_query, pair_rows,
):
    n_pix = x_ref.shape[1]
    step = pl.program_id(1)

    @pl.when(step == 0)
    def _():
        d_query[...] = jnp.zeros_like(d_query)

        def prepare(part, carry):
            cols = pl.ds(pl.multiple_of(part * 512, 512), 512)
            ids = ids_ref[:, cols]
            one = jnp.ones((1, 512), jnp.float32)
            zero = jnp.zeros((64, 512), jnp.float32)
            key = x_ref[HD : 2 * HD, cols].astype(jnp.float32)
            marks = rows_of(32, clip_rows(ids, 1.0, 0.0) + [one, one, one])
            stack = jnp.concatenate([key, key, key, marks], axis=0)
            keys[cols, :] = stack.T.astype(jnp.bfloat16)
            value = x_ref[2 * HD : 3 * HD, cols].astype(jnp.float32)
            stack = jnp.concatenate([value, rows_of(32, [one, one, one]), zero], axis=0)
            values[cols, :] = stack.T.astype(jnp.bfloat16)
            query = x_ref[:HD, cols].astype(jnp.float32)
            d_out = do_ref[:, cols].astype(jnp.float32)
            marks = rows_of(32, clip_rows(ids, 0.0, -BIG) + list(split_three(-lse_ref[0:1, cols])))
            stack = jnp.concatenate([*split_three(query * SCALE), marks], axis=0)
            queries[:, cols] = stack.astype(jnp.bfloat16)
            delta = jnp.sum(d_out * o_ref[:, cols].astype(jnp.float32), axis=0, keepdims=True)
            stack = jnp.concatenate([d_out, rows_of(32, split_three(-delta))], axis=0)
            d_outs[:, cols] = stack.astype(jnp.bfloat16)
            stack = jnp.concatenate([query, d_out, zero], axis=0).T.astype(jnp.bfloat16)
            pair_rows[cols, :] = stack
            return carry

        lax.fori_loop(0, n_pix // 512, prepare, 0)

    block = pl.ds(pl.multiple_of(step * bk, bk), bk)
    key, value = keys[block, :], values[block, :64]
    key_t = x_ref[HD : 2 * HD, block]
    d_value = jnp.zeros((bk, 128), jnp.float32)
    d_key = jnp.zeros((bk, 128), jnp.float32)
    for start in range(0, n_pix, bq):
        cols = slice(start, start + bq)
        probs = jnp.exp2(mxu(key, queries[:, cols]))
        d_scores = (probs * mxu(value, d_outs[:, cols])).astype(jnp.bfloat16)
        probs = probs.astype(jnp.bfloat16)
        d_value += mxu(probs, pair_rows[cols, :])
        d_key += mxu(d_scores, pair_rows[cols, :])
        d_query[:, cols] += mxu(key_t, d_scores)
    d_key, d_value = d_key.T[:HD], d_value.T[HD : 2 * HD]
    out_ref[HD : 2 * HD, block] = (d_key * (HD**-0.5)).astype(jnp.bfloat16)
    out_ref[2 * HD : 3 * HD, block] = d_value.astype(jnp.bfloat16)

    @pl.when(step == pl.num_programs(1) - 1)
    def _():
        out_ref[:HD, :] = (d_query[...] * (HD**-0.5)).astype(jnp.bfloat16)


def attention_backward(heads_x, log_total, d_heads, out_heads, pixel_ids, bq=1024, bk=1024):
    lanes, n_pix = heads_x.shape
    heads = lanes // (3 * HD)
    bq, bk = min(bq, n_pix), min(bk, n_pix)

    def rows(count):
        return pl.BlockSpec((count, n_pix), lambda h, i: (h, 0))

    return pl.pallas_call(
        functools.partial(backward_kernel, bq, bk),
        grid=(heads, n_pix // bk),
        in_specs=[
            rows(3 * HD),
            pl.BlockSpec((1, n_pix), lambda h, i: (0, 0)),
            rows(HD),
            rows(HD),
            rows(8),
        ],
        out_specs=rows(3 * HD),
        out_shape=jax.ShapeDtypeStruct((lanes, n_pix), jnp.bfloat16),
        scratch_shapes=[
            pltpu.VMEM((128, n_pix), jnp.bfloat16),
            pltpu.VMEM((n_pix, 128), jnp.bfloat16),
            pltpu.VMEM((n_pix, 128), jnp.bfloat16),
            pltpu.VMEM((64, n_pix), jnp.bfloat16),
            pltpu.VMEM((HD, n_pix), jnp.float32),
            pltpu.VMEM((n_pix, 128), jnp.bfloat16),
        ],
        compiler_params=pltpu.CompilerParams(vmem_limit_bytes=VMEM_LIMIT),
    )(heads_x, pixel_ids, d_heads, out_heads, log_total)


MESH = pl.DeviceIdType.MESH


def round_up(count, unit):
    return -(-count // unit) * unit


def greet(peers):
    barrier = pltpu.get_barrier_semaphore()
    for peer in peers:
        pl.semaphore_signal(barrier, inc=1, device_id=peer, device_id_type=MESH)
    pl.semaphore_wait(barrier, len(peers))


def push(src, dst, sems, slot, peer):
    copy = pltpu.make_async_remote_copy(
        src_ref=src,
        dst_ref=dst,
        send_sem=sems.at[0, slot],
        recv_sem=sems.at[1, slot],
        device_id=peer,
        device_id_type=MESH,
    )
    copy.start()
    return copy


FREQ = 16
PAD = 2 * FREQ
HIGH = lax.Precision.HIGHEST


def high(lhs_mat, rhs_mat, dims=NN):
    return lax.dot_general(
        lhs_mat, rhs_mat, dims, precision=HIGH, preferred_element_type=jnp.float32
    )


def low(value):
    return value.astype(jnp.bfloat16)


def frame_of(n_pix):
    return round_up(n_pix + 2 * PAD, 128)


def lane_taps(value, left, right, sign):
    n_lane = value.shape[1]
    freq = lax.broadcasted_iota(jnp.int32, value.shape, 1) & (FREQ - 1)
    parts = []
    for df in (-1, 0, 1):
        for dc in (-1, 0, 1):
            moved = sign * (FREQ * dc + df)
            part = value if moved == 0 else pltpu.roll(value, (-moved) % n_lane, 1)
            if sign * df < 0:
                part = jnp.where(freq > 0, part, 0.0)
            if sign * df > 0:
                part = jnp.where(freq < FREQ - 1, part, 0.0)
            if sign * dc < 0:
                part = part * left
            if sign * dc > 0:
                part = part * right
            parts.append(part)
    return jnp.concatenate(parts, axis=0)


def fill(value, rows):
    return jnp.concatenate(
        [value, jnp.zeros((rows - value.shape[0], value.shape[1]), value.dtype)], axis=0
    )


def silu(x):
    return x * jax.nn.sigmoid(x)


def table_parts(table):
    return low(fill(jnp.concatenate(split_three(table), axis=0), 128))


def group_table(sums, counts):
    size = C // GROUPS
    row = lax.broadcasted_iota(jnp.int32, (C, C), 0) & (C - size)
    col = lax.broadcasted_iota(jnp.int32, (C, C), 1) & (C - size)
    totals = high(sums, (row == col).astype(jnp.float32))
    return totals[:8] / counts, totals[8:] / counts


def clip_sums(hot_t, one, two):
    return jnp.concatenate([high(hot_t, one), high(hot_t, two)], axis=0)


def hot_rows(ids, rows):
    clip = lax.broadcasted_iota(jnp.int32, (rows, ids.shape[1]), 0)
    return ((clip & 7) == ids) & (clip < 24)


def row_shifts(value, keep):
    n_row = value.shape[0]
    freq = lax.broadcasted_iota(jnp.int32, value.shape, 0) & (FREQ - 1)
    keep[0] = low(jnp.where(freq > 0, pltpu.roll(value, 1, 0), 0.0))
    keep[1] = low(value)
    keep[2] = low(jnp.where(freq < FREQ - 1, pltpu.roll(value, n_row - 1, 0), 0.0))


def conv_rows(shifts, weight, left, right, n_pix):
    total = None
    for dc in range(3):
        part = None
        for df in range(3):
            tap = 3 * df + dc
            item = mxu(shifts[df, FREQ * dc : FREQ * dc + n_pix], weight[C * tap : C * (tap + 1)])
            part = item if part is None else part + item
        part = part if dc == 1 else part * (left if dc == 0 else right)
        total = part if total is None else total + part
    return total


def pull_windows(shifts, left, right, n_pix):
    for df in range(3):
        for dc in range(3):
            at = FREQ * (2 - dc)
            window = shifts[2 - df, at : at + n_pix]
            yield 3 * df + dc, window if dc == 1 else window * (right if dc == 0 else left)


def conv_weight_pull(shifts, act_t, grad, left, right, n_pix):
    for tap, window in pull_windows(shifts, left, right, n_pix):
        put_rows(grad, C * tap, mxu(act_t, window))


def conv_data_pull(shifts, weight, left, right, n_pix):
    total = None
    for tap, window in pull_windows(shifts, left, right, n_pix):
        item = mxu(window, weight[C * tap : C * (tap + 1)], NT)
        total = item if total is None else total + item
    return total


def layer_parts(x):
    centered = x - jnp.mean(x, axis=1, keepdims=True)
    inv_std = lax.rsqrt(jnp.mean(centered * centered, axis=1, keepdims=True) + EPS_NORM)
    return centered * inv_std, inv_std


def layer_pull(d_out, normed, inv_std, gain):
    scaled = d_out * gain
    return inv_std * (
        scaled
        - jnp.mean(scaled, axis=1, keepdims=True)
        - normed * jnp.mean(scaled * normed, axis=1, keepdims=True)
    )


class Ring:
    def __init__(self, n_b, sems, slots=None):
        self.n_b, self.sems = n_b, sems
        self.me = lax.axis_index("b")
        self.slots = iter(range(sems.shape[1])) if slots is None else slots
        self.places = [lax.rem(self.me + off, n_b) for off in range(1, n_b)]
        self.peers = [{"b": place} for place in self.places]

    def send(self, src, dst, peer):
        return push(src, dst, self.sems, next(self.slots), peer)

    def edges(self, first, last, left, right):
        return [self.send(last, left, self.peers[0]), self.send(first, right, self.peers[-1])]

    def sums(self, mine, held):
        held[self.me] = mine
        place = held.at[self.me]
        return [self.send(place, place, peer) for peer in self.peers]

    def total(self, held):
        total = held[0]
        for place in range(1, self.n_b):
            total = total + held[place]
        return total

    def rows_at(self, ref, place):
        count = ref.shape[0] // self.n_b
        return pl.ds(pl.multiple_of(place * count, 16), count)

    def cols_at(self, ref, place):
        count = ref.shape[1] // self.n_b
        return pl.ds(pl.multiple_of(place * count, 128), count)

    def spread(self, make, buf, out):
        copies = []
        for place, peer in zip(self.places, self.peers):
            rows = self.rows_at(buf, place)
            buf[rows] = make(rows)
            copies.append(self.send(buf.at[rows], out.at[:, self.cols_at(out, self.me)], peer))
        rows = self.rows_at(buf, self.me)
        out[:, self.cols_at(out, self.me)] = make(rows)
        return copies

    def collect(self, src, out):
        copies = []
        for place, peer in zip(self.places, self.peers):
            source = src.at[:, self.cols_at(src, place)]
            copies.append(self.send(source, out.at[self.rows_at(out, self.me)], peer))
        out[self.rows_at(out, self.me)] = src[:, self.cols_at(src, self.me)]
        return copies


def wait_all(copies):
    for copy in copies:
        copy.wait()


def own_hot(hot, n_pix):
    own = hot[PAD : PAD + n_pix].astype(jnp.float32)
    return own.T[:8], own[:, 24:25], own[:, 25:26]


def norm_wide(ring, held, wide, counts, hot, table_out):
    mean, square = group_table(ring.total(held), counts[...])
    inv_std = lax.rsqrt(square - mean * mean + EPS_NORM)
    table_out[:8] = mean
    table_out[8:] = inv_std
    return (wide[...] - mxu(hot, table_parts(mean))) * mxu(hot, table_parts(inv_std))


def front_kernel(n_a, n_b, *refs):
    n_move, n_gather = 2, len(GATHERED)
    refs = list(refs)
    moved_in, shards = refs[:n_move], refs[n_move : n_move + n_gather - 2]
    shards[1:1] = [None]
    at_conv = GATHERED.index("conv0")
    both = shards.pop(at_conv)
    shards[at_conv:at_conv] = [both.at[0], both.at[1]]
    refs = refs[n_move + n_gather - 2 :]
    moved, wholes = refs[: n_move + 2], refs[n_move + 2 : n_move + 2 + n_gather]
    refs = refs[n_move + 2 + n_gather :]
    heads_out, joined_out, base_out, wide_one, table_one, wide_two, table_two, film_out = refs[:8]
    hot, taps_out, target_out, gains, pixel_ids = refs[8:13]
    stem_buf, inner_buf, qkv_buf, shifts, held, sems = refs[13:]
    main_in, extra_in = moved_in
    main, extra, left_edge, right_edge = moved
    n_pix, n_lane = base_out.shape[0], main.shape[1]
    my_a, my_b, my_s = lax.axis_index("a"), lax.axis_index("b"), lax.axis_index("s")
    core, my_x = lax.rem(my_b, 2), lax.div(my_b, 2)
    n_x = n_b // 2
    n_d, n_j = n_a * n_b, n_a * n_x
    my_j = my_a * n_x + my_x
    slots = iter(range(sems.shape[1]))
    ring = Ring(n_b, sems, slots)

    def at(b, s):
        return {"b": lax.rem(b + n_b, n_b), "s": lax.rem(s + n_b, n_b)}

    dp_peers = []
    for off in range(1, n_d):
        there = lax.rem(my_a * n_b + my_b + off, n_d)
        dp_peers.append({"a": lax.div(there, n_b), "b": lax.rem(there, n_b)})
    mirrored = my_b != my_s
    shift = jnp.where(mirrored, 0, 1)
    greet(
        dp_peers
        + [at(my_s + 1, my_b), at(my_s - 1, my_b), at(my_s, my_b + 1), at(my_s, my_b - 1)]
        + [at(my_s + shift, my_b + shift)]
    )
    main_slot, extra_slot = next(slots), next(slots)

    @pl.when(mirrored)
    def _():
        push(main_in, main, sems, main_slot, at(my_s, my_b))
        push(extra_in, extra, sems, extra_slot, at(my_s, my_b))

    @pl.when(jnp.logical_not(mirrored))
    def _():
        main[...] = main_in[...]
        extra[...] = extra_in[...]

    end = (PAD + n_pix) // 128 * 128
    first, last = (main_in.at[pl.ds(0, 16), pl.ds(start, 128)] for start in (0, end))
    copies = [
        push(last, left_edge, sems, next(slots), at(my_s + 1, my_b)),
        push(first, right_edge, sems, next(slots), at(my_s - 1, my_b)),
    ]

    def rows_of_shard(whole, j, of_core):
        count = whole.shape[0] // n_d
        return whole.at[pl.ds(pl.multiple_of((2 * j + of_core) * count, 8), count)]

    sibling = {"b": my_b + 1 - 2 * core}
    near, far = {}, {}

    def launch(*names):
        for name in names:
            index = GATHERED.index(name)
            place = rows_of_shard(wholes[index], my_j, core)
            own = None if name == "count" else shards[index][...]
            if name == "count":
                known = extra_in[16:24, : pixel_ids.shape[1] // 8]
                known = jnp.sum(jnp.where(known < CLIPS, 1.0 * CIN, 0.0), axis=0, keepdims=True)
                own = jnp.broadcast_to(jnp.sum(known, axis=1, keepdims=True), place.shape)
            if name == "head":
                own = low(own)
            place[...] = (own.T if name == "proj" else own).astype(place.dtype)
            near[name] = []
            for off in range(1, n_j):
                there = lax.rem(my_j + off, n_j)
                peer = {"a": lax.div(there, n_x), "b": 2 * lax.rem(there, n_x) + core}
                near[name].append(push(place, place, sems, next(slots), peer))
            far[name] = [push(place, place, sems, next(slots), sibling)]

    def forward(*names):
        for name in names:
            whole = wholes[GATHERED.index(name)]
            for off, copy in enumerate(near[name]):
                copy.wait()
                rows = rows_of_shard(whole, lax.rem(my_j + n_j - off - 1, n_j), core)
                far[name].append(push(rows, rows, sems, next(slots), sibling))

    def arrived(*names):
        for name in names:
            wait_all(far[name])

    part = dict(zip(GATHERED, wholes))
    launch("front", "count", "conv0", "film")
    forward("front", "count")
    wait_all(copies)

    @pl.when(mirrored)
    def _():
        for source, target, slot in ((main_in, main, main_slot), (extra_in, extra, extra_slot)):
            pltpu.make_async_remote_copy(
                src_ref=source,
                dst_ref=target,
                send_sem=sems.at[0, slot],
                recv_sem=sems.at[1, slot],
                device_id=at(my_s, my_b),
                device_id_type=MESH,
            ).wait()

    lane = lax.broadcasted_iota(jnp.int32, (16, 128), 1)
    is_left, is_right = (lane >= FREQ) & (lane < PAD), (lane >= PAD) & (lane < PAD + FREQ)
    main[:16, :128] = jnp.where(is_left, left_edge[...], main[:16, :128])
    main[:16, end : end + 128] = jnp.where(is_right, right_edge[...], main[:16, end : end + 128])
    rows = main[16:24]
    ids, left, right = rows[0:1], rows[4:5], rows[5:6]
    target_out[...] = main[8:16]
    n_id = pixel_ids.shape[1] // 8
    for row in range(8):
        line = extra[16 + row : 17 + row, :n_id]
        pixel_ids[:, n_id * row : n_id * (row + 1)] = line.astype(jnp.int32)
    taps = lane_taps(low(main[:8]).astype(jnp.float32), left, right, 1)
    taps = fill(taps, 128)
    taps_out[...] = low(taps[:80])
    clip = lax.broadcasted_iota(jnp.int32, (128, n_lane), 0)
    marks = hot_rows(ids.astype(jnp.int32), 128).astype(jnp.float32)
    marks = marks + jnp.where(clip == 24, left, 0.0) + jnp.where(clip == 25, right, 0.0)
    hot[...] = low(marks.T)
    hot_t, left, right = own_hot(hot, n_pix)
    wide_hot = hot[FREQ : 3 * FREQ + n_pix]
    taps = low(taps.T)[PAD : PAD + n_pix]
    arrived("front", "count")
    stem_w = part["front"][...]
    gains[...] = stem_w.astype(jnp.float32).T[72:80]
    stem = mxu(taps, stem_w, NT)
    stem_buf[...] = stem
    counts = extra.at[pl.ds(8, 8), pl.ds(0, C)]

    copies = ring.edges(
        stem_buf.at[pl.ds(0, FREQ)],
        stem_buf.at[pl.ds(n_pix - FREQ, FREQ)],
        wide_one.at[pl.ds(0, FREQ)],
        wide_one.at[pl.ds(n_pix + FREQ, FREQ)],
    )
    copies += ring.sums(clip_sums(hot_t, stem, stem * stem), held.at[0])
    wide_one[FREQ : FREQ + n_pix] = stem
    forward("conv0", "film")
    wait_all(copies)
    launch("conv1", "skip")
    normed = norm_wide(ring, held.at[0], wide_one, counts, wide_hot, table_one)
    row_shifts(low(silu(normed * gains[0:1] + gains[1:2])).astype(jnp.float32), shifts)
    arrived("conv0")
    inner = conv_rows(shifts, part["conv0"], left, right, n_pix)
    inner_buf[...] = inner

    copies = ring.edges(
        inner_buf.at[pl.ds(0, FREQ)],
        inner_buf.at[pl.ds(n_pix - FREQ, FREQ)],
        wide_two.at[pl.ds(0, FREQ)],
        wide_two.at[pl.ds(n_pix + FREQ, FREQ)],
    )
    copies += ring.sums(clip_sums(hot_t, inner, inner * inner), held.at[1])
    wide_two[FREQ : FREQ + n_pix] = inner
    forward("conv1", "skip")
    arrived("film")
    film = mxu(low(extra[:8, : part["film"].shape[1]]), part["film"][...], NT)
    film_out[...] = film
    film_rows = mxu(wide_hot, table_parts(film))
    wait_all(copies)
    launch("proj", "down", "head")
    normed = norm_wide(ring, held.at[1], wide_two, counts, wide_hot, table_two)
    act = (normed * gains[2:3] + gains[3:4]) * (1.0 + film_rows[:, :C]) + film_rows[:, C:]
    row_shifts(low(silu(act)).astype(jnp.float32), shifts)
    arrived("conv1", "skip")
    branch = conv_rows(shifts, part["conv1"], left, right, n_pix)

    forward("proj")
    stem = stem_buf[...]
    joined_out[:, :C] = low(stem + branch)
    joined_out[:, C:] = low(stem)
    base = mxu(joined_out[...], part["skip"][...], NT)
    base_out[...] = base
    normed, _ = layer_parts(base)
    normed = low(normed * gains[4:5] + gains[5:6])
    arrived("proj")
    forward("down", "head")
    copies = ring.spread(lambda rows: low(mxu(part["proj"][rows], normed, NT)), qkv_buf, heads_out)
    arrived("down", "head")
    wait_all(copies)


def middle_kernel(
    n_b, heads, base, proj_t, down, head, target, main, gains, counts,
    d_mid_out, d_heads_out, g_up, g_down, g_out, g_head, g_gains, loss_out,
    attended, wide, act_t, pull_t, edge, d_att_buf, sems,
):
    n_pix = base.shape[0]
    n_lane = target.shape[1]
    n_hid = down.shape[0]
    ring = Ring(n_b, sems)
    greet(ring.peers)
    copies = ring.collect(heads, attended)
    rows = main[16:24]
    pix_count = jnp.sum(counts[:, 0:1], axis=0, keepdims=True) * 0.125
    blocks = [head[8 * place : 8 * (place + 1)] for place in range(head.shape[0] // 8)]
    blocks = jnp.concatenate(blocks, axis=1)
    blocks = [blocks[:, C * tap : C * (tap + 1)] for tap in range(9)]
    head_t = low(fill(jnp.concatenate(blocks, axis=0), 80))
    wait_all(copies)
    proj_out, proj_up = proj_t.at[pl.ds(3 * C, C)], proj_t.at[pl.ds(4 * C, n_hid)]
    mid = base[...] + mxu(low(attended[...].astype(jnp.float32).T), proj_out[...], NT)
    normed, inv_std = layer_parts(mid)
    ln_b = low(normed * gains[6:7] + gains[7:8])
    top_t = jnp.zeros((C, n_pix), jnp.float32)
    scale = math.sqrt(2.0 / math.pi)
    for start in range(0, n_hid, 256):
        part = slice(start, start + 256)
        hidden = mxu(proj_up[part], ln_b, NT)
        bend = jnp.tanh(scale * (hidden + 0.044715 * hidden * hidden * hidden))
        gate = 0.5 * (1.0 + bend)
        act = low(hidden * gate)
        act_t[part] = act
        pull_t[part] = gate + 0.5 * hidden * (1.0 - bend * bend) * scale * (
            1.0 + 3.0 * 0.044715 * hidden * hidden
        )
        top_t = top_t + mxu(low(down[part].astype(jnp.float32).T), act)
    top = low(mid + top_t.T)
    wide[PAD : PAD + n_pix] = top
    wide[2 * PAD + n_pix :] = jnp.zeros((n_lane - 2 * PAD - n_pix, C), jnp.bfloat16)
    edge[0] = top[:PAD]
    edge[1] = top[n_pix - PAD :]
    copies = ring.edges(
        edge.at[0], edge.at[1], wide.at[pl.ds(0, PAD)], wide.at[pl.ds(PAD + n_pix, PAD)]
    )
    wait_all(copies)
    left, right, valid, own = rows[4:5], rows[5:6], rows[3:4], rows[6:7]
    products = mxu(head_t, wide[...], NT)
    freq = lax.broadcasted_iota(jnp.int32, (8, n_lane), 1) & (FREQ - 1)
    pred = jnp.zeros((8, n_lane), jnp.float32)
    for df in (-1, 0, 1):
        for dc in (-1, 0, 1):
            tap = 3 * (df + 1) + dc + 1
            moved = FREQ * dc + df
            part = products[8 * tap : 8 * (tap + 1)]
            part = part if moved == 0 else pltpu.roll(part, (-moved) % n_lane, 1)
            if df != 0:
                part = jnp.where(freq > 0 if df < 0 else freq < FREQ - 1, part, 0.0)
            if dc != 0:
                part = part * (left if dc < 0 else right)
            pred = pred + part
    residue = jnp.where(valid > 0.0, pred - target[...], 0.0)
    loss = jnp.sum(own * residue * residue, axis=0, keepdims=True)
    lane = lax.broadcasted_iota(jnp.int32, (8, 128), 1)
    loss_out[...] = jnp.where(lane == 1, pix_count, jnp.sum(loss, axis=1, keepdims=True))
    d_pred = low(2.0 * residue / pix_count).astype(jnp.float32)
    taps = lane_taps(d_pred, left, right, -1) * own
    taps = fill(taps, 128)
    g_head[...] = mxu(low(taps[:80]), wide[...])
    d_top = mxu(low(taps.T)[PAD : PAD + n_pix], fill(head_t, 128))
    d_top_b = low(d_top)
    d_ln_t = jnp.zeros((C, n_pix), jnp.float32)
    for start in range(0, n_hid, 256):
        part = slice(start, start + 256)
        d_hidden = low(mxu(down[part], d_top_b, NT) * pull_t[part])
        g_up[part] = mxu(d_hidden, ln_b)
        g_down[part] = mxu(act_t[part], d_top_b)
        d_ln_t = d_ln_t + mxu(low(proj_up[part].astype(jnp.float32).T), d_hidden)
    d_ln = d_ln_t.T
    g_gains[...] = rows_of(
        8, [jnp.sum(d_ln * normed, axis=0, keepdims=True), jnp.sum(d_ln, axis=0, keepdims=True)]
    )
    d_mid = d_top + layer_pull(d_ln, normed, inv_std, gains[6:7])
    d_mid_out[...] = d_mid
    d_mid_b = low(d_mid)
    g_out[...] = mxu(attended[...], d_mid_b).T
    d_att_buf[...] = low(mxu(low(proj_out[...].astype(jnp.float32).T), d_mid_b, NT))
    wait_all(ring.spread(lambda rows: d_att_buf[rows], d_att_buf, d_heads_out))


def put_rows(ref, start, value):
    height = ref.shape[2]
    at = 0
    while at < value.shape[0]:
        shard, row = divmod(start + at, height)
        count = min(height - row, value.shape[0] - at)
        ref[shard // 2, shard % 2, row : row + count] = value[at : at + count]
        at += count


class Reducer:
    def __init__(self, n_a, n_b, n_s, chunks, scratch, outs, sems):
        self.n_a, self.n_b, self.n_x, self.n_s = n_a, n_b, n_b // 2, n_s
        self.bits = n_s.bit_length() - 1
        self.chunks, self.outs, self.sems = chunks, outs, sems
        self.slots = iter(range(sems.shape[1]))
        scratch = list(scratch)
        self.halves, self.accs, self.one, self.two, self.bit, self.halved = [], [], [], [], [], []
        for parts in chunks:
            self.halves.append([scratch.pop(0) for _ in parts])
            self.accs.append(scratch.pop(0))
            self.one.append([scratch.pop(0) for _ in range(2)])
            self.two.append([scratch.pop(0) for _ in range(2)])
            self.bit.append(scratch[0])
            self.halved.append(scratch.pop(0))
        self.my_a, self.my_b, self.my_s = (lax.axis_index(axis) for axis in ("a", "b", "s"))
        self.core, self.my_x = lax.rem(self.my_b, 2), lax.div(self.my_b, 2)
        self.place = self.my_a * n_b + self.my_b
        self.n_d = n_a * n_b
        plane = [(self.core_send, self.core_sum, 0)]
        plane += [(self.plane_send, self.plane_sum, stage) for stage in range(2)]
        halving = [(self.bit_send, self.bit_sum, bit) for bit in range(self.bits)]
        halving += [(self.bit_up, None, bit) for bit in reversed(range(self.bits))]
        direct = [(self.s_send, self.s_sum, 0), (self.up_send, None, 0)]
        self.steps = [plane + halving for _ in chunks[1:]] + [plane + direct]
        self.at = [0] * len(chunks)
        self.flying = [None] * len(chunks)

    @staticmethod
    def heights(shapes, n_s):
        return [
            round_up(sum(shape[2] * shape[3] // 256 for shape in parts), 8 * max(n_s, 2))
            for parts in shapes
        ]

    @staticmethod
    def scratch(shapes, n_a, n_b, n_s):
        n_x = n_b // 2
        result = []
        for parts, rows in zip(shapes, Reducer.heights(shapes, n_s)):
            half = rows // 2
            result += [(shape[0], *shape[2:]) for shape in parts]
            result += [(n_a, n_x, rows, 256)]
            result += [(n_x - 1, n_a, half, 256), (n_a - 1, n_x, half, 256)]
            result += [(n_a - 1, half, 256), (n_x - 1, half, 256)]
            if parts is shapes[-1]:
                result += [(n_s - 1, rows // n_s, 256)]
            else:
                result += [(n_s.bit_length() - 1, half, 256)]
        return result

    @staticmethod
    def copies(shapes, n_a, n_b, n_s):
        each = 2 * (n_b // 2 - 1 + n_a - 1 + n_s - 1)
        return sum(len(parts) + each for parts in shapes)

    def send(self, src, dst, peer):
        return push(src, dst, self.sems, next(self.slots), peer)

    def dp_peers(self):
        peers = []
        for off in range(1, self.n_d):
            there = lax.rem(self.place + off, self.n_d)
            peers.append({"a": lax.div(there, self.n_b), "b": lax.rem(there, self.n_b)})
        return peers

    def s_place(self, off):
        return lax.rem(self.my_s + off, self.n_s)

    def s_peers(self):
        return [{"s": self.s_place(off)} for off in range(1, self.n_s)]

    def spread_small(self, grads, held):
        copies = []
        for slot, peer in enumerate(self.dp_peers()):
            there = lax.rem(self.place + slot + 1, self.n_d)
            source = grads.at[lax.div(there, 2), lax.rem(there, 2)]
            copies.append(self.send(source, held.at[slot], peer))
        return copies

    def tick(self, *names):
        for c in names:
            at = self.at[c]
            if at > len(self.steps[c]):
                continue
            if at > 0:
                wait_all(self.flying[c])
                _, then, arg = self.steps[c][at - 1]
                if then is not None:
                    then(c, arg)
            if at < len(self.steps[c]):
                send, _, arg = self.steps[c][at]
                self.flying[c] = send(c, arg)
            self.at[c] += 1

    def drain(self):
        while any(at <= len(steps) for at, steps in zip(self.at, self.steps)):
            self.tick(*reversed(range(len(self.chunks))))

    def core_send(self, c, _):
        peer = {"b": self.my_b + 1 - 2 * self.core}
        return [
            self.send(item.at[:, 1 - self.core], half, peer)
            for item, half in zip(self.chunks[c], self.halves[c])
        ]

    def core_sum(self, c, _):
        acc, row, n_x = self.accs[c], 0, self.n_x
        for item, half in zip(self.chunks[c], self.halves[c]):
            rows, lanes = item.shape[2:]
            for lane in range(0, lanes, 256):
                cols = slice(lane, lane + 256)
                for j in range(self.n_a * n_x):
                    acc[j // n_x, j % n_x, row : row + rows] = (
                        item[j, self.core, :, cols] + half[j, :, cols]
                    )
                row += rows
        if row < acc.shape[2]:
            for j in range(self.n_a * n_x):
                acc[j // n_x, j % n_x, row:] = jnp.zeros((acc.shape[2] - row, 256), jnp.float32)

    def plane_moves(self, c, stage):
        rows = self.accs[c].shape[2] // 2
        for half in range(2):
            over_x = (half + stage) % 2 == 0
            for off in range(1, self.n_x if over_x else self.n_a):
                buf = (self.one, self.two)[stage][c][half].at[off - 1]
                yield over_x, off, pl.ds(half * rows, rows), buf

    def plane_send(self, c, stage):
        acc, copies = self.accs[c], []
        for over_x, off, rows, buf in self.plane_moves(c, stage):
            if over_x:
                there = lax.rem(self.my_x + off, self.n_x)
                src = acc.at[:, there, rows] if stage == 0 else acc.at[self.my_a, there, rows]
                peer = {"b": 2 * there + self.core}
            else:
                there = lax.rem(self.my_a + off, self.n_a)
                src = acc.at[there, :, rows] if stage == 0 else acc.at[there, self.my_x, rows]
                peer = {"a": there}
            copies.append(self.send(src, buf, peer))
        return copies

    def plane_sum(self, c, stage):
        acc, my_a, my_x = self.accs[c], self.my_a, self.my_x
        for over_x, _, rows, buf in self.plane_moves(c, stage):
            if stage == 1:
                acc[my_a, my_x, rows] += buf[...]
            elif over_x:
                for j in range(self.n_a):
                    acc[j, my_x, rows] += buf[j]
            else:
                for j in range(self.n_x):
                    acc[my_a, j, rows] += buf[j]

    def digit(self, bit):
        return lax.rem(lax.div(self.my_s, 1 << bit), 2)

    def bit_peer(self, bit):
        return {"s": self.my_s + (1 << bit) - 2 * (1 << bit) * self.digit(bit)}

    def span(self, c, level):
        length, start = self.accs[c].shape[2], 0
        for bit in range(level):
            length //= 2
            start = start + self.digit(bit) * length
        return start, length

    def bit_send(self, c, bit):
        start, length = self.span(c, bit)
        length //= 2
        rows = pl.ds(pl.multiple_of(start + (1 - self.digit(bit)) * length, 8), length)
        source = self.accs[c].at[self.my_a, self.my_x, rows]
        return [self.send(source, self.halved[c].at[bit, pl.ds(0, length)], self.bit_peer(bit))]

    def bit_sum(self, c, bit):
        start, length = self.span(c, bit + 1)
        rows = pl.ds(pl.multiple_of(start, 8), length)
        total = self.accs[c][self.my_a, self.my_x, rows] + self.halved[c][bit, :length]
        if bit == self.bits - 1:
            self.outs[c][rows] = total
        else:
            self.accs[c][self.my_a, self.my_x, rows] = total

    def bit_up(self, c, bit):
        start, length = self.span(c, bit + 1)
        rows = self.outs[c].at[pl.ds(pl.multiple_of(start, 8), length)]
        return [self.send(rows, rows, self.bit_peer(bit))]

    def piece(self, c, place):
        length = self.accs[c].shape[2] // self.n_s
        return pl.ds(pl.multiple_of(place * length, 8), length)

    def s_send(self, c, _):
        mine = self.accs[c].at[self.my_a, self.my_x]
        return [
            self.send(mine.at[self.piece(c, self.s_place(slot + 1))], self.bit[c].at[slot], peer)
            for slot, peer in enumerate(self.s_peers())
        ]

    def s_sum(self, c, _):
        rows = self.piece(c, self.my_s)
        total = self.accs[c][self.my_a, self.my_x, rows]
        for slot in range(self.n_s - 1):
            total = total + self.bit[c][slot]
        self.outs[c][rows] = total

    def up_send(self, c, _):
        rows = self.outs[c].at[self.piece(c, self.my_s)]
        return [self.send(rows, rows, peer) for peer in self.s_peers()]


def square_sum(value):
    return jnp.sum((value * value).reshape(value.shape[0] // 8, 8, 256), axis=0)


def adam(grad, state, outs):
    weight, m_old, v_old = (ref[...] for ref in state)
    m_new = BETA_ONE * m_old + (1.0 - BETA_ONE) * grad
    v_new = BETA_TWO * v_old + (1.0 - BETA_TWO) * grad * grad
    step_dir = (
        m_new / (1.0 - BETA_ONE**STEP) / (jnp.sqrt(v_new / (1.0 - BETA_TWO**STEP)) + ADAM_EPS)
    )
    outs[0][...] = weight - RATE * (step_dir + DECAY * weight)
    outs[1][...] = m_new
    outs[2][...] = v_new


def back_kernel(
    n_a, n_b, n_s, d_heads, base, d_mid, joined, proj_t, skip_t, weight_one, weight_two, wide_one, wide_two,
    table_one, table_two, film, hot, extra, gains, taps,
    g_up, g_out, g_down, g_head, gain_mid, loss, *refs,
):
    n_chunk = 5
    shards, (small_out, norm_out) = refs[:n_chunk], refs[n_chunk : n_chunk + 2]
    refs = refs[n_chunk + 2 :]
    d_qkv, shifts, wide, held, edge_b, edge_f, sems, red_sems, blocks = refs[:9]
    g_proj, g_two, g_skip, g_film, g_one, g_small, small_in, small_z = refs[9:17]
    scratch = refs[17:]
    chunks = [[g_down], [g_proj], [g_two], [g_skip, g_film], [g_one]]
    reducer = Reducer(n_a, n_b, n_s, chunks, scratch, shards, red_sems)
    n_pix = base.shape[0]
    ring = Ring(n_b, sems)
    greet(reducer.dp_peers() + reducer.s_peers())
    copies = ring.collect(d_heads, d_qkv)
    reducer.tick(0)
    put_rows(g_proj, 3 * C, g_out[...])
    put_rows(g_proj, 4 * C, g_up[...])
    counts = extra.at[pl.ds(8, 8), pl.ds(0, C)]
    cond = extra[:8, : g_film.shape[3]]
    own = slice(FREQ, FREQ + n_pix)
    normed, inv_std = layer_parts(base[...])
    ln_b = low(normed * gains[4:5] + gains[5:6])
    wait_all(copies)
    put_rows(g_proj, 0, mxu(d_qkv[...], ln_b))
    reducer.tick(1, 0)
    d_ln = mxu(low(proj_t[: 3 * C].astype(jnp.float32).T), d_qkv[...]).T
    sum_gain = [jnp.sum(d_ln * normed, axis=0, keepdims=True), jnp.sum(d_ln, axis=0, keepdims=True)]
    d_base = d_mid[...] + layer_pull(d_ln, normed, inv_std, gains[4:5])
    put_rows(g_skip, 0, mxu(low(d_base.T), joined[...]))
    d_joined = mxu(low(d_base), skip_t[...])
    d_branch = low(d_joined[:, :C])
    edge_b[0] = d_branch[:FREQ]
    edge_b[1] = d_branch[n_pix - FREQ :]
    copies = ring.edges(edge_b.at[0], edge_b.at[1], edge_b.at[2], edge_b.at[3])
    d_stem = d_joined[:, :C] + d_joined[:, C:]

    hot_t, left, right = own_hot(hot, n_pix)
    left_b, right_b = low(left), low(right)
    wide_hot = hot[FREQ : 3 * FREQ + n_pix]
    film_rows = mxu(wide_hot[own], table_parts(film[...]))
    inv_two = mxu(wide_hot, table_parts(table_two[8:]))
    norm_two = (wide_two[...] - mxu(wide_hot, table_parts(table_two[:8]))) * inv_two
    affine = norm_two[own] * gains[2:3] + gains[3:4]
    act = affine * (1.0 + film_rows[:, :C]) + film_rows[:, C:]
    gate = jax.nn.sigmoid(act)
    act_t = low((low(act * gate).astype(jnp.float32)).T)
    wide[own] = d_branch.astype(jnp.float32)
    wait_all(copies)
    reducer.tick(1, 0)
    wide[:FREQ] = edge_b[2].astype(jnp.float32)
    wide[FREQ + n_pix :] = edge_b[3].astype(jnp.float32)
    row_shifts(wide[...], shifts)
    conv_weight_pull(shifts, act_t, g_two, left_b, right_b, n_pix)
    reducer.tick(2, 1, 0)
    d_act = conv_data_pull(shifts, weight_two, left_b, right_b, n_pix)
    d_act = d_act * (gate + act * gate * (1.0 - gate))
    d_film = jnp.concatenate([high(hot_t, d_act * affine), high(hot_t, d_act)], axis=1)
    clip = lax.broadcasted_iota(jnp.int32, d_film.shape, 0)
    d_film = jnp.where(clip < CLIPS, d_film, 0.0)
    put_rows(g_film, 0, high(d_film.T, cond))
    reducer.tick(3, 2, 1, 0)
    d_act = d_act * (1.0 + film_rows[:, :C])
    sum_two = [
        jnp.sum(d_act * norm_two[own], axis=0, keepdims=True),
        jnp.sum(d_act, axis=0, keepdims=True),
    ]
    scaled = d_act * gains[2:3]
    wide[own] = scaled
    edge_f[0] = scaled[:FREQ]
    edge_f[1] = scaled[n_pix - FREQ :]
    copies = ring.edges(edge_f.at[0], edge_f.at[1], edge_f.at[2], edge_f.at[3])
    copies += ring.sums(clip_sums(hot_t, scaled, scaled * norm_two[own]), held.at[0])
    inv_one = mxu(wide_hot[own], table_parts(table_one[8:]))
    norm_one = (wide_one[own] - mxu(wide_hot[own], table_parts(table_one[:8]))) * inv_one
    act = norm_one * gains[0:1] + gains[1:2]
    gate = jax.nn.sigmoid(act)
    act_t = low((low(act * gate).astype(jnp.float32)).T)
    wait_all(copies)
    wide[:FREQ] = edge_f[2]
    wide[FREQ + n_pix :] = edge_f[3]
    mean, slope = group_table(ring.total(held.at[0]), counts[...])
    d_inner = inv_two * (
        wide[...] - mxu(wide_hot, table_parts(mean)) - norm_two * mxu(wide_hot, table_parts(slope))
    )
    row_shifts(low(d_inner).astype(jnp.float32), shifts)
    reducer.tick(3, 2, 1, 0)
    conv_weight_pull(shifts, act_t, g_one, left_b, right_b, n_pix)
    reducer.tick(4, 3, 2, 1, 0)
    d_act = conv_data_pull(shifts, weight_one, left_b, right_b, n_pix)
    d_act = d_act * (gate + act * gate * (1.0 - gate))
    sum_one = [
        jnp.sum(d_act * norm_one, axis=0, keepdims=True),
        jnp.sum(d_act, axis=0, keepdims=True),
    ]
    gain_rows = rows_of(8, sum_one + sum_two + sum_gain)
    scaled = d_act * gains[0:1]
    copies = ring.sums(clip_sums(hot_t, scaled, scaled * norm_one), held.at[1])
    reducer.tick(4, 3, 2, 1, 0)
    wait_all(copies)
    mean, slope = group_table(ring.total(held.at[1]), counts[...])
    hot_own = wide_hot[own]
    d_stem = d_stem + inv_one * (
        scaled - mxu(hot_own, table_parts(mean)) - norm_one * mxu(hot_own, table_parts(slope))
    )
    n_lane = taps.shape[1]
    d_stem = jnp.concatenate(
        [
            jnp.zeros((PAD, C), jnp.bfloat16),
            low(d_stem),
            jnp.zeros((n_lane - n_pix - PAD, C), jnp.bfloat16),
        ],
        axis=0,
    )
    clip = lax.broadcasted_iota(jnp.int32, (8, C), 0)
    gain_rows = jnp.where(clip < 6, gain_rows, pltpu.roll(gain_mid[...], 6, 0))
    lane = lax.broadcasted_iota(jnp.int32, (8, 256), 1)
    first = (clip == 0) & (lane == 0)
    small = [g_head[...], mxu(taps[...], d_stem), gain_rows, jnp.where(first, loss[0:1, 0:1], 0.0)]
    small = jnp.concatenate(small, axis=0)
    put_rows(g_small, 0, fill(small, 2 * g_small.shape[0] * g_small.shape[2]))
    copies = reducer.spread_small(g_small, small_in)
    reducer.tick(4, 3, 2)
    wait_all(copies)
    own_small = g_small[lax.div(reducer.place, 2), lax.rem(reducer.place, 2)]
    for slot in range(reducer.n_d - 1):
        own_small = own_small + small_in[slot]
    small_z[reducer.my_s] = own_small
    here = small_z.at[reducer.my_s]
    copies = [reducer.send(here, here, peer) for peer in reducer.s_peers()]
    reducer.tick(4, 3, 2)
    wait_all(copies)
    own_small = small_z[0]
    for slot in range(1, n_s):
        own_small = own_small + small_z[slot]
    reducer.drain()

    total = jnp.zeros((8, 256), jnp.float32)
    for shard in shards:
        total = total + square_sum(shard[...])
    count = g_small.shape[2]
    row = lax.broadcasted_iota(jnp.int32, (count, 256), 0) + reducer.place * count
    total = total + square_sum(jnp.where(row < 168, own_small, 0.0))
    total = jnp.sum(jnp.sum(total, axis=0, keepdims=True), axis=1, keepdims=True)
    blocks[reducer.place, :count] = own_small
    blocks[reducer.place, count:] = jnp.broadcast_to(total, (8, 256))
    here = blocks.at[reducer.place]
    wait_all([reducer.send(here, here, peer) for peer in reducer.dp_peers()])
    total = blocks[0, count:]
    small_out[:count] = blocks[0, :count]
    for place in range(1, reducer.n_d):
        total = total + blocks[place, count:]
        small_out[count * place : count * (place + 1)] = blocks[place, :count]
    norm_out[...] = jnp.sqrt(total)


def update_kernel(n_b, *refs):
    shards, (small, norm, sums), refs = refs[:5], refs[5:8], refs[8:]
    n_state = 3 * len(STATES)
    state, new_state, scalars = refs[:n_state], refs[n_state : 2 * n_state], refs[2 * n_state :]
    place = lax.axis_index("a") * n_b + lax.axis_index("b")
    factor = jnp.minimum(1.0, CLIP_NORM / norm[0:1, 0:1])
    scalars[0][...] = norm[0:1, 0:1]
    scalars[1][...] = small[168:169, 0:1]
    scalars[2][...] = sums[0:1, 1:2]

    def update(name, grad, part=None):
        first = 3 * STATES.index(name)
        item, new = state[first : first + 3], new_state[first : first + 3]
        if part is not None:
            item, new = [ref.at[part] for ref in item], [ref.at[part] for ref in new]
        adam(grad * factor, item, new)

    def shape(name):
        return state[3 * STATES.index(name)].shape

    def own_lanes(value, count):
        return pltpu.roll(value, (value.shape[1] - place * count) % value.shape[1], 1)[:, :count]

    for part, shard in ((0, shards[4]), (1, shards[2])):
        update("conv", shard[: shape("conv")[1]], part)
    update("proj", shards[1][: shape("proj")[1]].T)
    update("down", shards[0][: shape("down")[0]])
    start = 0
    for name in ("skip", "film"):
        rows = shape(name)[0]
        grads = shards[3][start : start + rows], shards[3][start + rows : start + 2 * rows]
        update(name, jnp.concatenate(grads, axis=1))
        start += 2 * rows
    count = shape("gains")[1]
    update("gains", own_lanes(small[160:168], count))
    stem = jnp.concatenate([small[80:160], jnp.zeros((48, C), jnp.float32)], axis=0)
    stem = own_lanes(stem, count)
    update("stem", stem.T[:, : shape("stem")[1]])
    head = [small[8 * tap : 8 * (tap + 1)] for tap in range(9)]
    update("head", own_lanes(jnp.concatenate(head, axis=1), shape("head")[1]))


def dense(kernel, operands, outs, scratch, collective_id=None):
    vmem = pl.BlockSpec(memory_space=pltpu.VMEM)
    params = dict(vmem_limit_bytes=61 << 20)
    if collective_id is not None:
        params.update(collective_id=collective_id, has_side_effects=True)
    return pl.pallas_call(
        kernel,
        in_specs=[vmem] * len(operands),
        out_specs=[vmem] * len(outs),
        out_shape=[jax.ShapeDtypeStruct(shape, dtype) for shape, dtype in outs],
        scratch_shapes=scratch,
        compiler_params=pltpu.CompilerParams(**params),
    )(*operands)


def body(
    clean_lat,
    noise_lat,
    column_ids,
    timesteps,
    clap_emb,
    conv_w,
    proj_w,
    film_w,
    skip_w,
    down_w,
    stem_w,
    head_w,
    gains,
    conv_m,
    proj_m,
    film_m,
    skip_m,
    down_m,
    stem_m,
    head_m,
    gains_m,
    conv_v,
    proj_v,
    film_v,
    skip_v,
    down_v,
    stem_v,
    head_v,
    gains_v,
):
    bf16, f32 = jnp.bfloat16, jnp.float32
    masters = (conv_w, proj_w, film_w, skip_w, down_w, stem_w, head_w, gains)
    firsts = (conv_m, proj_m, film_m, skip_m, down_m, stem_m, head_m, gains_m)
    seconds = (conv_v, proj_v, film_v, skip_v, down_v, stem_v, head_v, gains_v)
    n_dp, n_s = lax.axis_size(DP), lax.axis_size("s")
    n_a, n_b = lax.axis_size("a"), lax.axis_size("b")
    _, height, n_cols, _ = clean_lat.shape
    n_pix = height * n_cols
    n_lane = frame_of(n_pix)
    proj_cols, down_rows = proj_w.shape[1], down_w.shape[0]
    stem_rows = stem_w.shape[0]

    ids_row = column_ids[0]
    edge_pad = jnp.full((2,), -1, jnp.int32)
    ids_rim = lax.dynamic_slice_in_dim(
        jnp.concatenate([edge_pad, ids_row, edge_pad]), lax.axis_index("s") * n_cols, n_cols + 4
    )
    clip_hot = (ids_rim[:, None] == jnp.arange(CLIPS)[None, :]).astype(f32)
    place = jnp.arange(n_cols + 4)
    inner = (place > 0) & (place < n_cols + 3)
    own = (place > 1) & (place < n_cols + 2)
    same = ids_rim[1:] == ids_rim[:-1]
    off = jnp.zeros((1,), bool)
    cond_vec, alpha_clip, sigma_clip = clip_terms(timesteps[0], clap_emb[0])
    alpha_col = jnp.sum(clip_hot * alpha_clip[None], axis=1)
    sigma_col = jnp.sum(clip_hot * sigma_clip[None], axis=1)
    rows = [
        ids_rim,
        alpha_col,
        sigma_col,
        jnp.sum(clip_hot, axis=1) * inner,
        jnp.concatenate([off, same]),
        jnp.concatenate([same, off]),
        own,
        own,
    ]
    rows = jnp.stack([item.astype(f32) for item in rows])[:, :, None]
    clean, noise = (item[0].transpose(2, 1, 0) for item in (clean_lat, noise_lat))
    alpha, sigma = alpha_col[2:-2][None, :, None], sigma_col[2:-2][None, :, None]
    data = jnp.concatenate([alpha * clean + sigma * noise, alpha * noise - sigma * clean], axis=0)
    main = jnp.concatenate(
        [
            jnp.pad(data, ((0, 0), (2, 2), (0, 0))),
            jnp.broadcast_to(rows, (8, n_cols + 4, height)),
        ],
        axis=0,
    ).reshape(24, -1)
    main = jnp.pad(main, ((0, 0), (0, n_lane - main.shape[1])))
    labels = jnp.arange(8)
    counts = jnp.sum((ids_row[None] == labels[:, None]).astype(f32), axis=1) * (height * C // GROUPS)
    pixel_ids = jnp.repeat(ids_row.astype(f32), height).reshape(8, -1)
    lanes = max(COND, pixel_ids.shape[1])
    extra = [
        jnp.pad(jax.nn.silu(cond_vec).astype(bf16).astype(f32), ((0, 8 - CLIPS), (0, lanes - COND))),
        jnp.broadcast_to(jnp.maximum(counts, 1.0)[:, None], (8, lanes)),
        jnp.pad(pixel_ids, ((0, 0), (0, lanes - pixel_ids.shape[1]))),
    ]
    extra = jnp.concatenate(extra, axis=0)
    front = jnp.concatenate([stem_w, gains], axis=0)
    front = jnp.pad(front, ((0, 128 - front.shape[0]), (0, 0))).T
    shards = [
        front,
        film_w.T,
        skip_w.T,
        conv_w,
        proj_w,
        down_w,
        head_w.T,
    ]
    wholes = [(rows.shape, bf16) for rows in shards]
    wholes[1:1] = [((8, 128), f32)]
    wholes[4:5] = [(conv_w.shape[1:], bf16)] * 2
    wholes[6] = (proj_w.shape[::-1], bf16)
    wholes[8] = (shards[-1].shape, f32)
    wholes = [((n_dp * shape[0], shape[1]), dtype) for shape, dtype in wholes]
    n_wide = n_pix + PAD
    n_heads = 3 * C // n_b
    vmem = pltpu.VMEM

    def sems(count):
        return pltpu.SemaphoreType.DMA((2, count))

    moves = [main, extra]
    edge = ((2 * CIN, 128), f32)
    outs = dense(
        functools.partial(front_kernel, n_a, n_b),
        [*moves, *shards],
        [(item.shape, item.dtype) for item in moves]
        + [edge, edge]
        + wholes
        + [
            ((n_heads, n_b * n_pix), bf16),
            ((n_pix, 2 * C), bf16),
            ((n_pix, C), f32),
            ((n_wide, C), f32),
            ((16, C), f32),
            ((n_wide, C), f32),
            ((16, C), f32),
            ((8, 2 * C), f32),
            ((n_lane, 128), bf16),
            ((80, n_lane), bf16),
            ((8, n_lane), f32),
            ((8, C), f32),
            ((1, n_b * n_pix), jnp.int32),
        ],
        [
            vmem((n_pix, C), f32),
            vmem((n_pix, C), f32),
            vmem((3 * C, n_pix), bf16),
            vmem((3, n_wide, C), bf16),
            vmem((2, n_b, 16, C), f32),
            sems(4 + len(wholes) * (n_dp - 1) + 2 * (n_b + 1) + n_b - 1),
        ],
        0,
    )
    main, extra, _, _ = outs[:4]
    _, counts_all, film_t, skip_t, conv_one, conv_two, proj_t, down_b, head_b = outs[4:13]
    heads_x, joined, base_rows, wide_one, table_one, wide_two, table_two, film = outs[13:21]
    hot, taps, target, gain_f, pixel_ids = outs[21:]
    out_heads, log_total = attention_forward(heads_x, pixel_ids)
    n_hid = down_b.shape[0]
    d_mid, d_heads, g_up, g_down, g_out, g_head, gain_mid, loss = dense(
        functools.partial(middle_kernel, n_b),
        [out_heads, base_rows, proj_t, down_b, head_b, target, main, gain_f, counts_all],
        [
            ((n_pix, C), f32),
            ((C // n_b, n_b * n_pix), bf16),
            ((n_hid, C), f32),
            ((n_hid, C), f32),
            ((C, C), f32),
            ((80, C), f32),
            ((8, C), f32),
            ((8, 128), f32),
        ],
        [
            vmem((C, n_pix), bf16),
            vmem((n_lane, C), bf16),
            vmem((n_hid, n_pix), bf16),
            vmem((n_hid, n_pix), f32),
            vmem((2, PAD, C), bf16),
            vmem((C, n_pix), bf16),
            sems(2 * n_b),
        ],
        1,
    )
    d_heads_x = attention_backward(heads_x, log_total, d_heads, out_heads, pixel_ids)
    pairs = n_dp // 2
    proj_rows, skip_rows, film_rows = proj_w.shape[1], skip_w.shape[1], film_w.shape[1]
    small_rows = round_up(-(-176 // n_dp), 8)
    grads = [
        [(pairs, 2, down_rows, C)],
        [(pairs, 2, proj_rows, C)],
        [(pairs, 2, conv_w.shape[1], C)],
        [(pairs, 2, skip_rows, 2 * C), (pairs, 2, film_rows, COND)],
        [(pairs, 2, conv_w.shape[1], C)],
    ]
    small_shape = (pairs, 2, small_rows, 256)
    heights = Reducer.heights(grads, n_s)
    turn = {"film", "skip", "stem", "head"}
    state = []
    for index, name in enumerate(STATES):
        for group in (masters, firsts, seconds):
            state.append(group[index].T if name in turn else group[index])
    outs = dense(
        functools.partial(back_kernel, n_a, n_b, n_s),
        [
            d_heads_x, base_rows, d_mid, joined, proj_t, skip_t, conv_one, conv_two, wide_one,
            wide_two, table_one, table_two, film, hot, extra, gain_f, taps,
            g_up, g_out, g_down.reshape(grads[0][0]), g_head, gain_mid, loss,
        ],
        [((rows, 256), f32) for rows in heights]
        + [((n_dp * small_rows, 256), f32), ((8, 256), f32)],
        [
            vmem((3 * C, n_pix), bf16),
            vmem((3, n_wide, C), bf16),
            vmem((n_wide, C), f32),
            vmem((2, n_b, 16, C), f32),
            vmem((4, FREQ, C), bf16),
            vmem((4, FREQ, C), f32),
            sems(3 * n_b + 1),
            sems(Reducer.copies(grads, n_a, n_b, n_s) + 2 * (n_dp - 1) + n_s - 1),
            vmem((n_dp, small_rows + 8, 256), f32),
        ]
        + [vmem(shape, f32) for parts in grads[1:] for shape in parts]
        + [vmem(small_shape, f32)]
        + [vmem((count, small_rows, 256), f32) for count in (n_dp - 1, n_s)]
        + [vmem(shape, f32) for shape in Reducer.scratch(grads, n_a, n_b, n_s)],
        2,
    )
    *grad_shards, small, norm = outs
    new_state = dense(
        functools.partial(update_kernel, n_b),
        [*grad_shards, small, norm, loss, *state],
        [(item.shape, f32) for item in state] + [((1, 1), f32)] * 3,
        [],
    )
    new_w, new_m, new_v = {}, {}, {}
    for place, name in enumerate(STATES):
        for kind, group in enumerate((new_w, new_m, new_v)):
            item = new_state[3 * place + kind]
            group[name] = item.T if name in turn else item
    grad_norm, loss_sum, pix_count = (item[0, 0] for item in new_state[3 * len(STATES) :])
    return (
        *[new_w[name] for name in STATES],
        *[new_m[name] for name in STATES],
        *[new_v[name] for name in STATES],
        grad_norm,
        loss_sum,
        pix_count,
    )


def solution(mesh):
    n_dp, n_s = mesh.shape["dp"], mesh.shape["section"]
    blocks = jax.sharding.Mesh(mesh.devices.reshape(n_dp // n_s, n_s, n_s), ("a", "b", "s"))
    return jax.shard_map(
        body,
        mesh=blocks,
        in_specs=(
            P(DP, None, "s", None),
            P(DP, None, "s", None),
            P(DP, None),
            P(DP, None),
            P(DP, None, None),
            P(None, DP, None),
            P(None, DP),
            P(None, DP),
            P(None, DP),
            P(DP, None),
            P(None, DP),
            P(DP, None),
            P(None, DP),
            P(None, DP, None),
            P(None, DP),
            P(None, DP),
            P(None, DP),
            P(DP, None),
            P(None, DP),
            P(DP, None),
            P(None, DP),
            P(None, DP, None),
            P(None, DP),
            P(None, DP),
            P(None, DP),
            P(DP, None),
            P(None, DP),
            P(DP, None),
            P(None, DP),
        ),
        out_specs=(
            P(None, DP, None),
            P(None, DP),
            P(None, DP),
            P(None, DP),
            P(DP, None),
            P(None, DP),
            P(DP, None),
            P(None, DP),
            P(None, DP, None),
            P(None, DP),
            P(None, DP),
            P(None, DP),
            P(DP, None),
            P(None, DP),
            P(DP, None),
            P(None, DP),
            P(None, DP, None),
            P(None, DP),
            P(None, DP),
            P(None, DP),
            P(DP, None),
            P(None, DP),
            P(DP, None),
            P(None, DP),
            P(),
            P(),
            P(),
        ),
        check_vma=False,
    )
```

```python
import functools
import math

import jax
import jax.numpy as jnp
from jax import lax
from jax.experimental import pallas as pl
from jax.experimental.pallas import tpu as pltpu
from jax.sharding import PartitionSpec as P

CIN = 8
C = 256
HEADS = 8
HD = 32
COND = 512
GROUPS = 32
CLIPS = 4
STEP = 10


EPS_NORM = 1e-05
CLIP_NORM = 0.02
DP = ("a", "b")
STATES = ("conv", "proj", "film", "skip", "down", "stem", "head", "gains")
GATHERED = ("front", "count", "film", "skip", "conv0", "conv1", "proj", "down", "head")
RATE = 0.04
BETA_ONE = 0.9
BETA_TWO = 0.999
ADAM_EPS = 1e-08
DECAY = 0.1


def matmul(lhs_mat, rhs_mat):
    return jnp.dot(lhs_mat, rhs_mat, preferred_element_type=jnp.float32)


def clip_terms(timesteps, clap_emb):
    half_cond = COND // 2
    frequency = jnp.exp(-math.log(10000.0) * jnp.arange(half_cond, dtype=jnp.float32) / half_cond)
    angles = timesteps.astype(jnp.float32)[:, None] * frequency[None]
    cond_vec = clap_emb + jnp.concatenate([jnp.sin(angles), jnp.cos(angles)], axis=1)
    theta_clip = 0.5 * math.pi * (timesteps.astype(jnp.float32) + 1.0) / 1001.0
    return (cond_vec, jnp.cos(theta_clip), jnp.sin(theta_clip))


BIG = 1e30
LOG2E = 1.4426950408889634
SCALE = HD**-0.5 * LOG2E
VMEM_LIMIT = 56 << 20
NN = (((1,), (0,)), ((), ()))
NT = (((1,), (1,)), ((), ()))


def mxu(lhs_mat, rhs_mat, dims=NN):
    return lax.dot_general(lhs_mat, rhs_mat, dims, preferred_element_type=jnp.float32)


def split_three(value):
    high = value.astype(jnp.bfloat16).astype(jnp.float32)
    rest = value - high
    mid = rest.astype(jnp.bfloat16).astype(jnp.float32)
    return high, mid, rest - mid


def rows_of(height, parts):
    row = lax.broadcasted_iota(jnp.int32, (height, parts[0].shape[1]), 0)
    total = jnp.zeros(row.shape, jnp.float32)
    for place, part in enumerate(parts):
        total = jnp.where(row == place, part, total)
    return total


def clip_rows(ids, hit, miss):
    return [jnp.where(ids == clip, hit, miss) for clip in range(CLIPS + 1)]


def forward_kernel(bq, bk, x_ref, ids_ref, out_ref, lse_ref, keys, values):
    n_pix = x_ref.shape[1]
    step = pl.program_id(1)

    @pl.when(step == 0)
    def _():
        def prepare(part, carry):
            cols = pl.ds(pl.multiple_of(part * 512, 512), 512)
            key = x_ref[HD : 2 * HD, cols].astype(jnp.float32)
            marks = rows_of(32, clip_rows(ids_ref[:, cols], 1.0, 0.0))
            stack = jnp.concatenate([key, key, key, marks], axis=0)
            keys[cols, :] = stack.T.astype(jnp.bfloat16)
            ones = jnp.ones((16, 512), jnp.bfloat16)
            values[:, cols] = jnp.concatenate([x_ref[2 * HD : 3 * HD, cols], ones], axis=0)
            return carry

        lax.fori_loop(0, n_pix // 512, prepare, 0)

    block = pl.ds(pl.multiple_of(step * bq, bq), bq)
    marks = rows_of(32, clip_rows(ids_ref[:, block], 0.0, -BIG))
    query = split_three(x_ref[:HD, block].astype(jnp.float32) * SCALE)
    query = jnp.concatenate([*query, marks], axis=0).astype(jnp.bfloat16)
    acc = jnp.zeros((HD + 16, bq), jnp.float32)
    row_max = jnp.full((1, bq), -jnp.inf, jnp.float32)
    for start in range(0, n_pix, bk):
        scores = mxu(keys[start : start + bk, :], query)
        new_max = jnp.maximum(row_max, jnp.max(scores, axis=0, keepdims=True))
        probs = jnp.exp2(scores - new_max).astype(jnp.bfloat16)
        acc = acc * jnp.exp2(row_max - new_max) + mxu(values[:, start : start + bk], probs)
        row_max = new_max
    total = acc[HD : HD + 1]
    out_ref[...] = (acc[:HD] / total).astype(jnp.bfloat16)
    lse_ref[...] = jnp.broadcast_to(row_max + jnp.log2(total), (8, bq))


def attention_forward(heads_x, pixel_ids, bq=2048, bk=256):
    lanes, n_pix = heads_x.shape
    heads = lanes // (3 * HD)
    bq, bk = min(bq, n_pix), min(bk, n_pix)
    return pl.pallas_call(
        functools.partial(forward_kernel, bq, bk),
        grid=(heads, n_pix // bq),
        in_specs=[
            pl.BlockSpec((3 * HD, n_pix), lambda h, i: (h, 0)),
            pl.BlockSpec((1, n_pix), lambda h, i: (0, 0)),
        ],
        out_specs=[
            pl.BlockSpec((HD, bq), lambda h, i: (h, i)),
            pl.BlockSpec((8, bq), lambda h, i: (h, i)),
        ],
        out_shape=[
            jax.ShapeDtypeStruct((heads * HD, n_pix), jnp.bfloat16),
            jax.ShapeDtypeStruct((heads * 8, n_pix), jnp.float32),
        ],
        scratch_shapes=[
            pltpu.VMEM((n_pix, 128), jnp.bfloat16),
            pltpu.VMEM((HD + 16, n_pix), jnp.bfloat16),
        ],
        compiler_params=pltpu.CompilerParams(vmem_limit_bytes=VMEM_LIMIT),
    )(heads_x, pixel_ids)


def backward_kernel(
    bq, bk, x_ref, ids_ref, do_ref, o_ref, lse_ref, out_ref,
    queries, keys, values, d_outs, d_query, pair_rows,
):
    n_pix = x_ref.shape[1]
    step = pl.program_id(1)

    @pl.when(step == 0)
    def _():
        d_query[...] = jnp.zeros_like(d_query)

        def prepare(part, carry):
            cols = pl.ds(pl.multiple_of(part * 512, 512), 512)
            ids = ids_ref[:, cols]
            one = jnp.ones((1, 512), jnp.float32)
            zero = jnp.zeros((64, 512), jnp.float32)
            key = x_ref[HD : 2 * HD, cols].astype(jnp.float32)
            marks = rows_of(32, clip_rows(ids, 1.0, 0.0) + [one, one, one])
            stack = jnp.concatenate([key, key, key, marks], axis=0)
            keys[cols, :] = stack.T.astype(jnp.bfloat16)
            value = x_ref[2 * HD : 3 * HD, cols].astype(jnp.float32)
            stack = jnp.concatenate([value, rows_of(32, [one, one, one]), zero], axis=0)
            values[cols, :] = stack.T.astype(jnp.bfloat16)
            query = x_ref[:HD, cols].astype(jnp.float32)
            d_out = do_ref[:, cols].astype(jnp.float32)
            marks = rows_of(32, clip_rows(ids, 0.0, -BIG) + list(split_three(-lse_ref[0:1, cols])))
            stack = jnp.concatenate([*split_three(query * SCALE), marks], axis=0)
            queries[:, cols] = stack.astype(jnp.bfloat16)
            delta = jnp.sum(d_out * o_ref[:, cols].astype(jnp.float32), axis=0, keepdims=True)
            stack = jnp.concatenate([d_out, rows_of(32, split_three(-delta))], axis=0)
            d_outs[:, cols] = stack.astype(jnp.bfloat16)
            stack = jnp.concatenate([query, d_out, zero], axis=0).T.astype(jnp.bfloat16)
            pair_rows[cols, :] = stack
            return carry

        lax.fori_loop(0, n_pix // 512, prepare, 0)

    block = pl.ds(pl.multiple_of(step * bk, bk), bk)
    key, value = keys[block, :], values[block, :64]
    key_t = x_ref[HD : 2 * HD, block]
    d_value = jnp.zeros((bk, 128), jnp.float32)
    d_key = jnp.zeros((bk, 128), jnp.float32)
    for start in range(0, n_pix, bq):
        cols = slice(start, start + bq)
        probs = jnp.exp2(mxu(key, queries[:, cols]))
        d_scores = (probs * mxu(value, d_outs[:, cols])).astype(jnp.bfloat16)
        probs = probs.astype(jnp.bfloat16)
        d_value += mxu(probs, pair_rows[cols, :])
        d_key += mxu(d_scores, pair_rows[cols, :])
        d_query[:, cols] += mxu(key_t, d_scores)
    d_key, d_value = d_key.T[:HD], d_value.T[HD : 2 * HD]
    out_ref[HD : 2 * HD, block] = (d_key * (HD**-0.5)).astype(jnp.bfloat16)
    out_ref[2 * HD : 3 * HD, block] = d_value.astype(jnp.bfloat16)

    @pl.when(step == pl.num_programs(1) - 1)
    def _():
        out_ref[:HD, :] = (d_query[...] * (HD**-0.5)).astype(jnp.bfloat16)


def attention_backward(heads_x, log_total, d_heads, out_heads, pixel_ids, bq=1024, bk=1024):
    lanes, n_pix = heads_x.shape
    heads = lanes // (3 * HD)
    bq, bk = min(bq, n_pix), min(bk, n_pix)

    def rows(count):
        return pl.BlockSpec((count, n_pix), lambda h, i: (h, 0))

    return pl.pallas_call(
        functools.partial(backward_kernel, bq, bk),
        grid=(heads, n_pix // bk),
        in_specs=[
            rows(3 * HD),
            pl.BlockSpec((1, n_pix), lambda h, i: (0, 0)),
            rows(HD),
            rows(HD),
            rows(8),
        ],
        out_specs=rows(3 * HD),
        out_shape=jax.ShapeDtypeStruct((lanes, n_pix), jnp.bfloat16),
        scratch_shapes=[
            pltpu.VMEM((128, n_pix), jnp.bfloat16),
            pltpu.VMEM((n_pix, 128), jnp.bfloat16),
            pltpu.VMEM((n_pix, 128), jnp.bfloat16),
            pltpu.VMEM((64, n_pix), jnp.bfloat16),
            pltpu.VMEM((HD, n_pix), jnp.float32),
            pltpu.VMEM((n_pix, 128), jnp.bfloat16),
        ],
        compiler_params=pltpu.CompilerParams(vmem_limit_bytes=VMEM_LIMIT),
    )(heads_x, pixel_ids, d_heads, out_heads, log_total)


MESH = pl.DeviceIdType.MESH


def round_up(count, unit):
    return -(-count // unit) * unit


def greet(peers):
    barrier = pltpu.get_barrier_semaphore()
    for peer in peers:
        pl.semaphore_signal(barrier, inc=1, device_id=peer, device_id_type=MESH)
    pl.semaphore_wait(barrier, len(peers))


def push(src, dst, sems, slot, peer):
    copy = pltpu.make_async_remote_copy(
        src_ref=src,
        dst_ref=dst,
        send_sem=sems.at[0, slot],
        recv_sem=sems.at[1, slot],
        device_id=peer,
        device_id_type=MESH,
    )
    copy.start()
    return copy


FREQ = 16
PAD = 2 * FREQ
HIGH = lax.Precision.HIGHEST


def high(lhs_mat, rhs_mat, dims=NN):
    return lax.dot_general(
        lhs_mat, rhs_mat, dims, precision=HIGH, preferred_element_type=jnp.float32
    )


def low(value):
    return value.astype(jnp.bfloat16)


def frame_of(n_pix):
    return round_up(n_pix + 2 * PAD, 128)


def lane_taps(value, left, right, sign):
    n_lane = value.shape[1]
    freq = lax.broadcasted_iota(jnp.int32, value.shape, 1) & (FREQ - 1)
    parts = []
    for df in (-1, 0, 1):
        for dc in (-1, 0, 1):
            moved = sign * (FREQ * dc + df)
            part = value if moved == 0 else pltpu.roll(value, (-moved) % n_lane, 1)
            if sign * df < 0:
                part = jnp.where(freq > 0, part, 0.0)
            if sign * df > 0:
                part = jnp.where(freq < FREQ - 1, part, 0.0)
            if sign * dc < 0:
                part = part * left
            if sign * dc > 0:
                part = part * right
            parts.append(part)
    return jnp.concatenate(parts, axis=0)


def fill(value, rows):
    return jnp.concatenate(
        [value, jnp.zeros((rows - value.shape[0], value.shape[1]), value.dtype)], axis=0
    )


def silu(x):
    return x * jax.nn.sigmoid(x)


def table_parts(table):
    return low(fill(jnp.concatenate(split_three(table), axis=0), 128))


def group_table(sums, counts):
    size = C // GROUPS
    row = lax.broadcasted_iota(jnp.int32, (C, C), 0) & (C - size)
    col = lax.broadcasted_iota(jnp.int32, (C, C), 1) & (C - size)
    totals = high(sums, (row == col).astype(jnp.float32))
    return totals[:8] / counts, totals[8:] / counts


def clip_sums(hot_t, one, two):
    return jnp.concatenate([high(hot_t, one), high(hot_t, two)], axis=0)


def hot_rows(ids, rows):
    clip = lax.broadcasted_iota(jnp.int32, (rows, ids.shape[1]), 0)
    return ((clip & 7) == ids) & (clip < 24)


def row_shifts(value, keep):
    n_row = value.shape[0]
    freq = lax.broadcasted_iota(jnp.int32, value.shape, 0) & (FREQ - 1)
    keep[0] = low(jnp.where(freq > 0, pltpu.roll(value, 1, 0), 0.0))
    keep[1] = low(value)
    keep[2] = low(jnp.where(freq < FREQ - 1, pltpu.roll(value, n_row - 1, 0), 0.0))


def conv_rows(shifts, weight, left, right, n_pix):
    total = None
    for dc in range(3):
        part = None
        for df in range(3):
            tap = 3 * df + dc
            item = mxu(shifts[df, FREQ * dc : FREQ * dc + n_pix], weight[C * tap : C * (tap + 1)])
            part = item if part is None else part + item
        part = part if dc == 1 else part * (left if dc == 0 else right)
        total = part if total is None else total + part
    return total


def pull_windows(shifts, left, right, n_pix):
    for df in range(3):
        for dc in range(3):
            at = FREQ * (2 - dc)
            window = shifts[2 - df, at : at + n_pix]
            yield 3 * df + dc, window if dc == 1 else window * (right if dc == 0 else left)


def conv_weight_pull(shifts, act_t, grad, left, right, n_pix):
    for tap, window in pull_windows(shifts, left, right, n_pix):
        put_rows(grad, C * tap, mxu(act_t, window))


def conv_data_pull(shifts, weight, left, right, n_pix):
    total = None
    for tap, window in pull_windows(shifts, left, right, n_pix):
        item = mxu(window, weight[C * tap : C * (tap + 1)], NT)
        total = item if total is None else total + item
    return total


def layer_parts(x):
    centered = x - jnp.mean(x, axis=1, keepdims=True)
    inv_std = lax.rsqrt(jnp.mean(centered * centered, axis=1, keepdims=True) + EPS_NORM)
    return centered * inv_std, inv_std


def layer_pull(d_out, normed, inv_std, gain):
    scaled = d_out * gain
    return inv_std * (
        scaled
        - jnp.mean(scaled, axis=1, keepdims=True)
        - normed * jnp.mean(scaled * normed, axis=1, keepdims=True)
    )


class Ring:
    def __init__(self, n_b, sems, slots=None):
        self.n_b, self.sems = n_b, sems
        self.me = lax.axis_index("b")
        self.slots = iter(range(sems.shape[1])) if slots is None else slots
        self.places = [lax.rem(self.me + off, n_b) for off in range(1, n_b)]
        self.peers = [{"b": place} for place in self.places]

    def send(self, src, dst, peer):
        return push(src, dst, self.sems, next(self.slots), peer)

    def edges(self, first, last, left, right):
        return [self.send(last, left, self.peers[0]), self.send(first, right, self.peers[-1])]

    def sums(self, mine, held):
        held[self.me] = mine
        place = held.at[self.me]
        return [self.send(place, place, peer) for peer in self.peers]

    def total(self, held):
        total = held[0]
        for place in range(1, self.n_b):
            total = total + held[place]
        return total

    def rows_at(self, ref, place):
        count = ref.shape[0] // self.n_b
        return pl.ds(pl.multiple_of(place * count, 16), count)

    def cols_at(self, ref, place):
        count = ref.shape[1] // self.n_b
        return pl.ds(pl.multiple_of(place * count, 128), count)

    def spread(self, make, buf, out):
        copies = []
        for place, peer in zip(self.places, self.peers):
            rows = self.rows_at(buf, place)
            buf[rows] = make(rows)
            copies.append(self.send(buf.at[rows], out.at[:, self.cols_at(out, self.me)], peer))
        rows = self.rows_at(buf, self.me)
        out[:, self.cols_at(out, self.me)] = make(rows)
        return copies

    def collect(self, src, out):
        copies = []
        for place, peer in zip(self.places, self.peers):
            source = src.at[:, self.cols_at(src, place)]
            copies.append(self.send(source, out.at[self.rows_at(out, self.me)], peer))
        out[self.rows_at(out, self.me)] = src[:, self.cols_at(src, self.me)]
        return copies


def wait_all(copies):
    for copy in copies:
        copy.wait()


def own_hot(hot, n_pix):
    own = hot[PAD : PAD + n_pix].astype(jnp.float32)
    return own.T[:8], own[:, 24:25], own[:, 25:26]


def norm_wide(ring, held, wide, counts, hot, table_out):
    mean, square = group_table(ring.total(held), counts[...])
    inv_std = lax.rsqrt(square - mean * mean + EPS_NORM)
    table_out[:8] = mean
    table_out[8:] = inv_std
    return (wide[...] - mxu(hot, table_parts(mean))) * mxu(hot, table_parts(inv_std))


def front_kernel(n_a, n_b, *refs):
    n_move, n_gather = 2, len(GATHERED)
    refs = list(refs)
    moved_in, shards = refs[:n_move], refs[n_move : n_move + n_gather - 2]
    shards[1:1] = [None]
    at_conv = GATHERED.index("conv0")
    both = shards.pop(at_conv)
    shards[at_conv:at_conv] = [both.at[0], both.at[1]]
    refs = refs[n_move + n_gather - 2 :]
    moved, wholes = refs[: n_move + 2], refs[n_move + 2 : n_move + 2 + n_gather]
    refs = refs[n_move + 2 + n_gather :]
    heads_out, joined_out, base_out, wide_one, table_one, wide_two, table_two, film_out = refs[:8]
    hot, taps_out, target_out, gains, pixel_ids = refs[8:13]
    stem_buf, inner_buf, qkv_buf, shifts, held, sems = refs[13:]
    main_in, extra_in = moved_in
    main, extra, left_edge, right_edge = moved
    n_pix, n_lane = base_out.shape[0], main.shape[1]
    my_a, my_b, my_s = lax.axis_index("a"), lax.axis_index("b"), lax.axis_index("s")
    core, my_x = lax.rem(my_b, 2), lax.div(my_b, 2)
    n_x = n_b // 2
    n_d, n_j = n_a * n_b, n_a * n_x
    my_j = my_a * n_x + my_x
    slots = iter(range(sems.shape[1]))
    ring = Ring(n_b, sems, slots)

    def at(b, s):
        return {"b": lax.rem(b + n_b, n_b), "s": lax.rem(s + n_b, n_b)}

    dp_peers = []
    for off in range(1, n_d):
        there = lax.rem(my_a * n_b + my_b + off, n_d)
        dp_peers.append({"a": lax.div(there, n_b), "b": lax.rem(there, n_b)})
    mirrored = my_b != my_s
    shift = jnp.where(mirrored, 0, 1)
    greet(
        dp_peers
        + [at(my_s + 1, my_b), at(my_s - 1, my_b), at(my_s, my_b + 1), at(my_s, my_b - 1)]
        + [at(my_s + shift, my_b + shift)]
    )
    main_slot, extra_slot = next(slots), next(slots)

    @pl.when(mirrored)
    def _():
        push(main_in, main, sems, main_slot, at(my_s, my_b))
        push(extra_in, extra, sems, extra_slot, at(my_s, my_b))

    @pl.when(jnp.logical_not(mirrored))
    def _():
        main[...] = main_in[...]
        extra[...] = extra_in[...]

    end = (PAD + n_pix) // 128 * 128
    first, last = (main_in.at[pl.ds(0, 16), pl.ds(start, 128)] for start in (0, end))
    copies = [
        push(last, left_edge, sems, next(slots), at(my_s + 1, my_b)),
        push(first, right_edge, sems, next(slots), at(my_s - 1, my_b)),
    ]

    def rows_of_shard(whole, j, of_core):
        count = whole.shape[0] // n_d
        return whole.at[pl.ds(pl.multiple_of((2 * j + of_core) * count, 8), count)]

    sibling = {"b": my_b + 1 - 2 * core}
    near, far = {}, {}

    def launch(*names):
        for name in names:
            index = GATHERED.index(name)
            place = rows_of_shard(wholes[index], my_j, core)
            own = None if name == "count" else shards[index][...]
            if name == "count":
                known = extra_in[16:24, : pixel_ids.shape[1] // 8]
                known = jnp.sum(jnp.where(known < CLIPS, 1.0 * CIN, 0.0), axis=0, keepdims=True)
                own = jnp.broadcast_to(jnp.sum(known, axis=1, keepdims=True), place.shape)
            if name == "head":
                own = low(own)
            place[...] = (own.T if name == "proj" else own).astype(place.dtype)
            near[name] = []
            for off in range(1, n_j):
                there = lax.rem(my_j + off, n_j)
                peer = {"a": lax.div(there, n_x), "b": 2 * lax.rem(there, n_x) + core}
                near[name].append(push(place, place, sems, next(slots), peer))
            far[name] = [push(place, place, sems, next(slots), sibling)]

    def forward(*names):
        for name in names:
            whole = wholes[GATHERED.index(name)]
            for off, copy in enumerate(near[name]):
                copy.wait()
                rows = rows_of_shard(whole, lax.rem(my_j + n_j - off - 1, n_j), core)
                far[name].append(push(rows, rows, sems, next(slots), sibling))

    def arrived(*names):
        for name in names:
            wait_all(far[name])

    part = dict(zip(GATHERED, wholes))
    launch("front", "count", "conv0", "film")
    forward("front", "count")
    wait_all(copies)

    @pl.when(mirrored)
    def _():
        for source, target, slot in ((main_in, main, main_slot), (extra_in, extra, extra_slot)):
            pltpu.make_async_remote_copy(
                src_ref=source,
                dst_ref=target,
                send_sem=sems.at[0, slot],
                recv_sem=sems.at[1, slot],
                device_id=at(my_s, my_b),
                device_id_type=MESH,
            ).wait()

    lane = lax.broadcasted_iota(jnp.int32, (16, 128), 1)
    is_left, is_right = (lane >= FREQ) & (lane < PAD), (lane >= PAD) & (lane < PAD + FREQ)
    main[:16, :128] = jnp.where(is_left, left_edge[...], main[:16, :128])
    main[:16, end : end + 128] = jnp.where(is_right, right_edge[...], main[:16, end : end + 128])
    rows = main[16:24]
    ids, left, right = rows[0:1], rows[4:5], rows[5:6]
    target_out[...] = main[8:16]
    n_id = pixel_ids.shape[1] // 8
    for row in range(8):
        line = extra[16 + row : 17 + row, :n_id]
        pixel_ids[:, n_id * row : n_id * (row + 1)] = line.astype(jnp.int32)
    taps = lane_taps(low(main[:8]).astype(jnp.float32), left, right, 1)
    taps = fill(taps, 128)
    taps_out[...] = low(taps[:80])
    clip = lax.broadcasted_iota(jnp.int32, (128, n_lane), 0)
    marks = hot_rows(ids.astype(jnp.int32), 128).astype(jnp.float32)
    marks = marks + jnp.where(clip == 24, left, 0.0) + jnp.where(clip == 25, right, 0.0)
    hot[...] = low(marks.T)
    hot_t, left, right = own_hot(hot, n_pix)
    wide_hot = hot[FREQ : 3 * FREQ + n_pix]
    taps = low(taps.T)[PAD : PAD + n_pix]
    arrived("front", "count")
    stem_w = part["front"][...]
    gains[...] = stem_w.astype(jnp.float32).T[72:80]
    stem = mxu(taps, stem_w, NT)
    stem_buf[...] = stem
    counts = extra.at[pl.ds(8, 8), pl.ds(0, C)]

    copies = ring.edges(
        stem_buf.at[pl.ds(0, FREQ)],
        stem_buf.at[pl.ds(n_pix - FREQ, FREQ)],
        wide_one.at[pl.ds(0, FREQ)],
        wide_one.at[pl.ds(n_pix + FREQ, FREQ)],
    )
    copies += ring.sums(clip_sums(hot_t, stem, stem * stem), held.at[0])
    wide_one[FREQ : FREQ + n_pix] = stem
    forward("conv0", "film")
    wait_all(copies)
    launch("conv1", "skip")
    normed = norm_wide(ring, held.at[0], wide_one, counts, wide_hot, table_one)
    row_shifts(low(silu(normed * gains[0:1] + gains[1:2])).astype(jnp.float32), shifts)
    arrived("conv0")
    inner = conv_rows(shifts, part["conv0"], left, right, n_pix)
    inner_buf[...] = inner

    copies = ring.edges(
        inner_buf.at[pl.ds(0, FREQ)],
        inner_buf.at[pl.ds(n_pix - FREQ, FREQ)],
        wide_two.at[pl.ds(0, FREQ)],
        wide_two.at[pl.ds(n_pix + FREQ, FREQ)],
    )
    copies += ring.sums(clip_sums(hot_t, inner, inner * inner), held.at[1])
    wide_two[FREQ : FREQ + n_pix] = inner
    forward("conv1", "skip")
    arrived("film")
    film = mxu(low(extra[:8, : part["film"].shape[1]]), part["film"][...], NT)
    film_out[...] = film
    film_rows = mxu(wide_hot, table_parts(film))
    wait_all(copies)
    launch("proj", "down", "head")
    normed = norm_wide(ring, held.at[1], wide_two, counts, wide_hot, table_two)
    act = (normed * gains[2:3] + gains[3:4]) * (1.0 + film_rows[:, :C]) + film_rows[:, C:]
    row_shifts(low(silu(act)).astype(jnp.float32), shifts)
    arrived("conv1", "skip")
    branch = conv_rows(shifts, part["conv1"], left, right, n_pix)

    forward("proj")
    stem = stem_buf[...]
    joined_out[:, :C] = low(stem + branch)
    joined_out[:, C:] = low(stem)
    base = mxu(joined_out[...], part["skip"][...], NT)
    base_out[...] = base
    normed, _ = layer_parts(base)
    normed = low(normed * gains[4:5] + gains[5:6])
    arrived("proj")
    forward("down", "head")
    copies = ring.spread(lambda rows: low(mxu(part["proj"][rows], normed, NT)), qkv_buf, heads_out)
    arrived("down", "head")
    wait_all(copies)


def middle_kernel(
    n_b, heads, base, proj_t, down, head, target, main, gains, counts,
    d_mid_out, d_heads_out, g_up, g_down, g_out, g_head, g_gains, loss_out,
    attended, wide, act_t, pull_t, edge, d_att_buf, sems,
):
    n_pix = base.shape[0]
    n_lane = target.shape[1]
    n_hid = down.shape[0]
    ring = Ring(n_b, sems)
    greet(ring.peers)
    copies = ring.collect(heads, attended)
    rows = main[16:24]
    pix_count = jnp.sum(counts[:, 0:1], axis=0, keepdims=True) * 0.125
    blocks = [head[8 * place : 8 * (place + 1)] for place in range(head.shape[0] // 8)]
    blocks = jnp.concatenate(blocks, axis=1)
    blocks = [blocks[:, C * tap : C * (tap + 1)] for tap in range(9)]
    head_t = low(fill(jnp.concatenate(blocks, axis=0), 80))
    wait_all(copies)
    proj_out, proj_up = proj_t.at[pl.ds(3 * C, C)], proj_t.at[pl.ds(4 * C, n_hid)]
    mid = base[...] + mxu(low(attended[...].astype(jnp.float32).T), proj_out[...], NT)
    normed, inv_std = layer_parts(mid)
    ln_b = low(normed * gains[6:7] + gains[7:8])
    top_t = jnp.zeros((C, n_pix), jnp.float32)
    scale = math.sqrt(2.0 / math.pi)
    for start in range(0, n_hid, 256):
        part = slice(start, start + 256)
        hidden = mxu(proj_up[part], ln_b, NT)
        bend = jnp.tanh(scale * (hidden + 0.044715 * hidden * hidden * hidden))
        gate = 0.5 * (1.0 + bend)
        act = low(hidden * gate)
        act_t[part] = act
        pull_t[part] = gate + 0.5 * hidden * (1.0 - bend * bend) * scale * (
            1.0 + 3.0 * 0.044715 * hidden * hidden
        )
        top_t = top_t + mxu(low(down[part].astype(jnp.float32).T), act)
    top = low(mid + top_t.T)
    wide[PAD : PAD + n_pix] = top
    wide[2 * PAD + n_pix :] = jnp.zeros((n_lane - 2 * PAD - n_pix, C), jnp.bfloat16)
    edge[0] = top[:PAD]
    edge[1] = top[n_pix - PAD :]
    copies = ring.edges(
        edge.at[0], edge.at[1], wide.at[pl.ds(0, PAD)], wide.at[pl.ds(PAD + n_pix, PAD)]
    )
    wait_all(copies)
    left, right, valid, own = rows[4:5], rows[5:6], rows[3:4], rows[6:7]
    products = mxu(head_t, wide[...], NT)
    freq = lax.broadcasted_iota(jnp.int32, (8, n_lane), 1) & (FREQ - 1)
    pred = jnp.zeros((8, n_lane), jnp.float32)
    for df in (-1, 0, 1):
        for dc in (-1, 0, 1):
            tap = 3 * (df + 1) + dc + 1
            moved = FREQ * dc + df
            part = products[8 * tap : 8 * (tap + 1)]
            part = part if moved == 0 else pltpu.roll(part, (-moved) % n_lane, 1)
            if df != 0:
                part = jnp.where(freq > 0 if df < 0 else freq < FREQ - 1, part, 0.0)
            if dc != 0:
                part = part * (left if dc < 0 else right)
            pred = pred + part
    residue = jnp.where(valid > 0.0, pred - target[...], 0.0)
    loss = jnp.sum(own * residue * residue, axis=0, keepdims=True)
    lane = lax.broadcasted_iota(jnp.int32, (8, 128), 1)
    loss_out[...] = jnp.where(lane == 1, pix_count, jnp.sum(loss, axis=1, keepdims=True))
    d_pred = low(2.0 * residue / pix_count).astype(jnp.float32)
    taps = lane_taps(d_pred, left, right, -1) * own
    taps = fill(taps, 128)
    g_head[...] = mxu(low(taps[:80]), wide[...])
    d_top = mxu(low(taps.T)[PAD : PAD + n_pix], fill(head_t, 128))
    d_top_b = low(d_top)
    d_ln_t = jnp.zeros((C, n_pix), jnp.float32)
    for start in range(0, n_hid, 256):
        part = slice(start, start + 256)
        d_hidden = low(mxu(down[part], d_top_b, NT) * pull_t[part])
        g_up[part] = mxu(d_hidden, ln_b)
        g_down[part] = mxu(act_t[part], d_top_b)
        d_ln_t = d_ln_t + mxu(low(proj_up[part].astype(jnp.float32).T), d_hidden)
    d_ln = d_ln_t.T
    g_gains[...] = rows_of(
        8, [jnp.sum(d_ln * normed, axis=0, keepdims=True), jnp.sum(d_ln, axis=0, keepdims=True)]
    )
    d_mid = d_top + layer_pull(d_ln, normed, inv_std, gains[6:7])
    d_mid_out[...] = d_mid
    d_mid_b = low(d_mid)
    g_out[...] = mxu(attended[...], d_mid_b).T
    d_att_buf[...] = low(mxu(low(proj_out[...].astype(jnp.float32).T), d_mid_b, NT))
    wait_all(ring.spread(lambda rows: d_att_buf[rows], d_att_buf, d_heads_out))


def put_rows(ref, start, value):
    height = ref.shape[2]
    at = 0
    while at < value.shape[0]:
        shard, row = divmod(start + at, height)
        count = min(height - row, value.shape[0] - at)
        ref[shard // 2, shard % 2, row : row + count] = value[at : at + count]
        at += count


class Reducer:
    def __init__(self, n_a, n_b, n_s, chunks, scratch, outs, sems):
        self.n_a, self.n_b, self.n_x, self.n_s = n_a, n_b, n_b // 2, n_s
        self.bits = n_s.bit_length() - 1
        self.chunks, self.outs, self.sems = chunks, outs, sems
        self.slots = iter(range(sems.shape[1]))
        scratch = list(scratch)
        self.halves, self.accs, self.one, self.two, self.bit, self.halved = [], [], [], [], [], []
        for parts in chunks:
            self.halves.append([scratch.pop(0) for _ in parts])
            self.accs.append(scratch.pop(0))
            self.one.append([scratch.pop(0) for _ in range(2)])
            self.two.append([scratch.pop(0) for _ in range(2)])
            self.bit.append(scratch[0])
            self.halved.append(scratch.pop(0))
        self.my_a, self.my_b, self.my_s = (lax.axis_index(axis) for axis in ("a", "b", "s"))
        self.core, self.my_x = lax.rem(self.my_b, 2), lax.div(self.my_b, 2)
        self.place = self.my_a * n_b + self.my_b
        self.n_d = n_a * n_b
        plane = [(self.core_send, self.core_sum, 0)]
        plane += [(self.plane_send, self.plane_sum, stage) for stage in range(2)]
        halving = [(self.bit_send, self.bit_sum, bit) for bit in range(self.bits)]
        halving += [(self.bit_up, None, bit) for bit in reversed(range(self.bits))]
        direct = [(self.s_send, self.s_sum, 0), (self.up_send, None, 0)]
        self.steps = [plane + halving for _ in chunks[1:]] + [plane + direct]
        self.at = [0] * len(chunks)
        self.flying = [None] * len(chunks)

    @staticmethod
    def heights(shapes, n_s):
        return [
            round_up(sum(shape[2] * shape[3] // 256 for shape in parts), 8 * max(n_s, 2))
            for parts in shapes
        ]

    @staticmethod
    def scratch(shapes, n_a, n_b, n_s):
        n_x = n_b // 2
        result = []
        for parts, rows in zip(shapes, Reducer.heights(shapes, n_s)):
            half = rows // 2
            result += [(shape[0], *shape[2:]) for shape in parts]
            result += [(n_a, n_x, rows, 256)]
            result += [(n_x - 1, n_a, half, 256), (n_a - 1, n_x, half, 256)]
            result += [(n_a - 1, half, 256), (n_x - 1, half, 256)]
            if parts is shapes[-1]:
                result += [(n_s - 1, rows // n_s, 256)]
            else:
                result += [(n_s.bit_length() - 1, half, 256)]
        return result

    @staticmethod
    def copies(shapes, n_a, n_b, n_s):
        each = 2 * (n_b // 2 - 1 + n_a - 1 + n_s - 1)
        return sum(len(parts) + each for parts in shapes)

    def send(self, src, dst, peer):
        return push(src, dst, self.sems, next(self.slots), peer)

    def dp_peers(self):
        peers = []
        for off in range(1, self.n_d):
            there = lax.rem(self.place + off, self.n_d)
            peers.append({"a": lax.div(there, self.n_b), "b": lax.rem(there, self.n_b)})
        return peers

    def s_place(self, off):
        return lax.rem(self.my_s + off, self.n_s)

    def s_peers(self):
        return [{"s": self.s_place(off)} for off in range(1, self.n_s)]

    def spread_small(self, grads, held):
        copies = []
        for slot, peer in enumerate(self.dp_peers()):
            there = lax.rem(self.place + slot + 1, self.n_d)
            source = grads.at[lax.div(there, 2), lax.rem(there, 2)]
            copies.append(self.send(source, held.at[slot], peer))
        return copies

    def tick(self, *names):
        for c in names:
            at = self.at[c]
            if at > len(self.steps[c]):
                continue
            if at > 0:
                wait_all(self.flying[c])
                _, then, arg = self.steps[c][at - 1]
                if then is not None:
                    then(c, arg)
            if at < len(self.steps[c]):
                send, _, arg = self.steps[c][at]
                self.flying[c] = send(c, arg)
            self.at[c] += 1

    def drain(self):
        while any(at <= len(steps) for at, steps in zip(self.at, self.steps)):
            self.tick(*reversed(range(len(self.chunks))))

    def core_send(self, c, _):
        peer = {"b": self.my_b + 1 - 2 * self.core}
        return [
            self.send(item.at[:, 1 - self.core], half, peer)
            for item, half in zip(self.chunks[c], self.halves[c])
        ]

    def core_sum(self, c, _):
        acc, row, n_x = self.accs[c], 0, self.n_x
        for item, half in zip(self.chunks[c], self.halves[c]):
            rows, lanes = item.shape[2:]
            for lane in range(0, lanes, 256):
                cols = slice(lane, lane + 256)
                for j in range(self.n_a * n_x):
                    acc[j // n_x, j % n_x, row : row + rows] = (
                        item[j, self.core, :, cols] + half[j, :, cols]
                    )
                row += rows
        if row < acc.shape[2]:
            for j in range(self.n_a * n_x):
                acc[j // n_x, j % n_x, row:] = jnp.zeros((acc.shape[2] - row, 256), jnp.float32)

    def plane_moves(self, c, stage):
        rows = self.accs[c].shape[2] // 2
        for half in range(2):
            over_x = (half + stage) % 2 == 0
            for off in range(1, self.n_x if over_x else self.n_a):
                buf = (self.one, self.two)[stage][c][half].at[off - 1]
                yield over_x, off, pl.ds(half * rows, rows), buf

    def plane_send(self, c, stage):
        acc, copies = self.accs[c], []
        for over_x, off, rows, buf in self.plane_moves(c, stage):
            if over_x:
                there = lax.rem(self.my_x + off, self.n_x)
                src = acc.at[:, there, rows] if stage == 0 else acc.at[self.my_a, there, rows]
                peer = {"b": 2 * there + self.core}
            else:
                there = lax.rem(self.my_a + off, self.n_a)
                src = acc.at[there, :, rows] if stage == 0 else acc.at[there, self.my_x, rows]
                peer = {"a": there}
            copies.append(self.send(src, buf, peer))
        return copies

    def plane_sum(self, c, stage):
        acc, my_a, my_x = self.accs[c], self.my_a, self.my_x
        for over_x, _, rows, buf in self.plane_moves(c, stage):
            if stage == 1:
                acc[my_a, my_x, rows] += buf[...]
            elif over_x:
                for j in range(self.n_a):
                    acc[j, my_x, rows] += buf[j]
            else:
                for j in range(self.n_x):
                    acc[my_a, j, rows] += buf[j]

    def digit(self, bit):
        return lax.rem(lax.div(self.my_s, 1 << bit), 2)

    def bit_peer(self, bit):
        return {"s": self.my_s + (1 << bit) - 2 * (1 << bit) * self.digit(bit)}

    def span(self, c, level):
        length, start = self.accs[c].shape[2], 0
        for bit in range(level):
            length //= 2
            start = start + self.digit(bit) * length
        return start, length

    def bit_send(self, c, bit):
        start, length = self.span(c, bit)
        length //= 2
        rows = pl.ds(pl.multiple_of(start + (1 - self.digit(bit)) * length, 8), length)
        source = self.accs[c].at[self.my_a, self.my_x, rows]
        return [self.send(source, self.halved[c].at[bit, pl.ds(0, length)], self.bit_peer(bit))]

    def bit_sum(self, c, bit):
        start, length = self.span(c, bit + 1)
        rows = pl.ds(pl.multiple_of(start, 8), length)
        total = self.accs[c][self.my_a, self.my_x, rows] + self.halved[c][bit, :length]
        if bit == self.bits - 1:
            self.outs[c][rows] = total
        else:
            self.accs[c][self.my_a, self.my_x, rows] = total

    def bit_up(self, c, bit):
        start, length = self.span(c, bit + 1)
        rows = self.outs[c].at[pl.ds(pl.multiple_of(start, 8), length)]
        return [self.send(rows, rows, self.bit_peer(bit))]

    def piece(self, c, place):
        length = self.accs[c].shape[2] // self.n_s
        return pl.ds(pl.multiple_of(place * length, 8), length)

    def s_send(self, c, _):
        mine = self.accs[c].at[self.my_a, self.my_x]
        return [
            self.send(mine.at[self.piece(c, self.s_place(slot + 1))], self.bit[c].at[slot], peer)
            for slot, peer in enumerate(self.s_peers())
        ]

    def s_sum(self, c, _):
        rows = self.piece(c, self.my_s)
        total = self.accs[c][self.my_a, self.my_x, rows]
        for slot in range(self.n_s - 1):
            total = total + self.bit[c][slot]
        self.outs[c][rows] = total

    def up_send(self, c, _):
        rows = self.outs[c].at[self.piece(c, self.my_s)]
        return [self.send(rows, rows, peer) for peer in self.s_peers()]


def square_sum(value):
    return jnp.sum((value * value).reshape(value.shape[0] // 8, 8, 256), axis=0)


def adam(grad, state, outs):
    weight, m_old, v_old = (ref[...] for ref in state)
    m_new = BETA_ONE * m_old + (1.0 - BETA_ONE) * grad
    v_new = BETA_TWO * v_old + (1.0 - BETA_TWO) * grad * grad
    step_dir = (
        m_new / (1.0 - BETA_ONE**STEP) / (jnp.sqrt(v_new / (1.0 - BETA_TWO**STEP)) + ADAM_EPS)
    )
    outs[0][...] = weight - RATE * (step_dir + DECAY * weight)
    outs[1][...] = m_new
    outs[2][...] = v_new


def back_kernel(
    n_a, n_b, n_s, d_heads, base, d_mid, joined, proj_t, skip_t, weight_one, weight_two, wide_one, wide_two,
    table_one, table_two, film, hot, extra, gains, taps,
    g_up, g_out, g_down, g_head, gain_mid, loss, *refs,
):
    n_chunk = 5
    shards, (small_out, norm_out) = refs[:n_chunk], refs[n_chunk : n_chunk + 2]
    refs = refs[n_chunk + 2 :]
    d_qkv, shifts, wide, held, edge_b, edge_f, sems, red_sems, blocks = refs[:9]
    g_proj, g_two, g_skip, g_film, g_one, g_small, small_in, small_z = refs[9:17]
    scratch = refs[17:]
    chunks = [[g_down], [g_proj], [g_two], [g_skip, g_film], [g_one]]
    reducer = Reducer(n_a, n_b, n_s, chunks, scratch, shards, red_sems)
    n_pix = base.shape[0]
    ring = Ring(n_b, sems)
    greet(reducer.dp_peers() + reducer.s_peers())
    copies = ring.collect(d_heads, d_qkv)
    reducer.tick(0)
    put_rows(g_proj, 3 * C, g_out[...])
    put_rows(g_proj, 4 * C, g_up[...])
    counts = extra.at[pl.ds(8, 8), pl.ds(0, C)]
    cond = extra[:8, : g_film.shape[3]]
    own = slice(FREQ, FREQ + n_pix)
    normed, inv_std = layer_parts(base[...])
    ln_b = low(normed * gains[4:5] + gains[5:6])
    wait_all(copies)
    put_rows(g_proj, 0, mxu(d_qkv[...], ln_b))
    reducer.tick(1, 0)
    d_ln = mxu(low(proj_t[: 3 * C].astype(jnp.float32).T), d_qkv[...]).T
    sum_gain = [jnp.sum(d_ln * normed, axis=0, keepdims=True), jnp.sum(d_ln, axis=0, keepdims=True)]
    d_base = d_mid[...] + layer_pull(d_ln, normed, inv_std, gains[4:5])
    put_rows(g_skip, 0, mxu(low(d_base.T), joined[...]))
    d_joined = mxu(low(d_base), skip_t[...])
    d_branch = low(d_joined[:, :C])
    edge_b[0] = d_branch[:FREQ]
    edge_b[1] = d_branch[n_pix - FREQ :]
    copies = ring.edges(edge_b.at[0], edge_b.at[1], edge_b.at[2], edge_b.at[3])
    d_stem = d_joined[:, :C] + d_joined[:, C:]

    hot_t, left, right = own_hot(hot, n_pix)
    left_b, right_b = low(left), low(right)
    wide_hot = hot[FREQ : 3 * FREQ + n_pix]
    film_rows = mxu(wide_hot[own], table_parts(film[...]))
    inv_two = mxu(wide_hot, table_parts(table_two[8:]))
    norm_two = (wide_two[...] - mxu(wide_hot, table_parts(table_two[:8]))) * inv_two
    affine = norm_two[own] * gains[2:3] + gains[3:4]
    act = affine * (1.0 + film_rows[:, :C]) + film_rows[:, C:]
    gate = jax.nn.sigmoid(act)
    act_t = low((low(act * gate).astype(jnp.float32)).T)
    wide[own] = d_branch.astype(jnp.float32)
    wait_all(copies)
    reducer.tick(1, 0)
    wide[:FREQ] = edge_b[2].astype(jnp.float32)
    wide[FREQ + n_pix :] = edge_b[3].astype(jnp.float32)
    row_shifts(wide[...], shifts)
    conv_weight_pull(shifts, act_t, g_two, left_b, right_b, n_pix)
    reducer.tick(2, 1, 0)
    d_act = conv_data_pull(shifts, weight_two, left_b, right_b, n_pix)
    reducer.tick(2, 1, 0)
    d_act = d_act * (gate + act * gate * (1.0 - gate))
    d_film = jnp.concatenate([high(hot_t, d_act * affine), high(hot_t, d_act)], axis=1)
    clip = lax.broadcasted_iota(jnp.int32, d_film.shape, 0)
    d_film = jnp.where(clip < CLIPS, d_film, 0.0)
    put_rows(g_film, 0, high(d_film.T, cond))
    reducer.tick(3, 2, 1, 0)
    d_act = d_act * (1.0 + film_rows[:, :C])
    sum_two = [
        jnp.sum(d_act * norm_two[own], axis=0, keepdims=True),
        jnp.sum(d_act, axis=0, keepdims=True),
    ]
    scaled = d_act * gains[2:3]
    wide[own] = scaled
    edge_f[0] = scaled[:FREQ]
    edge_f[1] = scaled[n_pix - FREQ :]
    copies = ring.edges(edge_f.at[0], edge_f.at[1], edge_f.at[2], edge_f.at[3])
    copies += ring.sums(clip_sums(hot_t, scaled, scaled * norm_two[own]), held.at[0])
    inv_one = mxu(wide_hot[own], table_parts(table_one[8:]))
    norm_one = (wide_one[own] - mxu(wide_hot[own], table_parts(table_one[:8]))) * inv_one
    act = norm_one * gains[0:1] + gains[1:2]
    gate = jax.nn.sigmoid(act)
    act_t = low((low(act * gate).astype(jnp.float32)).T)
    wait_all(copies)
    wide[:FREQ] = edge_f[2]
    wide[FREQ + n_pix :] = edge_f[3]
    mean, slope = group_table(ring.total(held.at[0]), counts[...])
    d_inner = inv_two * (
        wide[...] - mxu(wide_hot, table_parts(mean)) - norm_two * mxu(wide_hot, table_parts(slope))
    )
    row_shifts(low(d_inner).astype(jnp.float32), shifts)
    reducer.tick(3, 2, 1, 0)
    conv_weight_pull(shifts, act_t, g_one, left_b, right_b, n_pix)
    reducer.tick(4, 3, 2, 1, 0)
    d_act = conv_data_pull(shifts, weight_one, left_b, right_b, n_pix)
    reducer.tick(3, 2, 1, 0)
    d_act = d_act * (gate + act * gate * (1.0 - gate))
    sum_one = [
        jnp.sum(d_act * norm_one, axis=0, keepdims=True),
        jnp.sum(d_act, axis=0, keepdims=True),
    ]
    gain_rows = rows_of(8, sum_one + sum_two + sum_gain)
    scaled = d_act * gains[0:1]
    copies = ring.sums(clip_sums(hot_t, scaled, scaled * norm_one), held.at[1])
    reducer.tick(4, 3, 2, 1, 0)
    wait_all(copies)
    mean, slope = group_table(ring.total(held.at[1]), counts[...])
    hot_own = wide_hot[own]
    d_stem = d_stem + inv_one * (
        scaled - mxu(hot_own, table_parts(mean)) - norm_one * mxu(hot_own, table_parts(slope))
    )
    n_lane = taps.shape[1]
    d_stem = jnp.concatenate(
        [
            jnp.zeros((PAD, C), jnp.bfloat16),
            low(d_stem),
            jnp.zeros((n_lane - n_pix - PAD, C), jnp.bfloat16),
        ],
        axis=0,
    )
    clip = lax.broadcasted_iota(jnp.int32, (8, C), 0)
    gain_rows = jnp.where(clip < 6, gain_rows, pltpu.roll(gain_mid[...], 6, 0))
    lane = lax.broadcasted_iota(jnp.int32, (8, 256), 1)
    first = (clip == 0) & (lane == 0)
    small = [g_head[...], mxu(taps[...], d_stem), gain_rows, jnp.where(first, loss[0:1, 0:1], 0.0)]
    small = jnp.concatenate(small, axis=0)
    put_rows(g_small, 0, fill(small, 2 * g_small.shape[0] * g_small.shape[2]))
    copies = reducer.spread_small(g_small, small_in)
    reducer.tick(4, 3, 2)
    wait_all(copies)
    own_small = g_small[lax.div(reducer.place, 2), lax.rem(reducer.place, 2)]
    for slot in range(reducer.n_d - 1):
        own_small = own_small + small_in[slot]
    small_z[reducer.my_s] = own_small
    here = small_z.at[reducer.my_s]
    copies = [reducer.send(here, here, peer) for peer in reducer.s_peers()]
    reducer.tick(4, 3, 2)
    wait_all(copies)
    own_small = small_z[0]
    for slot in range(1, n_s):
        own_small = own_small + small_z[slot]
    reducer.drain()

    total = jnp.zeros((8, 256), jnp.float32)
    for shard in shards:
        total = total + square_sum(shard[...])
    count = g_small.shape[2]
    row = lax.broadcasted_iota(jnp.int32, (count, 256), 0) + reducer.place * count
    total = total + square_sum(jnp.where(row < 168, own_small, 0.0))
    total = jnp.sum(jnp.sum(total, axis=0, keepdims=True), axis=1, keepdims=True)
    blocks[reducer.place, :count] = own_small
    blocks[reducer.place, count:] = jnp.broadcast_to(total, (8, 256))
    here = blocks.at[reducer.place]
    wait_all([reducer.send(here, here, peer) for peer in reducer.dp_peers()])
    total = blocks[0, count:]
    small_out[:count] = blocks[0, :count]
    for place in range(1, reducer.n_d):
        total = total + blocks[place, count:]
        small_out[count * place : count * (place + 1)] = blocks[place, :count]
    norm_out[...] = jnp.sqrt(total)


def update_kernel(n_b, *refs):
    shards, (small, norm, sums), refs = refs[:5], refs[5:8], refs[8:]
    n_state = 3 * len(STATES)
    state, new_state, scalars = refs[:n_state], refs[n_state : 2 * n_state], refs[2 * n_state :]
    place = lax.axis_index("a") * n_b + lax.axis_index("b")
    factor = jnp.minimum(1.0, CLIP_NORM / norm[0:1, 0:1])
    scalars[0][...] = norm[0:1, 0:1]
    scalars[1][...] = small[168:169, 0:1]
    scalars[2][...] = sums[0:1, 1:2]

    def update(name, grad, part=None):
        first = 3 * STATES.index(name)
        item, new = state[first : first + 3], new_state[first : first + 3]
        if part is not None:
            item, new = [ref.at[part] for ref in item], [ref.at[part] for ref in new]
        adam(grad * factor, item, new)

    def shape(name):
        return state[3 * STATES.index(name)].shape

    def own_lanes(value, count):
        return pltpu.roll(value, (value.shape[1] - place * count) % value.shape[1], 1)[:, :count]

    for part, shard in ((0, shards[4]), (1, shards[2])):
        update("conv", shard[: shape("conv")[1]], part)
    update("proj", shards[1][: shape("proj")[1]].T)
    update("down", shards[0][: shape("down")[0]])
    start = 0
    for name in ("skip", "film"):
        rows = shape(name)[0]
        grads = shards[3][start : start + rows], shards[3][start + rows : start + 2 * rows]
        update(name, jnp.concatenate(grads, axis=1))
        start += 2 * rows
    count = shape("gains")[1]
    update("gains", own_lanes(small[160:168], count))
    stem = jnp.concatenate([small[80:160], jnp.zeros((48, C), jnp.float32)], axis=0)
    stem = own_lanes(stem, count)
    update("stem", stem.T[:, : shape("stem")[1]])
    head = [small[8 * tap : 8 * (tap + 1)] for tap in range(9)]
    update("head", own_lanes(jnp.concatenate(head, axis=1), shape("head")[1]))


def dense(kernel, operands, outs, scratch, collective_id=None):
    vmem = pl.BlockSpec(memory_space=pltpu.VMEM)
    params = dict(vmem_limit_bytes=61 << 20)
    if collective_id is not None:
        params.update(collective_id=collective_id, has_side_effects=True)
    return pl.pallas_call(
        kernel,
        in_specs=[vmem] * len(operands),
        out_specs=[vmem] * len(outs),
        out_shape=[jax.ShapeDtypeStruct(shape, dtype) for shape, dtype in outs],
        scratch_shapes=scratch,
        compiler_params=pltpu.CompilerParams(**params),
    )(*operands)


def body(
    clean_lat,
    noise_lat,
    column_ids,
    timesteps,
    clap_emb,
    conv_w,
    proj_w,
    film_w,
    skip_w,
    down_w,
    stem_w,
    head_w,
    gains,
    conv_m,
    proj_m,
    film_m,
    skip_m,
    down_m,
    stem_m,
    head_m,
    gains_m,
    conv_v,
    proj_v,
    film_v,
    skip_v,
    down_v,
    stem_v,
    head_v,
    gains_v,
):
    bf16, f32 = jnp.bfloat16, jnp.float32
    masters = (conv_w, proj_w, film_w, skip_w, down_w, stem_w, head_w, gains)
    firsts = (conv_m, proj_m, film_m, skip_m, down_m, stem_m, head_m, gains_m)
    seconds = (conv_v, proj_v, film_v, skip_v, down_v, stem_v, head_v, gains_v)
    n_dp, n_s = lax.axis_size(DP), lax.axis_size("s")
    n_a, n_b = lax.axis_size("a"), lax.axis_size("b")
    _, height, n_cols, _ = clean_lat.shape
    n_pix = height * n_cols
    n_lane = frame_of(n_pix)
    proj_cols, down_rows = proj_w.shape[1], down_w.shape[0]
    stem_rows = stem_w.shape[0]

    ids_row = column_ids[0]
    edge_pad = jnp.full((2,), -1, jnp.int32)
    ids_rim = lax.dynamic_slice_in_dim(
        jnp.concatenate([edge_pad, ids_row, edge_pad]), lax.axis_index("s") * n_cols, n_cols + 4
    )
    clip_hot = (ids_rim[:, None] == jnp.arange(CLIPS)[None, :]).astype(f32)
    place = jnp.arange(n_cols + 4)
    inner = (place > 0) & (place < n_cols + 3)
    own = (place > 1) & (place < n_cols + 2)
    same = ids_rim[1:] == ids_rim[:-1]
    off = jnp.zeros((1,), bool)
    cond_vec, alpha_clip, sigma_clip = clip_terms(timesteps[0], clap_emb[0])
    alpha_col = jnp.sum(clip_hot * alpha_clip[None], axis=1)
    sigma_col = jnp.sum(clip_hot * sigma_clip[None], axis=1)
    rows = [
        ids_rim,
        alpha_col,
        sigma_col,
        jnp.sum(clip_hot, axis=1) * inner,
        jnp.concatenate([off, same]),
        jnp.concatenate([same, off]),
        own,
        own,
    ]
    rows = jnp.stack([item.astype(f32) for item in rows])[:, :, None]
    clean, noise = (item[0].transpose(2, 1, 0) for item in (clean_lat, noise_lat))
    alpha, sigma = alpha_col[2:-2][None, :, None], sigma_col[2:-2][None, :, None]
    data = jnp.concatenate([alpha * clean + sigma * noise, alpha * noise - sigma * clean], axis=0)
    main = jnp.concatenate(
        [
            jnp.pad(data, ((0, 0), (2, 2), (0, 0))),
            jnp.broadcast_to(rows, (8, n_cols + 4, height)),
        ],
        axis=0,
    ).reshape(24, -1)
    main = jnp.pad(main, ((0, 0), (0, n_lane - main.shape[1])))
    labels = jnp.arange(8)
    counts = jnp.sum((ids_row[None] == labels[:, None]).astype(f32), axis=1) * (height * C // GROUPS)
    pixel_ids = jnp.repeat(ids_row.astype(f32), height).reshape(8, -1)
    lanes = max(COND, pixel_ids.shape[1])
    extra = [
        jnp.pad(jax.nn.silu(cond_vec).astype(bf16).astype(f32), ((0, 8 - CLIPS), (0, lanes - COND))),
        jnp.broadcast_to(jnp.maximum(counts, 1.0)[:, None], (8, lanes)),
        jnp.pad(pixel_ids, ((0, 0), (0, lanes - pixel_ids.shape[1]))),
    ]
    extra = jnp.concatenate(extra, axis=0)
    front = jnp.concatenate([stem_w, gains], axis=0)
    front = jnp.pad(front, ((0, 128 - front.shape[0]), (0, 0))).T
    shards = [
        front,
        film_w.T,
        skip_w.T,
        conv_w,
        proj_w,
        down_w,
        head_w.T,
    ]
    wholes = [(rows.shape, bf16) for rows in shards]
    wholes[1:1] = [((8, 128), f32)]
    wholes[4:5] = [(conv_w.shape[1:], bf16)] * 2
    wholes[6] = (proj_w.shape[::-1], bf16)
    wholes[8] = (shards[-1].shape, f32)
    wholes = [((n_dp * shape[0], shape[1]), dtype) for shape, dtype in wholes]
    n_wide = n_pix + PAD
    n_heads = 3 * C // n_b
    vmem = pltpu.VMEM

    def sems(count):
        return pltpu.SemaphoreType.DMA((2, count))

    moves = [main, extra]
    edge = ((2 * CIN, 128), f32)
    outs = dense(
        functools.partial(front_kernel, n_a, n_b),
        [*moves, *shards],
        [(item.shape, item.dtype) for item in moves]
        + [edge, edge]
        + wholes
        + [
            ((n_heads, n_b * n_pix), bf16),
            ((n_pix, 2 * C), bf16),
            ((n_pix, C), f32),
            ((n_wide, C), f32),
            ((16, C), f32),
            ((n_wide, C), f32),
            ((16, C), f32),
            ((8, 2 * C), f32),
            ((n_lane, 128), bf16),
            ((80, n_lane), bf16),
            ((8, n_lane), f32),
            ((8, C), f32),
            ((1, n_b * n_pix), jnp.int32),
        ],
        [
            vmem((n_pix, C), f32),
            vmem((n_pix, C), f32),
            vmem((3 * C, n_pix), bf16),
            vmem((3, n_wide, C), bf16),
            vmem((2, n_b, 16, C), f32),
            sems(4 + len(wholes) * (n_dp - 1) + 2 * (n_b + 1) + n_b - 1),
        ],
        0,
    )
    main, extra, _, _ = outs[:4]
    _, counts_all, film_t, skip_t, conv_one, conv_two, proj_t, down_b, head_b = outs[4:13]
    heads_x, joined, base_rows, wide_one, table_one, wide_two, table_two, film = outs[13:21]
    hot, taps, target, gain_f, pixel_ids = outs[21:]
    out_heads, log_total = attention_forward(heads_x, pixel_ids)
    n_hid = down_b.shape[0]
    d_mid, d_heads, g_up, g_down, g_out, g_head, gain_mid, loss = dense(
        functools.partial(middle_kernel, n_b),
        [out_heads, base_rows, proj_t, down_b, head_b, target, main, gain_f, counts_all],
        [
            ((n_pix, C), f32),
            ((C // n_b, n_b * n_pix), bf16),
            ((n_hid, C), f32),
            ((n_hid, C), f32),
            ((C, C), f32),
            ((80, C), f32),
            ((8, C), f32),
            ((8, 128), f32),
        ],
        [
            vmem((C, n_pix), bf16),
            vmem((n_lane, C), bf16),
            vmem((n_hid, n_pix), bf16),
            vmem((n_hid, n_pix), f32),
            vmem((2, PAD, C), bf16),
            vmem((C, n_pix), bf16),
            sems(2 * n_b),
        ],
        1,
    )
    d_heads_x = attention_backward(heads_x, log_total, d_heads, out_heads, pixel_ids)
    pairs = n_dp // 2
    proj_rows, skip_rows, film_rows = proj_w.shape[1], skip_w.shape[1], film_w.shape[1]
    small_rows = round_up(-(-176 // n_dp), 8)
    grads = [
        [(pairs, 2, down_rows, C)],
        [(pairs, 2, proj_rows, C)],
        [(pairs, 2, conv_w.shape[1], C)],
        [(pairs, 2, skip_rows, 2 * C), (pairs, 2, film_rows, COND)],
        [(pairs, 2, conv_w.shape[1], C)],
    ]
    small_shape = (pairs, 2, small_rows, 256)
    heights = Reducer.heights(grads, n_s)
    turn = {"film", "skip", "stem", "head"}
    state = []
    for index, name in enumerate(STATES):
        for group in (masters, firsts, seconds):
            state.append(group[index].T if name in turn else group[index])
    outs = dense(
        functools.partial(back_kernel, n_a, n_b, n_s),
        [
            d_heads_x, base_rows, d_mid, joined, proj_t, skip_t, conv_one, conv_two, wide_one,
            wide_two, table_one, table_two, film, hot, extra, gain_f, taps,
            g_up, g_out, g_down.reshape(grads[0][0]), g_head, gain_mid, loss,
        ],
        [((rows, 256), f32) for rows in heights]
        + [((n_dp * small_rows, 256), f32), ((8, 256), f32)],
        [
            vmem((3 * C, n_pix), bf16),
            vmem((3, n_wide, C), bf16),
            vmem((n_wide, C), f32),
            vmem((2, n_b, 16, C), f32),
            vmem((4, FREQ, C), bf16),
            vmem((4, FREQ, C), f32),
            sems(3 * n_b + 1),
            sems(Reducer.copies(grads, n_a, n_b, n_s) + 2 * (n_dp - 1) + n_s - 1),
            vmem((n_dp, small_rows + 8, 256), f32),
        ]
        + [vmem(shape, f32) for parts in grads[1:] for shape in parts]
        + [vmem(small_shape, f32)]
        + [vmem((count, small_rows, 256), f32) for count in (n_dp - 1, n_s)]
        + [vmem(shape, f32) for shape in Reducer.scratch(grads, n_a, n_b, n_s)],
        2,
    )
    *grad_shards, small, norm = outs
    new_state = dense(
        functools.partial(update_kernel, n_b),
        [*grad_shards, small, norm, loss, *state],
        [(item.shape, f32) for item in state] + [((1, 1), f32)] * 3,
        [],
    )
    new_w, new_m, new_v = {}, {}, {}
    for place, name in enumerate(STATES):
        for kind, group in enumerate((new_w, new_m, new_v)):
            item = new_state[3 * place + kind]
            group[name] = item.T if name in turn else item
    grad_norm, loss_sum, pix_count = (item[0, 0] for item in new_state[3 * len(STATES) :])
    return (
        *[new_w[name] for name in STATES],
        *[new_m[name] for name in STATES],
        *[new_v[name] for name in STATES],
        grad_norm,
        loss_sum,
        pix_count,
    )


def solution(mesh):
    n_dp, n_s = mesh.shape["dp"], mesh.shape["section"]
    blocks = jax.sharding.Mesh(mesh.devices.reshape(n_dp // n_s, n_s, n_s), ("a", "b", "s"))
    return jax.shard_map(
        body,
        mesh=blocks,
        in_specs=(
            P(DP, None, "s", None),
            P(DP, None, "s", None),
            P(DP, None),
            P(DP, None),
            P(DP, None, None),
            P(None, DP, None),
            P(None, DP),
            P(None, DP),
            P(None, DP),
            P(DP, None),
            P(None, DP),
            P(DP, None),
            P(None, DP),
            P(None, DP, None),
            P(None, DP),
            P(None, DP),
            P(None, DP),
            P(DP, None),
            P(None, DP),
            P(DP, None),
            P(None, DP),
            P(None, DP, None),
            P(None, DP),
            P(None, DP),
            P(None, DP),
            P(DP, None),
            P(None, DP),
            P(DP, None),
            P(None, DP),
        ),
        out_specs=(
            P(None, DP, None),
            P(None, DP),
            P(None, DP),
            P(None, DP),
            P(DP, None),
            P(None, DP),
            P(DP, None),
            P(None, DP),
            P(None, DP, None),
            P(None, DP),
            P(None, DP),
            P(None, DP),
            P(DP, None),
            P(None, DP),
            P(DP, None),
            P(None, DP),
            P(None, DP, None),
            P(None, DP),
            P(None, DP),
            P(None, DP),
            P(DP, None),
            P(None, DP),
            P(DP, None),
            P(None, DP),
            P(),
            P(),
            P(),
        ),
        check_vma=False,
    )
```
